32 devices in a mesh: section: 4 (over y, x), dp: 4 (over z), mp: 2 (over core).
Axes of the slice: x: 2, y: 2, z: 4, core: 2. Of those that a mesh axis runs over, the one named last changes fastest.
Arguments:
- inputs: bfloat16 [8, 256, 1536], P('dp', 'mp'), may hold values from -6 to 6
- cotangent: bfloat16 [8, 256, 1536], P('dp', 'mp'), may hold values from -6 to 6
- width_index: int32 [8], P('dp'), may hold values from 0 to 3, as said below
- qkv_weight: bfloat16 [3, 3072, 1536], P(None, 'section', 'mp'), may hold values from -0.15625 to 0.15625
- out_weight: bfloat16 [3072, 1536], P('section', 'mp'), may hold values from -1.75 to 1.75
- attn_gain: bfloat16 [3072], P('section'), may hold values from 0.5 to 1.5
- ffn_gain: bfloat16 [3072], P('section'), may hold values from 0.5 to 1.5
- up_weight: bfloat16 [3072, 6144], P('section', 'mp'), may hold values from -0.15625 to 0.15625
- down_weight: bfloat16 [3072, 6144], P('section', 'mp'), may hold values from -0.15625 to 0.15625
Outputs:
- layer_out: bfloat16 [4, 8, 256, 1536], P('section', 'dp', 'mp')
- input_grad: bfloat16 [4, 8, 256, 1536], P('section', 'dp', 'mp')
- qkv_grad: float32 [3, 3072, 1536], P(None, ('section', 'dp'), 'mp')
- out_weight_grad: float32 [3072, 1536], P(('section', 'dp'), 'mp')
- attn_gain_grad: float32 [3072], P(('section', 'dp', 'mp'))
- ffn_gain_grad: float32 [3072], P(('section', 'dp', 'mp'))
- up_grad: float32 [3072, 6144], P(('section', 'dp'), 'mp')
- down_grad: float32 [3072, 6144], P(('section', 'dp'), 'mp')
The draws below stay inside these ranges and needn't reach their ends.
Inputs may be any that keep to these rules, and one draw needn't show every extreme that they name: `width_index`: in each aligned pair of sequences (2i and 2i+1) the two width indices add up to 3.
All inputs are finite; a program needn't handle non-finite values.
Results may differ from the reference program's by a relative error of at most 0.03.
Values may be sent and summed in bfloat16 or wider, within the bound.
A program may use at most 384 MiB of HBM per device.

```python
import jax
import jax.numpy as jnp
from jax import lax

D = 1536
HEADS = 12
HEAD_DIM = 128
FF = 6144
SEQ_LEN = 256
LAYERS = 2
SEQS = 8
N_SECTION = 4
N_MP = 2


def draw_width_index(key, part):
    key = jax.random.fold_in(key, 7)
    leading = jax.random.randint(key, (SEQS // 2,), 0, 4)
    corner = 3 * jax.random.randint(jax.random.fold_in(key, 1), (), 0, 2)
    leading = leading.at[0].set(corner)
    paired = jnp.stack([leading, 3 - leading], axis=1)
    return paired.reshape(SEQS).astype(jnp.int32)


def raised(result, key, source, target, shards_of, factor):
    owner, partner = [(jnp.arange(result.shape[axis_at]) // (result.shape[axis_at] // shards_of)).reshape([-1 if axis == axis_at else 1 for axis in range(result.ndim)]) for axis_at in (source, target)]
    chosen = jax.random.permutation(key, shards_of)[partner]
    strong = (owner == chosen) | (owner == (partner + shards_of // 2) % shards_of)
    return jnp.where(strong, factor * result, result)


def block_scale(key, extent, split, least, top_value):
    def one(axis_at, shards_of):
        draws = jax.random.uniform(jax.random.fold_in(jax.random.fold_in(key, 6), axis_at), (shards_of,), jnp.float32, least / len(split), top_value / len(split))
        return jnp.repeat(jnp.exp(draws), extent[axis_at] // shards_of).reshape((-1,) + (1,) * (len(extent) - axis_at - 1))

    gain = one(*split[0])
    for cut in split[1:]:
        gain = gain * one(*cut)
    return gain


def noise(own_key, dims, spread, limit, cuts=(), kind=jnp.bfloat16):
    loudness = block_scale(own_key, dims, cuts, -0.22, 0.18) if cuts else 1.0
    entries = jax.random.normal(own_key, dims, jnp.float32) * spread * loudness
    return jnp.minimum(jnp.maximum(entries, -limit), limit).astype(kind)


def noise_with(rng, extent, spread, bound, cuts, heavy, kind=jnp.bfloat16):
    result = spread * jax.random.normal(rng, extent, jnp.float32)
    if cuts:
        result = result * block_scale(rng, extent, cuts, -0.22, 0.18)
    return jnp.clip(raised(result, jax.random.fold_in(rng, 3), *heavy), -bound, bound).astype(kind)


def setup_inputs(seed: int = 0) -> dict:
    keys = jax.random.split(jax.random.key(seed), 10)
    inputs = noise_with(keys[0], (SEQS, SEQ_LEN, D), 1.0, 6.0, ((0, 4), (1, 2)), (0, 2, 4, 2.0))
    cotangent = noise_with(keys[1], (SEQS, SEQ_LEN, D), 1.0, 6.0, ((0, 4), (1, 2)), (0, 2, 4, 2.0))
    width_index = draw_width_index(jax.random.fold_in(keys[9], 71), 0)
    qkv_weight = noise(keys[3], (3, LAYERS * D, D), D ** -0.5, 0.15625, ((1, 4), (2, 2)))
    out_weight = noise(keys[4], (LAYERS * D, D), (max(D // 128, 4)) ** -0.5, 1.75, ((0, 4), (1, 2)))
    attn_gain = jnp.clip(1.0 + 0.1 * jax.random.normal(keys[5], (LAYERS * D,), jnp.float32), 0.5, 1.5).astype(jnp.bfloat16)
    ffn_gain = jnp.clip(1.0 + 0.1 * jax.random.normal(keys[6], (LAYERS * D,), jnp.float32), 0.5, 1.5).astype(jnp.bfloat16)
    up_weight = noise(keys[7], (LAYERS * D, FF), D ** -0.5, 0.15625, ((0, 4), (1, 2)))
    down_weight = noise(keys[8], (LAYERS * D, FF), (FF // 4) ** -0.5, 0.15625, ((0, 4), (1, 2)))
    return {"inputs": inputs, "cotangent": cotangent, "width_index": width_index, "qkv_weight": qkv_weight, "out_weight": out_weight, "attn_gain": attn_gain, "ffn_gain": ffn_gain, "up_weight": up_weight, "down_weight": down_weight}


EPSILON = 1e-05
HIGHEST = lax.Precision.HIGHEST

@jax.custom_vjp
def low(v):
    return lax.optimization_barrier(v.astype(jnp.bfloat16)).astype(jnp.float32)

@jax.custom_vjp
def low_back(v):
    return v

def low_keep(v):
    return (low(v), None)

def low_pass(kept, grad):
    return (grad,)

def back_keep(v):
    return (v, None)

def back_low(kept, grad):
    return (low(grad),)
low.defvjp(low_keep, low_pass)
low_back.defvjp(back_keep, back_low)

def product(left, right):
    return jnp.dot(left, right, precision=HIGHEST, preferred_element_type=jnp.float32)

def rotary(length):
    half_dim = HEAD_DIM // 2
    frequency = 10000.0 ** (-2.0 * jnp.arange(half_dim, dtype=jnp.float32) / HEAD_DIM)
    angles = jnp.arange(length, dtype=jnp.float32)[:, None] * frequency[None, :]
    cosine = jnp.concatenate([jnp.cos(angles), jnp.cos(angles)], axis=1)[:, None, :]
    sine_tab = jnp.concatenate([jnp.sin(angles), jnp.sin(angles)], axis=1)[:, None, :]
    return (cosine, sine_tab)

def turn_half(values):
    half_dim = values.shape[-1] // 2
    return jnp.concatenate([-values[..., half_dim:], values[..., :half_dim]], axis=-1)

def rotate(values, cosine, sine_tab):
    return values * cosine + turn_half(values) * sine_tab

def normalize(values, gain_row):
    return values * lax.rsqrt(lax.optimization_barrier(jnp.mean(values * values, axis=-1, keepdims=True)) + EPSILON) * gain_row

def attention_sublayer(current, qkv_w, out_w, gain_attn, cosine, sine_tab):
    length = current.shape[0]
    head_shape = (length, HEADS, HEAD_DIM)
    normed = low(normalize(current, gain_attn))
    queries = low(rotate(low_back(product(normed, qkv_w[0])).reshape(head_shape), cosine, sine_tab))
    all_keys = low(rotate(low_back(product(normed, qkv_w[1])).reshape(head_shape), cosine, sine_tab))
    all_values = low_back(low(product(normed, qkv_w[2]))).reshape(head_shape)
    scores = low_back(jnp.einsum('qhd,khd->hqk', queries, all_keys, precision=HIGHEST) * HEAD_DIM ** (-0.5))
    causal = jnp.arange(length)[:, None] >= jnp.arange(length)[None, :]
    scores = jnp.where(causal[None], scores, -1e+30)
    highest = lax.optimization_barrier(jnp.max(scores, axis=-1, keepdims=True))
    exponent = jnp.exp(scores - highest)
    probabilities = exponent / lax.optimization_barrier(jnp.sum(exponent, axis=-1, keepdims=True))
    mixture = jnp.einsum('hqk,khd->qhd', low(probabilities), all_values, precision=HIGHEST)
    mixture = low_back(low(mixture.reshape(length, D)))
    pieces = jnp.einsum('lrc,drc->rld', mixture.reshape(length, N_MP, D // N_MP), out_w.reshape(D, N_MP, D // N_MP), precision=HIGHEST)
    return low(current + low_back(lax.optimization_barrier(jnp.sum(low(pieces), axis=0))))

def ffn_sublayer(current, up_w, down_w, gain_ffn, chosen):
    length = current.shape[0]
    normed_ffn = low(normalize(current, gain_ffn))
    hidden = low_back(product(normed_ffn, up_w))
    columns = jnp.arange(FF) % (FF // N_MP)
    multiple = jnp.array([1, 2, 4, 8], dtype=jnp.int32)[chosen]
    active = (columns < FF // 8 // N_MP * multiple).astype(jnp.float32)
    activation = low(jax.nn.gelu(hidden, approximate=True)) * active
    pieces_ffn = jnp.einsum('lrc,drc->rld', activation.reshape(length, N_MP, FF // N_MP), down_w.reshape(D, N_MP, FF // N_MP), precision=HIGHEST)
    return low(current + low_back(lax.optimization_barrier(jnp.sum(low(pieces_ffn), axis=0))))

def per_sequence(start_row, shifts, chosen, layers, cosine, sine_tab):
    qkv_all, out_all, gain_attn, gain_ffn, up_all, down_all = layers
    current = start_row
    results = []
    for depth in range(LAYERS):
        current = current + shifts[2 * depth]
        current = attention_sublayer(current, qkv_all[:, depth], out_all[depth], gain_attn[depth], cosine, sine_tab)
        results.append(current)
        current = current + shifts[2 * depth + 1]
        current = ffn_sublayer(current, up_all[depth], down_all[depth], gain_ffn[depth], chosen)
        results.append(current)
    return jnp.stack(results)

def reference(inputs, cotangent, width_index, qkv_weight, out_weight, attn_gain, ffn_gain, up_weight, down_weight):
    cosine, sine_tab = rotary(SEQ_LEN)
    params = tuple((weight.astype(jnp.float32) for weight in (qkv_weight, out_weight, attn_gain, ffn_gain, up_weight, down_weight)))
    starts = inputs.astype(jnp.float32)
    offsets = jnp.zeros((SEQS, N_SECTION, SEQ_LEN, D), jnp.float32)

    def whole_model(weights, shifts):
        layers = (weights[0].reshape(3, LAYERS, D, D), weights[1].reshape(LAYERS, D, D), weights[2].reshape(LAYERS, D), weights[3].reshape(LAYERS, D), weights[4].reshape(LAYERS, D, FF), weights[5].reshape(LAYERS, D, FF))

        def one_sequence(member):
            return per_sequence(member[0], member[1], member[2], layers, cosine, sine_tab)
        return lax.map(jax.checkpoint(one_sequence), (starts, shifts, width_index))
    outputs, pullback = jax.vjp(whole_model, params, offsets)
    seed_grad = jnp.zeros_like(outputs).at[:, N_SECTION - 1].set(cotangent.astype(jnp.float32))
    grad_params, grad_offsets = pullback(seed_grad)
    layer_out = jnp.transpose(outputs, (1, 0, 2, 3)).astype(jnp.bfloat16)
    input_grad = jnp.transpose(grad_offsets, (1, 0, 2, 3)).astype(jnp.bfloat16)
    return (layer_out, input_grad, grad_params[0], grad_params[1], grad_params[2], grad_params[3], grad_params[4], grad_params[5])
```

```python
import jax
import jax.numpy as jnp
from jax import lax
from jax.sharding import PartitionSpec as P
from jax.experimental import pallas as pl
from jax.experimental.pallas import tpu as pltpu

HEAD_DIM = 128
EPSILON = 1e-05
GELU_C = 0.7978845608028654
GELU_A = 0.044715
MESH = pl.DeviceIdType.MESH
SLOTS = 9
F32 = jnp.float32
BF16 = jnp.bfloat16
VMEM_LIMIT = 60 * 2**20

FWD_RELAYED = ()
BWD_RELAYED = ()


def mm(a, b):
    return lax.dot_general(a, b, (((1,), (0,)), ((), ())), preferred_element_type=F32)


def mm_nt(a, b):
    return lax.dot_general(a, b, (((1,), (1,)), ((), ())), preferred_element_type=F32)


def mm_tn(a, b):
    return lax.dot_general(a, b, (((0,), (0,)), ((), ())), preferred_element_type=F32)


def to_row(column):
    rows = column.shape[0]
    return jnp.transpose(jnp.broadcast_to(column, (rows, 128)))[:8]


def from_row(row):
    return jnp.transpose(row)[:, :1]


def rotary(length, head_size):
    half_dim = head_size // 2
    frequency = 10000.0 ** (-2.0 * jnp.arange(half_dim, dtype=F32) / head_size)
    angles = jnp.arange(length, dtype=F32)[:, None] * frequency[None, :]
    cosine = jnp.concatenate([jnp.cos(angles), jnp.cos(angles)], axis=1)
    sine = jnp.concatenate([-jnp.sin(angles), jnp.sin(angles)], axis=1)
    return cosine, sine


def turned(values):
    return pltpu.roll(values, HEAD_DIM // 2, 1)


def remote(src, dst, send_sem, recv_sem, device):
    return pltpu.make_async_remote_copy(
        src_ref=src, dst_ref=dst, send_sem=send_sem, recv_sem=recv_sem,
        device_id=device, device_id_type=MESH,
    )


class Place:
    def __init__(self):
        section, dp, mp = (lax.axis_index(name) for name in ("section", "dp", "mp"))
        self.block, self.half, self.core = section // 2, section % 2, mp
        other_half = 1 - self.half
        other_block = 1 - self.block
        self.core_peer = (section, dp, 1 - mp)
        self.pair = (self.block * 2 + other_half, dp, mp)
        self.across = (other_block * 2 + self.half, dp, mp)
        self.corner = (other_block * 2 + other_half, dp, mp)

    def barrier(self):
        sem = pltpu.get_barrier_semaphore()
        peers = (self.core_peer, self.pair, self.across, self.corner)
        for peer in peers:
            pl.semaphore_signal(sem, inc=1, device_id=peer, device_id_type=MESH)
        pl.semaphore_wait(sem, len(peers))


class PairLink:
    def __init__(self, place, relayed, relay, send, recv, relay_send, relay_recv, targets):
        self.place, self.relayed, self.relay = place, relayed, relay
        self.send_sem, self.recv_sem = send, recv
        self.relay_send, self.relay_recv = relay_send, relay_recv
        self.targets = targets
        self.started = []

    def start(self, index, src):
        if index in self.relayed:
            at = self.relayed.index(index)
            copy = remote(src, self.relay.at[at], self.send_sem.at[index], self.relay_recv.at[at], self.place.across)
        else:
            copy = remote(src, self.targets(index, self.place.half), self.send_sem.at[index], self.recv_sem.at[index], self.place.pair)
        copy.start()
        self.started.append(copy)

    def wait(self, index):
        dst = self.targets(index, 1 - self.place.half)
        remote(dst, dst, self.send_sem.at[index], self.recv_sem.at[index], self.place.pair).wait_recv()

    def finish(self):
        for copy in self.started:
            copy.wait_send()
        self.started = []

    def forward(self, indices):
        copies = []
        for index in indices:
            if index not in self.relayed:
                continue
            at = self.relayed.index(index)
            held = self.relay.at[at]
            remote(held, held, self.relay_send.at[at], self.relay_recv.at[at], self.place.across).wait_recv()
            copy = remote(held, self.targets(index, self.place.half), self.relay_send.at[at], self.recv_sem.at[index], self.place.corner)
            copy.start()
            copies.append(copy)
        for copy in copies:
            copy.wait_send()


def spread(value, width):
    return jnp.broadcast_to(value, (value.shape[0], width))


def slot_columns(slot, weight, spare, unit):
    if slot in (4, 5):
        return spare[:, (slot - 4) * unit:(slot - 3) * unit]
    at = 0 if slot == 8 else slot * unit
    return weight[:, at:at + unit]


def fill_spare(spare, weight, flag, unit):
    upper = weight[:, 4 * unit:6 * unit].astype(F32)
    lower = weight[:, :2 * unit].astype(F32)
    spare[...] = (upper * flag + lower * (1.0 - flag)).astype(BF16)


def slot_rows(slot, ref, flag):
    if slot in (4, 5):
        mixed = ref[0].astype(F32) * flag + ref[1].astype(F32) * (1.0 - flag)
        return mixed.astype(ref.dtype)
    return ref[1] if slot == 8 else ref[0]


def mask_slot(slot, value, flag):
    return value if slot < 6 else value * flag


def add_slot(slot, totals, value, flag):
    wide, narrow = totals
    if slot in (4, 5):
        return wide + value * flag, narrow + value * (1.0 - flag)
    if slot == 8:
        return wide, narrow + value
    return wide + value, narrow


SLOT_ORDER = (0, 1, 2, 3, 6, 7, 4, 5, 8)


def forward_kernel(
    wide_ref, x0_ref, gain_a_ref, gain_f_ref, cos_ref, sin_ref, wqkv_hbm, wo_hbm, wu_hbm, wd_hbm,
    out_hbm, q_hbm, k_hbm, v_hbm, p_hbm, o_hbm, a_hbm, b_hbm, xa_hbm, xf_hbm, ra_hbm, rf_hbm, u_hbm, g_hbm,
    wqkv, wo, wu, wd, spare_u, spare_d, xa, xf, x2, xg, ab, bb, q, k, v, p, o, ra, rf, u, g,
    own_qkv, snd_qkv, rcv_qkv, snd_u, rcv_u, snd_sq, rcv_sq, snd_br, rcv_br, relay,
    load_sem, x_send, x_recv, relay_send, relay_recv, sq_send, sq_recv, core_send, core_recv,
    in_send, in_recv, in_local, y_send, y_recv, out_send, out_recv, out_local, save_sem,
):
    place = Place()
    half, core = place.half, place.core
    flag = wide_ref[:1, :1]
    seqs, length, feats = xa.shape
    cols = wo.shape[1]
    mine = cols // 2
    heads = mine // HEAD_DIM
    unit = wu.shape[1] // 8
    tokens = length // 2
    full_width = 2 * feats

    loads = [
        pltpu.make_async_copy(src, dst, load_sem.at[n])
        for n, (src, dst) in enumerate(((wqkv_hbm, wqkv), (wo_hbm, wo), (wu_hbm, wu), (wd_hbm, wd)))
    ]
    for load in loads:
        load.start()

    place.barrier()

    def targets(index, sender_half):
        if index < 6:
            return rcv_qkv.at[index // 3, index % 3]
        if index < 8:
            return o.at[index - 6, :, pl.ds(pl.multiple_of(sender_half * mine, mine), mine)]
        return rcv_u.at[index - 8]

    link = PairLink(place, FWD_RELAYED, relay, x_send, x_recv, relay_send, relay_recv, targets)
    every = tuple(range(6 + seqs + SLOTS))
    saves = []

    def save(src, dst):
        copy = pltpu.make_async_copy(src, dst, save_sem.at[len(saves)])
        copy.start()
        saves.append(copy)

    @pl.when(place.block == 1)
    def _():
        link.forward(every)

    my_rows = pl.ds(pl.multiple_of(core * tokens, tokens), tokens)
    my_feats = pl.ds(pl.multiple_of(half * feats, feats), feats)

    def in_copies(i):
        src = x0_ref.at[i, :, my_feats]
        dst = xa.at[i, my_rows, :]
        return (
            pltpu.make_async_copy(src, dst, in_local.at[i]),
            remote(src, dst, in_send.at[i], in_recv.at[i], place.core_peer),
        )

    @pl.when(place.block == 0)
    def _():
        for i in range(seqs):
            for copy in in_copies(i):
                copy.start()

    def wait_input(i):
        @pl.when(place.block == 0)
        def _():
            local, far = in_copies(i)
            local.wait()
            far.wait()

        @pl.when(place.block == 1)
        def _():
            remote(xa.at[i], xa.at[i], y_send.at[i], y_recv.at[i], place.across).wait_recv()

    def sq_copy(n):
        return remote(snd_sq.at[n], rcv_sq.at[n], sq_send.at[n], sq_recv.at[n], place.pair)

    def core_copy(n):
        return remote(snd_br.at[n], rcv_br.at[n], core_send.at[n], core_recv.at[n], place.core_peer)

    def out_piece(i, src_ref):
        return remote(src_ref.at[i, my_rows, :], out_hbm.at[i, :, my_feats], out_send.at[i], out_recv.at[i], place.pair)

    def emit(i, src_ref, owner):
        @pl.when(half == owner)
        def _():
            pltpu.make_async_copy(src_ref.at[i, my_rows, :], out_hbm.at[i, :, my_feats], out_local.at[i]).start()

        @pl.when(half != owner)
        def _():
            out_piece(i, src_ref).start()

    theirs = pl.multiple_of((1 - half) * mine, mine)
    ours = pl.multiple_of(half * mine, mine)
    gain_a = gain_a_ref[...]
    gain_f = gain_f_ref[...]
    for i in range(seqs):
        wait_input(i)
        x = xa[i].astype(F32)
        snd_sq[i] = to_row(jnp.sum(x * x, axis=-1, keepdims=True))
        sq_copy(i).start()
        xg[i] = (x * gain_a).astype(BF16)
        if i == 0:
            loads[0].wait()
        for t in range(3):
            snd_qkv[i, t] = mm(xg[i], wqkv[t, :, pl.ds(theirs, mine)]).astype(BF16)
            link.start(3 * i + t, snd_qkv.at[i, t])
        for t in range(3):
            own_qkv[i, t] = mm(xg[i], wqkv[t, :, pl.ds(ours, mine)])

    cosine, sine = cos_ref[...], sin_ref[...]
    scale = HEAD_DIM ** (-0.5)
    causal = lax.broadcasted_iota(jnp.int32, (length, length), 0) >= lax.broadcasted_iota(jnp.int32, (length, length), 1)
    for i in range(seqs):
        sq_copy(i).wait_recv()
        factor = lax.rsqrt((from_row(snd_sq[i]) + from_row(rcv_sq[i])) * (1.0 / full_width) + EPSILON)
        ra[i] = spread(factor, 128)
        for t in range(3):
            link.wait(3 * i + t)
        for j in range(heads):
            span = pl.ds(j * HEAD_DIM, HEAD_DIM)
            raw = [(own_qkv[i, t, :, span] + rcv_qkv[i, t, :, span].astype(F32)) * factor for t in range(3)]
            q_j = (raw[0] * cosine + turned(raw[0]) * sine).astype(BF16)
            k_j = (raw[1] * cosine + turned(raw[1]) * sine).astype(BF16)
            v_j = raw[2].astype(BF16)
            q[i, :, span], k[i, :, span], v[i, :, span] = q_j, k_j, v_j
            scores = jnp.where(causal, mm_nt(q_j, k_j) * scale, -1e30)
            exponent = jnp.exp(scores - jnp.max(scores, axis=-1, keepdims=True))
            probs = exponent / jnp.sum(exponent, axis=-1, keepdims=True)
            p[i, j] = probs
            o[i, :, pl.ds(pl.multiple_of(ours + j * HEAD_DIM, HEAD_DIM), HEAD_DIM)] = mm(probs.astype(BF16), v_j).astype(BF16)
        link.start(6 + i, o.at[i, :, pl.ds(ours, mine)])
        ab[i] = (xa[i].astype(F32) * factor * gain_a).astype(BF16)

    loads[1].wait()
    for i in range(seqs):
        link.wait(6 + i)
        snd_br[i] = mm_nt(o[i], wo[...]).astype(BF16)
        core_copy(i).start()

    def slot_start(slot):
        part = mm(slot_rows(slot, xg, flag), slot_columns(slot, wu, spare_u, unit))
        u[slot] = part
        snd_u[slot] = part.astype(BF16)
        link.start(8 + slot, snd_u.at[slot])

    loads[2].wait()
    fill_spare(spare_u, wu, flag, unit)
    for i in range(seqs):
        core_copy(i).wait_recv()
        xf[i] = (xa[i].astype(F32) + (snd_br[i].astype(F32) + rcv_br[i].astype(F32))).astype(BF16)
        emit(i, xf, 0)
        x = xf[i].astype(F32)
        snd_sq[2 + i] = to_row(jnp.sum(x * x, axis=-1, keepdims=True))
        sq_copy(2 + i).start()
        xg[i] = (x * gain_f).astype(BF16)
        for slot in SLOT_ORDER[:6] if i == 0 else SLOT_ORDER[6:]:
            slot_start(slot)

    for ref, dst in ((q, q_hbm), (k, k_hbm), (v, v_hbm), (p, p_hbm), (o, o_hbm), (ab, a_hbm), (xa, xa_hbm), (xf, xf_hbm), (ra, ra_hbm)):
        save(ref, dst)

    for i in range(seqs):
        sq_copy(2 + i).wait_recv()
        factor = lax.rsqrt((from_row(snd_sq[2 + i]) + from_row(rcv_sq[2 + i])) * (1.0 / full_width) + EPSILON)
        rf[i] = spread(factor, 128)
        bb[i] = (xf[i].astype(F32) * factor * gain_f).astype(BF16)

    loads[3].wait()
    fill_spare(spare_d, wd, flag, unit)
    totals = (jnp.zeros((length, feats), F32), jnp.zeros((length, feats), F32))
    for slot in SLOT_ORDER:
        link.wait(8 + slot)
        factor = slot_rows(slot, rf, flag)[:, :1]
        z = (u[slot] + rcv_u[slot].astype(F32)) * factor
        u[slot] = z
        active = 0.5 * z * (1.0 + jnp.tanh(GELU_C * (z + GELU_A * (z * z * z))))
        g_k = mask_slot(slot, active, flag).astype(BF16)
        g[slot] = g_k
        totals = add_slot(slot, totals, mm_nt(g_k, slot_columns(slot, wd, spare_d, unit)), flag)
    for i in range(seqs):
        snd_br[2 + i] = totals[i].astype(BF16)
        core_copy(2 + i).start()
    for ref, dst in ((bb, b_hbm), (rf, rf_hbm), (u, u_hbm), (g, g_hbm)):
        save(ref, dst)
    for i in range(seqs):
        core_copy(2 + i).wait_recv()
        x2[i] = (xf[i].astype(F32) + (snd_br[2 + i].astype(F32) + rcv_br[2 + i].astype(F32))).astype(BF16)

        @pl.when(place.block == 0)
        def _():
            remote(x2.at[i], xa.at[i], y_send.at[i], y_recv.at[i], place.across).start()

        emit(i, x2, 1)

    @pl.when(place.block == 0)
    def _():
        link.forward(every)

    link.finish()
    for n in range(4):
        sq_copy(n).wait_send()
        core_copy(n).wait_send()
    for i in range(seqs):
        @pl.when(place.block == 0)
        def _():
            remote(x2.at[i], xa.at[i], y_send.at[i], y_recv.at[i], place.across).wait_send()

        pltpu.make_async_copy(xf.at[i, my_rows, :], out_hbm.at[i, :, my_feats], out_local.at[i]).wait()
        out_piece(i, xf).wait()
    for copy in saves:
        copy.wait()


def backward_kernel(
    wide_ref, c0_ref, gain_a_ref, gain_f_ref, cos_ref, sin_ref, wqkv_hbm, wo_hbm, wu_hbm, wd_hbm,
    q_hbm, k_hbm, v_hbm, p_hbm, xa_hbm, xf_hbm, ra_hbm, rf_hbm, u_hbm,
    ig_hbm, d_hbm, du_hbm, dc_hbm, dqkv_hbm, gain_a_out, gain_f_out,
    wqkv, wo, wu, wd, q, k, v, p, xa, xf, ra, rf, u, spare_u, spare_d,
    e_in, e_bf, e_mid, e, d, dc, du, own_dg, snd_dg, rcv_dg, own_do, snd_do, rcv_do, dqkv,
    snd_row, rcv_row, snd_br, rcv_br, relay,
    load_sem, x_send, x_recv, relay_send, relay_recv, row_send, row_recv, core_send, core_recv,
    in_send, in_recv, in_local, y_send, y_recv, out_send, out_recv, out_local, save_sem,
):
    place = Place()
    half, core = place.half, place.core
    flag = wide_ref[:1, :1]
    seqs, length, feats = xa.shape
    cols = wo.shape[1]
    mine = cols // 2
    heads = mine // HEAD_DIM
    unit = wu.shape[1] // 8
    tokens = length // 2
    full_width = 2 * feats

    sources = (wd_hbm, u_hbm, wu_hbm, xf_hbm, rf_hbm, wo_hbm, q_hbm, k_hbm, v_hbm, p_hbm, wqkv_hbm, xa_hbm, ra_hbm)
    places = (wd, u, wu, xf, rf, wo, q, k, v, p, wqkv, xa, ra)
    loads = [pltpu.make_async_copy(src, dst, load_sem.at[n]) for n, (src, dst) in enumerate(zip(sources, places))]
    for load in loads:
        load.start()

    place.barrier()

    def targets(index, sender_half):
        if index < SLOTS:
            return rcv_dg.at[index]
        if index < SLOTS + seqs:
            return rcv_do.at[index - SLOTS]
        n = index - SLOTS - seqs
        return dqkv.at[n // 3, n % 3, :, pl.ds(pl.multiple_of(sender_half * mine, mine), mine)]

    link = PairLink(place, BWD_RELAYED, relay, x_send, x_recv, relay_send, relay_recv, targets)
    every = tuple(range(SLOTS + seqs + 6))
    saves = []

    def save(src, dst):
        copy = pltpu.make_async_copy(src, dst, save_sem.at[len(saves)])
        copy.start()
        saves.append(copy)

    my_rows = pl.ds(pl.multiple_of(core * tokens, tokens), tokens)
    my_feats = pl.ds(pl.multiple_of(half * feats, feats), feats)

    def in_copies(i):
        src = c0_ref.at[i, :, my_feats]
        dst = e_in.at[i, my_rows, :]
        return (
            pltpu.make_async_copy(src, dst, in_local.at[i]),
            remote(src, dst, in_send.at[i], in_recv.at[i], place.core_peer),
        )

    @pl.when(place.block == 1)
    def _():
        for i in range(seqs):
            for copy in in_copies(i):
                copy.start()

    @pl.when(place.block == 0)
    def _():
        link.forward(every)

    def wait_input(i):
        @pl.when(place.block == 1)
        def _():
            local, far = in_copies(i)
            local.wait()
            far.wait()

        @pl.when(place.block == 0)
        def _():
            remote(e_in.at[i], e_in.at[i], y_send.at[i], y_recv.at[i], place.across).wait_recv()

    def row_copy(n, peer):
        return remote(snd_row.at[n], rcv_row.at[n], row_send.at[n], row_recv.at[n], peer)

    def core_copy(n):
        return remote(snd_br.at[n], rcv_br.at[n], core_send.at[n], core_recv.at[n], place.core_peer)

    def out_piece(i, src_ref):
        return remote(src_ref.at[i, my_rows, :], ig_hbm.at[i, :, my_feats], out_send.at[i], out_recv.at[i], place.pair)

    def emit(i, src_ref, owner):
        @pl.when(half == owner)
        def _():
            pltpu.make_async_copy(src_ref.at[i, my_rows, :], ig_hbm.at[i, :, my_feats], out_local.at[i]).start()

        @pl.when(half != owner)
        def _():
            out_piece(i, src_ref).start()

    theirs = pl.multiple_of((1 - half) * mine, mine)
    ours = pl.multiple_of(half * mine, mine)
    gain_a = gain_a_ref[...]
    gain_f = gain_f_ref[...]

    def norm_back(i, n, x_ref, factor, gain, row_total):
        grad = snd_br[n].astype(F32) + rcv_br[n].astype(F32)
        scaled = x_ref[i].astype(F32) * factor
        mean = row_total * (1.0 / full_width)
        new = e[i] + factor * (grad * gain - scaled * mean)
        return new, jnp.sum(grad * scaled, axis=0, keepdims=True)

    def slot_start(slot):
        part = mm(slot_rows(slot, d, flag), slot_columns(slot, wd, spare_d, unit))
        own_dg[slot] = part
        snd_dg[slot] = part.astype(BF16)
        link.start(slot, snd_dg.at[slot])

    for i in range(seqs):
        wait_input(i)
        e[i] = e_in[i].astype(F32)
        d[i] = e_in[i]
        if i == 0:
            loads[0].wait()
            fill_spare(spare_d, wd, flag, unit)
        for slot in SLOT_ORDER[:6] if i == 0 else SLOT_ORDER[6:]:
            slot_start(slot)
    save(d, d_hbm)

    loads[1].wait()
    loads[2].wait()
    fill_spare(spare_u, wu, flag, unit)
    totals = (jnp.zeros((length, feats), F32), jnp.zeros((length, feats), F32))
    rows = (jnp.zeros((length, 1), F32), jnp.zeros((length, 1), F32))
    for slot in SLOT_ORDER:
        link.wait(slot)
        z = u[slot]
        grad = own_dg[slot] + rcv_dg[slot].astype(F32)
        squared = z * z
        bent = jnp.tanh(GELU_C * (z + GELU_A * (squared * z)))
        slope = 0.5 * (1.0 + bent) + 0.5 * z * (1.0 - bent * bent) * (GELU_C * (1.0 + 3.0 * GELU_A * squared))
        du_k = mask_slot(slot, grad * slope, flag).astype(BF16)
        du[slot] = du_k
        rows = add_slot(slot, rows, jnp.sum(du_k.astype(F32) * z, axis=-1, keepdims=True), flag)
        totals = add_slot(slot, totals, mm_nt(du_k, slot_columns(slot, wu, spare_u, unit)), flag)
    for i in range(seqs):
        snd_br[i] = totals[i].astype(BF16)
        core_copy(i).start()
        snd_row[i] = to_row(rows[i])
        row_copy(i, place.core_peer).start()
    save(du, du_hbm)

    loads[3].wait()
    loads[4].wait()
    loads[5].wait()
    gain_total = jnp.zeros((1, feats), F32)
    for i in range(seqs):
        core_copy(i).wait_recv()
        row_copy(i, place.core_peer).wait_recv()
        new, term = norm_back(i, i, xf, rf[i][:, :1], gain_f, from_row(snd_row[i]) + from_row(rcv_row[i]))
        gain_total = gain_total + term
        e[i] = new
        dc[i] = new.astype(BF16)
        emit(i, dc, 1)
        snd_do[i] = mm(dc[i], wo[:, pl.ds(theirs, mine)]).astype(BF16)
        link.start(SLOTS + i, snd_do.at[i])
        own_do[i] = mm(dc[i], wo[:, pl.ds(ours, mine)])
    gain_f_out[...] = jnp.broadcast_to(gain_total, gain_f_out.shape)
    save(dc, dc_hbm)

    for n in range(6, 10):
        loads[n].wait()
    cosine, sine = cos_ref[...], sin_ref[...]
    scale = HEAD_DIM ** (-0.5)
    for i in range(seqs):
        link.wait(SLOTS + i)
        row = jnp.zeros((length, 1), F32)
        for j in range(heads):
            span = pl.ds(j * HEAD_DIM, HEAD_DIM)
            do_j = (own_do[i, :, span] + rcv_do[i, :, span].astype(F32)).astype(BF16)
            q_j, k_j, v_j, probs = q[i, :, span], k[i, :, span], v[i, :, span], p[i, j]
            dp = mm_nt(do_j, v_j)
            dv = mm_tn(probs.astype(BF16), do_j)
            ds = (probs * (dp - jnp.sum(probs * dp, axis=-1, keepdims=True))).astype(BF16)
            dq = mm(ds, k_j) * scale
            dk = mm_tn(ds, q_j) * scale
            row = row + jnp.sum(dq * q_j.astype(F32) + dk * k_j.astype(F32) + dv * v_j.astype(F32), axis=-1, keepdims=True)
            at = pl.ds(pl.multiple_of(ours + j * HEAD_DIM, HEAD_DIM), HEAD_DIM)
            dqkv[i, 0, :, at] = (dq * cosine - turned(dq) * sine).astype(BF16)
            dqkv[i, 1, :, at] = (dk * cosine - turned(dk) * sine).astype(BF16)
            dqkv[i, 2, :, at] = dv.astype(BF16)
        snd_row[2 + i] = to_row(row)
        row_copy(2 + i, place.pair).start()
        for t in range(3):
            link.start(SLOTS + seqs + 3 * i + t, dqkv.at[i, t, :, pl.ds(ours, mine)])

    for n in range(10, 13):
        loads[n].wait()
    for i in range(seqs):
        part = jnp.zeros((length, feats), F32)
        for t in range(3):
            link.wait(SLOTS + seqs + 3 * i + t)
            part = part + mm_nt(dqkv[i, t], wqkv[t])
        snd_br[2 + i] = part.astype(BF16)
        core_copy(2 + i).start()
        row_copy(2 + i, place.pair).wait_recv()
        snd_row[4 + i] = snd_row[2 + i] + rcv_row[2 + i]
        row_copy(4 + i, place.core_peer).start()
    save(dqkv, dqkv_hbm)

    gain_total = jnp.zeros((1, feats), F32)
    for i in range(seqs):
        core_copy(2 + i).wait_recv()
        row_copy(4 + i, place.core_peer).wait_recv()
        new, term = norm_back(i, 2 + i, xa, ra[i][:, :1], gain_a, from_row(snd_row[4 + i]) + from_row(rcv_row[4 + i]))
        gain_total = gain_total + term
        e_bf[i] = new.astype(BF16)

        @pl.when(place.block == 1)
        def _():
            remote(e_bf.at[i], e_in.at[i], y_send.at[i], y_recv.at[i], place.across).start()

        emit(i, e_bf, 0)
    gain_a_out[...] = jnp.broadcast_to(gain_total, gain_a_out.shape)

    @pl.when(place.block == 1)
    def _():
        link.forward(every)

    link.finish()
    for n in range(6):
        row_copy(n, place.core_peer).wait_send()
    for n in range(4):
        core_copy(n).wait_send()
    for i in range(seqs):
        @pl.when(place.block == 1)
        def _():
            remote(e_bf.at[i], e_in.at[i], y_send.at[i], y_recv.at[i], place.across).wait_send()

        pltpu.make_async_copy(dc.at[i, my_rows, :], ig_hbm.at[i, :, my_feats], out_local.at[i]).wait()
        out_piece(i, dc).wait()
    for copy in saves:
        copy.wait()


def shape(dims, kind):
    return jax.ShapeDtypeStruct(dims, kind)


ANY = pl.BlockSpec(memory_space=pl.ANY)
IN_VMEM = pl.BlockSpec(memory_space=pltpu.VMEM)


def dma(count):
    return pltpu.SemaphoreType.DMA((count,))


def run_forward(wide, x0, gain_a, gain_f, cosine, sine, wqkv, wo, wu, wd):
    seqs, tokens, width = x0.shape
    length, feats, cols, hidden = 2 * tokens, wo.shape[0], wo.shape[1], wu.shape[1]
    mine, unit = cols // 2, hidden // 8
    heads = mine // HEAD_DIM
    out_shape = (
        shape((seqs, tokens, width), BF16),
        shape((seqs, length, mine), BF16),
        shape((seqs, length, mine), BF16),
        shape((seqs, length, mine), BF16),
        shape((seqs, heads, length, length), F32),
        shape((seqs, length, cols), BF16),
        shape((seqs, length, feats), BF16),
        shape((seqs, length, feats), BF16),
        shape((seqs, length, feats), BF16),
        shape((seqs, length, feats), BF16),
        shape((seqs, length, 128), F32),
        shape((seqs, length, 128), F32),
        shape((SLOTS, length, unit), F32),
        shape((SLOTS, length, unit), BF16),
    )
    state = (seqs, length, feats)
    messages = 6 + seqs + SLOTS
    scratch = [
        pltpu.VMEM(wqkv.shape, BF16), pltpu.VMEM(wo.shape, BF16), pltpu.VMEM(wu.shape, BF16), pltpu.VMEM(wd.shape, BF16),
        pltpu.VMEM((feats, 2 * unit), BF16), pltpu.VMEM((feats, 2 * unit), BF16),
        pltpu.VMEM(state, BF16), pltpu.VMEM(state, BF16), pltpu.VMEM(state, BF16), pltpu.VMEM(state, BF16),
        pltpu.VMEM(state, BF16), pltpu.VMEM(state, BF16),
        pltpu.VMEM((seqs, length, mine), BF16), pltpu.VMEM((seqs, length, mine), BF16), pltpu.VMEM((seqs, length, mine), BF16),
        pltpu.VMEM((seqs, heads, length, length), F32),
        pltpu.VMEM((seqs, length, cols), BF16),
        pltpu.VMEM((seqs, length, 128), F32), pltpu.VMEM((seqs, length, 128), F32),
        pltpu.VMEM((SLOTS, length, unit), F32), pltpu.VMEM((SLOTS, length, unit), BF16),
        pltpu.VMEM((seqs, 3, length, mine), F32), pltpu.VMEM((seqs, 3, length, mine), BF16), pltpu.VMEM((seqs, 3, length, mine), BF16),
        pltpu.VMEM((SLOTS, length, unit), BF16), pltpu.VMEM((SLOTS, length, unit), BF16),
        pltpu.VMEM((4, 8, length), F32), pltpu.VMEM((4, 8, length), F32),
        pltpu.VMEM((4, length, feats), BF16), pltpu.VMEM((4, length, feats), BF16),
        pltpu.VMEM((max(len(FWD_RELAYED), 1), length, mine), BF16),
        dma(4), dma(messages), dma(messages), dma(max(len(FWD_RELAYED), 1)), dma(max(len(FWD_RELAYED), 1)),
        dma(4), dma(4), dma(4), dma(4),
        dma(2), dma(2), dma(2), dma(2), dma(2), dma(2), dma(2), dma(2), dma(13),
    ]
    return pl.pallas_call(
        forward_kernel,
        out_shape=out_shape,
        in_specs=[IN_VMEM, ANY, IN_VMEM, IN_VMEM, IN_VMEM, IN_VMEM, ANY, ANY, ANY, ANY],
        out_specs=[ANY] * len(out_shape),
        scratch_shapes=scratch,
        compiler_params=pltpu.CompilerParams(collective_id=1, has_side_effects=True, vmem_limit_bytes=VMEM_LIMIT),
        name="forward",
    )(wide, x0, gain_a, gain_f, cosine, sine, wqkv, wo, wu, wd)


def run_backward(wide, c0, gain_a, gain_f, cosine, sine, wqkv, wo, wu, wd, q, k, v, p, xa, xf, ra, rf, u):
    seqs, tokens, width = c0.shape
    length, feats, cols, hidden = 2 * tokens, wo.shape[0], wo.shape[1], wu.shape[1]
    mine, unit = cols // 2, hidden // 8
    state = (seqs, length, feats)
    out_shape = (
        shape((seqs, tokens, width), BF16),
        shape(state, BF16),
        shape((SLOTS, length, unit), BF16),
        shape(state, BF16),
        shape((seqs, 3, length, cols), BF16),
        shape((8, feats), F32),
        shape((8, feats), F32),
    )
    messages = SLOTS + seqs + 6
    relayed = max(len(BWD_RELAYED), 1)
    scratch = [
        pltpu.VMEM(t.shape, t.dtype) for t in (wqkv, wo, wu, wd, q, k, v, p, xa, xf, ra, rf, u)
    ] + [
        pltpu.VMEM((feats, 2 * unit), BF16), pltpu.VMEM((feats, 2 * unit), BF16),
        pltpu.VMEM(state, BF16), pltpu.VMEM(state, BF16), pltpu.VMEM((1, 8, 128), BF16), pltpu.VMEM(state, F32),
        pltpu.VMEM(state, BF16), pltpu.VMEM(state, BF16),
        pltpu.VMEM((SLOTS, length, unit), BF16),
        pltpu.VMEM((SLOTS, length, unit), F32), pltpu.VMEM((SLOTS, length, unit), BF16), pltpu.VMEM((SLOTS, length, unit), BF16),
        pltpu.VMEM((seqs, length, mine), F32), pltpu.VMEM((seqs, length, mine), BF16), pltpu.VMEM((seqs, length, mine), BF16),
        pltpu.VMEM((seqs, 3, length, cols), BF16),
        pltpu.VMEM((6, 8, length), F32), pltpu.VMEM((6, 8, length), F32),
        pltpu.VMEM((4, length, feats), BF16), pltpu.VMEM((4, length, feats), BF16),
        pltpu.VMEM((relayed, length, mine), BF16),
        dma(13), dma(messages), dma(messages), dma(relayed), dma(relayed), dma(6), dma(6), dma(4), dma(4),
        dma(2), dma(2), dma(2), dma(2), dma(2), dma(2), dma(2), dma(2), dma(4),
    ]
    return pl.pallas_call(
        backward_kernel,
        out_shape=out_shape,
        in_specs=[IN_VMEM, ANY, IN_VMEM, IN_VMEM, IN_VMEM, IN_VMEM] + [ANY] * 13,
        out_specs=[ANY] * 5 + [IN_VMEM] * 2,
        scratch_shapes=scratch,
        compiler_params=pltpu.CompilerParams(collective_id=2, has_side_effects=True, vmem_limit_bytes=VMEM_LIMIT),
        name="backward",
    )(wide, c0, gain_a, gain_f, cosine, sine, wqkv, wo, wu, wd, q, k, v, p, xa, xf, ra, rf, u)


def unpacked(slots, is_wide):
    flag = is_wide > 0
    zero = jnp.zeros_like(slots[0])
    wide_tail = [jnp.where(flag, slots[4], zero), jnp.where(flag, slots[5], zero), slots[6], slots[7]]
    narrow = [jnp.where(flag, slots[8], slots[4]), jnp.where(flag, zero, slots[5])] + [zero] * 6
    wide = [slots[0], slots[1], slots[2], slots[3]] + wide_tail
    return jnp.concatenate([jnp.concatenate(wide, axis=1), jnp.concatenate(narrow, axis=1)], axis=0)


def weight_grad(rows, columns):
    return jnp.einsum("ld,lc->dc", rows, columns, preferred_element_type=F32).astype(BF16)


def local(inputs, cotangent, width_index, qkv_weight, out_weight, attn_gain, ffn_gain, up_weight, down_weight):
    seqs, tokens, width = inputs.shape
    length = 2 * tokens
    swap = width_index[0] < width_index[1]
    is_wide = (jnp.maximum(width_index[0], width_index[1]) == 3).astype(jnp.int32)
    wide = jnp.full((8, 128), is_wide, F32)

    def ordered(value):
        return jnp.where(swap, value[::-1], value)

    cosine, sine = rotary(length, HEAD_DIM)
    gain_a = attn_gain.astype(F32)[None]
    gain_f = ffn_gain.astype(F32)[None]
    weights = (qkv_weight, out_weight, up_weight, down_weight)
    layer_out, q, k, v, p, o, a, b, xa, xf, ra, rf, u, g = run_forward(
        wide, ordered(inputs), gain_a, gain_f, cosine, sine, *weights
    )
    input_grad, d, du, dc, dqkv, gain_a_term, gain_f_term = run_backward(
        wide, ordered(cotangent), gain_a, gain_f, cosine, sine, *weights, q, k, v, p, xa, xf, ra, rf, u
    )
    flat = lambda value: value.reshape(-1, value.shape[-1])
    down_term = weight_grad(flat(d), unpacked(g, is_wide))
    up_term = weight_grad(flat(b), unpacked(du, is_wide))
    out_term = weight_grad(flat(dc), flat(o))
    qkv_term = jnp.einsum("ild,itlc->tdc", a, dqkv, preferred_element_type=F32).astype(BF16)

    def summed(term, axis):
        return lax.psum_scatter(term, "dp", scatter_dimension=axis, tiled=True).astype(F32)

    core = lax.axis_index("mp")

    def gain_grad(term):
        part = lax.psum_scatter(term[0], "dp", scatter_dimension=0, tiled=True)
        size = part.shape[0] // 2
        return lax.dynamic_slice_in_dim(part, core * size, size)

    down_grad = summed(down_term, 0)
    up_grad = summed(up_term, 0)
    out_grad = summed(out_term, 0)
    qkv_grad = summed(qkv_term, 1)
    return (
        ordered(layer_out)[None],
        ordered(input_grad)[None],
        qkv_grad,
        out_grad,
        gain_grad(gain_a_term),
        gain_grad(gain_f_term),
        up_grad,
        down_grad,
    )


def solution(mesh):
    in_specs = (
        P("dp", "mp", None),
        P("dp", "mp", None),
        P("dp"),
        P(None, "section", "mp"),
        P("section", "mp"),
        P("section"),
        P("section"),
        P("section", "mp"),
        P("section", "mp"),
    )
    out_specs = (
        P("section", "dp", "mp", None),
        P("section", "dp", "mp", None),
        P(None, ("section", "dp"), "mp"),
        P(("section", "dp"), "mp"),
        P(("section", "dp", "mp")),
        P(("section", "dp", "mp")),
        P(("section", "dp"), "mp"),
        P(("section", "dp"), "mp"),
    )
    return jax.shard_map(local, mesh=mesh, in_specs=in_specs, out_specs=out_specs, check_vma=False)
```

```python
import jax
import jax.numpy as jnp
from jax import lax
from jax.sharding import PartitionSpec as P
from jax.experimental import pallas as pl
from jax.experimental.pallas import tpu as pltpu

HEAD_DIM = 128
EPSILON = 1e-05
GELU_C = 0.7978845608028654
GELU_A = 0.044715
MESH = pl.DeviceIdType.MESH
SLOTS = 9
F32 = jnp.float32
BF16 = jnp.bfloat16
VMEM_LIMIT = 60 * 2**20

FWD_RELAYED = (0, 3, 4, 8, 10, 14, 12)
BWD_RELAYED = (0, 2, 6, 4, 11, 14, 15)


def mm(a, b):
    return lax.dot_general(a, b, (((1,), (0,)), ((), ())), preferred_element_type=F32)


def mm_nt(a, b):
    return lax.dot_general(a, b, (((1,), (1,)), ((), ())), preferred_element_type=F32)


def mm_tn(a, b):
    return lax.dot_general(a, b, (((0,), (0,)), ((), ())), preferred_element_type=F32)


def to_row(column):
    rows = column.shape[0]
    return jnp.transpose(jnp.broadcast_to(column, (rows, 128)))[:8]


def from_row(row):
    return jnp.transpose(row)[:, :1]


def rotary(length, head_size):
    half_dim = head_size // 2
    frequency = 10000.0 ** (-2.0 * jnp.arange(half_dim, dtype=F32) / head_size)
    angles = jnp.arange(length, dtype=F32)[:, None] * frequency[None, :]
    cosine = jnp.concatenate([jnp.cos(angles), jnp.cos(angles)], axis=1)
    sine = jnp.concatenate([-jnp.sin(angles), jnp.sin(angles)], axis=1)
    return cosine, sine


def turned(values):
    return pltpu.roll(values, HEAD_DIM // 2, 1)


def remote(src, dst, send_sem, recv_sem, device):
    return pltpu.make_async_remote_copy(
        src_ref=src, dst_ref=dst, send_sem=send_sem, recv_sem=recv_sem,
        device_id=device, device_id_type=MESH,
    )


class Place:
    def __init__(self):
        section, dp, mp = (lax.axis_index(name) for name in ("section", "dp", "mp"))
        self.block, self.half, self.core = section // 2, section % 2, mp
        other_half = 1 - self.half
        other_block = 1 - self.block
        self.core_peer = (section, dp, 1 - mp)
        self.pair = (self.block * 2 + other_half, dp, mp)
        self.across = (other_block * 2 + self.half, dp, mp)
        self.corner = (other_block * 2 + other_half, dp, mp)

    def barrier(self):
        sem = pltpu.get_barrier_semaphore()
        peers = (self.core_peer, self.pair, self.across, self.corner)
        for peer in peers:
            pl.semaphore_signal(sem, inc=1, device_id=peer, device_id_type=MESH)
        pl.semaphore_wait(sem, len(peers))


class PairLink:
    def __init__(self, place, relayed, relay, send, recv, relay_send, relay_recv, targets):
        self.place, self.relayed, self.relay = place, relayed, relay
        self.send_sem, self.recv_sem = send, recv
        self.relay_send, self.relay_recv = relay_send, relay_recv
        self.targets = targets
        self.started = []

    def start(self, index, src):
        if index in self.relayed:
            at = self.relayed.index(index)
            copy = remote(src, self.relay.at[at], self.send_sem.at[index], self.relay_recv.at[at], self.place.across)
        else:
            copy = remote(src, self.targets(index, self.place.half), self.send_sem.at[index], self.recv_sem.at[index], self.place.pair)
        copy.start()
        self.started.append(copy)

    def wait(self, index):
        dst = self.targets(index, 1 - self.place.half)
        remote(dst, dst, self.send_sem.at[index], self.recv_sem.at[index], self.place.pair).wait_recv()

    def finish(self):
        for copy in self.started:
            copy.wait_send()
        self.started = []

    def forward(self):
        copies = []
        for at, index in enumerate(self.relayed):
            held = self.relay.at[at]
            remote(held, held, self.relay_send.at[at], self.relay_recv.at[at], self.place.across).wait_recv()
            copy = remote(held, self.targets(index, self.place.half), self.relay_send.at[at], self.recv_sem.at[index], self.place.corner)
            copy.start()
            copies.append(copy)
        for copy in copies:
            copy.wait_send()


def spread(value, width):
    return jnp.broadcast_to(value, (value.shape[0], width))


def slot_columns(slot, weight, spare, unit):
    if slot in (4, 5):
        return spare[:, (slot - 4) * unit:(slot - 3) * unit]
    at = 0 if slot == 8 else slot * unit
    return weight[:, at:at + unit]


def fill_spare(spare, weight, flag, unit):
    upper = weight[:, 4 * unit:6 * unit].astype(F32)
    lower = weight[:, :2 * unit].astype(F32)
    spare[...] = (upper * flag + lower * (1.0 - flag)).astype(BF16)


def slot_rows(slot, ref, flag):
    if slot in (4, 5):
        mixed = ref[0].astype(F32) * flag + ref[1].astype(F32) * (1.0 - flag)
        return mixed.astype(ref.dtype)
    return ref[1] if slot == 8 else ref[0]


def mask_slot(slot, value, flag):
    return value if slot < 6 else value * flag


def add_slot(slot, totals, value, flag):
    wide, narrow = totals
    if slot in (4, 5):
        return wide + value * flag, narrow + value * (1.0 - flag)
    if slot == 8:
        return wide, narrow + value
    return wide + value, narrow


SLOT_ORDER = (0, 1, 2, 3, 6, 7, 4, 5, 8)


def forward_kernel(
    wide_ref, x0_ref, gain_a_ref, gain_f_ref, cos_ref, sin_ref, wqkv_hbm, wo_hbm, wu_hbm, wd_hbm,
    out_hbm, q_hbm, k_hbm, v_hbm, p_hbm, o_hbm, a_hbm, b_hbm, xa_hbm, xf_hbm, ra_hbm, rf_hbm, u_hbm, g_hbm,
    wqkv, wo, wu, wd, spare_u, spare_d, xa, xf, x2, xg, ab, bb, q, k, v, p, o, ra, rf, u, g,
    own_qkv, snd_qkv, rcv_qkv, snd_u, rcv_u, snd_sq, rcv_sq, snd_br, rcv_br, relay,
    load_sem, x_send, x_recv, relay_send, relay_recv, sq_send, sq_recv, core_send, core_recv,
    in_send, in_recv, in_local, y_send, y_recv, out_send, out_recv, out_local, save_sem,
):
    place = Place()
    half, core = place.half, place.core
    flag = wide_ref[:1, :1]
    seqs, length, feats = xa.shape
    cols = wo.shape[1]
    mine = cols // 2
    heads = mine // HEAD_DIM
    unit = wu.shape[1] // 8
    tokens = length // 2
    full_width = 2 * feats

    loads = [
        pltpu.make_async_copy(src, dst, load_sem.at[n])
        for n, (src, dst) in enumerate(((wqkv_hbm, wqkv), (wo_hbm, wo), (wu_hbm, wu), (wd_hbm, wd)))
    ]
    for load in loads:
        load.start()

    place.barrier()

    def targets(index, sender_half):
        if index < 6:
            return rcv_qkv.at[index // 3, index % 3]
        if index < 8:
            return o.at[index - 6, :, pl.ds(pl.multiple_of(sender_half * mine, mine), mine)]
        return rcv_u.at[index - 8]

    link = PairLink(place, FWD_RELAYED, relay, x_send, x_recv, relay_send, relay_recv, targets)
    saves = []

    def save(src, dst):
        copy = pltpu.make_async_copy(src, dst, save_sem.at[len(saves)])
        copy.start()
        saves.append(copy)

    @pl.when(place.block == 1)
    def _():
        link.forward()

    my_rows = pl.ds(pl.multiple_of(core * tokens, tokens), tokens)
    my_feats = pl.ds(pl.multiple_of(half * feats, feats), feats)

    def in_copies(i):
        src = x0_ref.at[i, :, my_feats]
        dst = xa.at[i, my_rows, :]
        return (
            pltpu.make_async_copy(src, dst, in_local.at[i]),
            remote(src, dst, in_send.at[i], in_recv.at[i], place.core_peer),
        )

    @pl.when(place.block == 0)
    def _():
        for i in range(seqs):
            for copy in in_copies(i):
                copy.start()

    def wait_input(i):
        @pl.when(place.block == 0)
        def _():
            local, far = in_copies(i)
            local.wait()
            far.wait()

        @pl.when(place.block == 1)
        def _():
            remote(xa.at[i], xa.at[i], y_send.at[i], y_recv.at[i], place.across).wait_recv()

    def sq_copy(n):
        return remote(snd_sq.at[n], rcv_sq.at[n], sq_send.at[n], sq_recv.at[n], place.pair)

    def core_copy(n):
        return remote(snd_br.at[n], rcv_br.at[n], core_send.at[n], core_recv.at[n], place.core_peer)

    def out_piece(i, src_ref):
        return remote(src_ref.at[i, my_rows, :], out_hbm.at[i, :, my_feats], out_send.at[i], out_recv.at[i], place.pair)

    def emit(i, src_ref, owner):
        @pl.when(half == owner)
        def _():
            pltpu.make_async_copy(src_ref.at[i, my_rows, :], out_hbm.at[i, :, my_feats], out_local.at[i]).start()

        @pl.when(half != owner)
        def _():
            out_piece(i, src_ref).start()

    theirs = pl.multiple_of((1 - half) * mine, mine)
    ours = pl.multiple_of(half * mine, mine)
    gain_a = gain_a_ref[...]
    gain_f = gain_f_ref[...]
    for i in range(seqs):
        wait_input(i)
        x = xa[i].astype(F32)
        snd_sq[i] = to_row(jnp.sum(x * x, axis=-1, keepdims=True))
        sq_copy(i).start()
        xg[i] = (x * gain_a).astype(BF16)
        if i == 0:
            loads[0].wait()
        for t in range(3):
            snd_qkv[i, t] = mm(xg[i], wqkv[t, :, pl.ds(theirs, mine)]).astype(BF16)
            link.start(3 * i + t, snd_qkv.at[i, t])
        for t in range(3):
            own_qkv[i, t] = mm(xg[i], wqkv[t, :, pl.ds(ours, mine)])

    cosine, sine = cos_ref[...], sin_ref[...]
    scale = HEAD_DIM ** (-0.5)
    causal = lax.broadcasted_iota(jnp.int32, (length, length), 0) >= lax.broadcasted_iota(jnp.int32, (length, length), 1)
    for i in range(seqs):
        sq_copy(i).wait_recv()
        factor = lax.rsqrt((from_row(snd_sq[i]) + from_row(rcv_sq[i])) * (1.0 / full_width) + EPSILON)
        ra[i] = spread(factor, 128)
        for t in range(3):
            link.wait(3 * i + t)
        for j in range(heads):
            span = pl.ds(j * HEAD_DIM, HEAD_DIM)
            raw = [(own_qkv[i, t, :, span] + rcv_qkv[i, t, :, span].astype(F32)) * factor for t in range(3)]
            q_j = (raw[0] * cosine + turned(raw[0]) * sine).astype(BF16)
            k_j = (raw[1] * cosine + turned(raw[1]) * sine).astype(BF16)
            v_j = raw[2].astype(BF16)
            q[i, :, span], k[i, :, span], v[i, :, span] = q_j, k_j, v_j
            scores = jnp.where(causal, mm_nt(q_j, k_j) * scale, -1e30)
            exponent = jnp.exp(scores - jnp.max(scores, axis=-1, keepdims=True))
            probs = exponent / jnp.sum(exponent, axis=-1, keepdims=True)
            p[i, j] = probs
            o[i, :, pl.ds(pl.multiple_of(ours + j * HEAD_DIM, HEAD_DIM), HEAD_DIM)] = mm(probs.astype(BF16), v_j).astype(BF16)
        link.start(6 + i, o.at[i, :, pl.ds(ours, mine)])
        ab[i] = (xa[i].astype(F32) * factor * gain_a).astype(BF16)

    loads[1].wait()
    for i in range(seqs):
        link.wait(6 + i)
        snd_br[i] = mm_nt(o[i], wo[...]).astype(BF16)
        core_copy(i).start()

    def slot_start(slot):
        part = mm(slot_rows(slot, xg, flag), slot_columns(slot, wu, spare_u, unit))
        u[slot] = part
        snd_u[slot] = part.astype(BF16)
        link.start(8 + slot, snd_u.at[slot])

    loads[2].wait()
    fill_spare(spare_u, wu, flag, unit)
    for i in range(seqs):
        core_copy(i).wait_recv()
        xf[i] = (xa[i].astype(F32) + (snd_br[i].astype(F32) + rcv_br[i].astype(F32))).astype(BF16)
        emit(i, xf, 0)
        x = xf[i].astype(F32)
        snd_sq[2 + i] = to_row(jnp.sum(x * x, axis=-1, keepdims=True))
        sq_copy(2 + i).start()
        xg[i] = (x * gain_f).astype(BF16)
        for slot in SLOT_ORDER[:6] if i == 0 else SLOT_ORDER[6:]:
            slot_start(slot)

    for ref, dst in ((q, q_hbm), (k, k_hbm), (v, v_hbm), (p, p_hbm), (o, o_hbm), (ab, a_hbm), (xa, xa_hbm), (xf, xf_hbm), (ra, ra_hbm)):
        save(ref, dst)

    for i in range(seqs):
        sq_copy(2 + i).wait_recv()
        factor = lax.rsqrt((from_row(snd_sq[2 + i]) + from_row(rcv_sq[2 + i])) * (1.0 / full_width) + EPSILON)
        rf[i] = spread(factor, 128)
        bb[i] = (xf[i].astype(F32) * factor * gain_f).astype(BF16)

    loads[3].wait()
    fill_spare(spare_d, wd, flag, unit)
    totals = (jnp.zeros((length, feats), F32), jnp.zeros((length, feats), F32))
    for slot in SLOT_ORDER:
        link.wait(8 + slot)
        factor = slot_rows(slot, rf, flag)[:, :1]
        z = (u[slot] + rcv_u[slot].astype(F32)) * factor
        u[slot] = z
        active = 0.5 * z * (1.0 + jnp.tanh(GELU_C * (z + GELU_A * (z * z * z))))
        g_k = mask_slot(slot, active, flag).astype(BF16)
        g[slot] = g_k
        totals = add_slot(slot, totals, mm_nt(g_k, slot_columns(slot, wd, spare_d, unit)), flag)
    for i in range(seqs):
        snd_br[2 + i] = totals[i].astype(BF16)
        core_copy(2 + i).start()
    for ref, dst in ((bb, b_hbm), (rf, rf_hbm), (u, u_hbm), (g, g_hbm)):
        save(ref, dst)
    for i in range(seqs):
        core_copy(2 + i).wait_recv()
        x2[i] = (xf[i].astype(F32) + (snd_br[2 + i].astype(F32) + rcv_br[2 + i].astype(F32))).astype(BF16)

        @pl.when(place.block == 0)
        def _():
            remote(x2.at[i], xa.at[i], y_send.at[i], y_recv.at[i], place.across).start()

        emit(i, x2, 1)

    @pl.when(place.block == 0)
    def _():
        link.forward()

    link.finish()
    for n in range(4):
        sq_copy(n).wait_send()
        core_copy(n).wait_send()
    for i in range(seqs):
        @pl.when(place.block == 0)
        def _():
            remote(x2.at[i], xa.at[i], y_send.at[i], y_recv.at[i], place.across).wait_send()

        pltpu.make_async_copy(xf.at[i, my_rows, :], out_hbm.at[i, :, my_feats], out_local.at[i]).wait()
        out_piece(i, xf).wait()
    for copy in saves:
        copy.wait()


def backward_kernel(
    wide_ref, c0_ref, gain_a_ref, gain_f_ref, cos_ref, sin_ref, wqkv_hbm, wo_hbm, wu_hbm, wd_hbm,
    q_hbm, k_hbm, v_hbm, p_hbm, xa_hbm, xf_hbm, ra_hbm, rf_hbm, u_hbm,
    ig_hbm, d_hbm, du_hbm, dc_hbm, dqkv_hbm, gain_a_out, gain_f_out,
    wqkv, wo, wu, wd, q, k, v, p, xa, xf, ra, rf, u, spare_u, spare_d,
    e_in, e_bf, e_mid, e, d, dc, du, own_dg, snd_dg, rcv_dg, own_do, snd_do, rcv_do, dqkv,
    snd_row, rcv_row, snd_br, rcv_br, relay,
    load_sem, x_send, x_recv, relay_send, relay_recv, row_send, row_recv, core_send, core_recv,
    in_send, in_recv, in_local, y_send, y_recv, out_send, out_recv, out_local, save_sem,
):
    place = Place()
    half, core = place.half, place.core
    flag = wide_ref[:1, :1]
    seqs, length, feats = xa.shape
    cols = wo.shape[1]
    mine = cols // 2
    heads = mine // HEAD_DIM
    unit = wu.shape[1] // 8
    tokens = length // 2
    full_width = 2 * feats

    sources = (wd_hbm, u_hbm, wu_hbm, xf_hbm, rf_hbm, wo_hbm, q_hbm, k_hbm, v_hbm, p_hbm, wqkv_hbm, xa_hbm, ra_hbm)
    places = (wd, u, wu, xf, rf, wo, q, k, v, p, wqkv, xa, ra)
    loads = [pltpu.make_async_copy(src, dst, load_sem.at[n]) for n, (src, dst) in enumerate(zip(sources, places))]
    for load in loads:
        load.start()

    place.barrier()

    def targets(index, sender_half):
        if index < SLOTS:
            return rcv_dg.at[index]
        if index < SLOTS + seqs:
            return rcv_do.at[index - SLOTS]
        n = index - SLOTS - seqs
        return dqkv.at[n // 3, n % 3, :, pl.ds(pl.multiple_of(sender_half * mine, mine), mine)]

    link = PairLink(place, BWD_RELAYED, relay, x_send, x_recv, relay_send, relay_recv, targets)
    saves = []

    def save(src, dst):
        copy = pltpu.make_async_copy(src, dst, save_sem.at[len(saves)])
        copy.start()
        saves.append(copy)

    my_rows = pl.ds(pl.multiple_of(core * tokens, tokens), tokens)
    my_feats = pl.ds(pl.multiple_of(half * feats, feats), feats)

    def in_copies(i):
        src = c0_ref.at[i, :, my_feats]
        dst = e_in.at[i, my_rows, :]
        return (
            pltpu.make_async_copy(src, dst, in_local.at[i]),
            remote(src, dst, in_send.at[i], in_recv.at[i], place.core_peer),
        )

    @pl.when(place.block == 1)
    def _():
        for i in range(seqs):
            for copy in in_copies(i):
                copy.start()

    @pl.when(place.block == 0)
    def _():
        link.forward()

    def wait_input(i):
        @pl.when(place.block == 1)
        def _():
            local, far = in_copies(i)
            local.wait()
            far.wait()

        @pl.when(place.block == 0)
        def _():
            remote(e_in.at[i], e_in.at[i], y_send.at[i], y_recv.at[i], place.across).wait_recv()

    def row_copy(n, peer):
        return remote(snd_row.at[n], rcv_row.at[n], row_send.at[n], row_recv.at[n], peer)

    def core_copy(n):
        return remote(snd_br.at[n], rcv_br.at[n], core_send.at[n], core_recv.at[n], place.core_peer)

    def out_piece(i, src_ref):
        return remote(src_ref.at[i, my_rows, :], ig_hbm.at[i, :, my_feats], out_send.at[i], out_recv.at[i], place.pair)

    def emit(i, src_ref, owner):
        @pl.when(half == owner)
        def _():
            pltpu.make_async_copy(src_ref.at[i, my_rows, :], ig_hbm.at[i, :, my_feats], out_local.at[i]).start()

        @pl.when(half != owner)
        def _():
            out_piece(i, src_ref).start()

    theirs = pl.multiple_of((1 - half) * mine, mine)
    ours = pl.multiple_of(half * mine, mine)
    gain_a = gain_a_ref[...]
    gain_f = gain_f_ref[...]

    def norm_back(i, n, x_ref, factor, gain, row_total):
        grad = snd_br[n].astype(F32) + rcv_br[n].astype(F32)
        scaled = x_ref[i].astype(F32) * factor
        mean = row_total * (1.0 / full_width)
        new = e[i] + factor * (grad * gain - scaled * mean)
        return new, jnp.sum(grad * scaled, axis=0, keepdims=True)

    def slot_start(slot):
        part = mm(slot_rows(slot, d, flag), slot_columns(slot, wd, spare_d, unit))
        own_dg[slot] = part
        snd_dg[slot] = part.astype(BF16)
        link.start(slot, snd_dg.at[slot])

    for i in range(seqs):
        wait_input(i)
        e[i] = e_in[i].astype(F32)
        d[i] = e_in[i]
        if i == 0:
            loads[0].wait()
            fill_spare(spare_d, wd, flag, unit)
        for slot in SLOT_ORDER[:6] if i == 0 else SLOT_ORDER[6:]:
            slot_start(slot)
    save(d, d_hbm)

    loads[1].wait()
    loads[2].wait()
    fill_spare(spare_u, wu, flag, unit)
    totals = (jnp.zeros((length, feats), F32), jnp.zeros((length, feats), F32))
    rows = (jnp.zeros((length, 1), F32), jnp.zeros((length, 1), F32))
    for slot in SLOT_ORDER:
        link.wait(slot)
        z = u[slot]
        grad = own_dg[slot] + rcv_dg[slot].astype(F32)
        squared = z * z
        bent = jnp.tanh(GELU_C * (z + GELU_A * (squared * z)))
        slope = 0.5 * (1.0 + bent) + 0.5 * z * (1.0 - bent * bent) * (GELU_C * (1.0 + 3.0 * GELU_A * squared))
        du_k = mask_slot(slot, grad * slope, flag).astype(BF16)
        du[slot] = du_k
        rows = add_slot(slot, rows, jnp.sum(du_k.astype(F32) * z, axis=-1, keepdims=True), flag)
        totals = add_slot(slot, totals, mm_nt(du_k, slot_columns(slot, wu, spare_u, unit)), flag)
    for i in range(seqs):
        snd_br[i] = totals[i].astype(BF16)
        core_copy(i).start()
        snd_row[i] = to_row(rows[i])
        row_copy(i, place.core_peer).start()
    save(du, du_hbm)

    loads[3].wait()
    loads[4].wait()
    loads[5].wait()
    gain_total = jnp.zeros((1, feats), F32)
    for i in range(seqs):
        core_copy(i).wait_recv()
        row_copy(i, place.core_peer).wait_recv()
        new, term = norm_back(i, i, xf, rf[i][:, :1], gain_f, from_row(snd_row[i]) + from_row(rcv_row[i]))
        gain_total = gain_total + term
        e[i] = new
        dc[i] = new.astype(BF16)
        emit(i, dc, 1)
        snd_do[i] = mm(dc[i], wo[:, pl.ds(theirs, mine)]).astype(BF16)
        link.start(SLOTS + i, snd_do.at[i])
        own_do[i] = mm(dc[i], wo[:, pl.ds(ours, mine)])
    gain_f_out[...] = jnp.broadcast_to(gain_total, gain_f_out.shape)
    save(dc, dc_hbm)

    for n in range(6, 10):
        loads[n].wait()
    cosine, sine = cos_ref[...], sin_ref[...]
    scale = HEAD_DIM ** (-0.5)
    for i in range(seqs):
        link.wait(SLOTS + i)
        row = jnp.zeros((length, 1), F32)
        for j in range(heads):
            span = pl.ds(j * HEAD_DIM, HEAD_DIM)
            do_j = (own_do[i, :, span] + rcv_do[i, :, span].astype(F32)).astype(BF16)
            q_j, k_j, v_j, probs = q[i, :, span], k[i, :, span], v[i, :, span], p[i, j]
            dp = mm_nt(do_j, v_j)
            dv = mm_tn(probs.astype(BF16), do_j)
            ds = (probs * (dp - jnp.sum(probs * dp, axis=-1, keepdims=True))).astype(BF16)
            dq = mm(ds, k_j) * scale
            dk = mm_tn(ds, q_j) * scale
            row = row + jnp.sum(dq * q_j.astype(F32) + dk * k_j.astype(F32) + dv * v_j.astype(F32), axis=-1, keepdims=True)
            at = pl.ds(pl.multiple_of(ours + j * HEAD_DIM, HEAD_DIM), HEAD_DIM)
            dqkv[i, 0, :, at] = (dq * cosine - turned(dq) * sine).astype(BF16)
            dqkv[i, 1, :, at] = (dk * cosine - turned(dk) * sine).astype(BF16)
            dqkv[i, 2, :, at] = dv.astype(BF16)
        snd_row[2 + i] = to_row(row)
        row_copy(2 + i, place.pair).start()
        for t in range(3):
            link.start(SLOTS + seqs + 3 * i + t, dqkv.at[i, t, :, pl.ds(ours, mine)])

    for n in range(10, 13):
        loads[n].wait()
    for i in range(seqs):
        part = jnp.zeros((length, feats), F32)
        for t in range(3):
            link.wait(SLOTS + seqs + 3 * i + t)
            part = part + mm_nt(dqkv[i, t], wqkv[t])
        snd_br[2 + i] = part.astype(BF16)
        core_copy(2 + i).start()
        row_copy(2 + i, place.pair).wait_recv()
        snd_row[4 + i] = snd_row[2 + i] + rcv_row[2 + i]
        row_copy(4 + i, place.core_peer).start()
    save(dqkv, dqkv_hbm)

    gain_total = jnp.zeros((1, feats), F32)
    for i in range(seqs):
        core_copy(2 + i).wait_recv()
        row_copy(4 + i, place.core_peer).wait_recv()
        new, term = norm_back(i, 2 + i, xa, ra[i][:, :1], gain_a, from_row(snd_row[4 + i]) + from_row(rcv_row[4 + i]))
        gain_total = gain_total + term
        e_bf[i] = new.astype(BF16)

        @pl.when(place.block == 1)
        def _():
            remote(e_bf.at[i], e_in.at[i], y_send.at[i], y_recv.at[i], place.across).start()

        emit(i, e_bf, 0)
    gain_a_out[...] = jnp.broadcast_to(gain_total, gain_a_out.shape)

    @pl.when(place.block == 1)
    def _():
        link.forward()

    link.finish()
    for n in range(6):
        row_copy(n, place.core_peer).wait_send()
    for n in range(4):
        core_copy(n).wait_send()
    for i in range(seqs):
        @pl.when(place.block == 1)
        def _():
            remote(e_bf.at[i], e_in.at[i], y_send.at[i], y_recv.at[i], place.across).wait_send()

        pltpu.make_async_copy(dc.at[i, my_rows, :], ig_hbm.at[i, :, my_feats], out_local.at[i]).wait()
        out_piece(i, dc).wait()
    for copy in saves:
        copy.wait()


def shape(dims, kind):
    return jax.ShapeDtypeStruct(dims, kind)


ANY = pl.BlockSpec(memory_space=pl.ANY)
IN_VMEM = pl.BlockSpec(memory_space=pltpu.VMEM)


def dma(count):
    return pltpu.SemaphoreType.DMA((count,))


def run_forward(wide, x0, gain_a, gain_f, cosine, sine, wqkv, wo, wu, wd):
    seqs, tokens, width = x0.shape
    length, feats, cols, hidden = 2 * tokens, wo.shape[0], wo.shape[1], wu.shape[1]
    mine, unit = cols // 2, hidden // 8
    heads = mine // HEAD_DIM
    out_shape = (
        shape((seqs, tokens, width), BF16),
        shape((seqs, length, mine), BF16),
        shape((seqs, length, mine), BF16),
        shape((seqs, length, mine), BF16),
        shape((seqs, heads, length, length), F32),
        shape((seqs, length, cols), BF16),
        shape((seqs, length, feats), BF16),
        shape((seqs, length, feats), BF16),
        shape((seqs, length, feats), BF16),
        shape((seqs, length, feats), BF16),
        shape((seqs, length, 128), F32),
        shape((seqs, length, 128), F32),
        shape((SLOTS, length, unit), F32),
        shape((SLOTS, length, unit), BF16),
    )
    state = (seqs, length, feats)
    messages = 6 + seqs + SLOTS
    scratch = [
        pltpu.VMEM(wqkv.shape, BF16), pltpu.VMEM(wo.shape, BF16), pltpu.VMEM(wu.shape, BF16), pltpu.VMEM(wd.shape, BF16),
        pltpu.VMEM((feats, 2 * unit), BF16), pltpu.VMEM((feats, 2 * unit), BF16),
        pltpu.VMEM(state, BF16), pltpu.VMEM(state, BF16), pltpu.VMEM(state, BF16), pltpu.VMEM(state, BF16),
        pltpu.VMEM(state, BF16), pltpu.VMEM(state, BF16),
        pltpu.VMEM((seqs, length, mine), BF16), pltpu.VMEM((seqs, length, mine), BF16), pltpu.VMEM((seqs, length, mine), BF16),
        pltpu.VMEM((seqs, heads, length, length), F32),
        pltpu.VMEM((seqs, length, cols), BF16),
        pltpu.VMEM((seqs, length, 128), F32), pltpu.VMEM((seqs, length, 128), F32),
        pltpu.VMEM((SLOTS, length, unit), F32), pltpu.VMEM((SLOTS, length, unit), BF16),
        pltpu.VMEM((seqs, 3, length, mine), F32), pltpu.VMEM((seqs, 3, length, mine), BF16), pltpu.VMEM((seqs, 3, length, mine), BF16),
        pltpu.VMEM((SLOTS, length, unit), BF16), pltpu.VMEM((SLOTS, length, unit), BF16),
        pltpu.VMEM((4, 8, length), F32), pltpu.VMEM((4, 8, length), F32),
        pltpu.VMEM((4, length, feats), BF16), pltpu.VMEM((4, length, feats), BF16),
        pltpu.VMEM((max(len(FWD_RELAYED), 1), length, mine), BF16),
        dma(4), dma(messages), dma(messages), dma(max(len(FWD_RELAYED), 1)), dma(max(len(FWD_RELAYED), 1)),
        dma(4), dma(4), dma(4), dma(4),
        dma(2), dma(2), dma(2), dma(2), dma(2), dma(2), dma(2), dma(2), dma(13),
    ]
    return pl.pallas_call(
        forward_kernel,
        out_shape=out_shape,
        in_specs=[IN_VMEM, ANY, IN_VMEM, IN_VMEM, IN_VMEM, IN_VMEM, ANY, ANY, ANY, ANY],
        out_specs=[ANY] * len(out_shape),
        scratch_shapes=scratch,
        compiler_params=pltpu.CompilerParams(collective_id=1, has_side_effects=True, vmem_limit_bytes=VMEM_LIMIT),
        name="forward",
    )(wide, x0, gain_a, gain_f, cosine, sine, wqkv, wo, wu, wd)


def run_backward(wide, c0, gain_a, gain_f, cosine, sine, wqkv, wo, wu, wd, q, k, v, p, xa, xf, ra, rf, u):
    seqs, tokens, width = c0.shape
    length, feats, cols, hidden = 2 * tokens, wo.shape[0], wo.shape[1], wu.shape[1]
    mine, unit = cols // 2, hidden // 8
    state = (seqs, length, feats)
    out_shape = (
        shape((seqs, tokens, width), BF16),
        shape(state, BF16),
        shape((SLOTS, length, unit), BF16),
        shape(state, BF16),
        shape((seqs, 3, length, cols), BF16),
        shape((8, feats), F32),
        shape((8, feats), F32),
    )
    messages = SLOTS + seqs + 6
    relayed = max(len(BWD_RELAYED), 1)
    scratch = [
        pltpu.VMEM(t.shape, t.dtype) for t in (wqkv, wo, wu, wd, q, k, v, p, xa, xf, ra, rf, u)
    ] + [
        pltpu.VMEM((feats, 2 * unit), BF16), pltpu.VMEM((feats, 2 * unit), BF16),
        pltpu.VMEM(state, BF16), pltpu.VMEM(state, BF16), pltpu.VMEM((1, 8, 128), BF16), pltpu.VMEM(state, F32),
        pltpu.VMEM(state, BF16), pltpu.VMEM(state, BF16),
        pltpu.VMEM((SLOTS, length, unit), BF16),
        pltpu.VMEM((SLOTS, length, unit), F32), pltpu.VMEM((SLOTS, length, unit), BF16), pltpu.VMEM((SLOTS, length, unit), BF16),
        pltpu.VMEM((seqs, length, mine), F32), pltpu.VMEM((seqs, length, mine), BF16), pltpu.VMEM((seqs, length, mine), BF16),
        pltpu.VMEM((seqs, 3, length, cols), BF16),
        pltpu.VMEM((6, 8, length), F32), pltpu.VMEM((6, 8, length), F32),
        pltpu.VMEM((4, length, feats), BF16), pltpu.VMEM((4, length, feats), BF16),
        pltpu.VMEM((relayed, length, mine), BF16),
        dma(13), dma(messages), dma(messages), dma(relayed), dma(relayed), dma(6), dma(6), dma(4), dma(4),
        dma(2), dma(2), dma(2), dma(2), dma(2), dma(2), dma(2), dma(2), dma(4),
    ]
    return pl.pallas_call(
        backward_kernel,
        out_shape=out_shape,
        in_specs=[IN_VMEM, ANY, IN_VMEM, IN_VMEM, IN_VMEM, IN_VMEM] + [ANY] * 13,
        out_specs=[ANY] * 5 + [IN_VMEM] * 2,
        scratch_shapes=scratch,
        compiler_params=pltpu.CompilerParams(collective_id=2, has_side_effects=True, vmem_limit_bytes=VMEM_LIMIT),
        name="backward",
    )(wide, c0, gain_a, gain_f, cosine, sine, wqkv, wo, wu, wd, q, k, v, p, xa, xf, ra, rf, u)


def unpacked(slots, is_wide):
    flag = is_wide > 0
    zero = jnp.zeros_like(slots[0])
    wide_tail = [jnp.where(flag, slots[4], zero), jnp.where(flag, slots[5], zero), slots[6], slots[7]]
    narrow = [jnp.where(flag, slots[8], slots[4]), jnp.where(flag, zero, slots[5])] + [zero] * 6
    wide = [slots[0], slots[1], slots[2], slots[3]] + wide_tail
    return jnp.concatenate([jnp.concatenate(wide, axis=1), jnp.concatenate(narrow, axis=1)], axis=0)


def weight_grad(rows, columns):
    return jnp.einsum("ld,lc->dc", rows, columns, preferred_element_type=F32).astype(BF16)


def local(inputs, cotangent, width_index, qkv_weight, out_weight, attn_gain, ffn_gain, up_weight, down_weight):
    seqs, tokens, width = inputs.shape
    length = 2 * tokens
    swap = width_index[0] < width_index[1]
    is_wide = (jnp.maximum(width_index[0], width_index[1]) == 3).astype(jnp.int32)
    wide = jnp.full((8, 128), is_wide, F32)

    def ordered(value):
        return jnp.where(swap, value[::-1], value)

    cosine, sine = rotary(length, HEAD_DIM)
    gain_a = attn_gain.astype(F32)[None]
    gain_f = ffn_gain.astype(F32)[None]
    weights = (qkv_weight, out_weight, up_weight, down_weight)
    layer_out, q, k, v, p, o, a, b, xa, xf, ra, rf, u, g = run_forward(
        wide, ordered(inputs), gain_a, gain_f, cosine, sine, *weights
    )
    input_grad, d, du, dc, dqkv, gain_a_term, gain_f_term = run_backward(
        wide, ordered(cotangent), gain_a, gain_f, cosine, sine, *weights, q, k, v, p, xa, xf, ra, rf, u
    )
    flat = lambda value: value.reshape(-1, value.shape[-1])
    down_term = weight_grad(flat(d), unpacked(g, is_wide))
    up_term = weight_grad(flat(b), unpacked(du, is_wide))
    out_term = weight_grad(flat(dc), flat(o))
    qkv_term = jnp.einsum("ild,itlc->tdc", a, dqkv, preferred_element_type=F32).astype(BF16)

    def summed(term, axis):
        return lax.psum_scatter(term, "dp", scatter_dimension=axis, tiled=True).astype(F32)

    core = lax.axis_index("mp")

    def gain_grad(term):
        part = lax.psum_scatter(term[0], "dp", scatter_dimension=0, tiled=True)
        size = part.shape[0] // 2
        return lax.dynamic_slice_in_dim(part, core * size, size)

    down_grad = summed(down_term, 0)
    up_grad = summed(up_term, 0)
    out_grad = summed(out_term, 0)
    qkv_grad = summed(qkv_term, 1)
    return (
        ordered(layer_out)[None],
        ordered(input_grad)[None],
        qkv_grad,
        out_grad,
        gain_grad(gain_a_term),
        gain_grad(gain_f_term),
        up_grad,
        down_grad,
    )


def solution(mesh):
    in_specs = (
        P("dp", "mp", None),
        P("dp", "mp", None),
        P("dp"),
        P(None, "section", "mp"),
        P("section", "mp"),
        P("section"),
        P("section"),
        P("section", "mp"),
        P("section", "mp"),
    )
    out_specs = (
        P("section", "dp", "mp", None),
        P("section", "dp", "mp", None),
        P(None, ("section", "dp"), "mp"),
        P(("section", "dp"), "mp"),
        P(("section", "dp", "mp")),
        P(("section", "dp", "mp")),
        P(("section", "dp"), "mp"),
        P(("section", "dp"), "mp"),
    )
    return jax.shard_map(local, mesh=mesh, in_specs=in_specs, out_specs=out_specs, check_vma=False)
```

```python
import jax
import jax.numpy as jnp
from jax import lax
from jax.sharding import PartitionSpec as P
from jax.experimental import pallas as pl
from jax.experimental.pallas import tpu as pltpu

HEAD_DIM = 128
EPSILON = 1e-05
GELU_C = 0.7978845608028654
GELU_A = 0.044715
MESH = pl.DeviceIdType.MESH
SLOTS = 10
DIRECT_ROWS = 144
F32 = jnp.float32
BF16 = jnp.bfloat16
VMEM_LIMIT = 60 * 2**20


def mm(a, b):
    return lax.dot_general(a, b, (((1,), (0,)), ((), ())), preferred_element_type=F32)


def mm_nt(a, b):
    return lax.dot_general(a, b, (((1,), (1,)), ((), ())), preferred_element_type=F32)


def mm_tn(a, b):
    return lax.dot_general(a, b, (((0,), (0,)), ((), ())), preferred_element_type=F32)


def to_row(column):
    rows = column.shape[0]
    return jnp.transpose(jnp.broadcast_to(column, (rows, 128)))[:8]


def from_row(row):
    return jnp.transpose(row)[:, :1]


def rotary(length, head_size):
    half_dim = head_size // 2
    frequency = 10000.0 ** (-2.0 * jnp.arange(half_dim, dtype=F32) / head_size)
    angles = jnp.arange(length, dtype=F32)[:, None] * frequency[None, :]
    cosine = jnp.concatenate([jnp.cos(angles), jnp.cos(angles)], axis=1)
    sine = jnp.concatenate([-jnp.sin(angles), jnp.sin(angles)], axis=1)
    return cosine, sine


def turned(values):
    return pltpu.roll(values, HEAD_DIM // 2, 1)


def remote(src, dst, send_sem, recv_sem, device):
    return pltpu.make_async_remote_copy(
        src_ref=src, dst_ref=dst, send_sem=send_sem, recv_sem=recv_sem,
        device_id=device, device_id_type=MESH,
    )


class Place:
    def __init__(self):
        section, dp, mp = (lax.axis_index(name) for name in ("section", "dp", "mp"))
        self.block, self.half, self.core = section // 2, section % 2, mp
        other_half = 1 - self.half
        other_block = 1 - self.block
        self.core_peer = (section, dp, 1 - mp)
        self.pair = (self.block * 2 + other_half, dp, mp)
        self.across = (other_block * 2 + self.half, dp, mp)
        self.corner = (other_block * 2 + other_half, dp, mp)

    def barrier(self):
        sem = pltpu.get_barrier_semaphore()
        peers = (self.core_peer, self.pair, self.across, self.corner)
        for peer in peers:
            pl.semaphore_signal(sem, inc=1, device_id=peer, device_id_type=MESH)
        pl.semaphore_wait(sem, len(peers))


class PairLink:
    def __init__(self, place, relay, sems, targets):
        self.place, self.relay, self.targets = place, relay, targets
        self.send, self.recv, self.far_send, self.far_recv, self.relay_send, self.relay_recv = sems
        rows = DIRECT_ROWS + relay.shape[1]
        self.direct = slice(0, DIRECT_ROWS)
        self.detour = slice(DIRECT_ROWS, rows)
        self.sources = {}

    def copies(self, index):
        half, place, src = self.place.half, self.place, self.sources[index]
        far = remote(src(self.detour), self.relay.at[index], self.far_send.at[index], self.relay_recv.at[index], place.across)
        near = remote(src(self.direct), self.targets(index, half, self.direct), self.send.at[index], self.recv.at[index], place.pair)
        return far, near

    def start(self, index, src):
        self.sources[index] = src
        for copy in self.copies(index):
            copy.start()

    def wait(self, index):
        other = 1 - self.place.half
        for rows, sem in ((self.direct, self.recv), (self.detour, self.far_recv)):
            dst = self.targets(index, other, rows)
            remote(dst, dst, self.send.at[index], sem.at[index], self.place.pair).wait_recv()

    def finish(self, indices):
        for index in indices:
            for copy in self.copies(index):
                copy.wait_send()

    def forward(self, indices):
        copies = []
        for index in indices:
            held = self.relay.at[index]
            remote(held, held, self.relay_send.at[index], self.relay_recv.at[index], self.place.across).wait_recv()
            copy = remote(held, self.targets(index, self.place.half, self.detour), self.relay_send.at[index], self.far_recv.at[index], self.place.corner)
            copy.start()
            copies.append(copy)
        for copy in copies:
            copy.wait_send()


def spread(value, width):
    return jnp.broadcast_to(value, (value.shape[0], width))


def slot_block(slot):
    return (0, slot) if slot < 2 else (1, slot - 2)


def slot_weight(slot, weight):
    unit = weight.shape[1] // 8
    at = slot_block(slot)[1] * unit
    return weight[:, at:at + unit]


def mask_slot(slot, value, flag):
    if slot == 1:
        return value * (1.0 - flag)
    return value if slot < 6 else value * flag


NARROW, WIDE = (0, 1), tuple(range(2, SLOTS))


class Sizes:
    def __init__(self, feats, cols, hidden, tokens):
        self.feats, self.cols, self.unit, self.tokens = feats, cols, hidden // 8, tokens
        self.mine, self.length, self.width = cols // 2, 2 * tokens, 2 * feats
        self.heads = self.mine // HEAD_DIM


class Saver:
    def __init__(self, sem):
        self.sem, self.copies = sem, []

    def __call__(self, src, dst):
        copy = pltpu.make_async_copy(src, dst, self.sem.at[len(self.copies)])
        copy.start()
        self.copies.append(copy)

    def finish(self):
        for copy in self.copies:
            copy.wait()


class Loader:
    def __init__(self, pairs, sem):
        self.copies = [pltpu.make_async_copy(src, dst, sem.at[n]) for n, (src, dst) in enumerate(pairs)]
        for copy in self.copies:
            copy.start()

    def wait(self, *which):
        for n in which:
            self.copies[n].wait()


class Emitter:
    def __init__(self, place, out, sends, recvs, locals_):
        self.place, self.out, self.sems = place, out, (sends, recvs, locals_)

    def far(self, i, src):
        feats = src.shape[-1]
        span = pl.ds(pl.multiple_of(self.place.half * feats, feats), feats)
        return remote(src, self.out.at[i, :, span], self.sems[0].at[i], self.sems[1].at[i], self.place.pair)

    def near(self, i, src):
        feats = src.shape[-1]
        span = pl.ds(pl.multiple_of(self.place.half * feats, feats), feats)
        return pltpu.make_async_copy(src, self.out.at[i, :, span], self.sems[2].at[i])

    def start(self, i, src, owner):
        @pl.when(self.place.half == owner)
        def _():
            self.near(i, src).start()

        @pl.when(self.place.half != owner)
        def _():
            self.far(i, src).start()


def forward_kernel(
    wide_ref, x0_ref, gain_a_ref, gain_f_ref, cos_ref, sin_ref, wqkv_hbm, wo_hbm, wu_hbm, wd_hbm,
    out_hbm, q_hbm, k_hbm, v_hbm, p_hbm, o_hbm, a_hbm, b_hbm, xa_hbm, xf_hbm, ra_hbm, rf_hbm, u_hbm, g_hbm,
    wqkv, wo, wu, wd, xa, xf, x2, xg, ab, bb, q, k, v, p, o, ra, rf, u, g,
    own_qkv, snd_qkv, rcv_qkv, snd_u, rcv_u, snd_sq, rcv_sq, snd_br, rcv_br, rcv_half, relay,
    load_sem, x_send, x_recv, far_send, far_recv, relay_send, relay_recv, sq_send, sq_recv, core_send, core_recv,
    in_send, in_recv, in_local, y_send, y_recv, out_send, out_recv, out_local, save_sem,
):
    place = Place()
    half, core = place.half, place.core
    flag = wide_ref[:1, :1]
    seqs, length, feats = xa.shape
    z = Sizes(feats, wo.shape[1], wu.shape[1], length // 2)
    mine = z.mine

    loads = Loader(((wqkv_hbm, wqkv), (wo_hbm, wo), (wu_hbm, wu), (wd_hbm, wd)), load_sem)
    save = Saver(save_sem)
    place.barrier()

    def targets(index, sender_half, rows):
        if index < 6:
            return rcv_qkv.at[index // 3, index % 3, rows, :]
        if index < 8:
            return o.at[index - 6, rows, pl.ds(pl.multiple_of(sender_half * mine, mine), mine)]
        return rcv_u.at[index - 8, rows, :]

    link = PairLink(place, relay, (x_send, x_recv, far_send, far_recv, relay_send, relay_recv), targets)
    order = tuple(range(8 + SLOTS))
    my_rows = pl.ds(pl.multiple_of(core * z.tokens, z.tokens), z.tokens)
    their_rows = pl.ds(pl.multiple_of((1 - core) * z.tokens, z.tokens), z.tokens)
    my_feats = pl.ds(pl.multiple_of(half * feats, feats), feats)

    @pl.when(place.block == 1)
    def _():
        link.forward(order)

    def in_local_copy(i):
        return pltpu.make_async_copy(x0_ref.at[i, :, my_feats], xa.at[i, my_rows, :], in_local.at[i])

    def in_core(i, src):
        return remote(src, xa.at[i, my_rows, :], in_send.at[i], in_recv.at[i], place.core_peer)

    def y_copy(i):
        return remote(x2.at[i], xa.at[i, my_rows, :], y_send.at[i], y_recv.at[i], place.across)

    @pl.when(place.block == 0)
    def _():
        for i in range(seqs):
            in_local_copy(i).start()
            in_core(i, x0_ref.at[i, :, my_feats]).start()

    def wait_input(i):
        @pl.when(place.block == 0)
        def _():
            in_local_copy(i).wait()

        @pl.when(place.block == 1)
        def _():
            y_copy(i).wait_recv()
            in_core(i, xa.at[i, my_rows, :]).start()

        in_core(i, xa.at[i, my_rows, :]).wait()

    def sq_copy(n):
        return remote(snd_sq.at[n], rcv_sq.at[n], sq_send.at[n], sq_recv.at[n], place.pair)

    def core_copy(n):
        return remote(snd_br.at[n], rcv_br.at[n], core_send.at[n], core_recv.at[n], place.core_peer)

    def half_copy(i):
        return remote(snd_br.at[2 + i, their_rows, :], rcv_half.at[i], core_send.at[2 + i], core_recv.at[2 + i], place.core_peer)

    emit = Emitter(place, out_hbm, out_send, out_recv, out_local)
    theirs = pl.multiple_of((1 - half) * mine, mine)
    ours = pl.multiple_of(half * mine, mine)
    gain_a, gain_f = gain_a_ref[...], gain_f_ref[...]

    for i in range(seqs):
        wait_input(i)
        x = xa[i].astype(F32)
        snd_sq[i] = to_row(jnp.sum(x * x, axis=-1, keepdims=True))
        sq_copy(i).start()
        xg[i] = (x * gain_a).astype(BF16)
        if i == 0:
            loads.wait(0)
        for t in range(3):
            snd_qkv[i, t] = mm(xg[i], wqkv[t, :, pl.ds(theirs, mine)]).astype(BF16)
            link.start(3 * i + t, lambda rows, i=i, t=t: snd_qkv.at[i, t, rows, :])
    for i in range(seqs):
        for t in range(3):
            own_qkv[i, t] = mm(xg[i], wqkv[t, :, pl.ds(ours, mine)])

    cosine, sine = cos_ref[...], sin_ref[...]
    scale = HEAD_DIM ** (-0.5)
    causal = lax.broadcasted_iota(jnp.int32, (length, length), 0) >= lax.broadcasted_iota(jnp.int32, (length, length), 1)
    for i in range(seqs):
        sq_copy(i).wait_recv()
        factor = lax.rsqrt((from_row(snd_sq[i]) + from_row(rcv_sq[i])) * (1.0 / z.width) + EPSILON)
        ra[i] = spread(factor, 128)
        for t in range(3):
            link.wait(3 * i + t)
        for j in range(z.heads):
            span = pl.ds(j * HEAD_DIM, HEAD_DIM)
            raw = [(own_qkv[i, t, :, span] + rcv_qkv[i, t, :, span].astype(F32)) * factor for t in range(3)]
            q_j = (raw[0] * cosine + turned(raw[0]) * sine).astype(BF16)
            k_j = (raw[1] * cosine + turned(raw[1]) * sine).astype(BF16)
            v_j = raw[2].astype(BF16)
            q[i, :, span], k[i, :, span], v[i, :, span] = q_j, k_j, v_j
            scores = jnp.where(causal, mm_nt(q_j, k_j) * scale, -1e30)
            exponent = jnp.exp(scores - jnp.max(scores, axis=-1, keepdims=True))
            probs = exponent / jnp.sum(exponent, axis=-1, keepdims=True)
            p[i, j] = probs
            o[i, :, pl.ds(pl.multiple_of(ours + j * HEAD_DIM, HEAD_DIM), HEAD_DIM)] = mm(probs.astype(BF16), v_j).astype(BF16)
        link.start(6 + i, lambda rows, i=i: o.at[i, rows, pl.ds(ours, mine)])

    loads.wait(1)
    for i in range(seqs):
        link.wait(6 + i)
        snd_br[i] = mm_nt(o[i], wo[...]).astype(BF16)
        core_copy(i).start()

    def slot_start(slot):
        part = mm(xg[slot_block(slot)[0]], slot_weight(slot, wu))
        u[slot] = part
        snd_u[slot] = part.astype(BF16)
        link.start(8 + slot, lambda rows: snd_u.at[slot, rows, :])

    loads.wait(2)
    for i, slots in enumerate((NARROW, WIDE)):
        core_copy(i).wait_recv()
        xf[i] = (xa[i].astype(F32) + (snd_br[i].astype(F32) + rcv_br[i].astype(F32))).astype(BF16)
        x = xf[i].astype(F32)
        snd_sq[2 + i] = to_row(jnp.sum(x * x, axis=-1, keepdims=True))
        sq_copy(2 + i).start()
        xg[i] = (x * gain_f).astype(BF16)
        for slot in slots:
            slot_start(slot)
        emit.start(i, xf.at[i, my_rows, :], 0)

    for i in range(seqs):
        ab[i] = (xa[i].astype(F32) * ra[i][:, :1] * gain_a).astype(BF16)
    for ref, dst in ((q, q_hbm), (k, k_hbm), (v, v_hbm), (p, p_hbm), (o, o_hbm), (ab, a_hbm), (xa, xa_hbm), (xf, xf_hbm), (ra, ra_hbm)):
        save(ref, dst)

    factors = []
    for i in range(seqs):
        sq_copy(2 + i).wait_recv()
        factor = lax.rsqrt((from_row(snd_sq[2 + i]) + from_row(rcv_sq[2 + i])) * (1.0 / z.width) + EPSILON)
        rf[i] = spread(factor, 128)
        factors.append(factor)
        bb[i] = (xf[i].astype(F32) * factor * gain_f).astype(BF16)

    def activate(slot):
        link.wait(8 + slot)
        value = (u[slot] + rcv_u[slot].astype(F32)) * factors[slot_block(slot)[0]]
        u[slot] = value
        active = 0.5 * value * (1.0 + jnp.tanh(GELU_C * (value + GELU_A * (value * value * value))))
        g_k = mask_slot(slot, active, flag).astype(BF16)
        g[slot] = g_k
        return mm_nt(g_k, slot_weight(slot, wd))

    def finish_rows(i):
        half_copy(i).wait_recv()
        x2[i] = (xf[i, my_rows, :].astype(F32) + (snd_br[2 + i, my_rows, :].astype(F32) + rcv_half[i].astype(F32))).astype(BF16)

        @pl.when(place.block == 0)
        def _():
            y_copy(i).start()

        emit.start(i, x2.at[i], 1)

    loads.wait(3)
    snd_br[2] = (activate(0) + activate(1)).astype(BF16)
    half_copy(0).start()
    total = activate(2) + activate(3)
    finish_rows(0)
    for slot in WIDE[2:]:
        total = total + activate(slot)
    snd_br[3] = total.astype(BF16)
    half_copy(1).start()
    for ref, dst in ((bb, b_hbm), (rf, rf_hbm), (u, u_hbm)):
        save(ref, dst)
    g[1] = g[1] + g[6]
    save(g.at[0:6], g_hbm.at[0:6])
    save(g.at[7:10], g_hbm.at[6:9])
    finish_rows(1)

    @pl.when(place.block == 0)
    def _():
        link.forward(order)

    link.finish(order)
    for n in range(4):
        sq_copy(n).wait_send()
    for i in range(seqs):
        core_copy(i).wait_send()
        half_copy(i).wait_send()

        @pl.when(place.block == 0)
        def _():
            y_copy(i).wait_send()

        emit.near(i, x2.at[i]).wait()
        emit.far(i, x2.at[i]).wait()
    save.finish()


def backward_kernel(
    wide_ref, c0_ref, gain_a_ref, gain_f_ref, cos_ref, sin_ref, wqkv_hbm, wo_hbm, wu_hbm, wd_hbm,
    q_hbm, k_hbm, v_hbm, p_hbm, xa_hbm, xf_hbm, ra_hbm, rf_hbm, u_hbm, b_hbm,
    ig_hbm, dt_hbm, wug_hbm, dc_hbm, e_hbm, dqkv_hbm, gain_a_out, gain_f_out,
    wqkv, wo, wu, wd, q, k, v, p, xa, xf, ra, rf, u, bb,
    e_in, e, dc, du, own_dg, snd_dg, rcv_dg, dt, wug, e_out, own_do, snd_do, rcv_do, dqkv,
    snd_row, rcv_row, snd_br, rcv_br, rcv_half, relay,
    load_sem, x_send, x_recv, far_send, far_recv, relay_send, relay_recv, row_send, row_recv, core_send, core_recv,
    in_send, in_recv, in_local, y_send, y_recv, out_send, out_recv, out_local, save_sem,
):
    place = Place()
    half, core = place.half, place.core
    flag = wide_ref[:1, :1]
    seqs, length, feats = xa.shape
    z = Sizes(feats, wo.shape[1], wu.shape[1], length // 2)
    mine = z.mine

    sources = (wd_hbm, u_hbm, wu_hbm, xf_hbm, rf_hbm, b_hbm, wo_hbm, q_hbm, k_hbm, v_hbm, p_hbm, wqkv_hbm, xa_hbm, ra_hbm)
    places = (wd, u, wu, xf, rf, bb, wo, q, k, v, p, wqkv, xa, ra)
    loads = Loader(tuple(zip(sources, places)), load_sem)
    save = Saver(save_sem)
    place.barrier()

    def targets(index, sender_half, rows):
        if index < SLOTS:
            return rcv_dg.at[index, rows, :]
        if index < SLOTS + seqs:
            return rcv_do.at[index - SLOTS, rows, :]
        n = index - SLOTS - seqs
        return dqkv.at[n // 3, n % 3, rows, pl.ds(pl.multiple_of(sender_half * mine, mine), mine)]

    link = PairLink(place, relay, (x_send, x_recv, far_send, far_recv, relay_send, relay_recv), targets)
    ffn_order = tuple(range(SLOTS))
    attn_order = tuple(range(SLOTS, SLOTS + seqs + 6))
    my_rows = pl.ds(pl.multiple_of(core * z.tokens, z.tokens), z.tokens)
    their_rows = pl.ds(pl.multiple_of((1 - core) * z.tokens, z.tokens), z.tokens)
    my_feats = pl.ds(pl.multiple_of(half * feats, feats), feats)

    def in_local_copy(i):
        return pltpu.make_async_copy(c0_ref.at[i, :, my_feats], e_in.at[i, my_rows, :], in_local.at[i])

    def in_core(i, src):
        return remote(src, e_in.at[i, my_rows, :], in_send.at[i], in_recv.at[i], place.core_peer)

    def y_copy(i):
        return remote(e_out.at[i], e_in.at[i, my_rows, :], y_send.at[i], y_recv.at[i], place.across)

    @pl.when(place.block == 1)
    def _():
        for i in range(seqs):
            in_local_copy(i).start()
            in_core(i, c0_ref.at[i, :, my_feats]).start()

    @pl.when(place.block == 0)
    def _():
        link.forward(ffn_order + attn_order)

    def wait_input(i):
        @pl.when(place.block == 1)
        def _():
            in_local_copy(i).wait()

        @pl.when(place.block == 0)
        def _():
            y_copy(i).wait_recv()
            in_core(i, e_in.at[i, my_rows, :]).start()

        in_core(i, e_in.at[i, my_rows, :]).wait()

    def row_copy(n, peer):
        return remote(snd_row.at[n], rcv_row.at[n], row_send.at[n], row_recv.at[n], peer)

    def core_copy(n):
        return remote(snd_br.at[n], rcv_br.at[n], core_send.at[n], core_recv.at[n], place.core_peer)

    emit = Emitter(place, ig_hbm, out_send, out_recv, out_local)
    theirs = pl.multiple_of((1 - half) * mine, mine)
    ours = pl.multiple_of(half * mine, mine)
    gain_f = gain_f_ref[...]

    for i, slots in enumerate((NARROW, WIDE)):
        wait_input(i)
        if i == 0:
            loads.wait(0)
        for slot in slots:
            part = mm(e_in[i], slot_weight(slot, wd))
            own_dg[slot] = part
            snd_dg[slot] = part.astype(BF16)
            link.start(slot, lambda rows, slot=slot: snd_dg.at[slot, rows, :])
    loads.wait(1, 2, 3, 4, 5, 6)

    def slope_of(value):
        squared = value * value
        bent = jnp.tanh(GELU_C * (value + GELU_A * (squared * value)))
        return 0.5 * (1.0 + bent) + 0.5 * value * (1.0 - bent * bent) * (GELU_C * (1.0 + 3.0 * GELU_A * squared))

    def hidden_back(slot):
        link.wait(slot)
        value = u[slot]
        grad = own_dg[slot] + rcv_dg[slot].astype(F32)
        du_k = mask_slot(slot, grad * slope_of(value), flag).astype(BF16)
        du[slot] = du_k
        return mm_nt(du_k, slot_weight(slot, wu)), jnp.sum(du_k.astype(F32) * value, axis=-1, keepdims=True)

    def core_sum_start(i, slots):
        terms = [hidden_back(slot) for slot in slots]
        total, row = terms[0]
        for more, more_row in terms[1:]:
            total, row = total + more, row + more_row
        snd_br[i] = total.astype(BF16)
        core_copy(i).start()
        snd_row[i] = to_row(row)
        row_copy(i, place.core_peer).start()

    def ffn_done(i):
        core_copy(i).wait_recv()
        row_copy(i, place.core_peer).wait_recv()
        mean = (from_row(snd_row[i]) + from_row(rcv_row[i])) * (1.0 / z.width)
        grad = snd_br[i].astype(F32) + rcv_br[i].astype(F32)
        factor = rf[i][:, :1]
        scaled = xf[i].astype(F32) * factor
        new = e_in[i].astype(F32) + factor * (grad * gain_f - scaled * mean)
        e[i] = new
        dc[i] = new.astype(BF16)
        emit.start(i, dc.at[i, my_rows, :], 1)
        return jnp.sum(grad * scaled, axis=0, keepdims=True)

    core_sum_start(0, NARROW)
    for i in range(seqs):
        dt[:, i * length:(i + 1) * length] = jnp.transpose(e_in[i].astype(F32)).astype(BF16)
    save(dt, dt_hbm)
    gain_total = ffn_done(0)

    @pl.when(place.block == 1)
    def _():
        attention_grad_start(0, dc, wo, own_do, snd_do, link, SLOTS, theirs, ours, mine)

    core_sum_start(1, WIDE)
    unit = z.unit
    for block in range(8):
        part = mm_tn(bb[1], du[2 + block])
        if block < 2:
            part = part + mm_tn(bb[0], du[block])
        wug[:, block * unit:(block + 1) * unit] = part.astype(BF16)
    save(wug, wug_hbm)
    gain_total = gain_total + ffn_done(1)
    gain_f_out[...] = jnp.broadcast_to(gain_total, gain_f_out.shape)
    save(dc, dc_hbm)
    save(e, e_hbm)

    @pl.when(place.block == 1)
    def _():
        attention_grad_start(1, dc, wo, own_do, snd_do, link, SLOTS, theirs, ours, mine)
        loads.wait(7, 8, 9, 10, 11, 12, 13)
        attention_grad(
            place, z, seqs, e, cos_ref[...], sin_ref[...], gain_a_ref[...], wqkv, q, k, v, p, xa, ra, own_do, rcv_do, dqkv,
            snd_row, rcv_row, row_copy, 2, snd_br, rcv_half, core_send, core_recv, 2, link, SLOTS,
            my_rows, their_rows, ours, mine, e_out, gain_a_out, emit, y_copy,
        )
        copy = pltpu.make_async_copy(dqkv, dqkv_hbm, in_local.at[2])
        copy.start()
        link.forward(ffn_order)
        copy.wait()

    @pl.when(place.block == 0)
    def _():
        gain_a_out[...] = jnp.zeros_like(gain_a_out)
        loads.wait(7, 8, 9, 10, 11, 12, 13)

    for n in range(2):
        row_copy(n, place.core_peer).wait_send()
        core_copy(n).wait_send()
    link.finish(ffn_order)

    @pl.when(place.block == 1)
    def _():
        link.finish(attn_order)
        for n in range(2, 6):
            row_copy(n, place.core_peer).wait_send()
        for i in range(seqs):
            half_copy(place, snd_br, rcv_half, core_send, core_recv, 2, i, their_rows).wait_send()
            y_copy(i).wait_send()

    for i in range(seqs):
        @pl.when(half == 1)
        def _():
            emit.near(i, dc.at[i, my_rows, :]).wait()
            emit.far(i, dc.at[i, my_rows, :]).wait_recv()

        @pl.when(half == 0)
        def _():
            emit.far(i, dc.at[i, my_rows, :]).wait_send()

        @pl.when((half == 0) & (place.block == 1))
        def _():
            emit.near(i, e_out.at[i]).wait()
            emit.far(i, e_out.at[i]).wait_recv()

        @pl.when((half == 1) & (place.block == 1))
        def _():
            emit.far(i, e_out.at[i]).wait_send()
    save.finish()


def half_copy(place, snd_br, rcv_half, core_send, core_recv, first, i, their_rows):
    at = first + i
    return remote(snd_br.at[at, their_rows, :], rcv_half.at[i], core_send.at[at], core_recv.at[at], place.core_peer)


def attention_grad_start(i, dc, wo, own_do, snd_do, link, first, theirs, ours, mine):
    snd_do[i] = mm(dc[i], wo[:, pl.ds(theirs, mine)]).astype(BF16)
    link.start(first + i, lambda rows: snd_do.at[i, rows, :])
    own_do[i] = mm(dc[i], wo[:, pl.ds(ours, mine)])


def attention_grad(
    place, z, seqs, e, cosine, sine, gain_a, wqkv, q, k, v, p, xa, ra, own_do, rcv_do, dqkv,
    snd_row, rcv_row, row_copy, row_first, snd_br, rcv_half, core_send, core_recv, core_first, link, first,
    my_rows, their_rows, ours, mine, e_out, gain_a_out, emit, y_copy, between=None,
):
    length, feats = z.length, z.feats
    scale = HEAD_DIM ** (-0.5)
    for i in range(seqs):
        link.wait(first + i)
        row = jnp.zeros((length, 1), F32)
        for j in range(z.heads):
            span = pl.ds(j * HEAD_DIM, HEAD_DIM)
            do_j = (own_do[i, :, span] + rcv_do[i, :, span].astype(F32)).astype(BF16)
            q_j, k_j, v_j, probs = q[i, :, span], k[i, :, span], v[i, :, span], p[i, j]
            dp = mm_nt(do_j, v_j)
            dv = mm_tn(probs.astype(BF16), do_j)
            ds = (probs * (dp - jnp.sum(probs * dp, axis=-1, keepdims=True))).astype(BF16)
            dq = mm(ds, k_j) * scale
            dk = mm_tn(ds, q_j) * scale
            row = row + jnp.sum(dq * q_j.astype(F32) + dk * k_j.astype(F32) + dv * v_j.astype(F32), axis=-1, keepdims=True)
            at = pl.ds(pl.multiple_of(ours + j * HEAD_DIM, HEAD_DIM), HEAD_DIM)
            dqkv[i, 0, :, at] = (dq * cosine - turned(dq) * sine).astype(BF16)
            dqkv[i, 1, :, at] = (dk * cosine - turned(dk) * sine).astype(BF16)
            dqkv[i, 2, :, at] = dv.astype(BF16)
        snd_row[row_first + i] = to_row(row)
        row_copy(row_first + i, place.pair).start()
        for t in range(3):
            link.start(first + seqs + 3 * i + t, lambda rows, i=i, t=t: dqkv.at[i, t, rows, pl.ds(ours, mine)])

    if between is not None:
        between()
    for i in range(seqs):
        part = jnp.zeros((length, feats), F32)
        for t in range(3):
            link.wait(first + seqs + 3 * i + t)
            part = part + mm_nt(dqkv[i, t], wqkv[t])
        snd_br[core_first + i] = part.astype(BF16)
        half_copy(place, snd_br, rcv_half, core_send, core_recv, core_first, i, their_rows).start()
        row_copy(row_first + i, place.pair).wait_recv()
        snd_row[row_first + 2 + i] = snd_row[row_first + i] + rcv_row[row_first + i]
        row_copy(row_first + 2 + i, place.core_peer).start()

    gain_total = jnp.zeros((1, feats), F32)
    for i in range(seqs):
        half_copy(place, snd_br, rcv_half, core_send, core_recv, core_first, i, their_rows).wait_recv()
        row_copy(row_first + 2 + i, place.core_peer).wait_recv()
        mean = (from_row(snd_row[row_first + 2 + i]) + from_row(rcv_row[row_first + 2 + i])) * (1.0 / z.width)
        snd_row[row_first + 4 + i] = to_row(mean)
        own_mean = from_row(snd_row[row_first + 4 + i, :, my_rows])
        grad = snd_br[core_first + i, my_rows, :].astype(F32) + rcv_half[i].astype(F32)
        factor = ra[i, my_rows, :][:, :1]
        scaled = xa[i, my_rows, :].astype(F32) * factor
        e_out[i] = (e[i, my_rows, :] + factor * (grad * gain_a - scaled * own_mean)).astype(BF16)
        gain_total = gain_total + jnp.sum(grad * scaled, axis=0, keepdims=True)
        if y_copy is not None:
            y_copy(i).start()
        emit.start(i, e_out.at[i], 0)
    gain_a_out[...] = jnp.broadcast_to(gain_total, gain_a_out.shape)


def last_kernel(
    e_hbm, dc_hbm, gain_a_ref, cos_ref, sin_ref, wqkv_hbm, wo_hbm, q_hbm, k_hbm, v_hbm, p_hbm, xa_hbm, ra_hbm, o_hbm, a_hbm, dqkv_hbm,
    ig_hbm, wog_hbm, wqkvg_hbm, gain_a_out,
    e, dc, wqkv, wo, q, k, v, p, xa, ra, o, ab,
    own_do, snd_do, rcv_do, dqkv, e_out, wog, wqkvg, snd_row, rcv_row, snd_br, rcv_half, relay,
    load_sem, x_send, x_recv, far_send, far_recv, relay_send, relay_recv, row_send, row_recv, core_send, core_recv,
    out_send, out_recv, out_local, save_sem,
):
    place = Place()
    half, core = place.half, place.core
    seqs, length, feats = xa.shape
    z = Sizes(feats, wo.shape[1], 8, length // 2)
    mine = z.mine
    sources = (dc_hbm, wo_hbm, q_hbm, k_hbm, v_hbm, p_hbm, wqkv_hbm, e_hbm, xa_hbm, ra_hbm, o_hbm, a_hbm)
    loads = Loader(tuple(zip(sources, (dc, wo, q, k, v, p, wqkv, e, xa, ra, o, ab))), load_sem)
    save = Saver(save_sem)
    place.barrier()

    def targets(index, sender_half, rows):
        if index < seqs:
            return rcv_do.at[index, rows, :]
        n = index - seqs
        return dqkv.at[n // 3, n % 3, rows, pl.ds(pl.multiple_of(sender_half * mine, mine), mine)]

    link = PairLink(place, relay, (x_send, x_recv, far_send, far_recv, relay_send, relay_recv), targets)
    my_rows = pl.ds(pl.multiple_of(core * z.tokens, z.tokens), z.tokens)
    their_rows = pl.ds(pl.multiple_of((1 - core) * z.tokens, z.tokens), z.tokens)
    theirs = pl.multiple_of((1 - half) * mine, mine)
    ours = pl.multiple_of(half * mine, mine)
    emit = Emitter(place, ig_hbm, out_send, out_recv, out_local)

    def row_copy(n, peer):
        return remote(snd_row.at[n], rcv_row.at[n], row_send.at[n], row_recv.at[n], peer)

    held = pltpu.make_async_copy(dqkv_hbm, dqkv, load_sem.at[12])

    def out_weight_grad():
        wog[...] = (mm_tn(dc[0], o[0]) + mm_tn(dc[1], o[1])).astype(BF16)

    @pl.when(place.block == 1)
    def _():
        held.start()
        loads.wait(*range(12))
        held.wait()
        gain_a_out[...] = jnp.zeros_like(gain_a_out)
        link.forward(tuple(range(seqs + 6)))
        out_weight_grad()

    @pl.when(place.block == 0)
    def _():
        loads.wait(0, 1)
        for i in range(seqs):
            attention_grad_start(i, dc, wo, own_do, snd_do, link, 0, theirs, ours, mine)
        loads.wait(*range(2, 12))
        attention_grad(
            place, z, seqs, e, cos_ref[...], sin_ref[...], gain_a_ref[...], wqkv, q, k, v, p, xa, ra, own_do, rcv_do, dqkv,
            snd_row, rcv_row, row_copy, 0, snd_br, rcv_half, core_send, core_recv, 0, link, 0,
            my_rows, their_rows, ours, mine, e_out, gain_a_out, emit, None, out_weight_grad,
        )

    save(wog, wog_hbm)
    cols = z.cols
    for t in range(3):
        wqkvg[:, t * cols:(t + 1) * cols] = (mm_tn(ab[0], dqkv[0, t]) + mm_tn(ab[1], dqkv[1, t])).astype(BF16)
    save(wqkvg, wqkvg_hbm)

    @pl.when(place.block == 0)
    def _():
        link.finish(tuple(range(seqs + 6)))
        for n in range(4):
            row_copy(n, place.core_peer).wait_send()
        for i in range(seqs):
            half_copy(place, snd_br, rcv_half, core_send, core_recv, 0, i, their_rows).wait_send()

            @pl.when(half == 0)
            def _():
                emit.near(i, e_out.at[i]).wait()
                emit.far(i, e_out.at[i]).wait_recv()

            @pl.when(half == 1)
            def _():
                emit.far(i, e_out.at[i]).wait_send()

    save.finish()


def shape(dims, kind):
    return jax.ShapeDtypeStruct(dims, kind)


ANY = pl.BlockSpec(memory_space=pl.ANY)
IN_VMEM = pl.BlockSpec(memory_space=pltpu.VMEM)


def vmem(dims, kind):
    return pltpu.VMEM(tuple(dims), kind)


def dma(*counts):
    return [pltpu.SemaphoreType.DMA((count,)) for count in counts]


def like(*arrays):
    return [vmem(array.shape, array.dtype) for array in arrays]


def call(kernel, name, number, out_shape, in_vmem, out_vmem, scratch, args, flops):
    return pl.pallas_call(
        kernel,
        out_shape=tuple(out_shape),
        in_specs=[IN_VMEM if n in in_vmem else ANY for n in range(len(args))],
        out_specs=tuple(IN_VMEM if n in out_vmem else ANY for n in range(len(out_shape))),
        scratch_shapes=scratch,
        compiler_params=pltpu.CompilerParams(collective_id=number, has_side_effects=True, vmem_limit_bytes=VMEM_LIMIT),
        cost_estimate=pl.CostEstimate(flops=flops, bytes_accessed=10**6, transcendentals=0),
        name=name,
    )(*args)


def run_forward(wide, x0, gain_a, gain_f, cosine, sine, wqkv, wo, wu, wd):
    seqs, tokens, width = x0.shape
    z = Sizes(wo.shape[0], wo.shape[1], wu.shape[1], tokens)
    state, half_state, heads_state = (seqs, z.length, z.feats), (seqs, tokens, z.feats), (seqs, z.length, z.mine)
    scores, slots = (seqs, z.heads, z.length, z.length), (SLOTS, z.length, z.unit)
    qkv, messages = (seqs, 3, z.length, z.mine), 8 + SLOTS
    out_shape = [shape((seqs, tokens, width), BF16)] + [shape(heads_state, BF16)] * 3 + [
        shape(scores, F32), shape((seqs, z.length, z.cols), BF16),
    ] + [shape(state, BF16)] * 4 + [shape((seqs, z.length, 128), F32)] * 2 + [
        shape(slots, F32), shape((SLOTS - 1, z.length, z.unit), BF16),
    ]
    scratch = like(wqkv, wo, wu, wd) + [
        vmem(state, BF16), vmem(state, BF16), vmem(half_state, BF16), vmem(state, BF16), vmem(state, BF16), vmem(state, BF16),
        vmem(heads_state, BF16), vmem(heads_state, BF16), vmem(heads_state, BF16), vmem(scores, F32),
        vmem((seqs, z.length, z.cols), BF16), vmem((seqs, z.length, 128), F32), vmem((seqs, z.length, 128), F32),
        vmem(slots, F32), vmem(slots, BF16),
        vmem(qkv, F32), vmem(qkv, BF16), vmem(qkv, BF16), vmem(slots, BF16), vmem(slots, BF16),
        vmem((4, 8, z.length), F32), vmem((4, 8, z.length), F32),
        vmem((4, z.length, z.feats), BF16), vmem((2, z.length, z.feats), BF16), vmem(half_state, BF16),
        vmem((messages, z.length - DIRECT_ROWS, z.mine), BF16),
    ] + dma(4, *[messages] * 6, 4, 4, 4, 4, *[2] * 8, 14)
    args = (wide, x0, gain_a, gain_f, cosine, sine, wqkv, wo, wu, wd)
    return call(forward_kernel, "forward", 1, out_shape, (0, 2, 3, 4, 5), (), scratch, args, 10**11)


def run_backward(wide, c0, gain_a, gain_f, cosine, sine, wqkv, wo, wu, wd, q, k, v, p, xa, xf, ra, rf, u, b):
    seqs, tokens, width = c0.shape
    z = Sizes(wo.shape[0], wo.shape[1], wu.shape[1], tokens)
    state, half_state, heads_state = (seqs, z.length, z.feats), (seqs, tokens, z.feats), (seqs, z.length, z.mine)
    slots, qkv, messages = (SLOTS, z.length, z.unit), (seqs, 3, z.length, z.cols), SLOTS + seqs + 6
    gain = shape((8, z.feats), F32)
    out_shape = [
        shape((seqs, tokens, width), BF16), shape((z.feats, seqs * z.length), BF16), shape(wu.shape, BF16),
        shape(state, BF16), shape(state, F32), shape(qkv, BF16), gain, gain,
    ]
    scratch = like(wqkv, wo, wu, wd, q, k, v, p, xa, xf, ra, rf, u, b) + [
        vmem(state, BF16), vmem(state, F32), vmem(state, BF16),
        vmem(slots, BF16), vmem(slots, F32), vmem(slots, BF16), vmem(slots, BF16),
        vmem((z.feats, seqs * z.length), BF16), vmem(wu.shape, BF16), vmem(half_state, BF16),
        vmem(heads_state, F32), vmem(heads_state, BF16), vmem(heads_state, BF16), vmem(qkv, BF16),
        vmem((8, 8, z.length), F32), vmem((8, 8, z.length), F32),
        vmem((4, z.length, z.feats), BF16), vmem((2, z.length, z.feats), BF16), vmem(half_state, BF16),
        vmem((messages, z.length - DIRECT_ROWS, z.mine), BF16),
    ] + dma(14, *[messages] * 6, 6, 6, 4, 4, 2, 2, 3, *[2] * 5, 4)
    args = (wide, c0, gain_a, gain_f, cosine, sine, wqkv, wo, wu, wd, q, k, v, p, xa, xf, ra, rf, u, b)
    return call(backward_kernel, "backward", 2, out_shape, (0, 2, 3, 4, 5), (6, 7), scratch, args, 10**11)


def run_last(e, dc, gain_a, cosine, sine, wqkv, wo, q, k, v, p, xa, ra, o, a, dqkv):
    seqs, length, feats = e.shape
    z = Sizes(feats, wo.shape[1], 8, length // 2)
    state, half_state, heads_state = (seqs, length, feats), (seqs, z.tokens, feats), (seqs, length, z.mine)
    messages = seqs + 6
    out_shape = [
        shape((seqs, z.tokens, z.width), BF16), shape(wo.shape, BF16), shape((feats, 3 * z.cols), BF16), shape((8, feats), F32),
    ]
    scratch = like(e, dc, wqkv, wo, q, k, v, p, xa, ra, o, a) + [
        vmem(heads_state, F32), vmem(heads_state, BF16), vmem(heads_state, BF16), vmem(dqkv.shape, BF16),
        vmem(half_state, BF16), vmem(wo.shape, BF16), vmem((feats, 3 * z.cols), BF16),
        vmem((6, 8, length), F32), vmem((6, 8, length), F32), vmem((2, length, feats), BF16), vmem(half_state, BF16),
        vmem((messages, length - DIRECT_ROWS, z.mine), BF16),
    ] + dma(13, *[messages] * 6, 4, 4, 2, 2, 2, 2, 2, 2)
    args = (e, dc, gain_a, cosine, sine, wqkv, wo, q, k, v, p, xa, ra, o, a, dqkv)
    return call(last_kernel, "last", 3, out_shape, (2, 3, 4), (3,), scratch, args, 10**8)


def unpacked(slots, flag):
    zero = jnp.zeros_like(slots[0])
    narrow = [slots[0], jnp.where(flag > 0, zero, slots[1])] + [zero] * 6
    wide = [slots[2], slots[3], slots[4], slots[5], jnp.where(flag > 0, slots[1], zero), slots[6], slots[7], slots[8]]
    return jnp.concatenate([jnp.concatenate(narrow, axis=1), jnp.concatenate(wide, axis=1)], axis=0)


def local(inputs, cotangent, width_index, qkv_weight, out_weight, attn_gain, ffn_gain, up_weight, down_weight):
    seqs, tokens, width = inputs.shape
    swap = width_index[0] > width_index[1]
    flag = (jnp.maximum(width_index[0], width_index[1]) == 3).astype(F32)
    wide = jnp.full((8, 128), flag, F32)

    def ordered(value):
        return jnp.where(swap, value[::-1], value)

    cosine, sine = rotary(2 * tokens, HEAD_DIM)
    gain_a = attn_gain.astype(F32)[None]
    gain_f = ffn_gain.astype(F32)[None]
    layer_out, q, k, v, p, o, a, b, xa, xf, ra, rf, u, g = run_forward(
        wide, ordered(inputs), gain_a, gain_f, cosine, sine, qkv_weight, out_weight, up_weight, down_weight
    )
    every_g = lax.all_gather(g, "dp")
    every_flag = lax.all_gather(wide[:1], "dp")
    input_grad, dt, up_term, dc, e, dqkv, gain_a_term, gain_f_term = run_backward(
        wide, ordered(cotangent), gain_a, gain_f, cosine, sine, qkv_weight, out_weight, up_weight, down_weight,
        q, k, v, p, xa, xf, ra, rf, u, b,
    )

    up_sum = lax.psum_scatter(up_term, "dp", scatter_dimension=0, tiled=True)
    last_grad, out_term, qkv_term, last_gain = run_last(
        e, dc, gain_a, cosine, sine, qkv_weight, out_weight, q, k, v, p, xa, ra, o, a, dqkv
    )
    out_sum = lax.psum_scatter(out_term, "dp", scatter_dimension=0, tiled=True)
    qkv_sum = lax.psum_scatter(qkv_term, "dp", scatter_dimension=0, tiled=True)
    section = lax.axis_index("section")
    input_grad = jnp.where(section == 0, last_grad, input_grad)
    gain_a_term = jnp.where(section < 2, last_gain, gain_a_term)
    dt, every_g, every_flag, gain_a_term, gain_f_term, _ = lax.optimization_barrier(
        (dt, every_g, every_flag, gain_a_term, gain_f_term, last_gain)
    )
    every_d = lax.all_to_all(dt, "dp", split_axis=0, concat_axis=1, tiled=True)
    planes = every_g.shape[0]
    hidden = jnp.concatenate([unpacked(every_g[n], every_flag[n, 0, 0]) for n in range(planes)], axis=0)
    down_grad = jnp.dot(every_d, hidden, preferred_element_type=F32)
    up_sum, down_grad = lax.optimization_barrier((up_sum, down_grad))
    up_grad = up_sum.astype(F32)
    out_sum, qkv_sum, up_grad, down_grad = lax.optimization_barrier((out_sum, qkv_sum, up_grad, down_grad))
    out_grad, qkv_grad = out_sum.astype(F32), qkv_sum.astype(F32)

    def gain_grad(term, scale):
        return lax.psum_scatter(term[0] * scale, ("dp", "mp"), scatter_dimension=0, tiled=True)

    cols = out_weight.shape[1]
    return (
        ordered(layer_out)[None],
        ordered(input_grad)[None],
        jnp.stack([qkv_grad[:, t * cols:(t + 1) * cols] for t in range(3)]),
        out_grad,
        gain_grad(gain_a_term, 1.0),
        gain_grad(gain_f_term, 0.5),
        up_grad,
        down_grad,
    )


def solution(mesh):
    in_specs = (
        P("dp", "mp", None),
        P("dp", "mp", None),
        P("dp"),
        P(None, "section", "mp"),
        P("section", "mp"),
        P("section"),
        P("section"),
        P("section", "mp"),
        P("section", "mp"),
    )
    out_specs = (
        P("section", "dp", "mp", None),
        P("section", "dp", "mp", None),
        P(None, ("section", "dp"), "mp"),
        P(("section", "dp"), "mp"),
        P(("section", "dp", "mp")),
        P(("section", "dp", "mp")),
        P(("section", "dp"), "mp"),
        P(("section", "dp"), "mp"),
    )
    return jax.shard_map(local, mesh=mesh, in_specs=in_specs, out_specs=out_specs, check_vma=False)
```

```python
import jax
import jax.numpy as jnp
import numpy as np
from jax import lax
from jax.sharding import PartitionSpec as P
from jax.experimental import pallas as pl
from jax.experimental.pallas import tpu as pltpu

HEAD_DIM = 128
EPSILON = 1e-05
GELU_C = 0.7978845608028654
GELU_A = 0.044715
MESH = pl.DeviceIdType.MESH
SLOTS = 10
EARLY_STEPS = 2
DIRECT_ROWS = 144
F32 = jnp.float32
BF16 = jnp.bfloat16
VMEM_LIMIT = 62 * 2**20


def mm(a, b):
    return lax.dot_general(a, b, (((1,), (0,)), ((), ())), preferred_element_type=F32)


def mm_nt(a, b):
    return lax.dot_general(a, b, (((1,), (1,)), ((), ())), preferred_element_type=F32)


def mm_tn(a, b):
    return lax.dot_general(a, b, (((0,), (0,)), ((), ())), preferred_element_type=F32)


def to_row(column):
    rows = column.shape[0]
    return jnp.transpose(jnp.broadcast_to(column, (rows, 128)))[:8]


def from_row(row):
    return jnp.transpose(row)[:, :1]


def rotary(length, head_size):
    half_dim = head_size // 2
    frequency = np.float32(10000.0) ** (np.float32(-2.0 / head_size) * np.arange(half_dim, dtype=np.float32))
    angles = np.arange(length, dtype=np.float32)[:, None] * frequency[None, :].astype(np.float32)
    cosine, sine = np.cos(angles).astype(np.float32), np.sin(angles).astype(np.float32)
    return jnp.asarray(np.concatenate([cosine, cosine], axis=1)), jnp.asarray(np.concatenate([-sine, sine], axis=1))


def turned(values):
    return pltpu.roll(values, HEAD_DIM // 2, 1)


def remote(src, dst, send_sem, recv_sem, device):
    return pltpu.make_async_remote_copy(
        src_ref=src, dst_ref=dst, send_sem=send_sem, recv_sem=recv_sem,
        device_id=device, device_id_type=MESH,
    )


class Place:
    def __init__(self):
        section, dp, mp = (lax.axis_index(name) for name in ("section", "dp", "mp"))
        self.block, self.half, self.core = section // 2, section % 2, mp
        other_half = 1 - self.half
        other_block = 1 - self.block
        self.at = (section, dp, mp)
        self.core_peer = (section, dp, 1 - mp)
        self.pair = (self.block * 2 + other_half, dp, mp)
        self.across = (other_block * 2 + self.half, dp, mp)
        self.corner = (other_block * 2 + other_half, dp, mp)

    def plane(self, n):
        section, dp, mp = self.at
        return (section, lax.rem(dp + n, lax.axis_size("dp")), mp)

    def barrier(self):
        sem = pltpu.get_barrier_semaphore()
        peers = [self.core_peer, self.pair, self.across, self.corner]
        peers += [self.plane(n) for n in range(1, lax.axis_size("dp"))]
        for peer in peers:
            pl.semaphore_signal(sem, inc=1, device_id=peer, device_id_type=MESH)
        pl.semaphore_wait(sem, len(peers))


class Exchange:
    def __init__(self, place, piece, slots, sems):
        self.place, self.piece, self.slots = place, piece, slots
        self.send, self.recv, self.local = sems
        self.me, self.count = lax.axis_index("dp"), lax.axis_size("dp")

    def copy(self, n):
        target = lax.rem(self.me + n, self.count)
        return remote(self.piece(target), self.slots.at[self.me], self.send.at[n], self.recv.at[n], self.place.plane(n))

    def own(self):
        return pltpu.make_async_copy(self.piece(self.me), self.slots.at[self.me], self.local.at[0])

    def start(self):
        self.own().start()
        for n in range(1, self.count):
            self.copy(n).start()

    def finish(self):
        self.own().wait()
        for n in range(1, self.count):
            source = lax.rem(self.me + self.count - n, self.count)
            held = self.slots.at[source]
            remote(held, held, self.send.at[n], self.recv.at[n], self.place.plane(n)).wait_recv()
            self.copy(n).wait_send()


class PairLink:
    def __init__(self, place, relay, sems, targets):
        self.place, self.relay, self.targets = place, relay, targets
        self.send, self.recv, self.far_send, self.far_recv, self.relay_send, self.relay_recv = sems
        rows = DIRECT_ROWS + relay.shape[1]
        self.direct = slice(0, DIRECT_ROWS)
        self.detour = slice(DIRECT_ROWS, rows)
        self.sources = {}

    def copies(self, index):
        half, place, src = self.place.half, self.place, self.sources[index]
        near = remote(src(self.direct), self.targets(index, half, self.direct), self.send.at[index], self.recv.at[index], place.pair)
        far = remote(src(self.detour), self.relay.at[index], self.far_send.at[index], self.relay_recv.at[index], place.across)
        return near, far

    def whole(self, index):
        rows, src = slice(0, self.detour.stop), self.sources[index]
        dst = self.targets(index, self.place.half, rows)
        return remote(src(rows), dst, self.send.at[index], self.recv.at[index], self.place.pair)

    def start(self, index, src):
        self.sources[index] = src
        for copy in self.copies(index):
            copy.start()

    def start_near(self, index, src):
        self.sources[index] = src
        self.copies(index)[0].start()

    def start_far(self, index):
        self.copies(index)[1].start()

    def start_whole(self, index, src):
        self.sources[index] = src
        self.whole(index).start()

    def wait(self, index):
        other = 1 - self.place.half
        for rows, sem in ((self.direct, self.recv), (self.detour, self.far_recv)):
            dst = self.targets(index, other, rows)
            remote(dst, dst, self.send.at[index], sem.at[index], self.place.pair).wait_recv()

    def wait_whole(self, index):
        dst = self.targets(index, 1 - self.place.half, slice(0, self.detour.stop))
        remote(dst, dst, self.send.at[index], self.recv.at[index], self.place.pair).wait_recv()

    def finish(self, indices):
        for index in indices:
            for copy in self.copies(index):
                copy.wait_send()

    def finish_whole(self, indices):
        for index in indices:
            self.whole(index).wait_send()

    def forward(self, indices):
        copies = []
        for index in indices:
            held = self.relay.at[index]
            remote(held, held, self.relay_send.at[index], self.relay_recv.at[index], self.place.across).wait_recv()
            copy = remote(held, self.targets(index, self.place.half, self.detour), self.relay_send.at[index], self.far_recv.at[index], self.place.corner)
            copy.start()
            copies.append(copy)
        for copy in copies:
            copy.wait_send()


def spread(value, width):
    return jnp.broadcast_to(value, (value.shape[0], width))


def slot_block(slot):
    return (0, slot) if slot < 2 else (1, slot - 2)


def slot_weight(slot, weight):
    unit = weight.shape[1] // 8
    at = slot_block(slot)[1] * unit
    return weight[:, at:at + unit]


def mask_slot(slot, value, flag):
    if slot == 1:
        return value * (1.0 - flag)
    return value if slot < 6 else value * flag


NARROW, WIDE = (0, 1), tuple(range(2, SLOTS))
G_PLACE = (0, 1, 2, 3, 4, 5, 9, 6, 7, 8)
DG_STRAIGHT, DG_MIDDLE, DG_LATE = (0, 1, 2), (3, 4), (5, 6, 7, 8, 9)


class Sizes:
    def __init__(self, feats, cols, hidden, tokens):
        self.feats, self.cols, self.unit, self.tokens = feats, cols, hidden // 8, tokens
        self.mine, self.length, self.width = cols // 2, 2 * tokens, 2 * feats
        self.heads = self.mine // HEAD_DIM


class Saver:
    def __init__(self, sem):
        self.sem, self.copies = sem, []

    def __call__(self, src, dst):
        copy = pltpu.make_async_copy(src, dst, self.sem.at[len(self.copies)])
        copy.start()
        self.copies.append(copy)

    def finish(self):
        for copy in self.copies:
            copy.wait()


class Loader:
    def __init__(self, pairs, sem):
        self.copies = [pltpu.make_async_copy(src, dst, sem.at[n]) for n, (src, dst) in enumerate(pairs)]
        for copy in self.copies:
            copy.start()

    def wait(self, *which):
        for n in which:
            self.copies[n].wait()


class Emitter:
    def __init__(self, place, out, stage, swap, sems, first=0):
        self.place, self.out, self.stage, self.swap, self.sems, self.first = place, out, stage, swap, sems, first

    def span(self):
        feats = self.stage.shape[-1]
        return pl.ds(pl.multiple_of(self.place.half * feats, feats), feats)

    def far(self, i):
        at = self.first + i
        return remote(self.stage.at[i], self.out.at[i, :, self.span()], self.sems[0].at[at], self.sems[1].at[at], self.place.pair)

    def near(self, i):
        return pltpu.make_async_copy(self.stage.at[i], self.out.at[i, :, self.span()], self.sems[2].at[self.first + i])

    def start(self, values, owner):
        narrow, wide = (value.astype(F32) for value in values)
        self.stage[0] = (narrow * (1.0 - self.swap) + wide * self.swap).astype(BF16)
        self.stage[1] = (wide * (1.0 - self.swap) + narrow * self.swap).astype(BF16)

        @pl.when(self.place.half == owner)
        def _():
            for i in range(2):
                self.near(i).start()

        @pl.when(self.place.half != owner)
        def _():
            for i in range(2):
                self.far(i).start()

    def finish(self, owner, active=True):
        @pl.when((self.place.half == owner) & active)
        def _():
            for i in range(2):
                self.near(i).wait()
                self.far(i).wait_recv()

        @pl.when((self.place.half != owner) & active)
        def _():
            for i in range(2):
                self.far(i).wait_send()


class Gather:
    def __init__(self, place, mine, every, sems, first, last):
        self.me, self.count = lax.axis_index("dp"), lax.axis_size("dp")
        self.place, self.mine, self.every = place, mine, every
        self.right, self.left, self.recv, self.local = sems
        self.first, self.last = first, min(last, self.count - 1)

    def send(self, block, way, number):
        section, dp, mp = self.place.at
        sems = self.right if way > 0 else self.left
        src = self.mine if number == 1 else self.every.at[block]
        return remote(src, self.every.at[block], sems.at[block], self.recv.at[block], (section, dp + way, mp))

    def arrive(self, block):
        held = self.every.at[block]
        remote(held, held, self.right.at[block], self.recv.at[block], self.place.pair).wait_recv()

    def moves(self, number):
        me, last = self.me, self.count - 1
        right, left = me - number + 1, me + number - 1
        return ((1, right, (right >= 0) & (me < last)), (-1, left, (left <= last) & (me > 0)))

    def own(self):
        return pltpu.make_async_copy(self.mine, self.every.at[self.me], self.local.at[0])

    def step(self, number):
        if number == 1:
            self.own().start()
        if number > self.last:
            return
        for way, block, active in self.moves(number):
            @pl.when(active)
            def _(way=way, block=block):
                if number > self.first:
                    self.arrive(block)
                self.send(block, way, number).start()

    def rest(self, number):
        for more in range(number, self.last + 1):
            self.step(more)

    def finish(self):
        for number in range(self.first, self.last + 1):
            left, right = self.me - number, self.me + number
            done = number == self.last

            @pl.when((left >= 0) if done else (left >= 0) & (self.me == self.count - 1))
            def _(block=left):
                self.arrive(block)

            @pl.when((right < self.count) if done else (right < self.count) & (self.me == 0))
            def _(block=right):
                self.arrive(block)

            for way, block, active in self.moves(number):
                @pl.when(active)
                def _(way=way, block=block):
                    self.send(block, way, number).wait_send()
        if self.first == 1:
            self.own().wait()


def main_kernel(
    wide_ref, x0_ref, c0_ref, gain_a_ref, gain_f_ref, cos_ref, sin_ref, wqkv_hbm, wo_hbm, wu_hbm, wd_hbm,
    out_hbm, ig_hbm, q_hbm, k_hbm, v_hbm, p_hbm, xa_hbm, ra_hbm, every_hbm, every_o_hbm, every_d_hbm, every_flag_hbm, wug_hbm, dc_hbm, e_hbm, dqkv_hbm,
    gain_a_out, gain_f_out,
    wqkv, wo, wu, wd, xa, xf, x2, xg, q, k, v, p, o, ra, rf, u, g,
    own_qkv, snd_qkv, rcv_qkv, snd_u, rcv_u, snd_sq, rcv_sq, snd_br, rcv_br, rcv_half,
    e_in, e, dc, du, snd_dg, rcv_dg, dt, e_out, stage, own_do, snd_do, rcv_do, dqkv,
    snd_row, rcv_row, snd_db, rcv_db, rcv_db_half, relay,
    load_sem, x_send, x_recv, far_send, far_recv, relay_send, relay_recv, sq_send, sq_recv, core_send, core_recv,
    row_send, row_recv, db_send, db_recv, in_send, in_recv, in_local, y_send, y_recv, out_send, out_recv, out_local, save_sem,
    right_sem, left_sem, every_sem, every_local, o_right, o_left, o_sem, o_local, d_send, d_recv, d_local, flag_send, flag_recv, flag_local, wug_sem, go_sem,
):
    place = Place()
    half, core = place.half, place.core
    flag, swap = wide_ref[:1, :1], wide_ref[1:2, :1]
    seqs, length, feats = xa.shape
    z = Sizes(feats, wo.shape[1], wu.shape[1], length // 2)
    mine = z.mine

    @pl.when(place.block == 0)
    def _():
        for n, (src, dst) in enumerate(((wqkv_hbm, wqkv), (wo_hbm, wo), (wu_hbm, wu), (wd_hbm, wd))):
            pltpu.make_async_copy(src, dst, load_sem.at[n]).start()

    @pl.when(place.block == 1)
    def _():
        for n, (src, dst) in reversed(tuple(enumerate(((wqkv_hbm, wqkv), (wo_hbm, wo), (wu_hbm, wu), (wd_hbm, wd))))):
            pltpu.make_async_copy(src, dst, load_sem.at[n]).start()

    def loaded(n):
        dst = (wqkv, wo, wu, wd)[n]
        pltpu.make_async_copy(dst, dst, load_sem.at[n]).wait()

    save = Saver(save_sem)
    place.barrier()

    first_u, first_dg = 6 + seqs, 6 + seqs + SLOTS
    first_do = first_dg + SLOTS

    def targets(index, sender_half, rows):
        span = pl.ds(pl.multiple_of(sender_half * mine, mine), mine)
        if index < 6:
            return rcv_qkv.at[index // 3, index % 3, rows, :]
        if index < first_u:
            return o.at[index - 6, rows, span]
        if index < first_dg:
            return rcv_u.at[index - first_u, rows, :]
        if index < first_do:
            return rcv_dg.at[index - first_dg, rows, :]
        if index < first_do + seqs:
            return rcv_do.at[index - first_do, rows, :]
        n = index - first_do - seqs
        return dqkv.at[n // 3, n % 3, rows, span]

    link = PairLink(place, relay, (x_send, x_recv, far_send, far_recv, relay_send, relay_recv), targets)
    forward_order = tuple(range(first_dg))
    ffn_order = tuple(range(first_dg, first_do))
    attn_order = tuple(range(first_do, first_do + seqs + 6))
    my_rows = pl.ds(pl.multiple_of(core * z.tokens, z.tokens), z.tokens)
    their_rows = pl.ds(pl.multiple_of((1 - core) * z.tokens, z.tokens), z.tokens)
    my_feats = pl.ds(pl.multiple_of(half * feats, feats), feats)
    gather = Gather(place, g.at[0:SLOTS - 1], every_hbm, (right_sem, left_sem, every_sem, every_local), 1, EARLY_STEPS)
    gather_o = Gather(place, o, every_o_hbm, (o_right, o_left, o_sem, o_local), 1, z.length)
    share = feats // lax.axis_size("dp")

    def dt_rows(n):
        return dt.at[pl.ds(pl.multiple_of(n * share, share), share), :]

    exchange_d = Exchange(place, dt_rows, every_d_hbm, (d_send, d_recv, d_local))
    exchange_flag = Exchange(place, lambda n: wide_ref, every_flag_hbm, (flag_send, flag_recv, flag_local))
    exchange_flag.start()

    def local_copy(src, dst, n):
        return pltpu.make_async_copy(src, dst, in_local.at[n])

    def core_half(src, dst, n):
        return remote(src, dst, in_send.at[n], in_recv.at[n], place.core_peer)

    def x_copy(i):
        return remote(x2.at[i], xa.at[i, my_rows, :], y_send.at[i], y_recv.at[i], place.across)

    def e_copy(i):
        return remote(e_out.at[i], e_in.at[i, my_rows, :], y_send.at[i], y_recv.at[i], place.across)

    def start_half(src_ref, dst_ref, first):
        for i in range(seqs):
            local_copy(src_ref.at[i, :, my_feats], dst_ref.at[i, my_rows, :], first + i).start()
            core_half(src_ref.at[i, :, my_feats], dst_ref.at[i, my_rows, :], first + i).start()

    def ordered_halves(raw_ref, dst_ref, first):
        for i in range(seqs):
            local_copy(raw_ref.at[i, my_rows, :], raw_ref.at[i, my_rows, :], first + i).wait()
            core_half(raw_ref.at[i, my_rows, :], raw_ref.at[i, my_rows, :], first + i).wait()
        for i in range(seqs):
            mixed = raw_ref[i].astype(F32) * (1.0 - swap) + raw_ref[1 - i].astype(F32) * swap
            dst_ref[i] = mixed.astype(BF16)

    def pass_half(dst_ref, n, i):
        core_half(dst_ref.at[i, my_rows, :], dst_ref.at[i, my_rows, :], n).start()
        core_half(dst_ref.at[i, my_rows, :], dst_ref.at[i, my_rows, :], n).wait()

    def sq_copy(n):
        return remote(snd_sq.at[n], rcv_sq.at[n], sq_send.at[n], sq_recv.at[n], place.pair)

    def core_copy(n):
        return remote(snd_br.at[n], rcv_br.at[n], core_send.at[n], core_recv.at[n], place.core_peer)

    def core_rows(i):
        return remote(snd_br.at[2 + i, their_rows, :], rcv_half.at[i], core_send.at[2 + i], core_recv.at[2 + i], place.core_peer)

    def row_copy(n, peer):
        return remote(snd_row.at[n], rcv_row.at[n], row_send.at[n], row_recv.at[n], peer)

    def db_copy(n):
        return remote(snd_db.at[n], rcv_db.at[n], db_send.at[n], db_recv.at[n], place.core_peer)

    out_sems = (out_send, out_recv, out_local)
    def ready(n):
        pl.semaphore_signal(go_sem.at[n], inc=1, device_id=place.pair, device_id_type=MESH)

    def wait_ready(n):
        pl.semaphore_wait(go_sem.at[n], 1)

    emit_x1 = Emitter(place, out_hbm, stage.at[0], swap, out_sems, 0)
    emit_x2 = Emitter(place, out_hbm, stage.at[1], swap, out_sems, 2)
    emit_e1 = Emitter(place, ig_hbm, stage.at[2], swap, out_sems, 4)
    emit_e0 = Emitter(place, ig_hbm, stage.at[3], swap, out_sems, 6)
    theirs = pl.multiple_of((1 - half) * mine, mine)
    ours = pl.multiple_of(half * mine, mine)
    gain_a, gain_f = gain_a_ref[...], gain_f_ref[...]

    def dg_part(slot):
        snd_dg[slot] = mm(e_in[slot_block(slot)[0]], slot_weight(slot, wd)).astype(BF16)

    @pl.when(place.block == 0)
    def _():
        start_half(x0_ref, xf, 0)
        ordered_halves(xf, xa, 0)

    @pl.when(place.block == 1)
    def _():
        start_half(c0_ref, dc, 2)
        loaded(3)
        ordered_halves(dc, e_in, 2)
        for slot in range(SLOTS):
            dg_part(slot)
        for i in range(seqs):
            dt[:, i * length:(i + 1) * length] = jnp.transpose(e_in[i].astype(F32)).astype(BF16)
        exchange_d.start()
        link.forward(forward_order[:6])
        link.start_whole(first_dg, lambda rows: snd_dg.at[0, rows, :])
        link.forward(forward_order[6:8])
        link.start_whole(first_dg + 1, lambda rows: snd_dg.at[1, rows, :])
        link.forward(forward_order[8:])
        link.start_whole(first_dg + 2, lambda rows: snd_dg.at[2, rows, :])

    for i in range(seqs):
        @pl.when(place.block == 1)
        def _():
            x_copy(i).wait_recv()
            if i == 1:
                ready(0)
            pass_half(xa, i, i)

        x = xa[i].astype(F32)
        snd_sq[i] = to_row(jnp.sum(x * x, axis=-1, keepdims=True))
        sq_copy(i).start()
        xg[i] = (x * gain_a).astype(BF16)
        if i == 0:
            loaded(0)
        for t in range(3):
            snd_qkv[i, t] = mm(xg[i], wqkv[t, :, pl.ds(theirs, mine)]).astype(BF16)
            source = lambda rows, i=i, t=t: snd_qkv.at[i, t, rows, :]

            @pl.when(place.block == 0)
            def _():
                link.start(3 * i + t, source)

            @pl.when(place.block == 1)
            def _():
                if i == 0:
                    link.start_whole(t, source)
                else:
                    link.start_near(3 + t, source)
    @pl.when(place.block == 1)
    def _():
        wait_ready(0)
        for t in range(3):
            link.start_far(3 + t)

    for i in range(seqs):
        for t in range(3):
            own_qkv[i, t] = mm(xg[i], wqkv[t, :, pl.ds(ours, mine)])

    cosine, sine = cos_ref[...], sin_ref[...]
    scale = HEAD_DIM ** (-0.5)
    causal = lax.broadcasted_iota(jnp.int32, (length, length), 0) >= lax.broadcasted_iota(jnp.int32, (length, length), 1)
    for i in range(seqs):
        sq_copy(i).wait_recv()
        factor = lax.rsqrt((from_row(snd_sq[i]) + from_row(rcv_sq[i])) * (1.0 / z.width) + EPSILON)
        ra[i] = spread(factor, 128)
        if i == 0:
            @pl.when(place.block == 0)
            def _():
                for t in range(3):
                    link.wait(t)

            @pl.when(place.block == 1)
            def _():
                for t in range(3):
                    link.wait_whole(t)
        else:
            for t in range(3):
                link.wait(3 + t)
        for j in range(z.heads):
            span = pl.ds(j * HEAD_DIM, HEAD_DIM)
            raw = [(own_qkv[i, t, :, span] + rcv_qkv[i, t, :, span].astype(F32)) * factor for t in range(3)]
            q_j = (raw[0] * cosine + turned(raw[0]) * sine).astype(BF16)
            k_j = (raw[1] * cosine + turned(raw[1]) * sine).astype(BF16)
            v_j = raw[2].astype(BF16)
            q[i, :, span], k[i, :, span], v[i, :, span] = q_j, k_j, v_j
            scores = jnp.where(causal, mm_nt(q_j, k_j) * scale, -1e30)
            exponent = jnp.exp(scores - jnp.max(scores, axis=-1, keepdims=True))
            probs = exponent / jnp.sum(exponent, axis=-1, keepdims=True)
            p[i, j] = probs
            o[i, :, pl.ds(pl.multiple_of(ours + j * HEAD_DIM, HEAD_DIM), HEAD_DIM)] = mm(probs.astype(BF16), v_j).astype(BF16)
        link.start(6 + i, lambda rows, i=i: o.at[i, rows, pl.ds(ours, mine)])

    loaded(1)
    for i in range(seqs):
        link.wait(6 + i)
        snd_br[i] = mm_nt(o[i], wo[...]).astype(BF16)
        core_copy(i).start()

    @pl.when(place.block == 1)
    def _():
        for slot in DG_MIDDLE:
            link.start(first_dg + slot, lambda rows, slot=slot: snd_dg.at[slot, rows, :])

    gather_o.step(1)

    def slot_start(slot):
        part = mm(xg[slot_block(slot)[0]], slot_weight(slot, wu))
        u[slot] = part
        snd_u[slot] = part.astype(BF16)
        link.start(first_u + slot, lambda rows: snd_u.at[slot, rows, :])

    loaded(2)
    for i, slots in enumerate((NARROW, WIDE)):
        core_copy(i).wait_recv()
        xf[i] = (xa[i].astype(F32) + (snd_br[i].astype(F32) + rcv_br[i].astype(F32))).astype(BF16)
        x = xf[i].astype(F32)
        snd_sq[2 + i] = to_row(jnp.sum(x * x, axis=-1, keepdims=True))
        sq_copy(2 + i).start()
        xg[i] = (x * gain_f).astype(BF16)
        for slot in slots:
            slot_start(slot)

    @pl.when(place.block == 1)
    def _():
        for slot in DG_LATE:
            link.start(first_dg + slot, lambda rows, slot=slot: snd_dg.at[slot, rows, :])

    emit_x1.start([xf[i, my_rows, :] for i in range(seqs)], 0)

    for ref, dst in ((q, q_hbm), (k, k_hbm), (v, v_hbm), (p, p_hbm), (xa, xa_hbm), (ra, ra_hbm)):
        save(ref, dst)

    factors = {}

    def row_factor(i):
        sq_copy(2 + i).wait_recv()
        factors[i] = lax.rsqrt((from_row(snd_sq[2 + i]) + from_row(rcv_sq[2 + i])) * (1.0 / z.width) + EPSILON)
        rf[i] = spread(factors[i], 128)

    def activate(slot):
        link.wait(first_u + slot)
        value = (u[slot] + rcv_u[slot].astype(F32)) * factors[slot_block(slot)[0]]
        u[slot] = value
        active = 0.5 * value * (1.0 + jnp.tanh(GELU_C * (value + GELU_A * (value * value * value))))
        g_k = mask_slot(slot, active, flag).astype(BF16)
        g[G_PLACE[slot]] = g_k
        return mm_nt(g_k, slot_weight(slot, wd))

    def finish_rows(i):
        core_rows(i).wait_recv()
        x2[i] = (xf[i, my_rows, :].astype(F32) + (snd_br[2 + i, my_rows, :].astype(F32) + rcv_half[i].astype(F32))).astype(BF16)

        @pl.when(place.block == 0)
        def _():
            x_copy(i).start()

    @pl.when(place.block == 0)
    def _():
        loaded(3)

    row_factor(0)
    snd_br[2] = (activate(0) + activate(1)).astype(BF16)
    core_rows(0).start()
    gather_o.step(2)
    row_factor(1)
    total = activate(2) + activate(3)
    finish_rows(0)
    for slot in WIDE[2:]:
        total = total + activate(slot)
    snd_br[3] = total.astype(BF16)
    core_rows(1).start()
    g[1] = g[1] + g[SLOTS - 1]
    finish_rows(1)
    emit_x2.start([x2[i] for i in range(seqs)], 1)
    gather.step(1)
    gather_o.rest(3)

    def slope_of(value):
        squared = value * value
        bent = jnp.tanh(GELU_C * (value + GELU_A * (squared * value)))
        return 0.5 * (1.0 + bent) + 0.5 * value * (1.0 - bent * bent) * (GELU_C * (1.0 + 3.0 * GELU_A * squared))

    @pl.when(place.block == 0)
    def _():
        link.forward(forward_order[3:first_u])
        link.forward(tuple(first_dg + slot for slot in DG_MIDDLE))
        link.forward(forward_order[first_u:])
        gather.step(2)
        link.forward(tuple(first_dg + slot for slot in DG_LATE))
        link.forward(attn_order)
        for i, slots in enumerate((NARROW, WIDE)):
            e_copy(i).wait_recv()
            if i == 1:
                ready(1)
            pass_half(e_in, 2 + i, i)
            for slot in slots:
                dg_part(slot)
                source = lambda rows, slot=slot: snd_dg.at[slot, rows, :]
                if i == 0:
                    link.start_whole(first_dg + slot, source)
                else:
                    link.start_near(first_dg + slot, source)
                if i == 1 and slot == WIDE[1]:
                    wait_ready(1)
                    for sent in WIDE[:2]:
                        link.start_far(first_dg + sent)
                if i == 1 and slot > WIDE[1]:
                    link.start_far(first_dg + slot)
        for i in range(seqs):
            dt[:, i * length:(i + 1) * length] = jnp.transpose(e_in[i].astype(F32)).astype(BF16)
        exchange_d.start()

    def hidden_back(slot):
        @pl.when(place.block == 0)
        def _():
            (link.wait_whole if slot in NARROW else link.wait)(first_dg + slot)

        @pl.when(place.block == 1)
        def _():
            (link.wait_whole if slot in DG_STRAIGHT else link.wait)(first_dg + slot)

        value = u[slot]
        grad = snd_dg[slot].astype(F32) + rcv_dg[slot].astype(F32)
        du_k = mask_slot(slot, grad * slope_of(value), flag).astype(BF16)
        du[slot] = du_k
        return mm_nt(du_k, slot_weight(slot, wu)), jnp.sum(du_k.astype(F32) * value, axis=-1, keepdims=True)

    def wug_copy(block):
        return pltpu.make_async_copy(snd_qkv.at[block % 2], wug_hbm.at[:, :, block * z.unit:(block + 1) * z.unit], wug_sem.at[block % 2])

    def up_grad(block):
        part = mm_tn(xg[1], du[2 + block])
        if block < 2:
            part = part + mm_tn(xg[0], du[block])
        if block >= 2:
            wug_copy(block - 2).wait()
        for t in range(3):
            snd_qkv[block % 2, t] = part[t * length:(t + 1) * length].astype(BF16)
        wug_copy(block).start()

    def core_sum_start(i, slots):
        total = row = None
        for slot in slots:
            more, more_row = hidden_back(slot)
            total, row = (more, more_row) if total is None else (total + more, row + more_row)

            if i == 1:
                @pl.when(place.block == 0)
                def _(slot=slot):
                    up_grad(slot - 2)

        snd_db[i] = total.astype(BF16)
        db_copy(i).start()
        snd_row[i] = to_row(row)
        row_copy(i, place.core_peer).start()

    def ffn_done(i):
        db_copy(i).wait_recv()
        row_copy(i, place.core_peer).wait_recv()
        mean = (from_row(snd_row[i]) + from_row(rcv_row[i])) * (1.0 / z.width)
        grad = snd_db[i].astype(F32) + rcv_db[i].astype(F32)
        factor = rf[i][:, :1]
        scaled = xf[i].astype(F32) * factor
        new = e_in[i].astype(F32) + factor * (grad * gain_f - scaled * mean)
        e[i] = new
        dc[i] = new.astype(BF16)
        return jnp.sum(grad * scaled, axis=0, keepdims=True)

    @pl.when(place.block == 0)
    def _():
        link.finish(forward_order[:3])

    @pl.when(place.block == 1)
    def _():
        link.finish_whole(forward_order[:3])

    link.finish(forward_order[3:6])
    for i in range(seqs):
        xg[i] = (xf[i].astype(F32) * rf[i][:, :1] * gain_f).astype(BF16)
    core_sum_start(0, NARROW)
    gain_total = ffn_done(0)

    @pl.when(place.block == 1)
    def _():
        attention_grad_start(0, dc, wo, own_do, snd_do, link, first_do, theirs, ours, mine)

    core_sum_start(1, WIDE)
    gain_total = gain_total + ffn_done(1)
    gain_f_out[...] = jnp.broadcast_to(gain_total, gain_f_out.shape)

    @pl.when(place.block == 1)
    def _():
        attention_grad_start(1, dc, wo, own_do, snd_do, link, first_do, theirs, ours, mine)

    save(dc, dc_hbm)
    save(e, e_hbm)
    emit_e1.start([dc[i, my_rows, :] for i in range(seqs)], 1)

    @pl.when(place.block == 0)
    def _():
        gain_a_out[...] = jnp.zeros_like(gain_a_out)

    @pl.when(place.block == 1)
    def _():
        attention_grad(
            place, z, seqs, e, cosine, sine, gain_a, wqkv, q, k, v, p, xa, ra, own_do, rcv_do, dqkv,
            snd_row, rcv_row, row_copy, 2, snd_db, rcv_db_half, db_send, db_recv, 2, link, first_do,
            my_rows, their_rows, ours, mine, e_out, gain_a_out, emit_e0, e_copy,
        )
        copy = pltpu.make_async_copy(dqkv, dqkv_hbm, in_local.at[4])
        copy.start()
        gather.step(2)
        link.forward(ffn_order[len(NARROW):])
        for block in range(8):
            up_grad(block)
        copy.wait()

    for block in range(6, 8):
        wug_copy(block).wait()
    link.finish(forward_order[6:])
    for n in range(4):
        sq_copy(n).wait_send()
    for i in range(seqs):
        core_copy(i).wait_send()
        core_rows(i).wait_send()
        row_copy(i, place.core_peer).wait_send()
        db_copy(i).wait_send()

    @pl.when(place.block == 0)
    def _():
        link.finish_whole(ffn_order[:len(NARROW)])
        link.finish(ffn_order[len(NARROW):])
        for i in range(seqs):
            x_copy(i).wait_send()

    @pl.when(place.block == 1)
    def _():
        link.finish_whole(tuple(first_dg + slot for slot in DG_STRAIGHT))
        link.finish(tuple(first_dg + slot for slot in DG_MIDDLE + DG_LATE))
        link.finish(attn_order)
        for n in range(2, 6):
            row_copy(n, place.core_peer).wait_send()
        for i in range(seqs):
            half_copy(place, snd_db, rcv_db_half, db_send, db_recv, 2, i, their_rows).wait_send()
            e_copy(i).wait_send()

    emit_x1.finish(0)
    emit_x2.finish(1)
    emit_e1.finish(1)
    emit_e0.finish(0, place.block == 1)
    exchange_d.finish()
    exchange_flag.finish()
    gather.finish()
    gather_o.finish()
    save.finish()


def half_copy(place, snd_br, rcv_half, core_send, core_recv, first, i, their_rows):
    at = first + i
    return remote(snd_br.at[at, their_rows, :], rcv_half.at[i], core_send.at[at], core_recv.at[at], place.core_peer)


def attention_grad_start(i, dc, wo, own_do, snd_do, link, first, theirs, ours, mine):
    snd_do[i] = mm(dc[i], wo[:, pl.ds(theirs, mine)]).astype(BF16)
    link.start(first + i, lambda rows: snd_do.at[i, rows, :])
    own_do[i] = mm(dc[i], wo[:, pl.ds(ours, mine)])


def attention_grad(
    place, z, seqs, e, cosine, sine, gain_a, wqkv, q, k, v, p, xa, ra, own_do, rcv_do, dqkv,
    snd_row, rcv_row, row_copy, row_first, snd_br, rcv_half, core_send, core_recv, core_first, link, first,
    my_rows, their_rows, ours, mine, e_out, gain_a_out, emit, y_copy, between=None,
):
    length, feats = z.length, z.feats
    scale = HEAD_DIM ** (-0.5)
    for i in range(seqs):
        link.wait(first + i)
        row = jnp.zeros((length, 1), F32)
        for j in range(z.heads):
            span = pl.ds(j * HEAD_DIM, HEAD_DIM)
            do_j = (own_do[i, :, span] + rcv_do[i, :, span].astype(F32)).astype(BF16)
            q_j, k_j, v_j, probs = q[i, :, span], k[i, :, span], v[i, :, span], p[i, j]
            dp = mm_nt(do_j, v_j)
            dv = mm_tn(probs.astype(BF16), do_j)
            ds = (probs * (dp - jnp.sum(probs * dp, axis=-1, keepdims=True))).astype(BF16)
            dq = mm(ds, k_j) * scale
            dk = mm_tn(ds, q_j) * scale
            row = row + jnp.sum(dq * q_j.astype(F32) + dk * k_j.astype(F32) + dv * v_j.astype(F32), axis=-1, keepdims=True)
            at = pl.ds(pl.multiple_of(ours + j * HEAD_DIM, HEAD_DIM), HEAD_DIM)
            dqkv[i, 0, :, at] = (dq * cosine - turned(dq) * sine).astype(BF16)
            dqkv[i, 1, :, at] = (dk * cosine - turned(dk) * sine).astype(BF16)
            dqkv[i, 2, :, at] = dv.astype(BF16)
        snd_row[row_first + i] = to_row(row)
        row_copy(row_first + i, place.pair).start()
        for t in range(3):
            link.start(first + seqs + 3 * i + t, lambda rows, i=i, t=t: dqkv.at[i, t, rows, pl.ds(ours, mine)])

    if between is not None:
        between()
    for i in range(seqs):
        part = jnp.zeros((length, feats), F32)
        for t in range(3):
            link.wait(first + seqs + 3 * i + t)
            part = part + mm_nt(dqkv[i, t], wqkv[t])
        snd_br[core_first + i] = part.astype(BF16)
        half_copy(place, snd_br, rcv_half, core_send, core_recv, core_first, i, their_rows).start()
        row_copy(row_first + i, place.pair).wait_recv()
        snd_row[row_first + 2 + i] = snd_row[row_first + i] + rcv_row[row_first + i]
        row_copy(row_first + 2 + i, place.core_peer).start()

    gain_total = jnp.zeros((1, feats), F32)
    for i in range(seqs):
        half_copy(place, snd_br, rcv_half, core_send, core_recv, core_first, i, their_rows).wait_recv()
        row_copy(row_first + 2 + i, place.core_peer).wait_recv()
        mean = (from_row(snd_row[row_first + 2 + i]) + from_row(rcv_row[row_first + 2 + i])) * (1.0 / z.width)
        snd_row[row_first + 4 + i] = to_row(mean)
        own_mean = from_row(snd_row[row_first + 4 + i, :, my_rows])
        grad = snd_br[core_first + i, my_rows, :].astype(F32) + rcv_half[i].astype(F32)
        factor = ra[i, my_rows, :][:, :1]
        scaled = xa[i, my_rows, :].astype(F32) * factor
        e_out[i] = (e[i, my_rows, :] + factor * (grad * gain_a - scaled * own_mean)).astype(BF16)
        gain_total = gain_total + jnp.sum(grad * scaled, axis=0, keepdims=True)
        if y_copy is not None:
            y_copy(i).start()
    emit.start([e_out[i] for i in range(seqs)], 0)
    gain_a_out[...] = jnp.broadcast_to(gain_total, gain_a_out.shape)


def last_kernel(
    wide_ref, e_hbm, dc_hbm, gain_a_ref, gain_a_in, gain_f_in, cos_ref, sin_ref, wqkv_hbm, wo_hbm, q_hbm, k_hbm, v_hbm, p_hbm,
    xa_hbm, ra_hbm, dqkv_hbm, every_o_hbm, every_d_hbm, every_flag_hbm, every_in, ig_in,
    ig_hbm, every_hbm, qkv_out, wo_out, wd_out, gains_out,
    e, dc, wqkv, wo, q, k, v, p, xa, ra, ab,
    own_do, snd_do, rcv_do, dqkv, e_out, stage, snd_row, rcv_row, snd_br, rcv_half, relay,
    dct, every_c, mine_grad, from_left, from_right, block_g, block_o, block_d, flags, wd_sum, wo_sum, gains, core_gains, every_gain, gain_a_new,
    load_sem, x_send, x_recv, far_send, far_recv, relay_send, relay_recv, row_send, row_recv, core_send, core_recv,
    out_send, out_recv, out_local, right_sem, left_sem, every_sem, c_send, c_recv, c_local, gain_send, gain_recv, gain_local,
    pair_send, pair_recv, scatter_right, scatter_left, got_left, got_right, block_sem, out_sem,
):
    place = Place()
    half, core = place.half, place.core
    swap = wide_ref[1:2, :1]
    seqs, length, feats = xa.shape
    z = Sizes(feats, wo.shape[1], 8, length // 2)
    mine = z.mine
    me, planes = lax.axis_index("dp"), lax.axis_size("dp")
    share = feats // planes
    sources = (dc_hbm, wo_hbm, q_hbm, k_hbm, v_hbm, p_hbm, wqkv_hbm, e_hbm, xa_hbm, ra_hbm, every_flag_hbm)
    loads = Loader(tuple(zip(sources, (dc, wo, q, k, v, p, wqkv, e, xa, ra, flags))), load_sem)
    place.barrier()

    def targets(index, sender_half, rows):
        if index < seqs:
            return rcv_do.at[index, rows, :]
        n = index - seqs
        return dqkv.at[n // 3, n % 3, rows, pl.ds(pl.multiple_of(sender_half * mine, mine), mine)]

    link = PairLink(place, relay, (x_send, x_recv, far_send, far_recv, relay_send, relay_recv), targets)
    my_rows = pl.ds(pl.multiple_of(core * z.tokens, z.tokens), z.tokens)
    their_rows = pl.ds(pl.multiple_of((1 - core) * z.tokens, z.tokens), z.tokens)
    theirs = pl.multiple_of((1 - half) * mine, mine)
    ours = pl.multiple_of(half * mine, mine)
    emit = Emitter(place, ig_hbm, stage, swap, (out_send, out_recv, out_local))

    def row_copy(n, peer):
        return remote(snd_row.at[n], rcv_row.at[n], row_send.at[n], row_recv.at[n], peer)

    held = pltpu.make_async_copy(dqkv_hbm, dqkv, load_sem.at[11])
    gather = Gather(place, every_hbm.at[0], every_hbm, (right_sem, left_sem, every_sem, None), EARLY_STEPS + 1, z.length)
    gather.rest(EARLY_STEPS + 1)

    def share_rows(n):
        return pl.ds(pl.multiple_of(n * share, share), share)

    exchange_c = Exchange(place, lambda n: dct.at[share_rows(n), :], every_c, (c_send, c_recv, c_local))

    def normed():
        for i in range(seqs):
            ab[i] = (xa[i].astype(F32) * ra[i][:, :1] * gain_a_ref[...]).astype(BF16)

    def exchange_dc():
        for i in range(seqs):
            dct[:, i * length:(i + 1) * length] = jnp.transpose(dc[i].astype(F32)).astype(BF16)
        exchange_c.start()

    def fetch(src, dst, n):
        copy = pltpu.make_async_copy(src, dst, block_sem.at[n])
        copy.start()
        return copy

    def plane_down(n):
        copies = [fetch(every_hbm.at[n], block_g, 0), fetch(every_d_hbm.at[n], block_d, 1)]
        for copy in copies:
            copy.wait()
        flag = flags[n][:1, :1]
        shared = block_g[1].astype(F32)
        upper, lower = (shared * flag).astype(BF16), (shared * (1.0 - flag)).astype(BF16)
        narrow, wide = block_d[:, :length], block_d[:, length:]
        unit = block_g.shape[2]
        for block in range(8):
            right = upper if block == 4 else block_g[2 + block if block < 4 else 1 + block]
            part = mm(wide, right)
            if block < 2:
                part = part + mm(narrow, block_g[0] if block == 0 else lower)
            span = slice(block * unit, (block + 1) * unit)
            wd_sum[:, span] = wd_sum[:, span] + part

    def far(n):
        return (n - me > EARLY_STEPS) | (me - n > EARLY_STEPS)

    def down_grad(late):
        def body(n, carry):
            @pl.when(far(n) if late else jnp.logical_not(far(n)))
            def _():
                plane_down(n)
            return carry
        lax.fori_loop(0, planes, body, 0)

    def out_grad():
        def body(n, carry):
            fetch(every_o_hbm.at[n], block_o, 0).wait()
            wo_sum[...] = wo_sum[...] + mm(every_c[n][:, :length], block_o[0]) + mm(every_c[n][:, length:], block_o[1])
            return carry
        lax.fori_loop(0, planes, body, 0)

    def scatter(target, t, way):
        edge = me == (0 if way > 0 else planes - 1)
        got, sem_in = (from_left, got_left) if way > 0 else (from_right, got_right)
        sems = scatter_right if way > 0 else scatter_left
        own = mine_grad.at[t, share_rows(target), :]
        slot = got.at[target, t]
        at = target * 3 + t
        section, dp, mp = place.at
        peer = (section, dp + way, mp)

        @pl.when((me < target) if way > 0 else (me > target))
        def _():
            @pl.when(edge)
            def _():
                remote(own, slot, sems.at[at], sem_in.at[at], peer).start()

            @pl.when(jnp.logical_not(edge))
            def _():
                remote(slot, slot, sems.at[at], sem_in.at[at], place.pair).wait_recv()
                got[target, t] = (got[target, t].astype(F32) + mine_grad[t, share_rows(target), :].astype(F32)).astype(BF16)
                remote(slot, slot, sems.at[at], sem_in.at[at], peer).start()

    def scatter_end(target, t, way):
        slot = (from_left if way > 0 else from_right).at[target, t]
        at = target * 3 + t

        @pl.when((me < target) if way > 0 else (me > target))
        def _():
            sems, sem_in = (scatter_right, got_left) if way > 0 else (scatter_left, got_right)
            remote(slot, slot, sems.at[at], sem_in.at[at], place.pair).wait_send()

    def scatter_last(t):
        at = me * 3 + t
        total = mine_grad[t, share_rows(me), :].astype(F32)

        @pl.when(me > 0)
        def _():
            slot = from_left.at[me, t]
            remote(slot, slot, scatter_right.at[at], got_left.at[at], place.pair).wait_recv()

        @pl.when(me < planes - 1)
        def _():
            slot = from_right.at[me, t]
            remote(slot, slot, scatter_left.at[at], got_right.at[at], place.pair).wait_recv()

        qkv_sum = total
        left = jnp.where(me > 0, 1.0, 0.0)
        right = jnp.where(me < planes - 1, 1.0, 0.0)
        qkv_out[t] = qkv_sum + from_left[me, t].astype(F32) * left + from_right[me, t].astype(F32) * right

    for ref in (wd_sum, wo_sum):
        ref[...] = jnp.zeros_like(ref)

    @pl.when(me == 0)
    def _():
        from_left[0] = jnp.zeros_like(from_left[0])

    @pl.when(me == planes - 1)
    def _():
        from_right[planes - 1] = jnp.zeros_like(from_right[planes - 1])

    @pl.when(place.block == 1)
    def _():
        held.start()
        loads.wait(*range(11))
        held.wait()
        gain_a_new[...] = gain_a_in[...]
        exchange_dc()
        link.forward(tuple(range(seqs + 6)))
        normed()

    @pl.when(place.block == 0)
    def _():
        loads.wait(0, 1)
        for i in range(seqs):
            attention_grad_start(i, dc, wo, own_do, snd_do, link, 0, theirs, ours, mine)
        loads.wait(*range(2, 11))
        exchange_dc()

        def between():
            normed()
            down_grad(False)

        attention_grad(
            place, z, seqs, e, cos_ref[...], sin_ref[...], gain_a_ref[...], wqkv, q, k, v, p, xa, ra, own_do, rcv_do, dqkv,
            snd_row, rcv_row, row_copy, 0, snd_br, rcv_half, core_send, core_recv, 0, link, 0,
            my_rows, their_rows, ours, mine, e_out, gain_a_new, emit, None, between,
        )

    for t in range(3):
        mine_grad[t] = (mm_tn(ab[0], dqkv[0, t]) + mm_tn(ab[1], dqkv[1, t])).astype(BF16)
        if t == 0:
            gains[0:8, :] = jnp.concatenate([gain_a_new[0:1, :], 0.5 * gain_f_in[0:1, :], jnp.zeros_like(gain_a_new[0:6, :])], axis=0)
            pair_gains = remote(gains, core_gains, pair_send.at[0], pair_recv.at[0], place.core_peer)
            pair_gains.start()
        scatter(planes - 1, t, 1)
        scatter(0, t, -1)
    pair_gains.wait()
    every_gain[me] = gains[...] + core_gains[...]
    exchange_gain = Exchange(place, lambda n: every_gain.at[me], every_gain, (gain_send, gain_recv, gain_local))
    for n in range(1, planes):
        exchange_gain.copy(n).start()

    @pl.when(place.block == 1)
    def _():
        down_grad(False)

    for n in range(1, planes - 1):
        for t in range(3):
            scatter(planes - 1 - n, t, 1)
            scatter(n, t, -1)
    exchange_c.finish()
    out_grad()
    wo_copy = pltpu.make_async_copy(wo_sum, wo_out, out_sem.at[0])
    wo_copy.start()
    gather.finish()
    down_grad(True)
    wd_copy = pltpu.make_async_copy(wd_sum, wd_out, out_sem.at[1])
    wd_copy.start()
    for n in range(1, planes):
        source = lax.rem(me + planes - n, planes)
        slot = every_gain.at[source]
        remote(slot, slot, gain_send.at[n], gain_recv.at[n], place.pair).wait_recv()
        exchange_gain.copy(n).wait_send()
    total = every_gain[0]
    for n in range(1, planes):
        total = total + every_gain[n]
    gains_out[...] = total
    for t in range(3):
        scatter_last(t)
    for n in range(planes - 1):
        for t in range(3):
            scatter_end(planes - 1 - n, t, 1)
            scatter_end(n, t, -1)
    wo_copy.wait()
    wd_copy.wait()

    @pl.when(place.block == 0)
    def _():
        link.finish(tuple(range(seqs + 6)))
        for n in range(4):
            row_copy(n, place.core_peer).wait_send()
        for i in range(seqs):
            half_copy(place, snd_br, rcv_half, core_send, core_recv, 0, i, their_rows).wait_send()

    emit.finish(0, place.block == 0)


def shape(dims, kind):
    return jax.ShapeDtypeStruct(dims, kind)


ANY = pl.BlockSpec(memory_space=pl.ANY)
IN_VMEM = pl.BlockSpec(memory_space=pltpu.VMEM)


def vmem(dims, kind):
    return pltpu.VMEM(tuple(dims), kind)


def dma(*counts):
    return [pltpu.SemaphoreType.DMA((count,)) for count in counts]


def like(*arrays):
    return [vmem(array.shape, array.dtype) for array in arrays]


def call(kernel, name, number, out_shape, in_vmem, out_vmem, scratch, args, flops, aliases={}):
    return pl.pallas_call(
        kernel,
        out_shape=tuple(out_shape),
        in_specs=[IN_VMEM if n in in_vmem else ANY for n in range(len(args))],
        out_specs=tuple(IN_VMEM if n in out_vmem else ANY for n in range(len(out_shape))),
        scratch_shapes=scratch,
        compiler_params=pltpu.CompilerParams(collective_id=number, has_side_effects=True, vmem_limit_bytes=VMEM_LIMIT),
        cost_estimate=pl.CostEstimate(flops=flops, bytes_accessed=10**6, transcendentals=0),
        input_output_aliases=aliases,
        name=name,
    )(*args)


def run_main(wide, x0, c0, gain_a, gain_f, cosine, sine, wqkv, wo, wu, wd):
    seqs, tokens, width = x0.shape
    planes = lax.axis_size("dp")
    z = Sizes(wo.shape[0], wo.shape[1], wu.shape[1], tokens)
    state, half_state, heads_state = (seqs, z.length, z.feats), (seqs, tokens, z.feats), (seqs, z.length, z.mine)
    scores, slots = (seqs, z.heads, z.length, z.length), (SLOTS, z.length, z.unit)
    qkv, dqkv, messages = (seqs, 3, z.length, z.mine), (seqs, 3, z.length, z.cols), 12 + 2 * seqs + 2 * SLOTS
    gain, row = shape((8, z.feats), F32), (seqs, z.length, 128)
    out_shape = [shape((seqs, tokens, width), BF16)] * 2 + [shape(heads_state, BF16)] * 3 + [
        shape(scores, F32), shape(state, BF16), shape(row, F32), shape((planes, SLOTS - 1, z.length, z.unit), BF16),
        shape((planes, seqs, z.length, z.cols), BF16), shape((planes, z.feats // planes, seqs * z.length), BF16),
        shape((planes, 8, 128), F32),
        shape((3, z.length, wu.shape[1]), BF16),
        shape(state, BF16), shape(state, F32), shape(dqkv, BF16), gain, gain,
    ]
    small = (8, 8, z.length)
    scratch = like(wqkv, wo, wu, wd) + [
        vmem(state, BF16), vmem(state, BF16), vmem(half_state, BF16), vmem(state, BF16),
        vmem(heads_state, BF16), vmem(heads_state, BF16), vmem(heads_state, BF16), vmem(scores, F32),
        vmem((seqs, z.length, z.cols), BF16), vmem(row, F32), vmem(row, F32), vmem(slots, F32), vmem(slots, BF16),
        vmem(qkv, F32), vmem(qkv, BF16), vmem(qkv, BF16), vmem(slots, BF16), vmem(slots, BF16),
        vmem((4, 8, z.length), F32), vmem((4, 8, z.length), F32),
        vmem((4, z.length, z.feats), BF16), vmem((2, z.length, z.feats), BF16), vmem(half_state, BF16),
        vmem(state, BF16), vmem(state, F32), vmem(state, BF16), vmem(slots, BF16), vmem(slots, BF16), vmem(slots, BF16),
        vmem((z.feats, seqs * z.length), BF16), vmem(half_state, BF16), vmem((4, *half_state), BF16),
        vmem(heads_state, F32), vmem(heads_state, BF16), vmem(heads_state, BF16), vmem(dqkv, BF16),
        vmem(small, F32), vmem(small, F32),
        vmem((4, z.length, z.feats), BF16), vmem((2, z.length, z.feats), BF16), vmem(half_state, BF16),
        vmem((messages, z.length - DIRECT_ROWS, z.mine), BF16),
    ] + dma(4, *[messages] * 6, 4, 4, 4, 4, 6, 6, 4, 4, 4, 4, 5, 2, 2, 8, 8, 8, 10, *[planes, planes, planes, 1] * 2, *[planes, planes, 1] * 2, 2) + [pltpu.SemaphoreType.REGULAR((2,))]
    args = (wide, x0, c0, gain_a, gain_f, cosine, sine, wqkv, wo, wu, wd)
    return call(main_kernel, "main", 1, out_shape, (0, 3, 4, 5, 6), (16, 17), scratch, args, 10**11)


def run_last(
    wide, e, dc, gain_a, gain_a_in, gain_f_in, cosine, sine, wqkv, wo, q, k, v, p, xa, ra, dqkv, every_o, every_d, every_flag, every_g, ig,
):
    seqs, length, feats = e.shape
    z = Sizes(feats, wo.shape[1], 8, length // 2)
    planes, hidden = every_g.shape[0], 8 * every_g.shape[3]
    share = feats // planes
    state, half_state, heads_state = (seqs, length, feats), (seqs, z.tokens, feats), (seqs, length, z.mine)
    messages, row, pieces = seqs + 6, (8, feats), (planes, 3, share, z.cols)
    out_shape = [
        shape(ig.shape, BF16), shape(every_g.shape, BF16), shape((3, share, z.cols), F32), shape((share, z.cols), F32),
        shape((share, hidden), F32), shape(row, F32),
    ]
    scratch = like(e, dc, wqkv, wo, q, k, v, p, xa, ra) + [
        vmem(state, BF16),
        vmem(heads_state, F32), vmem(heads_state, BF16), vmem(heads_state, BF16), vmem(dqkv.shape, BF16),
        vmem(half_state, BF16), vmem(half_state, BF16),
        vmem((6, 8, length), F32), vmem((6, 8, length), F32), vmem((2, length, feats), BF16), vmem(half_state, BF16),
        vmem((messages, length - DIRECT_ROWS, z.mine), BF16),
        vmem((feats, seqs * length), BF16), vmem((planes, share, seqs * length), BF16), vmem((3, feats, z.cols), BF16),
        vmem(pieces, BF16), vmem(pieces, BF16), vmem(every_g.shape[1:], BF16), vmem(every_o.shape[1:], BF16),
        vmem(every_d.shape[1:], BF16), vmem(every_flag.shape, F32), vmem((share, hidden), F32), vmem((share, z.cols), F32),
        vmem(row, F32), vmem(row, F32), vmem((planes, *row), F32), vmem(row, F32),
    ] + dma(12, *[messages] * 6, 4, 4, 2, 2, 2, 2, 2, planes, planes, planes, planes, planes, 1, planes, planes, 1, 1, 1, *[3 * planes] * 4, 2, 2)
    args = (wide, e, dc, gain_a, gain_a_in, gain_f_in, cosine, sine, wqkv, wo, q, k, v, p, xa, ra, dqkv, every_o, every_d, every_flag, every_g, ig)
    return call(last_kernel, "last", 3, out_shape, (0, 3, 4, 5, 6, 7), (2, 5), scratch, args, 10**8, {20: 1, 21: 0})


def local(inputs, cotangent, width_index, qkv_weight, out_weight, attn_gain, ffn_gain, up_weight, down_weight):
    seqs, tokens, width = inputs.shape
    swap = width_index[0] > width_index[1]
    flag = (jnp.max(width_index) == 3).astype(F32)
    row = lax.broadcasted_iota(jnp.int32, (8, 128), 0)
    wide = jnp.where(row == 0, flag, jnp.where(row == 1, swap.astype(F32), 0.0))

    cosine, sine = rotary(2 * tokens, HEAD_DIM)
    gain_a = attn_gain.astype(F32)[None]
    gain_f = ffn_gain.astype(F32)[None]
    layer_out, input_grad, q, k, v, p, xa, ra, every_g, every_o, every_d, every_flag, up_term, dc, e, dqkv, gain_a_term, gain_f_term = run_main(
        wide, inputs, cotangent, gain_a, gain_f, cosine, sine, qkv_weight, out_weight, up_weight, down_weight
    )
    up_sum = lax.psum_scatter(up_term.reshape(up_weight.shape), "dp", scatter_dimension=0, tiled=True)
    input_grad, _, qkv_grad, out_grad, down_grad, gains = run_last(
        wide, e, dc, gain_a, gain_a_term, gain_f_term, cosine, sine, qkv_weight, out_weight, q, k, v, p, xa, ra, dqkv,
        every_o, every_d, every_flag, every_g, input_grad,
    )
    up_sum, qkv_grad = lax.optimization_barrier((up_sum, qkv_grad))
    size = gains.shape[1] // (2 * lax.axis_size("dp"))
    own = (lax.axis_index("dp") * 2 + lax.axis_index("mp")) * size
    gain_grads = lax.dynamic_slice_in_dim(gains[:2], own, size, axis=1)
    return (
        layer_out[None],
        input_grad[None],
        qkv_grad,
        out_grad,
        gain_grads[0],
        gain_grads[1],
        up_sum.astype(F32),
        down_grad,
    )


def solution(mesh):
    in_specs = (
        P("dp", "mp", None),
        P("dp", "mp", None),
        P("dp"),
        P(None, "section", "mp"),
        P("section", "mp"),
        P("section"),
        P("section"),
        P("section", "mp"),
        P("section", "mp"),
    )
    out_specs = (
        P("section", "dp", "mp", None),
        P("section", "dp", "mp", None),
        P(None, ("section", "dp"), "mp"),
        P(("section", "dp"), "mp"),
        P(("section", "dp", "mp")),
        P(("section", "dp", "mp")),
        P(("section", "dp"), "mp"),
        P(("section", "dp"), "mp"),
    )
    return jax.shard_map(local, mesh=mesh, in_specs=in_specs, out_specs=out_specs, check_vma=False)
```

```python
import functools
import types

import jax
import jax.numpy as jnp
import numpy as np
from jax import lax
from jax.sharding import PartitionSpec as P
from jax.experimental import pallas as pl
from jax.experimental.pallas import tpu as pltpu

HEAD_DIM = 128
EPSILON = 1e-05
GELU_C = 0.7978845608028654
GELU_A = 0.044715
MESH = pl.DeviceIdType.MESH
SLOTS = 10
LAG = 5
GRADS_TURN = 10
DIRECT_ROWS = 144
F32 = jnp.float32
BF16 = jnp.bfloat16
VMEM_LIMIT = 62 * 2**20


def mm(a, b):
    return lax.dot_general(a, b, (((1,), (0,)), ((), ())), preferred_element_type=F32)


def mm_nt(a, b):
    return lax.dot_general(a, b, (((1,), (1,)), ((), ())), preferred_element_type=F32)


def mm_tn(a, b):
    return lax.dot_general(a, b, (((0,), (0,)), ((), ())), preferred_element_type=F32)


def to_row(column):
    rows = column.shape[0]
    return jnp.transpose(jnp.broadcast_to(column, (rows, 128)))[:8]


def from_row(row):
    return jnp.transpose(row)[:, :1]


def rotary(length, head_size):
    half_dim = head_size // 2
    frequency = np.float32(10000.0) ** (np.float32(-2.0 / head_size) * np.arange(half_dim, dtype=np.float32))
    angles = np.arange(length, dtype=np.float32)[:, None] * frequency[None, :].astype(np.float32)
    cosine, sine = np.cos(angles).astype(np.float32), np.sin(angles).astype(np.float32)
    return jnp.asarray(np.concatenate([cosine, cosine], axis=1)), jnp.asarray(np.concatenate([-sine, sine], axis=1))


def turned(values):
    return pltpu.roll(values, HEAD_DIM // 2, 1)


def remote(src, dst, send_sem, recv_sem, device):
    return pltpu.make_async_remote_copy(
        src_ref=src, dst_ref=dst, send_sem=send_sem, recv_sem=recv_sem,
        device_id=device, device_id_type=MESH,
    )


class Place:
    def __init__(self):
        section, dp, mp = (lax.axis_index(name) for name in ("section", "dp", "mp"))
        self.block, self.half, self.core = section // 2, section % 2, mp
        other_half = 1 - self.half
        other_block = 1 - self.block
        self.at = (section, dp, mp)
        self.core_peer = (section, dp, 1 - mp)
        self.pair = (self.block * 2 + other_half, dp, mp)
        self.across = (other_block * 2 + self.half, dp, mp)
        self.corner = (other_block * 2 + other_half, dp, mp)

    def plane(self, n):
        section, dp, mp = self.at
        return (section, lax.rem(dp + n, lax.axis_size("dp")), mp)

    def barrier(self):
        sem = pltpu.get_barrier_semaphore()
        peers = [self.core_peer, self.pair, self.across, self.corner]
        peers += [self.plane(n) for n in range(1, lax.axis_size("dp"))]
        for peer in peers:
            pl.semaphore_signal(sem, inc=1, device_id=peer, device_id_type=MESH)
        pl.semaphore_wait(sem, len(peers))


class Exchange:
    def __init__(self, place, piece, slots, sems):
        self.place, self.piece, self.slots = place, piece, slots
        self.send, self.recv, self.local = sems
        self.me, self.count = lax.axis_index("dp"), lax.axis_size("dp")

    def copy(self, n):
        target = lax.rem(self.me + n, self.count)
        return remote(self.piece(target), self.slots.at[self.me], self.send.at[n], self.recv.at[n], self.place.plane(n))

    def own(self):
        return pltpu.make_async_copy(self.piece(self.me), self.slots.at[self.me], self.local.at[0])

    def start(self):
        self.own().start()
        for n in range(1, self.count):
            self.copy(n).start()

    def finish(self):
        self.own().wait()
        for n in range(1, self.count):
            source = lax.rem(self.me + self.count - n, self.count)
            held = self.slots.at[source]
            remote(held, held, self.send.at[n], self.recv.at[n], self.place.plane(n)).wait_recv()
            self.copy(n).wait_send()


class PairLink:
    def __init__(self, place, relay, sems, targets):
        self.place, self.relay, self.targets = place, relay, targets
        self.send, self.recv, self.far_send, self.far_recv, self.relay_send, self.relay_recv = sems
        rows = DIRECT_ROWS + relay.shape[1]
        self.direct = slice(0, DIRECT_ROWS)
        self.detour = slice(DIRECT_ROWS, rows)
        self.sources = {}

    def near(self, index):
        src, dst = self.sources[index](self.direct), self.targets(index, self.place.half, self.direct)
        return remote(src, dst, self.send.at[index], self.recv.at[index], self.place.pair)

    def far(self, index):
        src = self.sources[index](self.detour)
        return remote(src, self.relay.at[index], self.far_send.at[index], self.relay_recv.at[index], self.place.across)

    def whole(self, index):
        rows, src = slice(0, self.detour.stop), self.sources[index]
        dst = self.targets(index, self.place.half, rows)
        return remote(src(rows), dst, self.send.at[index], self.recv.at[index], self.place.pair)

    def start(self, index, src):
        self.sources[index] = src
        self.near(index).start()
        self.far(index).start()

    def start_near(self, index, src):
        self.sources[index] = src
        self.near(index).start()

    def start_far(self, index):
        self.far(index).start()

    def start_whole(self, index, src):
        self.sources[index] = src
        self.whole(index).start()

    def wait(self, index):
        other = 1 - self.place.half
        for rows, sem in ((self.direct, self.recv), (self.detour, self.far_recv)):
            dst = self.targets(index, other, rows)
            remote(dst, dst, self.send.at[index], sem.at[index], self.place.pair).wait_recv()

    def wait_whole(self, index):
        dst = self.targets(index, 1 - self.place.half, slice(0, self.detour.stop))
        remote(dst, dst, self.send.at[index], self.recv.at[index], self.place.pair).wait_recv()

    def finish(self, indices):
        for index in indices:
            self.near(index).wait_send()
            self.far(index).wait_send()

    def finish_whole(self, indices):
        for index in indices:
            self.whole(index).wait_send()

    def forward(self, indices):
        copies = []
        for index in indices:
            held = self.relay.at[index]
            remote(held, held, self.relay_send.at[index], self.relay_recv.at[index], self.place.across).wait_recv()
            copy = remote(held, self.targets(index, self.place.half, self.detour), self.relay_send.at[index], self.far_recv.at[index], self.place.corner)
            copy.start()
            copies.append(copy)
        for copy in copies:
            copy.wait_send()


def spread(value, width):
    return jnp.broadcast_to(value, (value.shape[0], width))


def slot_block(slot):
    return (0, slot) if slot < 2 else (1, slot - 2)


def slot_weight(slot, weight):
    unit = weight.shape[1] // 8
    at = slot_block(slot)[1] * unit
    return weight[:, at:at + unit]


def mask_slot(slot, value, flag):
    if slot == 1:
        return value * (1.0 - flag)
    return value if slot < 6 else value * flag


NARROW, WIDE = (0, 1), tuple(range(2, SLOTS))
G_PLACE = (0, 1, 2, 3, 4, 5, 9, 6, 7, 8)
DG_STRAIGHT, DG_MIDDLE, DG_LATE = (0, 1, 2), (3, 4), (5, 6, 7, 8, 9)


class Sizes:
    def __init__(self, feats, cols, hidden, tokens):
        self.feats, self.cols, self.unit, self.tokens = feats, cols, hidden // 8, tokens
        self.mine, self.length, self.width = cols // 2, 2 * tokens, 2 * feats
        self.heads = self.mine // HEAD_DIM


class Emitter:
    def __init__(self, place, out, stage, swap, sems, first=0):
        self.place, self.out, self.stage, self.swap, self.sems, self.first = place, out, stage, swap, sems, first

    def span(self):
        feats = self.stage.shape[-1]
        return pl.ds(pl.multiple_of(self.place.half * feats, feats), feats)

    def far(self, i):
        at = self.first + i
        return remote(self.stage.at[i], self.out.at[i, :, self.span()], self.sems[0].at[at], self.sems[1].at[at], self.place.pair)

    def near(self, i):
        return pltpu.make_async_copy(self.stage.at[i], self.out.at[i, :, self.span()], self.sems[2].at[self.first + i])

    def prepare(self, values):
        narrow, wide = (value.astype(F32) for value in values)
        self.stage[0] = (narrow * (1.0 - self.swap) + wide * self.swap).astype(BF16)
        self.stage[1] = (wide * (1.0 - self.swap) + narrow * self.swap).astype(BF16)

    def start(self, owner):
        @pl.when(self.place.half == owner)
        def _():
            for i in range(2):
                self.near(i).start()

        @pl.when(self.place.half != owner)
        def _():
            for i in range(2):
                self.far(i).start()

    def finish(self, owner):
        @pl.when(self.place.half == owner)
        def _():
            for i in range(2):
                self.near(i).wait()
                self.far(i).wait_recv()

        @pl.when(self.place.half != owner)
        def _():
            for i in range(2):
                self.far(i).wait_send()


class Gather:
    def __init__(self, place, mine, every, sems, first, last):
        self.me, self.count = lax.axis_index("dp"), lax.axis_size("dp")
        self.place, self.mine, self.every = place, mine, every
        self.right, self.left, self.recv, self.local = sems
        self.first, self.last = first, min(last, self.count - 1)

    def send(self, block, way, number):
        section, dp, mp = self.place.at
        sems = self.right if way > 0 else self.left
        src = self.mine if number == 1 else self.every.at[block]
        return remote(src, self.every.at[block], sems.at[block], self.recv.at[block], (section, dp + way, mp))

    def arrive(self, block):
        held = self.every.at[block]
        remote(held, held, self.right.at[block], self.recv.at[block], self.place.pair).wait_recv()

    def moves(self, number):
        me, last = self.me, self.count - 1
        right, left = me - number + 1, me + number - 1
        return ((1, right, (right >= 0) & (me < last)), (-1, left, (left <= last) & (me > 0)))

    def own(self):
        return pltpu.make_async_copy(self.mine, self.every.at[self.me], self.local.at[0])

    def step(self, number):
        if number == 1:
            self.own().start()
        if number > self.last:
            return
        for way, block, active in self.moves(number):
            @pl.when(active)
            def _(way=way, block=block):
                if number > self.first:
                    self.arrive(block)
                self.send(block, way, number).start()

    def rest(self, number):
        for more in range(number, self.last + 1):
            self.step(more)

    def finish(self):
        for number in range(self.first, self.last + 1):
            left, right = self.me - number, self.me + number
            done = number == self.last

            @pl.when((left >= 0) if done else (left >= 0) & (self.me == self.count - 1))
            def _(block=left):
                self.arrive(block)

            @pl.when((right < self.count) if done else (right < self.count) & (self.me == 0))
            def _(block=right):
                self.arrive(block)

            for way, block, active in self.moves(number):
                @pl.when(active)
                def _(way=way, block=block):
                    self.send(block, way, number).wait_send()
        if self.first == 1:
            self.own().wait()


class Scatter:
    def __init__(self, place, piece, landing, sends, arrivals, slots, intake, in_sem, chunks):
        self.place, self.piece, self.landing, self.sends, self.arrivals = place, piece, landing, sends, arrivals
        self.slots, self.intake, self.in_sem, self.chunks = slots, intake, in_sem, chunks
        self.me, self.count = lax.axis_index("dp"), lax.axis_size("dp")

    def send(self, way, target, chunk, src):
        section, dp, mp = self.place.at
        at = target * self.chunks + chunk
        return remote(src, self.landing[way].at[target, chunk], self.sends[way].at[at], self.arrivals[way].at[at], (section, dp + way, mp))

    def fetch(self, way, target, chunk):
        at = target * self.chunks + chunk
        held = self.landing[way].at[target, chunk]
        remote(held, held, self.sends[way].at[at], self.arrivals[way].at[at], self.place.pair).wait_recv()
        copy = pltpu.make_async_copy(held, self.intake[way], self.in_sem.at[0])
        copy.start()
        copy.wait()
        return self.intake[way][...].astype(F32)

    def each(self, way, body):
        def step_body(step, carry):
            body(step, self.count - 1 - step if way > 0 else step)
            return carry
        lax.fori_loop(0, self.count - 1, step_body, 0)

    def from_edge(self, way, chunk):
        @pl.when(self.me == (0 if way > 0 else self.count - 1))
        def _():
            self.each(way, lambda step, target: self.send(way, target, chunk, self.piece(chunk, target)).start())

    def edges(self, chunk):
        self.from_edge(1, chunk)
        self.from_edge(-1, chunk)

    def between(self, way, target):
        if way > 0:
            return (self.me > 0) & (self.me < target)
        return (self.me < self.count - 1) & (self.me > target)

    def turns(self):
        return range(self.chunks + max(self.count - 3, 0))

    def middle(self, turn):
        if self.count < 3 or turn not in self.turns():
            return
        def pass_on(way, step, target):
            depth = self.me if way > 0 else self.count - 1 - self.me
            chunk = turn + 1 - depth

            @pl.when(self.between(way, target) & (chunk >= 0) & (chunk < self.chunks))
            def _():
                slot = self.slots(way, lax.rem(chunk, 2) * (self.count - 1) + step)
                total = self.fetch(way, target, chunk) + self.piece(chunk, target)[...].astype(F32)

                @pl.when(chunk >= 2)
                def _():
                    self.send(way, target, chunk - 2, slot).wait_send()

                slot[...] = total.astype(BF16)
                self.send(way, target, chunk, slot).start()

        def both(step, carry):
            pass_on(1, step, self.count - 1 - step)
            pass_on(-1, step, step)
            return carry

        lax.fori_loop(0, self.count - 1, both, 0)

    def last(self, chunk, total_ref):
        total_ref[...] = self.piece(chunk, self.me)[...].astype(F32)
        for way, there in ((1, self.me > 0), (-1, self.me < self.count - 1)):
            @pl.when(there)
            def _(way=way):
                total_ref[...] = total_ref[...] + self.fetch(way, self.me, chunk)

    def finish(self):
        for way in (1, -1):
            edge = self.me == (0 if way > 0 else self.count - 1)

            def sent(chunk, step, target, way=way, edge=edge):
                active = (edge | self.between(way, target)) if chunk >= self.chunks - 2 else edge

                @pl.when(active)
                def _():
                    self.send(way, target, chunk, self.piece(chunk, target)).wait_send()

            for chunk in range(self.chunks):
                self.each(way, functools.partial(sent, chunk))


def main_kernel(names, *refs):
    r = types.SimpleNamespace(**dict(zip(names, refs)))
    place = Place()
    half, core = place.half, place.core
    me, planes = lax.axis_index("dp"), lax.axis_size("dp")
    seqs, length, feats = r.xa.shape
    z = Sizes(feats, r.wo.shape[1], r.wud.shape[2], length // 2)
    mine, unit = z.mine, z.unit
    share = feats // planes

    r.wu, r.wd = r.wud.at[0], r.wud.at[1]
    weights = ((r.wqkv_hbm, r.wqkv), (r.wo_hbm, r.wo), (r.wu_hbm, r.wu), (r.wd_hbm, r.wd))

    @pl.when(place.block == 0)
    def _():
        for n in range(4):
            pltpu.make_async_copy(*weights[n], r.load_sem.at[n]).start()

    @pl.when(place.block == 1)
    def _():
        for n in range(3, -1, -1):
            pltpu.make_async_copy(*weights[n], r.load_sem.at[n]).start()

    def loaded(n):
        pltpu.make_async_copy(*weights[n], r.load_sem.at[n]).wait()

    first_width, second_width = r.width[0], r.width[1]
    r.wide[...] = jnp.zeros_like(r.wide)
    r.wide[0:1, :] = jnp.full((1, 128), 1.0 - 0.5 * (first_width * second_width).astype(F32), F32)
    r.wide[1:2, :] = jnp.full((1, 128), lax.shift_right_logical(first_width, 1).astype(F32), F32)
    flag, swap = r.wide[0:1, :1], r.wide[1:2, :1]
    gain_a = r.gain_a[...].reshape(1, feats).astype(F32)
    gain_f = r.gain_f[...].reshape(1, feats).astype(F32)

    place.barrier()

    first_u, first_dg = 6 + seqs, 6 + seqs + SLOTS
    first_do = first_dg + SLOTS
    first_dqkv = first_do + seqs

    def targets(index, sender_half, rows):
        span = pl.ds(pl.multiple_of(sender_half * mine, mine), mine)
        if index < 6:
            return r.rcv_qkv.at[index // 3, index % 3, rows, :]
        if index < first_u:
            return r.o.at[index - 6, rows, span]
        if index < first_dg:
            return r.rcv_u.at[index - first_u, rows, :]
        if index < first_do:
            return r.rcv_dg.at[index - first_dg, rows, :]
        if index < first_dqkv:
            return r.rcv_do.at[index - first_do, rows, :]
        n = index - first_dqkv
        return r.dqkv.at[n // 3, n % 3, rows, span]

    link = PairLink(place, r.relay, (r.x_send, r.x_recv, r.far_send, r.far_recv, r.relay_send, r.relay_recv), targets)
    forward_order = tuple(range(first_dg))
    ffn_order = tuple(range(first_dg, first_do))
    do_order = tuple(range(first_do, first_dqkv))
    dqkv_order = tuple(range(first_dqkv, first_dqkv + 6))
    my_rows = pl.ds(pl.multiple_of(core * z.tokens, z.tokens), z.tokens)
    their_rows = pl.ds(pl.multiple_of((1 - core) * z.tokens, z.tokens), z.tokens)
    my_feats = pl.ds(pl.multiple_of(half * feats, feats), feats)

    def share_rows(n):
        return pl.ds(pl.multiple_of(n * share, share), share)

    gather = Gather(place, r.g.at[0:SLOTS - 1], r.every_g, (r.g_right, r.g_left, r.g_sem, r.g_local), 1, length)
    gather_o = Gather(place, r.o, r.every_o, (r.o_right, r.o_left, r.o_sem, r.o_local), 1, length)
    exchange_d = Exchange(place, lambda n: r.dt.at[share_rows(n), :], r.every_d, (r.d_send, r.d_recv, r.d_local))
    exchange_c = Exchange(place, lambda n: r.dt.at[share_rows(n), :], r.every_c, (r.c_send, r.c_recv, r.c_local))
    exchange_flag = Exchange(place, lambda n: r.wide, r.every_flag, (r.flag_send, r.flag_recv, r.flag_local))
    exchange_flag.start()

    def local_copy(src, dst, n):
        return pltpu.make_async_copy(src, dst, r.in_local.at[n])

    def core_half(src, dst, n):
        return remote(src, dst, r.in_send.at[n], r.in_recv.at[n], place.core_peer)

    def x_copy(i):
        return remote(r.x2.at[i], r.xa.at[i, my_rows, :], r.y_send.at[i], r.y_recv.at[i], place.across)

    def e_copy(i):
        return remote(r.e_out.at[i], r.e_in.at[i, my_rows, :], r.y_send.at[i], r.y_recv.at[i], place.across)

    def start_half(src_ref, dst_ref, first):
        for i in range(seqs):
            local_copy(src_ref.at[i, :, my_feats], dst_ref.at[i, my_rows, :], first + i).start()
            core_half(src_ref.at[i, :, my_feats], dst_ref.at[i, my_rows, :], first + i).start()

    def ordered_halves(raw_ref, dst_ref, first):
        for i in range(seqs):
            local_copy(raw_ref.at[i, my_rows, :], raw_ref.at[i, my_rows, :], first + i).wait()
            core_half(raw_ref.at[i, my_rows, :], raw_ref.at[i, my_rows, :], first + i).wait()
        for i in range(seqs):
            mixed = raw_ref[i].astype(F32) * (1.0 - swap) + raw_ref[1 - i].astype(F32) * swap
            dst_ref[i] = mixed.astype(BF16)

    def pass_half(dst_ref, n, i):
        core_half(dst_ref.at[i, my_rows, :], dst_ref.at[i, my_rows, :], n).start()
        core_half(dst_ref.at[i, my_rows, :], dst_ref.at[i, my_rows, :], n).wait()

    def sq_copy(n):
        return remote(r.snd_sq.at[n], r.rcv_sq.at[n], r.sq_send.at[n], r.sq_recv.at[n], place.pair)

    def core_copy(n):
        return remote(r.snd_br.at[n], r.rcv_br.at[n], r.core_send.at[n], r.core_recv.at[n], place.core_peer)

    def core_rows(i):
        return remote(r.snd_br.at[2 + i, their_rows, :], r.rcv_half.at[i], r.core_send.at[2 + i], r.core_recv.at[2 + i], place.core_peer)

    def row_copy(n, peer):
        return remote(r.snd_row.at[n], r.rcv_row.at[n], r.row_send.at[n], r.row_recv.at[n], peer)

    def db_copy(n):
        return remote(r.snd_db.at[n], r.rcv_db.at[n], r.db_send.at[n], r.db_recv.at[n], place.core_peer)

    def da_rows(i):
        return remote(r.snd_db.at[2 + i, their_rows, :], r.rcv_da.at[i], r.db_send.at[2 + i], r.db_recv.at[2 + i], place.core_peer)

    def ready(n):
        pl.semaphore_signal(r.go_sem.at[n], inc=1, device_id=place.pair, device_id_type=MESH)

    def wait_ready(n):
        pl.semaphore_wait(r.go_sem.at[n], 1)

    out_sems = (r.out_send, r.out_recv, r.out_local)
    emit_x1 = Emitter(place, r.layer_out, r.stage.at[0], swap, out_sems, 0)
    emit_x2 = Emitter(place, r.layer_out, r.stage.at[1], swap, out_sems, 2)
    emit_e1 = Emitter(place, r.input_grad, r.stage.at[2], swap, out_sems, 4)
    emit_e0 = Emitter(place, r.input_grad, r.stage.at[3], swap, out_sems, 6)
    theirs = pl.multiple_of((1 - half) * mine, mine)
    ours = pl.multiple_of(half * mine, mine)

    def dg_part(slot):
        r.snd_dg[slot] = mm(r.e_in[slot_block(slot)[0]], slot_weight(slot, r.wd)).astype(BF16)

    def dg_source(slot):
        return lambda rows: r.snd_dg.at[slot, rows, :]

    def transposed(src_ref):
        for i in range(seqs):
            r.dt[:, i * length:(i + 1) * length] = jnp.transpose(src_ref[i].astype(F32)).astype(BF16)

    @pl.when(place.block == 0)
    def _():
        start_half(r.x0, r.xf, 0)
        ordered_halves(r.xf, r.xa, 0)

    @pl.when(place.block == 1)
    def _():
        start_half(r.c0, r.dc, 2)
        loaded(3)
        ordered_halves(r.dc, r.e_in, 2)
        for slot in range(SLOTS):
            dg_part(slot)
        transposed(r.e_in)
        exchange_d.start()
        link.forward(forward_order[:6])
        link.start_whole(first_dg, dg_source(0))
        link.forward(forward_order[6:8])
        link.start_whole(first_dg + 1, dg_source(1))
        link.forward(forward_order[8:])
        link.start_whole(first_dg + 2, dg_source(2))

    for i in range(seqs):
        @pl.when(place.block == 1)
        def _():
            x_copy(i).wait_recv()
            if i == 1:
                ready(0)
            pass_half(r.xa, i, i)

        x = r.xa[i].astype(F32)
        r.snd_sq[i] = to_row(jnp.sum(x * x, axis=-1, keepdims=True))
        sq_copy(i).start()
        r.xg[i] = (x * gain_a).astype(BF16)
        if i == 0:
            loaded(0)
        for t in range(3):
            r.snd_qkv[i, t] = mm(r.xg[i], r.wqkv[t, :, pl.ds(theirs, mine)]).astype(BF16)
            source = lambda rows, i=i, t=t: r.snd_qkv.at[i, t, rows, :]

            @pl.when(place.block == 0)
            def _():
                link.start(3 * i + t, source)

            @pl.when(place.block == 1)
            def _():
                if i == 0:
                    link.start_whole(t, source)
                else:
                    link.start_near(3 + t, source)

    @pl.when(place.block == 1)
    def _():
        wait_ready(0)
        for t in range(3):
            link.start_far(3 + t)

    for i in range(seqs):
        for t in range(3):
            r.own_qkv[i, t] = mm(r.xg[i], r.wqkv[t, :, pl.ds(ours, mine)])

    cosine, sine = r.cosine[...], r.sine[...]
    scale = HEAD_DIM ** (-0.5)
    causal = lax.broadcasted_iota(jnp.int32, (length, length), 0) >= lax.broadcasted_iota(jnp.int32, (length, length), 1)
    for i in range(seqs):
        sq_copy(i).wait_recv()
        factor = lax.rsqrt((from_row(r.snd_sq[i]) + from_row(r.rcv_sq[i])) * (1.0 / z.width) + EPSILON)
        r.ra[i] = spread(factor, 128)
        if i == 0:
            @pl.when(place.block == 0)
            def _():
                for t in range(3):
                    link.wait(t)

            @pl.when(place.block == 1)
            def _():
                for t in range(3):
                    link.wait_whole(t)
        else:
            for t in range(3):
                link.wait(3 + t)
        for j in range(z.heads):
            span = pl.ds(j * HEAD_DIM, HEAD_DIM)
            raw = [(r.own_qkv[i, t, :, span] + r.rcv_qkv[i, t, :, span].astype(F32)) * factor for t in range(3)]
            q_j = (raw[0] * cosine + turned(raw[0]) * sine).astype(BF16)
            k_j = (raw[1] * cosine + turned(raw[1]) * sine).astype(BF16)
            v_j = raw[2].astype(BF16)
            r.q[i, :, span], r.k[i, :, span], r.v[i, :, span] = q_j, k_j, v_j
            scores = jnp.where(causal, mm_nt(q_j, k_j) * scale, -1e30)
            exponent = jnp.exp(scores - jnp.max(scores, axis=-1, keepdims=True))
            probs = exponent / jnp.sum(exponent, axis=-1, keepdims=True)
            r.p[i, j] = probs
            r.o[i, :, pl.ds(pl.multiple_of(ours + j * HEAD_DIM, HEAD_DIM), HEAD_DIM)] = mm(probs.astype(BF16), v_j).astype(BF16)
        link.start(6 + i, lambda rows, i=i: r.o.at[i, rows, pl.ds(ours, mine)])

    loaded(1)
    for i in range(seqs):
        link.wait(6 + i)
        r.snd_br[i] = mm_nt(r.o[i], r.wo[...]).astype(BF16)
        core_copy(i).start()

    @pl.when(place.block == 1)
    def _():
        for slot in DG_MIDDLE:
            link.start(first_dg + slot, dg_source(slot))

    gather_o.step(1)

    def slot_start(slot):
        part = mm(r.xg[slot_block(slot)[0]], slot_weight(slot, r.wu))
        r.u[slot] = part
        r.snd_u[slot] = part.astype(BF16)
        link.start(first_u + slot, lambda rows: r.snd_u.at[slot, rows, :])

    loaded(2)
    for i, slots in enumerate((NARROW, WIDE)):
        core_copy(i).wait_recv()
        r.xf[i] = (r.xa[i].astype(F32) + (r.snd_br[i].astype(F32) + r.rcv_br[i].astype(F32))).astype(BF16)
        x = r.xf[i].astype(F32)
        r.snd_sq[2 + i] = to_row(jnp.sum(x * x, axis=-1, keepdims=True))
        sq_copy(2 + i).start()
        r.xg[i] = (x * gain_f).astype(BF16)
        for slot in slots:
            slot_start(slot)

    @pl.when(place.block == 1)
    def _():
        for slot in DG_LATE:
            link.start(first_dg + slot, dg_source(slot))

    emit_x1.prepare([r.xf[i, my_rows, :] for i in range(seqs)])
    factors = {}

    def row_factor(i):
        sq_copy(2 + i).wait_recv()
        factors[i] = lax.rsqrt((from_row(r.snd_sq[2 + i]) + from_row(r.rcv_sq[2 + i])) * (1.0 / z.width) + EPSILON)
        r.rf[i] = spread(factors[i], 128)

    def activate(slot):
        link.wait(first_u + slot)
        value = (r.u[slot] + r.rcv_u[slot].astype(F32)) * factors[slot_block(slot)[0]]
        squared = value * value
        bent = jnp.tanh(GELU_C * (value + GELU_A * (squared * value)))
        slope = 0.5 * (1.0 + bent) + 0.5 * value * (1.0 - bent * bent) * (GELU_C * (1.0 + 3.0 * GELU_A * squared))
        r.u[slot] = value
        r.rcv_u[slot] = mask_slot(slot, slope, flag).astype(BF16)
        g_k = mask_slot(slot, 0.5 * value * (1.0 + bent), flag).astype(BF16)
        r.g[G_PLACE[slot]] = g_k
        return mm_nt(g_k, slot_weight(slot, r.wd))

    def finish_rows(i):
        core_rows(i).wait_recv()
        total = r.snd_br[2 + i, my_rows, :].astype(F32) + r.rcv_half[i].astype(F32)
        r.x2[i] = (r.xf[i, my_rows, :].astype(F32) + total).astype(BF16)

        @pl.when(place.block == 0)
        def _():
            x_copy(i).start()

    @pl.when(place.block == 0)
    def _():
        loaded(3)

    row_factor(0)
    r.snd_br[2] = (activate(0) + activate(1)).astype(BF16)
    core_rows(0).start()
    gather_o.step(2)
    row_factor(1)
    total = activate(2) + activate(3)
    finish_rows(0)
    for slot in WIDE[2:]:
        total = total + activate(slot)
    r.snd_br[3] = total.astype(BF16)
    core_rows(1).start()
    r.g[1] = r.g[1] + r.g[SLOTS - 1]
    finish_rows(1)
    emit_x2.prepare([r.x2[i] for i in range(seqs)])
    gather.step(1)
    gather_o.rest(3)

    def piece(chunk, target):
        column = pl.multiple_of(lax.rem(chunk, 8) * unit, unit)
        return r.wud.at[lax.div(chunk, 8), share_rows(target), pl.ds(column, unit)]

    def slots(way, n):
        per = max(length // share, 1)
        ref = r.snd_qkv if way > 0 else r.rcv_qkv
        at = lax.div(n, per)
        return ref.at[lax.div(at, 3), lax.rem(at, 3), share_rows(lax.rem(n, per)), :]

    intake = {1: r.snd_u.at[0, 0:share, :], -1: r.snd_u.at[1, 0:share, :]}
    scatter = Scatter(
        place, piece, {1: r.from_left, -1: r.from_right}, {1: r.sum_right, -1: r.sum_left}, {1: r.got_left, -1: r.got_right},
        slots, intake, r.intake_sem, 14,
    )

    @pl.when(place.block == 0)
    def _():
        link.forward(forward_order[3:first_u])
        link.forward(tuple(first_dg + slot for slot in DG_MIDDLE))
        link.forward(forward_order[first_u:])
        gather.step(2)
        link.forward(tuple(first_dg + slot for slot in DG_LATE))
        link.forward(do_order + dqkv_order)
        gather.rest(3)
        for i, slot_list in enumerate((NARROW, WIDE)):
            e_copy(i).wait_recv()
            if i == 1:
                ready(1)
            pass_half(r.e_in, 2 + i, i)
            for slot in slot_list:
                dg_part(slot)
                if i == 0:
                    link.start_whole(first_dg + slot, dg_source(slot))
                else:
                    link.start_near(first_dg + slot, dg_source(slot))
                if i == 1 and slot == WIDE[1]:
                    wait_ready(1)
                    for sent in WIDE[:2]:
                        link.start_far(first_dg + sent)
                if i == 1 and slot > WIDE[1]:
                    link.start_far(first_dg + slot)
        transposed(r.e_in)
        exchange_d.start()
        link.finish(forward_order[:3])

    @pl.when(place.block == 1)
    def _():
        link.finish_whole(forward_order[:3])

    link.finish(forward_order[3:])
    for i in range(seqs):
        r.xg[i] = (r.xf[i].astype(F32) * r.rf[i][:, :1] * gain_f).astype(BF16)

    def hidden_back(slot):
        @pl.when(place.block == 0)
        def _():
            (link.wait_whole if slot in NARROW else link.wait)(first_dg + slot)

        @pl.when(place.block == 1)
        def _():
            (link.wait_whole if slot in DG_STRAIGHT else link.wait)(first_dg + slot)

        grad = r.snd_dg[slot].astype(F32) + r.rcv_dg[slot].astype(F32)
        du_k = (grad * r.rcv_u[slot].astype(F32)).astype(BF16)
        r.du[slot] = du_k
        return mm_nt(du_k, slot_weight(slot, r.wu)), jnp.sum(du_k.astype(F32) * r.u[slot], axis=-1, keepdims=True)

    def up_grad(block):
        part = mm_tn(r.xg[1], r.du[2 + block])
        if block < 2:
            part = part + mm_tn(r.xg[0], r.du[block])
        r.wu[:, block * unit:(block + 1) * unit] = part.astype(BF16)
        scatter.edges(block)

    def core_sum_start(i, slot_list):
        total = row = None
        for slot in slot_list:
            more, more_row = hidden_back(slot)
            total, row = (more, more_row) if total is None else (total + more, row + more_row)

            if i == 1:
                @pl.when(place.block == 0)
                def _(slot=slot):
                    up_grad(slot - 2)

        r.snd_db[i] = total.astype(BF16)
        db_copy(i).start()
        r.snd_row[i] = to_row(row)
        row_copy(i, place.core_peer).start()

    def ffn_done(i):
        db_copy(i).wait_recv()
        row_copy(i, place.core_peer).wait_recv()
        mean = (from_row(r.snd_row[i]) + from_row(r.rcv_row[i])) * (1.0 / z.width)
        grad = r.snd_db[i].astype(F32) + r.rcv_db[i].astype(F32)
        factor = r.rf[i][:, :1]
        scaled = r.xf[i].astype(F32) * factor
        new = r.e_in[i].astype(F32) + factor * (grad * gain_f - scaled * mean)
        r.e[i] = new
        r.dc[i] = new.astype(BF16)
        r.snd_do[i] = mm(r.dc[i], r.wo[:, pl.ds(theirs, mine)]).astype(BF16)
        link.start(first_do + i, lambda rows: r.snd_do.at[i, rows, :])
        r.own_do[i] = mm(r.dc[i], r.wo[:, pl.ds(ours, mine)])
        return jnp.sum(grad * scaled, axis=0, keepdims=True)

    core_sum_start(0, NARROW)
    gain_f_sum = ffn_done(0)
    core_sum_start(1, WIDE)
    gain_f_sum = gain_f_sum + ffn_done(1)
    r.gains[...] = jnp.zeros_like(r.gains)
    r.gains[1:2, :] = 0.5 * gain_f_sum
    emit_e1.prepare([r.dc[i, my_rows, :] for i in range(seqs)])
    exchange_d.finish()
    transposed(r.dc)
    exchange_c.start()

    for i in range(seqs):
        link.wait(first_do + i)
        row = jnp.zeros((length, 1), F32)
        for j in range(z.heads):
            span = pl.ds(j * HEAD_DIM, HEAD_DIM)
            do_j = (r.own_do[i, :, span] + r.rcv_do[i, :, span].astype(F32)).astype(BF16)
            q_j, k_j, v_j, probs = r.q[i, :, span], r.k[i, :, span], r.v[i, :, span], r.p[i, j]
            dp = mm_nt(do_j, v_j)
            dv = mm_tn(probs.astype(BF16), do_j)
            ds = (probs * (dp - jnp.sum(probs * dp, axis=-1, keepdims=True))).astype(BF16)
            dq = mm(ds, k_j) * scale
            dk = mm_tn(ds, q_j) * scale
            row = row + jnp.sum(dq * q_j.astype(F32) + dk * k_j.astype(F32) + dv * v_j.astype(F32), axis=-1, keepdims=True)
            at = pl.ds(pl.multiple_of(ours + j * HEAD_DIM, HEAD_DIM), HEAD_DIM)
            r.dqkv[i, 0, :, at] = (dq * cosine - turned(dq) * sine).astype(BF16)
            r.dqkv[i, 1, :, at] = (dk * cosine - turned(dk) * sine).astype(BF16)
            r.dqkv[i, 2, :, at] = dv.astype(BF16)
        r.snd_row[2 + i] = to_row(row)
        row_copy(2 + i, place.pair).start()
        for t in range(3):
            link.start(first_dqkv + 3 * i + t, lambda rows, i=i, t=t: r.dqkv.at[i, t, rows, pl.ds(ours, mine)])
        if i == 0:
            @pl.when(place.block == 0)
            def _():
                scatter.middle(0)

    @pl.when(place.block == 0)
    def _():
        for chunk in range(1, 4):
            scatter.middle(chunk)

    for i in range(seqs):
        part = jnp.zeros((length, feats), F32)
        for t in range(3):
            link.wait(first_dqkv + 3 * i + t)
            part = part + mm_nt(r.dqkv[i, t], r.wqkv[t])
        r.snd_db[2 + i] = part.astype(BF16)
        da_rows(i).start()
        row_copy(2 + i, place.pair).wait_recv()
        r.snd_row[4 + i] = r.snd_row[2 + i] + r.rcv_row[2 + i]
        row_copy(4 + i, place.core_peer).start()

    gain_a_sum = jnp.zeros((1, feats), F32)
    for i in range(seqs):
        da_rows(i).wait_recv()
        row_copy(4 + i, place.core_peer).wait_recv()
        r.snd_row[6 + i] = (r.snd_row[4 + i] + r.rcv_row[4 + i]) * (1.0 / z.width)
        mean = from_row(r.snd_row[6 + i, :, my_rows])
        grad = r.snd_db[2 + i, my_rows, :].astype(F32) + r.rcv_da[i].astype(F32)
        factor = r.ra[i, my_rows, :][:, :1]
        scaled = r.xa[i, my_rows, :].astype(F32) * factor
        r.e_out[i] = (r.e[i, my_rows, :] + factor * (grad * gain_a - scaled * mean)).astype(BF16)
        gain_a_sum = gain_a_sum + jnp.sum(grad * scaled, axis=0, keepdims=True)

        @pl.when(place.block == 1)
        def _():
            e_copy(i).start()

    r.gains[0:1, :] = gain_a_sum
    emit_e0.prepare([r.e_out[i] for i in range(seqs)])

    def qkv_grad():
        for i in range(seqs):
            r.xg[i] = (r.xa[i].astype(F32) * r.ra[i][:, :1] * gain_a).astype(BF16)
        for t in range(3):
            r.wd[:, t * z.cols:(t + 1) * z.cols] = (mm_tn(r.xg[0], r.dqkv[0, t]) + mm_tn(r.xg[1], r.dqkv[1, t])).astype(BF16)
            for chunk in range(8 + 2 * t, 10 + 2 * t):
                scatter.edges(chunk)

    @pl.when(place.block == 1)
    def _():
        gather.step(2)
        for block in range(8):
            up_grad(block)
        qkv_grad()
        link.forward(ffn_order[len(NARROW):])
        link.forward(do_order)
        gather.rest(3)
        scatter.middle(0)
        link.forward(dqkv_order)
        for chunk in range(1, 4):
            scatter.middle(chunk)

    @pl.when(place.block == 0)
    def _():
        qkv_grad()

    emit_x1.start(0)
    emit_x2.start(1)
    emit_e1.start(1)
    emit_e0.start(0)
    gains_copy = remote(r.gains, r.core_gains, r.pair_send.at[0], r.pair_recv.at[0], place.core_peer)
    gains_copy.start()
    exchange_flag.finish()
    scatter.middle(4)
    gains_copy.wait()
    r.every_gain[me] = r.gains[...] + r.core_gains[...]
    exchange_gain = Exchange(place, lambda n: r.every_gain.at[me], r.every_gain, (r.gain_send, r.gain_recv, None))
    for n in range(1, planes):
        exchange_gain.copy(n).start()

    rows = slice(0, share)
    for n in range(SLOTS):
        r.u[n, rows, :] = jnp.zeros_like(r.u[n, rows, :])
    flags_copy = pltpu.make_async_copy(r.every_flag, r.flags, r.block_sem.at[0])
    flags_copy.start()
    flags_copy.wait()

    def plane_grads(n, carry):
        block_g = r.du.at[0:SLOTS - 1]
        sources = ((r.every_g, block_g), (r.every_o, r.xf), (r.every_d, r.block_d), (r.every_c, r.block_c))
        copies = [pltpu.make_async_copy(src.at[n], dst, r.block_sem.at[at]) for at, (src, dst) in enumerate(sources)]
        for copy in copies:
            copy.start()
        for copy in copies:
            copy.wait()
        on = r.flags[n][:1, :1]
        shared = block_g[1].astype(F32)
        upper, lower = (shared * on).astype(BF16), (shared * (1.0 - on)).astype(BF16)
        narrow, wide = r.block_d[:, :length], r.block_d[:, length:]
        for block in range(8):
            right = upper if block == 4 else block_g[2 + block if block < 4 else 1 + block]
            part = mm(wide, right)
            if block < 2:
                part = part + mm(narrow, block_g[0] if block == 0 else lower)
            r.u[block, rows, :] = r.u[block, rows, :] + part
        for side in range(2):
            span = slice(side * unit, (side + 1) * unit)
            part = mm(r.block_c[:, :length], r.xf[0, :, span]) + mm(r.block_c[:, length:], r.xf[1, :, span])
            r.u[8 + side, rows, :] = r.u[8 + side, rows, :] + part
        return carry

    def grad_copy(n):
        dst = r.down_grad.at[:, n * unit:(n + 1) * unit] if n < 8 else r.out_grad.at[:, (n - 8) * unit:(n - 7) * unit]
        return pltpu.make_async_copy(r.u.at[n, rows, :], dst, r.grad_sem.at[n])

    def total_slot(chunk):
        at = chunk % 6
        return r.own_qkv.at[at // 3, at % 3, rows, :]

    def total_copy(chunk):
        if chunk < 8:
            dst = r.up_grad.at[:, chunk * unit:(chunk + 1) * unit]
        else:
            t, side = (chunk - 8) // 2, (chunk - 8) % 2
            dst = r.qkv_grad.at[t, :, side * unit:(side + 1) * unit]
        return pltpu.make_async_copy(total_slot(chunk), dst, r.total_sem.at[chunk % 6])

    def final(chunk):
        if chunk >= 6:
            total_copy(chunk - 6).wait()
        scatter.last(chunk, total_slot(chunk))
        total_copy(chunk).start()

    for turn in range(5, 14 + LAG):
        scatter.middle(turn)
        if turn >= LAG:
            final(turn - LAG)
        if turn == GRADS_TURN:
            gather.finish()
            gather_o.finish()
            exchange_c.finish()
            lax.fori_loop(0, planes, plane_grads, 0)
            for n in range(SLOTS):
                grad_copy(n).start()
    for turn in range(14 + LAG, len(scatter.turns())):
        scatter.middle(turn)
    for n in range(1, planes):
        source = lax.rem(me + planes - n, planes)
        slot = r.every_gain.at[source]
        remote(slot, slot, r.gain_send.at[n], r.gain_recv.at[n], place.pair).wait_recv()
        exchange_gain.copy(n).wait_send()
    gain_total = r.every_gain[0]
    for n in range(1, planes):
        gain_total = gain_total + r.every_gain[n]
    r.gain_grads[...] = gain_total

    scatter.finish()
    for chunk in range(8, 14):
        total_copy(chunk).wait()
    for n in range(SLOTS):
        grad_copy(n).wait()
    for n in range(4):
        sq_copy(n).wait_send()
    for i in range(seqs):
        core_copy(i).wait_send()
        core_rows(i).wait_send()
        row_copy(i, place.core_peer).wait_send()
        row_copy(2 + i, place.pair).wait_send()
        row_copy(4 + i, place.core_peer).wait_send()
        db_copy(i).wait_send()
        da_rows(i).wait_send()
    link.finish(do_order + dqkv_order)

    @pl.when(place.block == 0)
    def _():
        link.finish_whole(ffn_order[:len(NARROW)])
        link.finish(ffn_order[len(NARROW):])
        for i in range(seqs):
            x_copy(i).wait_send()

    @pl.when(place.block == 1)
    def _():
        link.finish_whole(tuple(first_dg + slot for slot in DG_STRAIGHT))
        link.finish(tuple(first_dg + slot for slot in DG_MIDDLE + DG_LATE))
        for i in range(seqs):
            e_copy(i).wait_send()

    emit_x1.finish(0)
    emit_x2.finish(1)
    emit_e1.finish(1)
    emit_e0.finish(0)


def shape(dims, kind):
    return jax.ShapeDtypeStruct(dims, kind)


ANY = pl.BlockSpec(memory_space=pl.ANY)
IN_VMEM = pl.BlockSpec(memory_space=pltpu.VMEM)


def vmem(dims, kind):
    return pltpu.VMEM(tuple(dims), kind)


def run_main(width_index, x0, c0, gain_a, gain_f, wqkv, wo, wu, wd):
    seqs, tokens, width = x0.shape
    planes = lax.axis_size("dp")
    z = Sizes(wo.shape[0], wo.shape[1], wu.shape[1], tokens)
    share, chunks = z.feats // planes, 14
    cosine, sine = rotary(z.length, HEAD_DIM)
    args = {
        "width": width_index, "x0": x0, "c0": c0, "gain_a": gain_a, "gain_f": gain_f, "cosine": cosine, "sine": sine,
        "wqkv_hbm": wqkv, "wo_hbm": wo, "wu_hbm": wu, "wd_hbm": wd,
    }
    places = {"width": pl.BlockSpec(memory_space=pltpu.SMEM)}
    places.update({name: IN_VMEM for name in ("gain_a", "gain_f", "cosine", "sine", "gain_grads")})
    row = (8, z.feats)
    outs = {
        "layer_out": shape((seqs, tokens, width), BF16), "input_grad": shape((seqs, tokens, width), BF16),
        "qkv_grad": shape((3, share, z.cols), F32), "out_grad": shape((share, z.cols), F32),
        "up_grad": shape((share, 8 * z.unit), F32), "down_grad": shape((share, 8 * z.unit), F32), "gain_grads": shape(row, F32),
        "every_g": shape((planes, SLOTS - 1, z.length, z.unit), BF16), "every_o": shape((planes, seqs, z.length, z.cols), BF16),
        "every_d": shape((planes, share, seqs * z.length), BF16), "every_c": shape((planes, share, seqs * z.length), BF16),
        "every_flag": shape((planes, 8, 128), F32),
        "from_left": shape((planes, chunks, share, z.unit), BF16), "from_right": shape((planes, chunks, share, z.unit), BF16),
    }
    state, half_state, heads_state = (seqs, z.length, z.feats), (seqs, tokens, z.feats), (seqs, z.length, z.mine)
    slots, qkv, messages = (SLOTS, z.length, z.unit), (seqs, 3, z.length, z.mine), 12 + 2 * seqs + 2 * SLOTS
    small, factor, pair = (8, 8, z.length), (seqs, z.length, 128), (4, z.length, z.feats)
    scratch = {"wqkv": vmem(wqkv.shape, BF16), "wo": vmem(wo.shape, BF16), "wud": vmem((2, *wu.shape), BF16)}
    for dims, kind, group in (
        (state, BF16, "xa xf xg e_in dc"), (state, F32, "e"), (half_state, BF16, "x2 e_out rcv_half rcv_da"),
        (heads_state, BF16, "q k v snd_do rcv_do"), (heads_state, F32, "own_do"),
        ((seqs, z.heads, z.length, z.length), F32, "p"), ((seqs, z.length, z.cols), BF16, "o"), (factor, F32, "ra rf"),
        (slots, F32, "u"), (slots, BF16, "g snd_u rcv_u du snd_dg rcv_dg"), (qkv, F32, "own_qkv"), (qkv, BF16, "snd_qkv rcv_qkv"),
        ((4, 8, z.length), F32, "snd_sq rcv_sq"), (small, F32, "snd_row rcv_row"), (pair, BF16, "snd_br snd_db"),
        ((2, z.length, z.feats), BF16, "rcv_br rcv_db"), ((z.feats, seqs * z.length), BF16, "dt"), ((4, *half_state), BF16, "stage"),
        ((seqs, 3, z.length, z.cols), BF16, "dqkv"), ((messages, z.length - DIRECT_ROWS, z.mine), BF16, "relay"),
        ((8, 128), F32, "wide"), ((planes, 8, 128), F32, "flags"), ((share, seqs * z.length), BF16, "block_d block_c"),
        (row, F32, "gains core_gains"), ((planes, *row), F32, "every_gain"),
    ):
        scratch.update({name: vmem(dims, kind) for name in group.split()})
    for count, group in (
        (4, "load_sem sq_send sq_recv core_send core_recv db_send db_recv in_send in_recv in_local block_sem"),
        (messages, "x_send x_recv far_send far_recv relay_send relay_recv"), (6, "row_send row_recv total_sem"),
        (2, "y_send y_recv"), (8, "out_send out_recv out_local"), (1, "g_local o_local d_local c_local flag_local pair_send pair_recv intake_sem"),
        (planes, "g_right g_left g_sem o_right o_left o_sem d_send d_recv c_send c_recv flag_send flag_recv gain_send gain_recv"),
        (planes * chunks, "sum_right sum_left got_left got_right"), (SLOTS, "grad_sem"),
    ):
        scratch.update({name: pltpu.SemaphoreType.DMA((count,)) for name in group.split()})
    scratch["go_sem"] = pltpu.SemaphoreType.REGULAR((2,))
    results = pl.pallas_call(
        functools.partial(main_kernel, (*args, *outs, *scratch)),
        out_shape=tuple(outs.values()),
        in_specs=[places.get(name, ANY) for name in args],
        out_specs=tuple(places.get(name, ANY) for name in outs),
        scratch_shapes=list(scratch.values()),
        compiler_params=pltpu.CompilerParams(collective_id=1, has_side_effects=True, vmem_limit_bytes=VMEM_LIMIT),
        name="main",
    )(*args.values())
    return dict(zip(outs, results))


def local(inputs, cotangent, width_index, qkv_weight, out_weight, attn_gain, ffn_gain, up_weight, down_weight):
    found = run_main(width_index, inputs, cotangent, attn_gain, ffn_gain, qkv_weight, out_weight, up_weight, down_weight)
    gains = found["gain_grads"]
    size = gains.shape[1] // (2 * lax.axis_size("dp"))
    own = (lax.axis_index("dp") * 2 + lax.axis_index("mp")) * size
    gain_grads = lax.dynamic_slice_in_dim(gains[:2], own, size, axis=1)
    return (
        found["layer_out"][None],
        found["input_grad"][None],
        found["qkv_grad"],
        found["out_grad"],
        gain_grads[0],
        gain_grads[1],
        found["up_grad"],
        found["down_grad"],
    )


def solution(mesh):
    in_specs = (
        P("dp", "mp", None),
        P("dp", "mp", None),
        P("dp"),
        P(None, "section", "mp"),
        P("section", "mp"),
        P("section"),
        P("section"),
        P("section", "mp"),
        P("section", "mp"),
    )
    out_specs = (
        P("section", "dp", "mp", None),
        P("section", "dp", "mp", None),
        P(None, ("section", "dp"), "mp"),
        P(("section", "dp"), "mp"),
        P(("section", "dp", "mp")),
        P(("section", "dp", "mp")),
        P(("section", "dp"), "mp"),
        P(("section", "dp"), "mp"),
    )
    return jax.shard_map(local, mesh=mesh, in_specs=in_specs, out_specs=out_specs, check_vma=False)
```

```python
import functools
import types

import jax
import jax.numpy as jnp
import numpy as np
from jax import lax
from jax.sharding import PartitionSpec as P
from jax.experimental import pallas as pl
from jax.experimental.pallas import tpu as pltpu

HEAD_DIM = 128
EPSILON = 1e-05
GELU_C = 0.7978845608028654
GELU_A = 0.044715
MESH = pl.DeviceIdType.MESH
SLOTS = 10
AHEAD = 3
SHARED = 6
DIRECT_ROWS = 144
URGENT_ROWS = 192
F32 = jnp.float32
BF16 = jnp.bfloat16
VMEM_LIMIT = 63 * 2**20


def mm(a, b):
    return lax.dot_general(a, b, (((1,), (0,)), ((), ())), preferred_element_type=F32)


def mm_nt(a, b):
    return lax.dot_general(a, b, (((1,), (1,)), ((), ())), preferred_element_type=F32)


def mm_tn(a, b):
    return lax.dot_general(a, b, (((0,), (0,)), ((), ())), preferred_element_type=F32)


def to_row(column):
    rows = column.shape[0]
    return jnp.transpose(jnp.broadcast_to(column, (rows, 128)))[:8]


def from_row(row):
    return jnp.transpose(row)[:, :1]


def rotary(length, head_size):
    half_dim = head_size // 2
    frequency = np.float32(10000.0) ** (np.float32(-2.0 / head_size) * np.arange(half_dim, dtype=np.float32))
    angles = np.arange(length, dtype=np.float32)[:, None] * frequency[None, :].astype(np.float32)
    cosine, sine = np.cos(angles).astype(np.float32), np.sin(angles).astype(np.float32)
    return jnp.asarray(np.concatenate([cosine, cosine], axis=1)), jnp.asarray(np.concatenate([-sine, sine], axis=1))


def turned(values):
    return pltpu.roll(values, HEAD_DIM // 2, 1)


def remote(src, dst, send_sem, recv_sem, device):
    return pltpu.make_async_remote_copy(
        src_ref=src, dst_ref=dst, send_sem=send_sem, recv_sem=recv_sem,
        device_id=device, device_id_type=MESH,
    )


class Place:
    def __init__(self):
        section, dp, mp = (lax.axis_index(name) for name in ("section", "dp", "mp"))
        self.block, self.half, self.core = section // 2, section % 2, mp
        other_half = 1 - self.half
        other_block = 1 - self.block
        self.at = (section, dp, mp)
        self.core_peer = (section, dp, 1 - mp)
        self.pair = (self.block * 2 + other_half, dp, mp)
        self.across = (other_block * 2 + self.half, dp, mp)
        self.corner = (other_block * 2 + other_half, dp, mp)

    def plane(self, n):
        section, dp, mp = self.at
        return (section, lax.rem(dp + n, lax.axis_size("dp")), mp)

    def barrier(self):
        sem = pltpu.get_barrier_semaphore()
        peers = [self.core_peer, self.pair, self.across, self.corner]
        peers += [self.plane(n) for n in range(1, lax.axis_size("dp"))]
        for peer in peers:
            pl.semaphore_signal(sem, inc=1, device_id=peer, device_id_type=MESH)
        pl.semaphore_wait(sem, len(peers))


class Exchange:
    def __init__(self, place, piece, slots, sems):
        self.place, self.piece, self.slots = place, piece, slots
        self.send, self.recv, self.local = sems
        self.me, self.count = lax.axis_index("dp"), lax.axis_size("dp")

    def copy(self, n):
        target = lax.rem(self.me + n, self.count)
        return remote(self.piece(target), self.slots.at[self.me], self.send.at[n], self.recv.at[n], self.place.plane(n))

    def own(self):
        return pltpu.make_async_copy(self.piece(self.me), self.slots.at[self.me], self.local.at[0])

    def start(self):
        self.own().start()
        for n in range(1, self.count):
            self.copy(n).start()

    def finish(self):
        self.own().wait()
        for n in range(1, self.count):
            source = lax.rem(self.me + self.count - n, self.count)
            held = self.slots.at[source]
            remote(held, held, self.send.at[n], self.recv.at[n], self.place.plane(n)).wait_recv()
            self.copy(n).wait_send()


class PairLink:
    def __init__(self, place, relay, sems, targets, urgent):
        self.place, self.relay, self.targets = place, relay, targets
        self.send, self.recv, self.far_send, self.far_recv, self.relay_send, self.relay_recv = sems
        self.rows = DIRECT_ROWS + relay.shape[1]
        self.urgent = urgent
        self.sources = {}

    def direct(self, index):
        return slice(0, URGENT_ROWS if index in self.urgent else DIRECT_ROWS)

    def detour(self, index):
        return slice(URGENT_ROWS if index in self.urgent else DIRECT_ROWS, self.rows)

    def held(self, index):
        rows = self.detour(index)
        return self.relay.at[index, 0:rows.stop - rows.start]

    def near(self, index):
        rows = self.direct(index)
        src, dst = self.sources[index](rows), self.targets(index, self.place.half, rows)
        return remote(src, dst, self.send.at[index], self.recv.at[index], self.place.pair)

    def far(self, index):
        src = self.sources[index](self.detour(index))
        return remote(src, self.held(index), self.far_send.at[index], self.relay_recv.at[index], self.place.across)

    def whole(self, index):
        rows, src = slice(0, self.rows), self.sources[index]
        dst = self.targets(index, self.place.half, rows)
        return remote(src(rows), dst, self.send.at[index], self.recv.at[index], self.place.pair)

    def start(self, index, src):
        self.sources[index] = src
        self.near(index).start()
        self.far(index).start()

    def start_near(self, index, src):
        self.sources[index] = src
        self.near(index).start()

    def start_far(self, index):
        self.far(index).start()

    def start_whole(self, index, src):
        self.sources[index] = src
        self.whole(index).start()

    def wait(self, index):
        other = 1 - self.place.half
        for rows, sem in ((self.direct(index), self.recv), (self.detour(index), self.far_recv)):
            dst = self.targets(index, other, rows)
            remote(dst, dst, self.send.at[index], sem.at[index], self.place.pair).wait_recv()

    def wait_whole(self, index):
        dst = self.targets(index, 1 - self.place.half, slice(0, self.rows))
        remote(dst, dst, self.send.at[index], self.recv.at[index], self.place.pair).wait_recv()

    def finish(self, indices):
        for index in indices:
            self.near(index).wait_send()
            self.far(index).wait_send()

    def finish_whole(self, indices):
        for index in indices:
            self.whole(index).wait_send()

    def passed(self, index):
        dst = self.targets(index, self.place.half, self.detour(index))
        return remote(self.held(index), dst, self.relay_send.at[index], self.far_recv.at[index], self.place.corner)

    def forward(self, indices):
        for index in indices:
            held = self.held(index)
            remote(held, held, self.relay_send.at[index], self.relay_recv.at[index], self.place.across).wait_recv()
            self.passed(index).start()

    def finish_forward(self, indices):
        for index in indices:
            self.passed(index).wait_send()


def spread(value, width):
    return jnp.broadcast_to(value, (value.shape[0], width))


def slot_block(slot):
    return (0, slot) if slot < 2 else (1, slot - 2)


def slot_weight(slot, weight):
    unit = weight.shape[1] // 8
    at = slot_block(slot)[1] * unit
    return weight[:, at:at + unit]


def mask_slot(slot, value, flag):
    if slot == 1:
        return value * (1.0 - flag)
    return value if slot < 6 else value * flag


NARROW, WIDE = (0, 1), tuple(range(2, SLOTS))
G_PLACE = (0, 1, 2, 3, 4, 5, 9, 6, 7, 8)
DG_STRAIGHT, DG_MIDDLE, DG_LATE = (0, 1, 2), (3, 4), (5, 6, 7, 8, 9)


class Sizes:
    def __init__(self, feats, cols, hidden, tokens):
        self.feats, self.cols, self.unit, self.tokens = feats, cols, hidden // 8, tokens
        self.mine, self.length, self.width = cols // 2, 2 * tokens, 2 * feats
        self.heads = self.mine // HEAD_DIM


class Emitter:
    def __init__(self, place, out, stage, swap, sems, first=0):
        self.place, self.out, self.stage, self.swap, self.sems, self.first = place, out, stage, swap, sems, first

    def span(self):
        feats = self.stage.shape[-1]
        return pl.ds(pl.multiple_of(self.place.half * feats, feats), feats)

    def far(self, i):
        at = self.first + i
        return remote(self.stage.at[i], self.out.at[i, :, self.span()], self.sems[0].at[at], self.sems[1].at[at], self.place.pair)

    def near(self, i):
        return pltpu.make_async_copy(self.stage.at[i], self.out.at[i, :, self.span()], self.sems[2].at[self.first + i])

    def prepare(self, values):
        narrow, wide = (value.astype(F32) for value in values)
        self.stage[0] = (narrow * (1.0 - self.swap) + wide * self.swap).astype(BF16)
        self.stage[1] = (wide * (1.0 - self.swap) + narrow * self.swap).astype(BF16)

    def start(self, owner):
        @pl.when(self.place.half == owner)
        def _():
            for i in range(2):
                self.near(i).start()

        @pl.when(self.place.half != owner)
        def _():
            for i in range(2):
                self.far(i).start()

    def finish(self, owner):
        @pl.when(self.place.half == owner)
        def _():
            for i in range(2):
                self.near(i).wait()
                self.far(i).wait_recv()

        @pl.when(self.place.half != owner)
        def _():
            for i in range(2):
                self.far(i).wait_send()


class Gather:
    def __init__(self, place, mine, every, sems):
        self.me, self.count = lax.axis_index("dp"), lax.axis_size("dp")
        self.place, self.mine, self.every = place, mine, every
        self.right, self.left, self.recv, self.local = sems
        self.last = self.count - 1

    def send(self, block, way, number):
        section, dp, mp = self.place.at
        sems = self.right if way > 0 else self.left
        src = self.mine if number == 1 else self.every.at[block]
        return remote(src, self.every.at[block], sems.at[block], self.recv.at[block], (section, dp + way, mp))

    def arrive(self, block):
        held = self.every.at[block]
        remote(held, held, self.right.at[block], self.recv.at[block], self.place.pair).wait_recv()

    def moves(self, number):
        me, last = self.me, self.count - 1
        right, left = me - number + 1, me + number - 1
        return ((1, right, (right >= 0) & (me < last)), (-1, left, (left <= last) & (me > 0)))

    def own(self):
        return pltpu.make_async_copy(self.mine, self.every.at[self.me], self.local.at[0])

    def step(self, number):
        if number == 1:
            self.own().start()
        if number > self.last:
            return
        for way, block, active in self.moves(number):
            @pl.when(active)
            def _(way=way, block=block):
                if number > 1:
                    self.arrive(block)
                self.send(block, way, number).start()

    def rest(self, number):
        for more in range(number, self.last + 1):
            self.step(more)

    def settle(self, first, last):
        for number in range(first, min(last, self.last) + 1):
            left, right = self.me - number, self.me + number
            done = number == self.last

            @pl.when((left >= 0) if done else (left >= 0) & (self.me == self.count - 1))
            def _(block=left):
                self.arrive(block)

            @pl.when((right < self.count) if done else (right < self.count) & (self.me == 0))
            def _(block=right):
                self.arrive(block)

    def settle_all(self):
        self.own().wait()
        self.settle(1, self.last)

    def finish(self):
        for number in range(1, self.last + 1):
            for way, block, active in self.moves(number):
                @pl.when(active)
                def _(way=way, block=block):
                    self.send(block, way, number).wait_send()


class Scatter:
    def __init__(self, place, piece, which, total, landing, sends, arrivals, slots, places, intake, in_sem, chunks):
        self.places = places
        self.place, self.piece, self.which, self.total = place, piece, which, total
        self.landing, self.sends, self.arrivals = landing, sends, arrivals
        self.slots, self.intake, self.in_sem, self.chunks = slots, intake, in_sem, chunks
        self.me, self.count = lax.axis_index("dp"), lax.axis_size("dp")

    def send(self, way, target, number, src):
        section, dp, mp = self.place.at
        dst = self.landing[way].at[target, number]
        send_sem = self.sends[way].at[target * 4 + lax.rem(number, 4)]
        return remote(src, dst, send_sem, self.arrivals[way].at[target * self.chunks + number], (section, dp + way, mp))

    def own(self, number, target):
        return self.piece(self.which(number), target)

    def arrived(self, way, target, number):
        held = self.landing[way].at[target, number]
        got = self.arrivals[way].at[target * self.chunks + number]
        remote(held, held, self.sends[way].at[0], got, self.place.pair).wait_recv()

    def taken(self, way, target, number, buffer):
        return pltpu.make_async_copy(self.landing[way].at[target, number], self.intake(buffer), self.in_sem.at[buffer])

    def each(self, way, body):
        def step_body(step, carry):
            body(step, self.count - 1 - step if way > 0 else step)
            return carry
        lax.fori_loop(0, self.count - 1, step_body, 0)

    def at_edge(self, way):
        return self.me == (0 if way > 0 else self.count - 1)

    def edges(self, number):
        for way in (1, -1):
            @pl.when(self.at_edge(way) & (number < self.total))
            def _(way=way):
                self.each(way, lambda step, target: self.send(way, target, number, self.own(number, target)).start())

    def between(self, way, target):
        if way > 0:
            return (self.me > 0) & (self.me < target)
        return (self.me < self.count - 1) & (self.me > target)

    def staging(self, way):
        live = jnp.maximum(self.count - 1 - self.me if way > 0 else self.me, 1)
        return jnp.minimum(lax.div(self.places, live), 4), live

    def turns(self):
        return range(self.chunks + max(self.count - 3, 0))

    def turn(self, turn):
        if turn + AHEAD < self.chunks:
            for way in (1, -1):
                @pl.when(self.at_edge(way) & (turn + AHEAD < self.total))
                def _(way=way):
                    self.each(way, lambda step, target: self.send(way, target, turn, self.own(turn, target)).wait_send())
            self.edges(turn + AHEAD)
        if self.count < 3 or turn not in self.turns():
            return

        ways = ((1, 0, lambda step: self.count - 1 - step), (-1, 1, lambda step: step))

        def number_of(way, target):
            depth = self.me if way > 0 else self.count - 1 - self.me
            number = turn + 1 - depth
            return number, self.between(way, target) & (number >= 0) & (number < self.total)

        def take(step, carry):
            for way, side, target_of in ways:
                target = target_of(step)
                number, active = number_of(way, target)

                @pl.when(active)
                def _(way=way, side=side, target=target, number=number):
                    self.arrived(way, target, number)
                    self.taken(way, target, number, 2 * step + side).start()
            return carry

        def pass_on(step, carry):
            for way, side, target_of in ways:
                target = target_of(step)
                number, active = number_of(way, target)

                @pl.when(active)
                def _(way=way, side=side, target=target, number=number):
                    depth, live = self.staging(way)
                    slot = self.slots(way, lax.rem(number, depth) * live + step)
                    buffer = 2 * step + side
                    self.taken(way, target, number, buffer).wait()
                    total = self.intake(buffer)[...].astype(F32) + self.own(number, target)[...].astype(F32)

                    @pl.when(number >= depth)
                    def _():
                        self.send(way, target, number - depth, slot).wait_send()

                    slot[...] = total.astype(BF16)
                    self.send(way, target, number, slot).start()
            return carry

        lax.fori_loop(0, self.count - 1, take, 0)
        lax.fori_loop(0, self.count - 1, pass_on, 0)

    def last(self, number, total_ref):
        ways = ((1, 0, self.me > 0), (-1, 1, self.me < self.count - 1))
        for way, side, there in ways:
            @pl.when(there)
            def _(way=way, side=side):
                self.arrived(way, self.me, number)
                self.taken(way, self.me, number, side).start()
        total_ref[...] = self.own(number, self.me)[...].astype(F32)
        for way, side, there in ways:
            @pl.when(there)
            def _(way=way, side=side):
                self.taken(way, self.me, number, side).wait()
                total_ref[...] = total_ref[...] + self.intake(side)[...].astype(F32)

    def finish(self):
        for way in (1, -1):
            depth, _ = self.staging(way)
            for back in range(1, 5):
                number = self.total - back

                def sent(step, target, way=way, back=back, number=number, depth=depth):
                    active = self.between(way, target) & (back <= depth)
                    if back <= AHEAD:
                        active = active | self.at_edge(way)

                    @pl.when(active)
                    def _():
                        self.send(way, target, number, self.own(number, target)).wait_send()

                self.each(way, sent)


def main_kernel(names, *refs):
    r = types.SimpleNamespace(**dict(zip(names, refs)))
    place = Place()
    half, core = place.half, place.core
    me, planes = lax.axis_index("dp"), lax.axis_size("dp")
    seqs, length, feats = r.xa.shape
    z = Sizes(feats, r.wo.shape[1], r.wud.shape[2], length // 2)
    mine, unit = z.mine, z.unit
    share = feats // planes

    r.wu, r.wd = r.wud.at[0], r.wud.at[1]
    weights = ((r.wqkv_hbm, r.wqkv), (r.wo_hbm, r.wo), (r.wu_hbm, r.wu), (r.wd_hbm, r.wd))

    @pl.when(place.block == 0)
    def _():
        for n in range(4):
            pltpu.make_async_copy(*weights[n], r.load_sem.at[n]).start()

    @pl.when(place.block == 1)
    def _():
        for n in range(3, -1, -1):
            pltpu.make_async_copy(*weights[n], r.load_sem.at[n]).start()

    def loaded(n):
        pltpu.make_async_copy(*weights[n], r.load_sem.at[n]).wait()

    first_width, second_width = r.width[0], r.width[1]
    r.wide[...] = jnp.zeros_like(r.wide)
    r.wide[0:1, :] = jnp.full((1, 128), 1.0 - 0.5 * (first_width * second_width).astype(F32), F32)
    r.wide[1:2, :] = jnp.full((1, 128), lax.shift_right_logical(first_width, 1).astype(F32), F32)
    flag, swap = r.wide[0:1, :1], r.wide[1:2, :1]
    gain_a = r.gain_a[...].reshape(1, feats).astype(F32)
    gain_f = r.gain_f[...].reshape(1, feats).astype(F32)

    place.barrier()

    first_u, first_dg = 6 + seqs, 6 + seqs + SLOTS
    first_do = first_dg + SLOTS
    first_dqkv = first_do + seqs

    def targets(index, sender_half, rows):
        span = pl.ds(pl.multiple_of(sender_half * mine, mine), mine)
        if index < 6:
            return r.rcv_qkv.at[index // 3, index % 3, rows, :]
        if index < first_u:
            return r.o.at[index - 6, rows, span]
        if index < first_dg:
            return r.rcv_u.at[index - first_u, rows, :]
        if index < first_do:
            return r.rcv_dg.at[index - first_dg, rows, :]
        if index < first_dqkv:
            return r.rcv_do.at[index - first_do, rows, :]
        n = index - first_dqkv
        return r.dqkv.at[n // 3, n % 3, rows, span]

    link = PairLink(place, r.relay, (r.x_send, r.x_recv, r.far_send, r.far_recv, r.relay_send, r.relay_recv), targets, (6, 7, first_do, first_do + 1))
    forward_order = tuple(range(first_dg))
    ffn_order = tuple(range(first_dg, first_do))
    do_order = tuple(range(first_do, first_dqkv))
    dqkv_order = tuple(range(first_dqkv, first_dqkv + 6))
    my_rows = pl.ds(pl.multiple_of(core * z.tokens, z.tokens), z.tokens)
    their_rows = pl.ds(pl.multiple_of((1 - core) * z.tokens, z.tokens), z.tokens)
    my_feats = pl.ds(pl.multiple_of(half * feats, feats), feats)

    def share_rows(n):
        return pl.ds(pl.multiple_of(n * share, share), share)

    gathers = [
        Gather(
            place, r.g.at[3 * n:3 * n + 3], r.every_g.at[n],
            (r.g_right.at[n], r.g_left.at[n], r.g_sem.at[n], r.g_local.at[n:n + 1]),
        )
        for n in range(3)
    ]
    gather_o = Gather(place, r.o, r.every_o, (r.o_right, r.o_left, r.o_sem, r.o_local))
    exchange_d = Exchange(place, lambda n: r.dt.at[share_rows(n), :], r.every_d, (r.d_send, r.d_recv, r.d_local))
    exchange_c = Exchange(place, lambda n: r.dt.at[share_rows(n), :], r.every_c, (r.c_send, r.c_recv, r.c_local))
    gather_u = Gather(place, r.du.at[SLOTS - SHARED:SLOTS], r.every_u, (r.u_right, r.u_left, r.u_sem, r.u_local))
    exchange_b = Exchange(place, lambda n: r.dt.at[share_rows(n), 0:length], r.every_b, (r.b_send, r.b_recv, r.b_local))
    exchange_flag = Exchange(place, lambda n: r.wide, r.every_flag, (r.flag_send, r.flag_recv, r.flag_local))
    exchange_flag.start()

    def local_copy(src, dst, n):
        return pltpu.make_async_copy(src, dst, r.in_local.at[n])

    def core_half(src, dst, n):
        return remote(src, dst, r.in_send.at[n], r.in_recv.at[n], place.core_peer)

    def x_copy(i):
        return remote(r.x2.at[i], r.xa.at[i, my_rows, :], r.y_send.at[i], r.y_recv.at[i], place.across)

    def e_copy(i):
        return remote(r.x2.at[i], r.e_in.at[i, my_rows, :], r.y_send.at[i], r.y_recv.at[i], place.across)

    def start_half(src_ref, dst_ref, first):
        for i in range(seqs):
            local_copy(src_ref.at[i, :, my_feats], dst_ref.at[i, my_rows, :], first + i).start()
            core_half(src_ref.at[i, :, my_feats], dst_ref.at[i, my_rows, :], first + i).start()

    def ordered_halves(raw_ref, dst_ref, first):
        for i in range(seqs):
            local_copy(raw_ref.at[i, my_rows, :], raw_ref.at[i, my_rows, :], first + i).wait()
            core_half(raw_ref.at[i, my_rows, :], raw_ref.at[i, my_rows, :], first + i).wait()
        for i in range(seqs):
            mixed = raw_ref[i].astype(F32) * (1.0 - swap) + raw_ref[1 - i].astype(F32) * swap
            dst_ref[i] = mixed.astype(BF16)

    def pass_half(dst_ref, n, i):
        core_half(dst_ref.at[i, my_rows, :], dst_ref.at[i, my_rows, :], n).start()
        core_half(dst_ref.at[i, my_rows, :], dst_ref.at[i, my_rows, :], n).wait()

    def sq_copy(n):
        return remote(r.snd_sq.at[n], r.rcv_sq.at[n], r.sq_send.at[n], r.sq_recv.at[n], place.pair)

    def core_copy(n):
        return remote(r.snd_br.at[n], r.rcv_br.at[n], r.core_send.at[n], r.core_recv.at[n], place.core_peer)

    def core_rows(i):
        return remote(r.snd_br.at[2 + i, their_rows, :], r.rcv_half.at[i], r.core_send.at[2 + i], r.core_recv.at[2 + i], place.core_peer)

    def row_copy(n, peer):
        return remote(r.snd_row.at[n], r.rcv_row.at[n], r.row_send.at[n], r.row_recv.at[n], peer)

    def db_copy(n):
        return remote(r.snd_db.at[n], r.rcv_db.at[n], r.db_send.at[n], r.db_recv.at[n], place.core_peer)

    def da_rows(i):
        return remote(r.snd_db.at[2 + i, their_rows, :], r.rcv_half.at[i], r.db_send.at[2 + i], r.db_recv.at[2 + i], place.core_peer)

    def ready(n):
        pl.semaphore_signal(r.go_sem.at[n], inc=1, device_id=place.pair, device_id_type=MESH)

    def wait_ready(n):
        pl.semaphore_wait(r.go_sem.at[n], 1)

    out_sems = (r.out_send, r.out_recv, r.out_local)
    emit_x1 = Emitter(place, r.layer_out, r.stage.at[0], swap, out_sems, 0)
    emit_x2 = Emitter(place, r.layer_out, r.stage.at[1], swap, out_sems, 2)
    emit_e1 = Emitter(place, r.input_grad, r.stage.at[2], swap, out_sems, 4)
    emit_e0 = Emitter(place, r.input_grad, r.stage.at[3], swap, out_sems, 6)
    theirs = pl.multiple_of((1 - half) * mine, mine)
    ours = pl.multiple_of(half * mine, mine)

    def dg_part(slot):
        r.snd_dg[slot] = mm(r.e_in[slot_block(slot)[0]], slot_weight(slot, r.wd)).astype(BF16)

    def dg_source(slot):
        return lambda rows: r.snd_dg.at[slot, rows, :]

    def transposed(src_ref):
        for i in range(seqs):
            r.dt[:, i * length:(i + 1) * length] = jnp.transpose(src_ref[i].astype(F32)).astype(BF16)

    @pl.when(place.block == 0)
    def _():
        start_half(r.x0, r.xf, 0)
        ordered_halves(r.xf, r.xa, 0)

    @pl.when(place.block == 1)
    def _():
        start_half(r.c0, r.dc, 2)
        loaded(3)
        ordered_halves(r.dc, r.e_in, 2)
        for slot in range(SLOTS):
            dg_part(slot)
        transposed(r.e_in)
        exchange_d.start()
        link.forward(forward_order[:6])
        link.start_whole(first_dg, dg_source(0))
        link.forward(forward_order[6:8])
        link.start_whole(first_dg + 1, dg_source(1))
        link.forward(forward_order[8:])
        link.start_whole(first_dg + 2, dg_source(2))

    for i in range(seqs):
        @pl.when(place.block == 1)
        def _():
            x_copy(i).wait_recv()
            if i == 1:
                ready(0)
            pass_half(r.xa, i, i)

        x = r.xa[i].astype(F32)
        r.snd_sq[i] = to_row(jnp.sum(x * x, axis=-1, keepdims=True))
        sq_copy(i).start()
        r.xg[i] = (x * gain_a).astype(BF16)
        if i == 0:
            loaded(0)
        for t in range(3):
            r.snd_qkv[i, t] = mm(r.xg[i], r.wqkv[t, :, pl.ds(theirs, mine)]).astype(BF16)
            source = lambda rows, i=i, t=t: r.snd_qkv.at[i, t, rows, :]

            @pl.when(place.block == 0)
            def _():
                link.start(3 * i + t, source)

            @pl.when(place.block == 1)
            def _():
                if i == 0:
                    link.start_whole(t, source)
                else:
                    link.start_near(3 + t, source)

    @pl.when(place.block == 1)
    def _():
        wait_ready(0)
        for t in range(3):
            link.start_far(3 + t)

    for i in range(seqs):
        for t in range(3):
            r.own_qkv[i, t] = mm(r.xg[i], r.wqkv[t, :, pl.ds(ours, mine)])

    cosine, sine = r.cosine[...], r.sine[...]
    scale = HEAD_DIM ** (-0.5)
    causal = lax.broadcasted_iota(jnp.int32, (length, length), 0) >= lax.broadcasted_iota(jnp.int32, (length, length), 1)
    for i in range(seqs):
        sq_copy(i).wait_recv()
        factor = lax.rsqrt((from_row(r.snd_sq[i]) + from_row(r.rcv_sq[i])) * (1.0 / z.width) + EPSILON)
        r.ra[i] = spread(factor, 128)
        if i == 0:
            @pl.when(place.block == 0)
            def _():
                for t in range(3):
                    link.wait(t)

            @pl.when(place.block == 1)
            def _():
                for t in range(3):
                    link.wait_whole(t)
        else:
            for t in range(3):
                link.wait(3 + t)
        for j in range(z.heads):
            span = pl.ds(j * HEAD_DIM, HEAD_DIM)
            raw = [(r.own_qkv[i, t, :, span] + r.rcv_qkv[i, t, :, span].astype(F32)) * factor for t in range(3)]
            q_j = (raw[0] * cosine + turned(raw[0]) * sine).astype(BF16)
            k_j = (raw[1] * cosine + turned(raw[1]) * sine).astype(BF16)
            v_j = raw[2].astype(BF16)
            r.q[i, :, span], r.k[i, :, span], r.v[i, :, span] = q_j, k_j, v_j
            scores = jnp.where(causal, mm_nt(q_j, k_j) * scale, -1e30)
            exponent = jnp.exp(scores - jnp.max(scores, axis=-1, keepdims=True))
            probs = exponent / jnp.sum(exponent, axis=-1, keepdims=True)
            r.p[i, j] = probs
            r.o[i, :, pl.ds(pl.multiple_of(ours + j * HEAD_DIM, HEAD_DIM), HEAD_DIM)] = mm(probs.astype(BF16), v_j).astype(BF16)
        link.start(6 + i, lambda rows, i=i: r.o.at[i, rows, pl.ds(ours, mine)])

    loaded(1)
    for i in range(seqs):
        link.wait(6 + i)
        r.snd_br[i] = mm_nt(r.o[i], r.wo[...]).astype(BF16)
        core_copy(i).start()

    @pl.when(place.block == 1)
    def _():
        for slot in DG_MIDDLE:
            link.start(first_dg + slot, dg_source(slot))

    gather_o.step(1)

    def slot_start(slot):
        part = mm(r.xg[slot_block(slot)[0]], slot_weight(slot, r.wu))
        r.u[slot] = part
        r.snd_u[slot] = part.astype(BF16)
        link.start(first_u + slot, lambda rows: r.snd_u.at[slot, rows, :])

    loaded(2)
    for i, slots in enumerate((NARROW, WIDE)):
        core_copy(i).wait_recv()
        r.xf[i] = (r.xa[i].astype(F32) + (r.snd_br[i].astype(F32) + r.rcv_br[i].astype(F32))).astype(BF16)
        x = r.xf[i].astype(F32)
        r.snd_sq[2 + i] = to_row(jnp.sum(x * x, axis=-1, keepdims=True))
        sq_copy(2 + i).start()
        r.xg[i] = (x * gain_f).astype(BF16)
        for slot in slots:
            slot_start(slot)

    @pl.when(place.block == 1)
    def _():
        for slot in DG_LATE:
            link.start(first_dg + slot, dg_source(slot))

    emit_x1.prepare([r.xf[i, my_rows, :] for i in range(seqs)])
    factors = {}

    def row_factor(i):
        sq_copy(2 + i).wait_recv()
        factors[i] = lax.rsqrt((from_row(r.snd_sq[2 + i]) + from_row(r.rcv_sq[2 + i])) * (1.0 / z.width) + EPSILON)
        r.rf[i] = spread(factors[i], 128)

    def activate(slot):
        link.wait(first_u + slot)
        value = (r.u[slot] + r.rcv_u[slot].astype(F32)) * factors[slot_block(slot)[0]]
        squared = value * value
        bent = jnp.tanh(GELU_C * (value + GELU_A * (squared * value)))
        slope = 0.5 * (1.0 + bent) + 0.5 * value * (1.0 - bent * bent) * (GELU_C * (1.0 + 3.0 * GELU_A * squared))
        r.u[slot] = value
        r.rcv_u[slot] = mask_slot(slot, slope, flag).astype(BF16)
        g_k = mask_slot(slot, 0.5 * value * (1.0 + bent), flag).astype(BF16)
        r.g[G_PLACE[slot]] = g_k
        return mm_nt(g_k, slot_weight(slot, r.wd))

    def finish_rows(i):
        core_rows(i).wait_recv()
        total = r.snd_br[2 + i, my_rows, :].astype(F32) + r.rcv_half[i].astype(F32)
        r.x2[i] = (r.xf[i, my_rows, :].astype(F32) + total).astype(BF16)

        @pl.when(place.block == 0)
        def _():
            x_copy(i).start()

    @pl.when(place.block == 0)
    def _():
        loaded(3)

    row_factor(0)
    r.snd_br[2] = (activate(0) + activate(1)).astype(BF16)
    core_rows(0).start()
    gather_o.step(2)
    row_factor(1)
    total = activate(2) + activate(3)
    finish_rows(0)
    for slot in WIDE[2:]:
        total = total + activate(slot)
    r.snd_br[3] = total.astype(BF16)
    core_rows(1).start()
    r.g[1] = r.g[1] + r.g[SLOTS - 1]
    finish_rows(1)
    emit_x2.prepare([r.x2[i] for i in range(seqs)])
    for part in gathers:
        part.step(1)

    def normed_again():
        for i in range(seqs):
            r.xg[i] = (r.xf[i].astype(F32) * r.rf[i][:, :1] * gain_f).astype(BF16)

    @pl.when(place.block == 0)
    def _():
        normed_again()
        r.dt[:, :length] = jnp.transpose(r.xg[1].astype(F32)).astype(BF16)
        exchange_b.start()

    def piece(chunk, target):
        column = pl.multiple_of(lax.rem(chunk, 8) * unit, unit)
        return r.wud.at[lax.div(chunk, 8), share_rows(target), pl.ds(column, unit)]

    per = max(length // share, 1)

    def slots(way, n):
        ref = r.snd_qkv if way > 0 else r.rcv_qkv
        at = lax.div(n, per)
        return ref.at[lax.div(at, 3), lax.rem(at, 3), share_rows(lax.rem(n, per)), :]

    def intake(n):
        return r.snd_u.at[lax.div(n, per), share_rows(lax.rem(n, per)), :]

    def which(number):
        after = min(number // 2, 1) if isinstance(number, int) else jnp.minimum(lax.div(number, 2), 1)
        return number + SHARED * after * (1 - place.block)

    scatter = Scatter(
        place, piece, which, 14 - SHARED * (1 - place.block), {1: r.from_left, -1: r.from_right}, {1: r.sum_right, -1: r.sum_left}, {1: r.got_left, -1: r.got_right},
        slots, 6 * per, intake, r.intake_sem, 14,
    )

    @pl.when(place.block == 0)
    def _():
        gather_o.rest(3)
        link.forward(forward_order[3:first_u])
        link.forward(tuple(first_dg + slot for slot in DG_MIDDLE))
        link.forward(forward_order[first_u:])
        for part in gathers:
            part.step(2)
        link.forward(tuple(first_dg + slot for slot in DG_LATE))
        link.forward(do_order + dqkv_order)
        for part in gathers:
            part.rest(3)
        for i, slot_list in enumerate((NARROW, WIDE)):
            e_copy(i).wait_recv()
            if i == 1:
                ready(1)
            pass_half(r.e_in, 2 + i, i)
            for slot in slot_list:
                dg_part(slot)
                if i == 0:
                    link.start_whole(first_dg + slot, dg_source(slot))
                else:
                    link.start_near(first_dg + slot, dg_source(slot))
                if i == 1 and slot == WIDE[1]:
                    wait_ready(1)
                    for sent in WIDE[:2]:
                        link.start_far(first_dg + sent)
                if i == 1 and slot > WIDE[1]:
                    link.start_far(first_dg + slot)
        exchange_b.finish()
        transposed(r.e_in)
        exchange_d.start()
        link.finish(forward_order[:3])

    @pl.when(place.block == 1)
    def _():
        link.finish_whole(forward_order[:3])

    link.finish(forward_order[3:])

    def hidden_back(slot):
        @pl.when(place.block == 0)
        def _():
            (link.wait_whole if slot in NARROW else link.wait)(first_dg + slot)

        @pl.when(place.block == 1)
        def _():
            (link.wait_whole if slot in DG_STRAIGHT else link.wait)(first_dg + slot)

        grad = r.snd_dg[slot].astype(F32) + r.rcv_dg[slot].astype(F32)
        du_k = (grad * r.rcv_u[slot].astype(F32)).astype(BF16)
        r.du[slot] = du_k
        return mm_nt(du_k, slot_weight(slot, r.wu)), jnp.sum(du_k.astype(F32) * r.u[slot], axis=-1, keepdims=True)

    def flipped(value):
        return jnp.transpose(value.astype(F32)).astype(BF16)

    def up_grads(blocks):
        wide = flipped(r.xg[1])
        for block in blocks:
            part = mm(wide, r.du[2 + block])
            if block < 2:
                part = part + mm_tn(r.xg[0], r.du[block])
            r.wu[:, block * unit:(block + 1) * unit] = part.astype(BF16)
            if block < AHEAD:
                scatter.edges(block)

    def core_sum_start(i, slot_list):
        total = row = None
        for slot in slot_list:
            more, more_row = hidden_back(slot)
            total, row = (more, more_row) if total is None else (total + more, row + more_row)

            if i == 1 and slot - 2 < 8 - SHARED:
                @pl.when(place.block == 0)
                def _(slot=slot):
                    up_grads((slot - 2,))

        if i == 1:
            @pl.when(place.block == 0)
            def _():
                gather_u.step(1)

        r.snd_db[i] = total.astype(BF16)
        db_copy(i).start()
        r.snd_row[i] = to_row(row)
        row_copy(i, place.core_peer).start()

    def ffn_done(i):
        db_copy(i).wait_recv()
        row_copy(i, place.core_peer).wait_recv()
        mean = (from_row(r.snd_row[i]) + from_row(r.rcv_row[i])) * (1.0 / z.width)
        grad = r.snd_db[i].astype(F32) + r.rcv_db[i].astype(F32)
        factor = r.rf[i][:, :1]
        scaled = r.xf[i].astype(F32) * factor
        new = r.e_in[i].astype(F32) + factor * (grad * gain_f - scaled * mean)
        r.e[i] = new
        r.dc[i] = new.astype(BF16)
        core_copy(i).wait_send()
        r.snd_br[i, :, :mine] = mm(r.dc[i], r.wo[:, pl.ds(theirs, mine)]).astype(BF16)
        link.start(first_do + i, lambda rows: r.snd_br.at[i, rows, 0:mine])
        r.own_qkv[i, 0] = mm(r.dc[i], r.wo[:, pl.ds(ours, mine)])
        return jnp.sum(grad * scaled, axis=0, keepdims=True)

    core_sum_start(0, NARROW)
    gain_f_sum = ffn_done(0)
    core_sum_start(1, WIDE)
    gain_f_sum = gain_f_sum + ffn_done(1)
    r.gains[...] = jnp.zeros_like(r.gains)
    r.gains[1:2, :] = 0.5 * gain_f_sum
    emit_e1.prepare([r.dc[i, my_rows, :] for i in range(seqs)])

    @pl.when(place.block == 1)
    def _():
        exchange_d.finish()
        transposed(r.dc)
        exchange_c.start()

    rows = slice(0, share)
    inner = (me > 0) & (me < planes - 1)

    def grads_ready():
        exchange_flag.finish()
        for n in range(SLOTS):
            r.u[n, rows, :] = jnp.zeros_like(r.u[n, rows, :])
        flags_copy = pltpu.make_async_copy(r.every_flag, r.flags, r.block_sem.at[0])
        flags_copy.start()
        flags_copy.wait()

    def planes_of(part, first, last):
        def body(k, carry):
            part(jnp.where(me < planes // 2, lax.rem(me + k, planes), lax.rem(me + planes - k, planes)))
            return carry
        lax.fori_loop(lax.div(first * planes, 4), lax.div(last * planes, 4), body, 0)

    def fetched(*pairs):
        copies = [pltpu.make_async_copy(src, dst, r.block_sem.at[at]) for at, (src, dst) in enumerate(pairs)]
        for copy in copies:
            copy.start()
        for copy in copies:
            copy.wait()

    def down_part(n):
        block_g = r.snd_dg.at[0:SLOTS - 1]
        fetched(*((r.every_g.at[k, n], r.snd_dg.at[3 * k:3 * k + 3]) for k in range(3)), (r.every_d.at[n], r.block_d))
        on = r.flags[n][:1, :1]
        shared = block_g[1].astype(F32)
        upper, lower = (shared * on).astype(BF16), (shared * (1.0 - on)).astype(BF16)
        narrow, wide = r.block_d[:, :length], r.block_d[:, length:]
        for block in range(8):
            right = upper if block == 4 else block_g[2 + block if block < 4 else 1 + block]
            part = mm(wide, right)
            if block < 2:
                part = part + mm(narrow, block_g[0] if block == 0 else lower)
            r.u[block, rows, :] = r.u[block, rows, :] + part

    def out_part(n):
        fetched((r.every_o.at[n], r.xf), (r.every_c.at[n], r.block_c))
        for side in range(2):
            span = slice(side * unit, (side + 1) * unit)
            part = mm(r.block_c[:, :length], r.xf[0, :, span]) + mm(r.block_c[:, length:], r.xf[1, :, span])
            r.u[8 + side, rows, :] = r.u[8 + side, rows, :] + part

    def gather_done():
        for part in gathers:
            part.settle_all()

    def up_part(n):
        block_u, block_b = r.rcv_dg.at[0:SHARED], r.rcv_dg.at[SHARED, rows, 0:length]
        fetched((r.every_u.at[n], block_u), (r.every_b.at[n], block_b))
        for k in range(SHARED):
            r.own_qkv[k // 3, k % 3, rows, :] = r.own_qkv[k // 3, k % 3, rows, :] + mm(block_b[...], block_u[k])

    for i in range(seqs):
        link.wait(first_do + i)
        row = jnp.zeros((length, 1), F32)
        for j in range(z.heads):
            span = pl.ds(j * HEAD_DIM, HEAD_DIM)
            do_j = (r.own_qkv[i, 0, :, span] + r.rcv_do[i, :, span].astype(F32)).astype(BF16)
            q_j, k_j, v_j, probs = r.q[i, :, span], r.k[i, :, span], r.v[i, :, span], r.p[i, j]
            dp = mm_nt(do_j, v_j)
            dv = mm_tn(probs.astype(BF16), do_j)
            ds = (probs * (dp - jnp.sum(probs * dp, axis=-1, keepdims=True))).astype(BF16)
            dq = mm(ds, k_j) * scale
            dk = mm_tn(ds, q_j) * scale
            row = row + jnp.sum(dq * q_j.astype(F32) + dk * k_j.astype(F32) + dv * v_j.astype(F32), axis=-1, keepdims=True)
            at = pl.ds(pl.multiple_of(ours + j * HEAD_DIM, HEAD_DIM), HEAD_DIM)
            r.dqkv[i, 0, :, at] = (dq * cosine - turned(dq) * sine).astype(BF16)
            r.dqkv[i, 1, :, at] = (dk * cosine - turned(dk) * sine).astype(BF16)
            r.dqkv[i, 2, :, at] = dv.astype(BF16)
        r.snd_row[2 + i] = to_row(row)
        row_copy(2 + i, place.pair).start()
        for t in range(3):
            link.start(first_dqkv + 3 * i + t, lambda rows, i=i, t=t: r.dqkv.at[i, t, rows, pl.ds(ours, mine)])

    def first_grads():
        link.finish_whole(ffn_order[:len(NARROW)])
        link.finish(ffn_order[len(NARROW):])
        exchange_d.finish()
        transposed(r.dc)
        exchange_c.start()
        grads_ready()
        gather_done()

    @pl.when((place.block == 0) & inner)
    def _():
        first_grads()
        planes_of(down_part, 0, 1)

    for i in range(seqs):
        if i == 1:
            @pl.when(place.block == 0)
            def _():
                gather_u.step(2)

        part = jnp.zeros((length, feats), F32)
        for t in range(3):
            link.wait(first_dqkv + 3 * i + t)
            part = part + mm_nt(r.dqkv[i, t], r.wqkv[t])
        r.snd_db[2 + i] = part.astype(BF16)
        da_rows(i).start()
        row_copy(2 + i, place.pair).wait_recv()
        r.snd_row[4 + i] = r.snd_row[2 + i] + r.rcv_row[2 + i]
        row_copy(4 + i, place.core_peer).start()

    @pl.when(place.block == 0)
    def _():
        for i in range(seqs):
            x_copy(i).wait_send()

    gain_a_sum = jnp.zeros((1, feats), F32)
    for i in range(seqs):
        da_rows(i).wait_recv()
        row_copy(4 + i, place.core_peer).wait_recv()
        r.snd_row[6 + i] = (r.snd_row[4 + i] + r.rcv_row[4 + i]) * (1.0 / z.width)
        mean = from_row(r.snd_row[6 + i, :, my_rows])
        grad = r.snd_db[2 + i, my_rows, :].astype(F32) + r.rcv_half[i].astype(F32)
        factor = r.ra[i, my_rows, :][:, :1]
        scaled = r.xa[i, my_rows, :].astype(F32) * factor
        r.x2[i] = (r.e[i, my_rows, :] + factor * (grad * gain_a - scaled * mean)).astype(BF16)
        gain_a_sum = gain_a_sum + jnp.sum(grad * scaled, axis=0, keepdims=True)

        @pl.when(place.block == 1)
        def _():
            e_copy(i).start()

    r.gains[0:1, :] = gain_a_sum
    emit_e0.prepare([r.x2[i] for i in range(seqs)])

    def qkv_grad():
        for i in range(seqs):
            r.xg[i] = (r.xa[i].astype(F32) * r.ra[i][:, :1] * gain_a).astype(BF16)
        first, second = flipped(r.xg[0]), flipped(r.xg[1])
        for t in range(3):
            r.wd[:, t * z.cols:(t + 1) * z.cols] = (mm(first, r.dqkv[0, t]) + mm(second, r.dqkv[1, t])).astype(BF16)

    @pl.when(place.block == 1)
    def _():
        gather_o.rest(3)
        for part in gathers:
            part.step(2)
        normed_again()
        up_grads(range(8))
        qkv_grad()
        link.forward(ffn_order[len(NARROW):])
        scatter.turn(0)
        link.forward(do_order)
        link.forward(dqkv_order)
        scatter.turn(1)
        gathers[0].rest(3)
        scatter.turn(2)
        scatter.turn(3)
        gathers[1].rest(3)

    @pl.when(place.block == 0)
    def _():
        qkv_grad()
        scatter.edges(2)

        @pl.when(jnp.logical_not(inner))
        def _():
            first_grads()
            planes_of(down_part, 0, 4)

        @pl.when(inner)
        def _():
            planes_of(down_part, 1, 4)

        gather_o.settle_all()
        gather_u.own().wait()
        gather_u.rest(3)
        for k in range(SHARED):
            r.own_qkv[k // 3, k % 3, rows, :] = jnp.zeros_like(r.own_qkv[k // 3, k % 3, rows, :])
        for turn in range(4):
            scatter.turn(turn)

            @pl.when(inner)
            def _(turn=turn):
                planes_of(up_part, turn, turn + 1)

    @pl.when(place.block == 1)
    def _():
        link.finish_whole(tuple(first_dg + slot for slot in DG_STRAIGHT))
        link.finish(tuple(first_dg + slot for slot in DG_MIDDLE + DG_LATE))
        grads_ready()

    emit_x1.start(0)
    emit_x2.start(1)
    emit_e1.start(1)
    emit_e0.start(0)
    gains_copy = remote(r.gains, r.core_gains, r.pair_send.at[0], r.pair_recv.at[0], place.core_peer)
    gains_copy.start()
    scatter.turn(4)
    gains_copy.wait()
    r.every_gain[me] = r.gains[...] + r.core_gains[...]
    exchange_gain = Exchange(place, lambda n: r.every_gain.at[me], r.every_gain, (r.gain_send, r.gain_recv, None))
    for n in range(1, planes):
        exchange_gain.copy(n).start()

    def grad_copy(n):
        dst = r.down_grad.at[:, n * unit:(n + 1) * unit] if n < 8 else r.out_grad.at[:, (n - 8) * unit:(n - 7) * unit]
        return pltpu.make_async_copy(r.u.at[n, rows, :], dst, r.grad_sem.at[n])

    def shared_copy(k):
        dst = r.up_grad.at[:, (8 - SHARED + k) * unit:(9 - SHARED + k) * unit]
        return pltpu.make_async_copy(r.own_qkv.at[k // 3, k % 3, rows, :], dst, r.shared_sem.at[k])

    def total_slot(number):
        at = lax.rem(number, 4)
        column = pl.multiple_of(lax.rem(at, 2) * unit, unit)
        return r.e.at[lax.div(at, 2), rows, pl.ds(column, unit)]

    def total_copy(number, action):
        chunk = which(number)
        src, sem = total_slot(number), r.total_sem.at[lax.rem(number, 4)]

        @pl.when(chunk < 8)
        def _():
            dst = r.up_grad.at[:, pl.ds(pl.multiple_of(chunk * unit, unit), unit)]
            action(pltpu.make_async_copy(src, dst, sem))

        @pl.when(chunk >= 8)
        def _():
            column = pl.multiple_of(lax.rem(chunk, 2) * unit, unit)
            dst = r.qkv_grad.at[lax.div(chunk - 8, 2), :, pl.ds(column, unit)]
            action(pltpu.make_async_copy(src, dst, sem))

    def final(number, carry):
        @pl.when(number >= 4)
        def _():
            total_copy(number - 4, lambda copy: copy.wait())

        scatter.last(number, total_slot(number))
        total_copy(number, lambda copy: copy.start())
        return carry

    finals = (
        {5: 3, 6: 5, 7: 6, 8: 7, 9: 8},
        {5: 1, 6: 2, 7: 3, 8: 4, 9: 5, 10: 6, 11: 7, 12: 9, 13: 11, 14: 13, 15: 14},
        {11: 8, 12: 10, 13: 11, 14: 13, 15: 14},
    )

    def finals_by(turn):
        first, inside, outside = (max([count for at, count in table.items() if at <= turn], default=0) for table in finals)
        return jnp.where(place.block == 0, first, jnp.where(inner, inside, outside))

    def once(block, where, body):
        pl.when((place.block == block) & (inner if where else jnp.logical_not(inner)))(body)

    def all_planes(*parts):
        for part in parts:
            planes_of(part, 0, 4)

    def edge_parts():
        gather_u.settle(1, gather_u.last - 1)
        planes_of(up_part, 0, 3)
        exchange_c.finish()
        planes_of(out_part, 0, 4)
        gather_u.settle(gather_u.last, gather_u.last)
        planes_of(up_part, 3, 4)

    def late_edge_parts():
        gather_done()
        gather_o.settle_all()
        exchange_c.finish()
        all_planes(down_part, out_part)

    def inner_start():
        gather_done()
        gather_o.settle_all()
        exchange_c.finish()

    def out_start():
        exchange_c.finish()
        planes_of(out_part, 0, 2)

    for turn in range(5, max(16, len(scatter.turns()))):
        scatter.turn(turn)
        if turn == 5:
            once(0, False, edge_parts)
        if turn == 12:
            once(1, False, late_edge_parts)
        lax.fori_loop(finals_by(turn - 1), finals_by(turn), final, 0)
        if turn == 5:
            pl.when(place.block == 1)(lambda: gathers[2].rest(3))
            once(0, True, out_start)
        if turn == 6:
            once(0, True, lambda: planes_of(out_part, 2, 4))
        if turn == 7:
            once(1, True, inner_start)
        if 7 <= turn < 11:
            once(1, True, lambda turn=turn: planes_of(down_part, turn - 7, turn - 6))
        if turn == 7:
            @pl.when(place.block == 0)
            def _():
                for n in range(SLOTS):
                    grad_copy(n).start()
                for k in range(SHARED):
                    shared_copy(k).start()
        if turn == 11:
            once(1, True, lambda: planes_of(out_part, 0, 4))
        if turn == 12:
            @pl.when(place.block == 1)
            def _():
                for n in range(SLOTS):
                    grad_copy(n).start()
    for n in range(1, planes):
        source = lax.rem(me + planes - n, planes)
        slot = r.every_gain.at[source]
        remote(slot, slot, r.gain_send.at[n], r.gain_recv.at[n], place.pair).wait_recv()
        exchange_gain.copy(n).wait_send()
    gain_total = r.every_gain[0]
    for n in range(1, planes):
        gain_total = gain_total + r.every_gain[n]
    r.gain_grads[...] = gain_total

    scatter.finish()
    for back in range(1, 5):
        total_copy(scatter.total - back, lambda copy: copy.wait())

    @pl.when(place.block == 0)
    def _():
        for k in range(SHARED):
            shared_copy(k).wait()

    for n in range(SLOTS):
        grad_copy(n).wait()
    for n in range(4):
        sq_copy(n).wait_send()
    for i in range(seqs):
        core_rows(i).wait_send()
        row_copy(i, place.core_peer).wait_send()
        row_copy(2 + i, place.pair).wait_send()
        row_copy(4 + i, place.core_peer).wait_send()
        db_copy(i).wait_send()
        da_rows(i).wait_send()
    link.finish(do_order + dqkv_order)

    @pl.when(place.block == 0)
    def _():
        link.finish_forward(forward_order[3:] + tuple(first_dg + slot for slot in DG_MIDDLE + DG_LATE) + do_order + dqkv_order)

    @pl.when(place.block == 1)
    def _():
        link.finish_forward(forward_order + ffn_order[len(NARROW):] + do_order + dqkv_order)
        for i in range(seqs):
            e_copy(i).wait_send()

    for part in (*gathers, gather_o):
        part.finish()
    pl.when(place.block == 0)(gather_u.finish)
    emit_x1.finish(0)
    emit_x2.finish(1)
    emit_e1.finish(1)
    emit_e0.finish(0)


def shape(dims, kind):
    return jax.ShapeDtypeStruct(dims, kind)


ANY = pl.BlockSpec(memory_space=pl.ANY)
IN_VMEM = pl.BlockSpec(memory_space=pltpu.VMEM)


def vmem(dims, kind):
    return pltpu.VMEM(tuple(dims), kind)


def run_main(width_index, x0, c0, gain_a, gain_f, wqkv, wo, wu, wd):
    seqs, tokens, width = x0.shape
    planes = lax.axis_size("dp")
    z = Sizes(wo.shape[0], wo.shape[1], wu.shape[1], tokens)
    share, chunks = z.feats // planes, 14
    cosine, sine = rotary(z.length, HEAD_DIM)
    args = {
        "width": width_index, "x0": x0, "c0": c0, "gain_a": gain_a, "gain_f": gain_f, "cosine": cosine, "sine": sine,
        "wqkv_hbm": wqkv, "wo_hbm": wo, "wu_hbm": wu, "wd_hbm": wd,
    }
    places = {"width": pl.BlockSpec(memory_space=pltpu.SMEM)}
    places.update({name: IN_VMEM for name in ("gain_a", "gain_f", "cosine", "sine", "gain_grads")})
    row = (8, z.feats)
    outs = {
        "layer_out": shape((seqs, tokens, width), BF16), "input_grad": shape((seqs, tokens, width), BF16),
        "qkv_grad": shape((3, share, z.cols), F32), "out_grad": shape((share, z.cols), F32),
        "up_grad": shape((share, 8 * z.unit), F32), "down_grad": shape((share, 8 * z.unit), F32), "gain_grads": shape(row, F32),
        "every_g": shape((3, planes, 3, z.length, z.unit), BF16), "every_o": shape((planes, seqs, z.length, z.cols), BF16),
        "every_d": shape((planes, share, seqs * z.length), BF16), "every_c": shape((planes, share, seqs * z.length), BF16),
        "every_u": shape((planes, SHARED, z.length, z.unit), BF16), "every_b": shape((planes, share, z.length), BF16),
        "every_flag": shape((planes, 8, 128), F32),
        "from_left": shape((planes, chunks, share, z.unit), BF16), "from_right": shape((planes, chunks, share, z.unit), BF16),
    }
    state, half_state, heads_state = (seqs, z.length, z.feats), (seqs, tokens, z.feats), (seqs, z.length, z.mine)
    slots, qkv, messages = (SLOTS, z.length, z.unit), (seqs, 3, z.length, z.mine), 12 + 2 * seqs + 2 * SLOTS
    small, factor, pair = (8, 8, z.length), (seqs, z.length, 128), (4, z.length, z.feats)
    scratch = {"wqkv": vmem(wqkv.shape, BF16), "wo": vmem(wo.shape, BF16), "wud": vmem((2, *wu.shape), BF16)}
    for dims, kind, group in (
        (state, BF16, "xa xf xg e_in dc"), (state, F32, "e"), (half_state, BF16, "x2 rcv_half"),
        (heads_state, BF16, "q k v rcv_do"),
        ((seqs, z.heads, z.length, z.length), F32, "p"), ((seqs, z.length, z.cols), BF16, "o"), (factor, F32, "ra rf"),
        (slots, F32, "u"), (slots, BF16, "g snd_u rcv_u du snd_dg rcv_dg"), (qkv, F32, "own_qkv"), (qkv, BF16, "snd_qkv rcv_qkv"),
        ((4, 8, z.length), F32, "snd_sq rcv_sq"), (small, F32, "snd_row rcv_row"), (pair, BF16, "snd_br snd_db"),
        ((2, z.length, z.feats), BF16, "rcv_br rcv_db"), ((z.feats, seqs * z.length), BF16, "dt"), ((4, *half_state), BF16, "stage"),
        ((seqs, 3, z.length, z.cols), BF16, "dqkv"), ((messages, z.length - DIRECT_ROWS, z.mine), BF16, "relay"),
        ((8, 128), F32, "wide"), ((planes, 8, 128), F32, "flags"), ((share, seqs * z.length), BF16, "block_d block_c"),
        (row, F32, "gains core_gains"), ((planes, *row), F32, "every_gain"),
    ):
        scratch.update({name: vmem(dims, kind) for name in group.split()})
    for count, group in (
        (4, "load_sem sq_send sq_recv core_send core_recv db_send db_recv in_send in_recv in_local block_sem"),
        (messages, "x_send x_recv far_send far_recv relay_send relay_recv"), (6, "row_send row_recv total_sem"),
        (2, "y_send y_recv"), (8, "out_send out_recv out_local"), (1, "o_local d_local c_local flag_local pair_send pair_recv"),
        (planes, "o_right o_left o_sem d_send d_recv c_send c_recv flag_send flag_recv gain_send gain_recv"),
        (2 * planes, "intake_sem"), (planes * chunks, "got_left got_right"), (4 * planes, "sum_right sum_left"), (SHARED, "shared_sem"),
        (planes, "u_right u_left u_sem b_send b_recv"), (1, "u_local b_local"), (SLOTS, "grad_sem"),
    ):
        scratch.update({name: pltpu.SemaphoreType.DMA((count,)) for name in group.split()})
    scratch["g_local"] = pltpu.SemaphoreType.DMA((3,))
    scratch.update({name: pltpu.SemaphoreType.DMA((3, planes)) for name in ("g_right", "g_left", "g_sem")})
    scratch["go_sem"] = pltpu.SemaphoreType.REGULAR((2,))
    results = pl.pallas_call(
        functools.partial(main_kernel, (*args, *outs, *scratch)),
        out_shape=tuple(outs.values()),
        in_specs=[places.get(name, ANY) for name in args],
        out_specs=tuple(places.get(name, ANY) for name in outs),
        scratch_shapes=list(scratch.values()),
        compiler_params=pltpu.CompilerParams(collective_id=1, has_side_effects=True, vmem_limit_bytes=VMEM_LIMIT),
        name="main",
    )(*args.values())
    return dict(zip(outs, results))


def local(inputs, cotangent, width_index, qkv_weight, out_weight, attn_gain, ffn_gain, up_weight, down_weight):
    found = run_main(width_index, inputs, cotangent, attn_gain, ffn_gain, qkv_weight, out_weight, up_weight, down_weight)
    gains = found["gain_grads"]
    size = gains.shape[1] // (2 * lax.axis_size("dp"))
    own = (lax.axis_index("dp") * 2 + lax.axis_index("mp")) * size
    gain_grads = lax.dynamic_slice_in_dim(gains[:2], own, size, axis=1)
    return (
        found["layer_out"][None],
        found["input_grad"][None],
        found["qkv_grad"],
        found["out_grad"],
        gain_grads[0],
        gain_grads[1],
        found["up_grad"],
        found["down_grad"],
    )


def solution(mesh):
    in_specs = (
        P("dp", "mp", None),
        P("dp", "mp", None),
        P("dp"),
        P(None, "section", "mp"),
        P("section", "mp"),
        P("section"),
        P("section"),
        P("section", "mp"),
        P("section", "mp"),
    )
    out_specs = (
        P("section", "dp", "mp", None),
        P("section", "dp", "mp", None),
        P(None, ("section", "dp"), "mp"),
        P(("section", "dp"), "mp"),
        P(("section", "dp", "mp")),
        P(("section", "dp", "mp")),
        P(("section", "dp"), "mp"),
        P(("section", "dp"), "mp"),
    )
    return jax.shard_map(local, mesh=mesh, in_specs=in_specs, out_specs=out_specs, check_vma=False)
```

```python
import functools
import types

import jax
import jax.numpy as jnp
import numpy as np
from jax import lax
from jax.sharding import PartitionSpec as P
from jax.experimental import pallas as pl
from jax.experimental.pallas import tpu as pltpu

HEAD_DIM = 128
EPSILON = 1e-05
GELU_C = 0.7978845608028654
GELU_A = 0.044715
MESH = pl.DeviceIdType.MESH
SLOTS = 10
AHEAD = 3
SHARED = 3
DIRECT_ROWS = 144
URGENT_ROWS = 192
F32 = jnp.float32
BF16 = jnp.bfloat16
VMEM_LIMIT = 63 * 2**20


def mm(a, b):
    return lax.dot_general(a, b, (((1,), (0,)), ((), ())), preferred_element_type=F32)


def mm_nt(a, b):
    return lax.dot_general(a, b, (((1,), (1,)), ((), ())), preferred_element_type=F32)


def mm_tn(a, b):
    return lax.dot_general(a, b, (((0,), (0,)), ((), ())), preferred_element_type=F32)


def to_row(column):
    rows = column.shape[0]
    return jnp.transpose(jnp.broadcast_to(column, (rows, 128)))[:8]


def from_row(row):
    return jnp.transpose(row)[:, :1]


def rotary(length, head_size):
    half_dim = head_size // 2
    frequency = np.float32(10000.0) ** (np.float32(-2.0 / head_size) * np.arange(half_dim, dtype=np.float32))
    angles = np.arange(length, dtype=np.float32)[:, None] * frequency[None, :].astype(np.float32)
    cosine, sine = np.cos(angles).astype(np.float32), np.sin(angles).astype(np.float32)
    return jnp.asarray(np.concatenate([cosine, cosine], axis=1)), jnp.asarray(np.concatenate([-sine, sine], axis=1))


def turned(values):
    return pltpu.roll(values, HEAD_DIM // 2, 1)


def remote(src, dst, send_sem, recv_sem, device):
    return pltpu.make_async_remote_copy(
        src_ref=src, dst_ref=dst, send_sem=send_sem, recv_sem=recv_sem,
        device_id=device, device_id_type=MESH,
    )


class Place:
    def __init__(self):
        section, dp, mp = (lax.axis_index(name) for name in ("section", "dp", "mp"))
        self.block, self.half, self.core = section // 2, section % 2, mp
        other_half = 1 - self.half
        other_block = 1 - self.block
        self.at = (section, dp, mp)
        self.core_peer = (section, dp, 1 - mp)
        self.pair = (self.block * 2 + other_half, dp, mp)
        self.across = (other_block * 2 + self.half, dp, mp)
        self.corner = (other_block * 2 + other_half, dp, mp)

    def plane(self, n):
        section, dp, mp = self.at
        return (section, lax.rem(dp + n, lax.axis_size("dp")), mp)

    def barrier(self):
        sem = pltpu.get_barrier_semaphore()
        peers = [self.core_peer, self.pair, self.across, self.corner]
        peers += [self.plane(n) for n in range(1, lax.axis_size("dp"))]
        for peer in peers:
            pl.semaphore_signal(sem, inc=1, device_id=peer, device_id_type=MESH)
        pl.semaphore_wait(sem, len(peers))


class Exchange:
    def __init__(self, place, piece, slots, sems):
        self.place, self.piece, self.slots = place, piece, slots
        self.send, self.recv, self.local = sems
        self.me, self.count = lax.axis_index("dp"), lax.axis_size("dp")

    def copy(self, n):
        target = lax.rem(self.me + n, self.count)
        return remote(self.piece(target), self.slots.at[self.me], self.send.at[n], self.recv.at[n], self.place.plane(n))

    def own(self):
        return pltpu.make_async_copy(self.piece(self.me), self.slots.at[self.me], self.local.at[0])

    def start(self):
        self.own().start()
        for n in range(1, self.count):
            self.copy(n).start()

    def finish(self):
        self.own().wait()
        for n in range(1, self.count):
            source = lax.rem(self.me + self.count - n, self.count)
            held = self.slots.at[source]
            remote(held, held, self.send.at[n], self.recv.at[n], self.place.plane(n)).wait_recv()
            self.copy(n).wait_send()


class PairLink:
    def __init__(self, place, relay, sems, targets, urgent):
        self.place, self.relay, self.targets = place, relay, targets
        self.send, self.recv, self.far_send, self.far_recv, self.relay_send, self.relay_recv = sems
        self.rows = DIRECT_ROWS + relay.shape[1]
        self.urgent = urgent
        self.sources = {}

    def direct(self, index):
        return slice(0, URGENT_ROWS if index in self.urgent else DIRECT_ROWS)

    def detour(self, index):
        return slice(URGENT_ROWS if index in self.urgent else DIRECT_ROWS, self.rows)

    def held(self, index):
        rows = self.detour(index)
        return self.relay.at[index, 0:rows.stop - rows.start]

    def near(self, index):
        rows = self.direct(index)
        src, dst = self.sources[index](rows), self.targets(index, self.place.half, rows)
        return remote(src, dst, self.send.at[index], self.recv.at[index], self.place.pair)

    def far(self, index):
        src = self.sources[index](self.detour(index))
        return remote(src, self.held(index), self.far_send.at[index], self.relay_recv.at[index], self.place.across)

    def whole(self, index):
        rows, src = slice(0, self.rows), self.sources[index]
        dst = self.targets(index, self.place.half, rows)
        return remote(src(rows), dst, self.send.at[index], self.recv.at[index], self.place.pair)

    def start(self, index, src):
        self.sources[index] = src
        self.near(index).start()
        self.far(index).start()

    def start_near(self, index, src):
        self.sources[index] = src
        self.near(index).start()

    def start_far(self, index):
        self.far(index).start()

    def start_whole(self, index, src):
        self.sources[index] = src
        self.whole(index).start()

    def wait(self, index):
        other = 1 - self.place.half
        for rows, sem in ((self.direct(index), self.recv), (self.detour(index), self.far_recv)):
            dst = self.targets(index, other, rows)
            remote(dst, dst, self.send.at[index], sem.at[index], self.place.pair).wait_recv()

    def wait_whole(self, index):
        dst = self.targets(index, 1 - self.place.half, slice(0, self.rows))
        remote(dst, dst, self.send.at[index], self.recv.at[index], self.place.pair).wait_recv()

    def finish(self, indices):
        for index in indices:
            self.near(index).wait_send()
            self.far(index).wait_send()

    def finish_whole(self, indices):
        for index in indices:
            self.whole(index).wait_send()

    def passed(self, index):
        dst = self.targets(index, self.place.half, self.detour(index))
        return remote(self.held(index), dst, self.relay_send.at[index], self.far_recv.at[index], self.place.corner)

    def forward(self, indices):
        for index in indices:
            held = self.held(index)
            remote(held, held, self.relay_send.at[index], self.relay_recv.at[index], self.place.across).wait_recv()
            self.passed(index).start()

    def finish_forward(self, indices):
        for index in indices:
            self.passed(index).wait_send()


def spread(value, width):
    return jnp.broadcast_to(value, (value.shape[0], width))


def slot_block(slot):
    return (0, slot) if slot < 2 else (1, slot - 2)


def slot_weight(slot, weight):
    unit = weight.shape[1] // 8
    at = slot_block(slot)[1] * unit
    return weight[:, at:at + unit]


def mask_slot(slot, value, flag):
    if slot == 1:
        return value * (1.0 - flag)
    return value if slot < 6 else value * flag


NARROW, WIDE = (0, 1), tuple(range(2, SLOTS))
G_PLACE = (0, 1, 2, 3, 4, 5, 9, 6, 7, 8)
DG_STRAIGHT, DG_MIDDLE, DG_LATE = (0, 1, 2), (3, 4), (5, 6, 7, 8, 9)


class Sizes:
    def __init__(self, feats, cols, hidden, tokens):
        self.feats, self.cols, self.unit, self.tokens = feats, cols, hidden // 8, tokens
        self.mine, self.length, self.width = cols // 2, 2 * tokens, 2 * feats
        self.heads = self.mine // HEAD_DIM


class Emitter:
    def __init__(self, place, out, stage, swap, sems, first=0):
        self.place, self.out, self.stage, self.swap, self.sems, self.first = place, out, stage, swap, sems, first

    def span(self):
        feats = self.stage.shape[-1]
        return pl.ds(pl.multiple_of(self.place.half * feats, feats), feats)

    def far(self, i):
        at = self.first + i
        return remote(self.stage.at[i], self.out.at[i, :, self.span()], self.sems[0].at[at], self.sems[1].at[at], self.place.pair)

    def near(self, i):
        return pltpu.make_async_copy(self.stage.at[i], self.out.at[i, :, self.span()], self.sems[2].at[self.first + i])

    def prepare(self, values):
        narrow, wide = (value.astype(F32) for value in values)
        self.stage[0] = (narrow * (1.0 - self.swap) + wide * self.swap).astype(BF16)
        self.stage[1] = (wide * (1.0 - self.swap) + narrow * self.swap).astype(BF16)

    def start(self, owner):
        @pl.when(self.place.half == owner)
        def _():
            for i in range(2):
                self.near(i).start()

        @pl.when(self.place.half != owner)
        def _():
            for i in range(2):
                self.far(i).start()

    def finish(self, owner):
        @pl.when(self.place.half == owner)
        def _():
            for i in range(2):
                self.near(i).wait()
                self.far(i).wait_recv()

        @pl.when(self.place.half != owner)
        def _():
            for i in range(2):
                self.far(i).wait_send()


class Gather:
    def __init__(self, place, mine, every, sems):
        self.me, self.count = lax.axis_index("dp"), lax.axis_size("dp")
        self.place, self.mine, self.every = place, mine, every
        self.right, self.left, self.recv, self.local = sems
        self.last = self.count - 1

    def send(self, block, way, number):
        section, dp, mp = self.place.at
        sems = self.right if way > 0 else self.left
        src = self.mine if number == 1 else self.every.at[block]
        return remote(src, self.every.at[block], sems.at[block], self.recv.at[block], (section, dp + way, mp))

    def arrive(self, block):
        held = self.every.at[block]
        remote(held, held, self.right.at[block], self.recv.at[block], self.place.pair).wait_recv()

    def moves(self, number):
        me, last = self.me, self.count - 1
        right, left = me - number + 1, me + number - 1
        return ((1, right, (right >= 0) & (me < last)), (-1, left, (left <= last) & (me > 0)))

    def own(self):
        return pltpu.make_async_copy(self.mine, self.every.at[self.me], self.local.at[0])

    def step(self, number):
        if number == 1:
            self.own().start()
        if number > self.last:
            return
        for way, block, active in self.moves(number):
            @pl.when(active)
            def _(way=way, block=block):
                if number > 1:
                    self.arrive(block)
                self.send(block, way, number).start()

    def rest(self, number):
        for more in range(number, self.last + 1):
            self.step(more)

    def settle(self, first, last):
        for number in range(first, min(last, self.last) + 1):
            left, right = self.me - number, self.me + number
            done = number == self.last

            @pl.when((left >= 0) if done else (left >= 0) & (self.me == self.count - 1))
            def _(block=left):
                self.arrive(block)

            @pl.when((right < self.count) if done else (right < self.count) & (self.me == 0))
            def _(block=right):
                self.arrive(block)

    def settle_all(self):
        self.own().wait()
        self.settle(1, self.last)

    def finish(self):
        for number in range(1, self.last + 1):
            for way, block, active in self.moves(number):
                @pl.when(active)
                def _(way=way, block=block):
                    self.send(block, way, number).wait_send()


class Scatter:
    def __init__(self, place, piece, which, total, landing, sends, arrivals, slots, places, intake, in_sem, chunks):
        self.places = places
        self.place, self.piece, self.which, self.total = place, piece, which, total
        self.landing, self.sends, self.arrivals = landing, sends, arrivals
        self.slots, self.intake, self.in_sem, self.chunks = slots, intake, in_sem, chunks
        self.me, self.count = lax.axis_index("dp"), lax.axis_size("dp")

    def send(self, way, target, number, src):
        section, dp, mp = self.place.at
        dst = self.landing[way].at[target, number]
        send_sem = self.sends[way].at[target * 4 + lax.rem(number, 4)]
        return remote(src, dst, send_sem, self.arrivals[way].at[target * self.chunks + number], (section, dp + way, mp))

    def own(self, number, target):
        return self.piece(self.which(number), target)

    def arrived(self, way, target, number):
        held = self.landing[way].at[target, number]
        got = self.arrivals[way].at[target * self.chunks + number]
        remote(held, held, self.sends[way].at[0], got, self.place.pair).wait_recv()

    def taken(self, way, target, number, buffer):
        return pltpu.make_async_copy(self.landing[way].at[target, number], self.intake(buffer), self.in_sem.at[buffer])

    def each(self, way, body):
        def step_body(step, carry):
            body(step, self.count - 1 - step if way > 0 else step)
            return carry
        lax.fori_loop(0, self.count - 1, step_body, 0)

    def at_edge(self, way):
        return self.me == (0 if way > 0 else self.count - 1)

    def edges(self, number):
        for way in (1, -1):
            @pl.when(self.at_edge(way) & (number < self.total))
            def _(way=way):
                self.each(way, lambda step, target: self.send(way, target, number, self.own(number, target)).start())

    def between(self, way, target):
        if way > 0:
            return (self.me > 0) & (self.me < target)
        return (self.me < self.count - 1) & (self.me > target)

    def staging(self, way):
        live = jnp.maximum(self.count - 1 - self.me if way > 0 else self.me, 1)
        return jnp.minimum(lax.div(self.places, live), 4), live

    def turns(self):
        return range(self.chunks + max(self.count - 3, 0))

    def turn(self, turn):
        if turn + AHEAD < self.chunks:
            for way in (1, -1):
                @pl.when(self.at_edge(way) & (turn + AHEAD < self.total))
                def _(way=way):
                    self.each(way, lambda step, target: self.send(way, target, turn, self.own(turn, target)).wait_send())
            self.edges(turn + AHEAD)
        if self.count < 3 or turn not in self.turns():
            return

        ways = ((1, 0, lambda step: self.count - 1 - step), (-1, 1, lambda step: step))

        def number_of(way, target):
            depth = self.me if way > 0 else self.count - 1 - self.me
            number = turn + 1 - depth
            return number, self.between(way, target) & (number >= 0) & (number < self.total)

        def take(step, carry):
            for way, side, target_of in ways:
                target = target_of(step)
                number, active = number_of(way, target)

                @pl.when(active)
                def _(way=way, side=side, target=target, number=number):
                    self.arrived(way, target, number)
                    self.taken(way, target, number, 2 * step + side).start()
            return carry

        def pass_on(step, carry):
            for way, side, target_of in ways:
                target = target_of(step)
                number, active = number_of(way, target)

                @pl.when(active)
                def _(way=way, side=side, target=target, number=number):
                    depth, live = self.staging(way)
                    slot = self.slots(way, lax.rem(number, depth) * live + step)
                    buffer = 2 * step + side
                    self.taken(way, target, number, buffer).wait()
                    total = self.intake(buffer)[...].astype(F32) + self.own(number, target)[...].astype(F32)

                    @pl.when(number >= depth)
                    def _():
                        self.send(way, target, number - depth, slot).wait_send()

                    slot[...] = total.astype(BF16)
                    self.send(way, target, number, slot).start()
            return carry

        lax.fori_loop(0, self.count - 1, take, 0)
        lax.fori_loop(0, self.count - 1, pass_on, 0)

    def last(self, number, total_ref):
        ways = ((1, 0, self.me > 0), (-1, 1, self.me < self.count - 1))
        for way, side, there in ways:
            @pl.when(there)
            def _(way=way, side=side):
                self.arrived(way, self.me, number)
                self.taken(way, self.me, number, side).start()
        total_ref[...] = self.own(number, self.me)[...].astype(F32)
        for way, side, there in ways:
            @pl.when(there)
            def _(way=way, side=side):
                self.taken(way, self.me, number, side).wait()
                total_ref[...] = total_ref[...] + self.intake(side)[...].astype(F32)

    def finish(self):
        for way in (1, -1):
            depth, _ = self.staging(way)
            for back in range(1, 5):
                number = self.total - back

                def sent(step, target, way=way, back=back, number=number, depth=depth):
                    active = self.between(way, target) & (back <= depth)
                    if back <= AHEAD:
                        active = active | self.at_edge(way)

                    @pl.when(active)
                    def _():
                        self.send(way, target, number, self.own(number, target)).wait_send()

                self.each(way, sent)


def main_kernel(names, *refs):
    r = types.SimpleNamespace(**dict(zip(names, refs)))
    place = Place()
    half, core = place.half, place.core
    me, planes = lax.axis_index("dp"), lax.axis_size("dp")
    seqs, length, feats = r.xa.shape
    z = Sizes(feats, r.wo.shape[1], r.wud.shape[2], length // 2)
    mine, unit = z.mine, z.unit
    share = feats // planes

    r.wu, r.wd = r.wud.at[0], r.wud.at[1]
    weights = ((r.wqkv_hbm, r.wqkv), (r.wo_hbm, r.wo), (r.wu_hbm, r.wu), (r.wd_hbm, r.wd))

    @pl.when(place.block == 0)
    def _():
        for n in range(4):
            pltpu.make_async_copy(*weights[n], r.load_sem.at[n]).start()

    @pl.when(place.block == 1)
    def _():
        for n in range(3, -1, -1):
            pltpu.make_async_copy(*weights[n], r.load_sem.at[n]).start()

    def loaded(n):
        pltpu.make_async_copy(*weights[n], r.load_sem.at[n]).wait()

    first_width, second_width = r.width[0], r.width[1]
    r.wide[...] = jnp.zeros_like(r.wide)
    r.wide[0:1, :] = jnp.full((1, 128), 1.0 - 0.5 * (first_width * second_width).astype(F32), F32)
    r.wide[1:2, :] = jnp.full((1, 128), lax.shift_right_logical(first_width, 1).astype(F32), F32)
    flag, swap = r.wide[0:1, :1], r.wide[1:2, :1]
    gain_a = r.gain_a[...].reshape(1, feats).astype(F32)
    gain_f = r.gain_f[...].reshape(1, feats).astype(F32)

    place.barrier()

    first_u, first_dg = 6 + seqs, 6 + seqs + SLOTS
    first_do = first_dg + SLOTS
    first_dqkv = first_do + seqs

    def targets(index, sender_half, rows):
        span = pl.ds(pl.multiple_of(sender_half * mine, mine), mine)
        if index < 6:
            return r.rcv_qkv.at[index // 3, index % 3, rows, :]
        if index < first_u:
            return r.o.at[index - 6, rows, span]
        if index < first_dg:
            return r.rcv_u.at[index - first_u, rows, :]
        if index < first_do:
            return r.rcv_dg.at[index - first_dg, rows, :]
        if index < first_dqkv:
            return r.rcv_do.at[index - first_do, rows, :]
        n = index - first_dqkv
        return r.dqkv.at[n // 3, n % 3, rows, span]

    link = PairLink(place, r.relay, (r.x_send, r.x_recv, r.far_send, r.far_recv, r.relay_send, r.relay_recv), targets, (6, 7, first_do, first_do + 1))
    forward_order = tuple(range(first_dg))
    ffn_order = tuple(range(first_dg, first_do))
    do_order = tuple(range(first_do, first_dqkv))
    dqkv_order = tuple(range(first_dqkv, first_dqkv + 6))
    my_rows = pl.ds(pl.multiple_of(core * z.tokens, z.tokens), z.tokens)
    their_rows = pl.ds(pl.multiple_of((1 - core) * z.tokens, z.tokens), z.tokens)
    my_feats = pl.ds(pl.multiple_of(half * feats, feats), feats)

    def share_rows(n):
        return pl.ds(pl.multiple_of(n * share, share), share)

    gathers = [
        Gather(
            place, r.g.at[3 * n:3 * n + 3], r.every_g.at[n],
            (r.g_right.at[n], r.g_left.at[n], r.g_sem.at[n], r.g_local.at[n:n + 1]),
        )
        for n in range(3)
    ]
    gather_o = Gather(place, r.o, r.every_o, (r.o_right, r.o_left, r.o_sem, r.o_local))
    exchange_d = Exchange(place, lambda n: r.dt.at[share_rows(n), :], r.every_d, (r.d_send, r.d_recv, r.d_local))
    exchange_c = Exchange(place, lambda n: r.dt.at[share_rows(n), :], r.every_c, (r.c_send, r.c_recv, r.c_local))
    gather_u = Gather(place, r.du.at[SLOTS - SHARED:SLOTS], r.every_u, (r.u_right, r.u_left, r.u_sem, r.u_local))
    exchange_b = Exchange(place, lambda n: r.dt.at[share_rows(n), 0:length], r.every_b, (r.b_send, r.b_recv, r.b_local))
    exchange_flag = Exchange(place, lambda n: r.wide, r.every_flag, (r.flag_send, r.flag_recv, r.flag_local))
    exchange_flag.start()

    def local_copy(src, dst, n):
        return pltpu.make_async_copy(src, dst, r.in_local.at[n])

    def core_half(src, dst, n):
        return remote(src, dst, r.in_send.at[n], r.in_recv.at[n], place.core_peer)

    def x_copy(i):
        return remote(r.x2.at[i], r.xa.at[i, my_rows, :], r.y_send.at[i], r.y_recv.at[i], place.across)

    def e_copy(i):
        return remote(r.x2.at[i], r.e_in.at[i, my_rows, :], r.y_send.at[i], r.y_recv.at[i], place.across)

    def start_half(src_ref, dst_ref, first):
        for i in range(seqs):
            local_copy(src_ref.at[i, :, my_feats], dst_ref.at[i, my_rows, :], first + i).start()
            core_half(src_ref.at[i, :, my_feats], dst_ref.at[i, my_rows, :], first + i).start()

    def ordered_halves(raw_ref, dst_ref, first):
        for i in range(seqs):
            local_copy(raw_ref.at[i, my_rows, :], raw_ref.at[i, my_rows, :], first + i).wait()
            core_half(raw_ref.at[i, my_rows, :], raw_ref.at[i, my_rows, :], first + i).wait()
        for i in range(seqs):
            mixed = raw_ref[i].astype(F32) * (1.0 - swap) + raw_ref[1 - i].astype(F32) * swap
            dst_ref[i] = mixed.astype(BF16)

    def pass_half(dst_ref, n, i):
        core_half(dst_ref.at[i, my_rows, :], dst_ref.at[i, my_rows, :], n).start()
        core_half(dst_ref.at[i, my_rows, :], dst_ref.at[i, my_rows, :], n).wait()

    def sq_copy(n):
        return remote(r.snd_sq.at[n], r.rcv_sq.at[n], r.sq_send.at[n], r.sq_recv.at[n], place.pair)

    def core_copy(n):
        return remote(r.snd_br.at[n], r.rcv_br.at[n], r.core_send.at[n], r.core_recv.at[n], place.core_peer)

    def core_rows(i):
        return remote(r.snd_br.at[2 + i, their_rows, :], r.rcv_half.at[i], r.core_send.at[2 + i], r.core_recv.at[2 + i], place.core_peer)

    def row_copy(n, peer):
        return remote(r.snd_row.at[n], r.rcv_row.at[n], r.row_send.at[n], r.row_recv.at[n], peer)

    def db_copy(n):
        return remote(r.snd_db.at[n], r.rcv_db.at[n], r.db_send.at[n], r.db_recv.at[n], place.core_peer)

    def da_rows(i):
        return remote(r.snd_db.at[2 + i, their_rows, :], r.rcv_half.at[i], r.db_send.at[2 + i], r.db_recv.at[2 + i], place.core_peer)

    def ready(n):
        pl.semaphore_signal(r.go_sem.at[n], inc=1, device_id=place.pair, device_id_type=MESH)

    def wait_ready(n):
        pl.semaphore_wait(r.go_sem.at[n], 1)

    out_sems = (r.out_send, r.out_recv, r.out_local)
    emit_x1 = Emitter(place, r.layer_out, r.stage.at[0], swap, out_sems, 0)
    emit_x2 = Emitter(place, r.layer_out, r.stage.at[1], swap, out_sems, 2)
    emit_e1 = Emitter(place, r.input_grad, r.stage.at[2], swap, out_sems, 4)
    emit_e0 = Emitter(place, r.input_grad, r.stage.at[3], swap, out_sems, 6)
    theirs = pl.multiple_of((1 - half) * mine, mine)
    ours = pl.multiple_of(half * mine, mine)

    def dg_part(slot):
        r.snd_dg[slot] = mm(r.e_in[slot_block(slot)[0]], slot_weight(slot, r.wd)).astype(BF16)

    def dg_source(slot):
        return lambda rows: r.snd_dg.at[slot, rows, :]

    def transposed(src_ref):
        for i in range(seqs):
            r.dt[:, i * length:(i + 1) * length] = jnp.transpose(src_ref[i].astype(F32)).astype(BF16)

    @pl.when(place.block == 0)
    def _():
        start_half(r.x0, r.xf, 0)
        ordered_halves(r.xf, r.xa, 0)

    @pl.when(place.block == 1)
    def _():
        start_half(r.c0, r.dc, 2)
        loaded(3)
        ordered_halves(r.dc, r.e_in, 2)
        for slot in range(SLOTS):
            dg_part(slot)
        transposed(r.e_in)
        exchange_d.start()
        link.forward(forward_order[:6])
        link.start_whole(first_dg, dg_source(0))
        link.forward(forward_order[6:8])
        link.start_whole(first_dg + 1, dg_source(1))
        link.forward(forward_order[8:])
        link.start_whole(first_dg + 2, dg_source(2))

    for i in range(seqs):
        @pl.when(place.block == 1)
        def _():
            x_copy(i).wait_recv()
            if i == 1:
                ready(0)
            pass_half(r.xa, i, i)

        x = r.xa[i].astype(F32)
        r.snd_sq[i] = to_row(jnp.sum(x * x, axis=-1, keepdims=True))
        sq_copy(i).start()
        r.xg[i] = (x * gain_a).astype(BF16)
        if i == 0:
            loaded(0)
        for t in range(3):
            r.snd_qkv[i, t] = mm(r.xg[i], r.wqkv[t, :, pl.ds(theirs, mine)]).astype(BF16)
            source = lambda rows, i=i, t=t: r.snd_qkv.at[i, t, rows, :]

            @pl.when(place.block == 0)
            def _():
                link.start(3 * i + t, source)

            @pl.when(place.block == 1)
            def _():
                if i == 0:
                    link.start_whole(t, source)
                else:
                    link.start_near(3 + t, source)

    @pl.when(place.block == 1)
    def _():
        wait_ready(0)
        for t in range(3):
            link.start_far(3 + t)

    for i in range(seqs):
        for t in range(3):
            r.own_qkv[i, t] = mm(r.xg[i], r.wqkv[t, :, pl.ds(ours, mine)])

    cosine, sine = r.cosine[...], r.sine[...]
    scale = HEAD_DIM ** (-0.5)
    causal = lax.broadcasted_iota(jnp.int32, (length, length), 0) >= lax.broadcasted_iota(jnp.int32, (length, length), 1)
    for i in range(seqs):
        sq_copy(i).wait_recv()
        factor = lax.rsqrt((from_row(r.snd_sq[i]) + from_row(r.rcv_sq[i])) * (1.0 / z.width) + EPSILON)
        r.ra[i] = spread(factor, 128)
        if i == 0:
            @pl.when(place.block == 0)
            def _():
                for t in range(3):
                    link.wait(t)

            @pl.when(place.block == 1)
            def _():
                for t in range(3):
                    link.wait_whole(t)
        else:
            for t in range(3):
                link.wait(3 + t)
        for j in range(z.heads):
            span = pl.ds(j * HEAD_DIM, HEAD_DIM)
            raw = [(r.own_qkv[i, t, :, span] + r.rcv_qkv[i, t, :, span].astype(F32)) * factor for t in range(3)]
            q_j = (raw[0] * cosine + turned(raw[0]) * sine).astype(BF16)
            k_j = (raw[1] * cosine + turned(raw[1]) * sine).astype(BF16)
            v_j = raw[2].astype(BF16)
            r.q[i, :, span], r.k[i, :, span], r.v[i, :, span] = q_j, k_j, v_j
            scores = jnp.where(causal, mm_nt(q_j, k_j) * scale, -1e30)
            exponent = jnp.exp(scores - jnp.max(scores, axis=-1, keepdims=True))
            probs = exponent / jnp.sum(exponent, axis=-1, keepdims=True)
            r.p[i, j] = probs
            r.o[i, :, pl.ds(pl.multiple_of(ours + j * HEAD_DIM, HEAD_DIM), HEAD_DIM)] = mm(probs.astype(BF16), v_j).astype(BF16)
        link.start(6 + i, lambda rows, i=i: r.o.at[i, rows, pl.ds(ours, mine)])

    loaded(1)
    for i in range(seqs):
        link.wait(6 + i)
        r.snd_br[i] = mm_nt(r.o[i], r.wo[...]).astype(BF16)
        core_copy(i).start()

    @pl.when(place.block == 1)
    def _():
        for slot in DG_MIDDLE:
            link.start(first_dg + slot, dg_source(slot))

    gather_o.step(1)

    def slot_start(slot):
        part = mm(r.xg[slot_block(slot)[0]], slot_weight(slot, r.wu))
        r.u[slot] = part
        r.snd_u[slot] = part.astype(BF16)
        link.start(first_u + slot, lambda rows: r.snd_u.at[slot, rows, :])

    loaded(2)
    for i, slots in enumerate((NARROW, WIDE)):
        core_copy(i).wait_recv()
        r.xf[i] = (r.xa[i].astype(F32) + (r.snd_br[i].astype(F32) + r.rcv_br[i].astype(F32))).astype(BF16)
        x = r.xf[i].astype(F32)
        r.snd_sq[2 + i] = to_row(jnp.sum(x * x, axis=-1, keepdims=True))
        sq_copy(2 + i).start()
        r.xg[i] = (x * gain_f).astype(BF16)
        for slot in slots:
            slot_start(slot)

    @pl.when(place.block == 1)
    def _():
        for slot in DG_LATE:
            link.start(first_dg + slot, dg_source(slot))

    emit_x1.prepare([r.xf[i, my_rows, :] for i in range(seqs)])
    factors = {}

    def row_factor(i):
        sq_copy(2 + i).wait_recv()
        factors[i] = lax.rsqrt((from_row(r.snd_sq[2 + i]) + from_row(r.rcv_sq[2 + i])) * (1.0 / z.width) + EPSILON)
        r.rf[i] = spread(factors[i], 128)

    def activate(slot):
        link.wait(first_u + slot)
        value = (r.u[slot] + r.rcv_u[slot].astype(F32)) * factors[slot_block(slot)[0]]
        squared = value * value
        bent = jnp.tanh(GELU_C * (value + GELU_A * (squared * value)))
        slope = 0.5 * (1.0 + bent) + 0.5 * value * (1.0 - bent * bent) * (GELU_C * (1.0 + 3.0 * GELU_A * squared))
        r.u[slot] = value
        r.rcv_u[slot] = mask_slot(slot, slope, flag).astype(BF16)
        g_k = mask_slot(slot, 0.5 * value * (1.0 + bent), flag).astype(BF16)
        r.g[G_PLACE[slot]] = g_k
        return mm_nt(g_k, slot_weight(slot, r.wd))

    def finish_rows(i):
        core_rows(i).wait_recv()
        total = r.snd_br[2 + i, my_rows, :].astype(F32) + r.rcv_half[i].astype(F32)
        r.x2[i] = (r.xf[i, my_rows, :].astype(F32) + total).astype(BF16)

        @pl.when(place.block == 0)
        def _():
            x_copy(i).start()

    @pl.when(place.block == 0)
    def _():
        loaded(3)

    row_factor(0)
    r.snd_br[2] = (activate(0) + activate(1)).astype(BF16)
    core_rows(0).start()
    gather_o.step(2)
    row_factor(1)
    total = activate(2) + activate(3)
    finish_rows(0)
    for slot in WIDE[2:]:
        total = total + activate(slot)
    r.snd_br[3] = total.astype(BF16)
    core_rows(1).start()
    r.g[1] = r.g[1] + r.g[SLOTS - 1]
    finish_rows(1)
    emit_x2.prepare([r.x2[i] for i in range(seqs)])
    for part in gathers:
        part.step(1)

    def normed_again():
        for i in range(seqs):
            r.xg[i] = (r.xf[i].astype(F32) * r.rf[i][:, :1] * gain_f).astype(BF16)

    @pl.when(place.block == 0)
    def _():
        normed_again()
        r.dt[:, :length] = jnp.transpose(r.xg[1].astype(F32)).astype(BF16)
        exchange_b.start()

    def piece(chunk, target):
        column = pl.multiple_of(lax.rem(chunk, 8) * unit, unit)
        return r.wud.at[lax.div(chunk, 8), share_rows(target), pl.ds(column, unit)]

    per = max(length // share, 1)

    def slots(way, n):
        ref = r.snd_qkv if way > 0 else r.rcv_qkv
        at = lax.div(n, per)
        return ref.at[lax.div(at, 3), lax.rem(at, 3), share_rows(lax.rem(n, per)), :]

    def intake(n):
        return r.snd_u.at[lax.div(n, per), share_rows(lax.rem(n, per)), :]

    def which(number):
        first = 8 - SHARED
        after = min(number // first, 1) if isinstance(number, int) else jnp.minimum(lax.div(number, first), 1)
        return number + SHARED * after * (1 - place.block)

    scatter = Scatter(
        place, piece, which, 14 - SHARED * (1 - place.block), {1: r.from_left, -1: r.from_right}, {1: r.sum_right, -1: r.sum_left}, {1: r.got_left, -1: r.got_right},
        slots, 6 * per, intake, r.intake_sem, 14,
    )

    @pl.when(place.block == 0)
    def _():
        gather_o.rest(3)
        link.forward(forward_order[3:first_u])
        link.forward(tuple(first_dg + slot for slot in DG_MIDDLE))
        link.forward(forward_order[first_u:])
        for part in gathers:
            part.step(2)
        link.forward(tuple(first_dg + slot for slot in DG_LATE))
        link.forward(do_order + dqkv_order)
        for part in gathers:
            part.rest(3)
        for i, slot_list in enumerate((NARROW, WIDE)):
            e_copy(i).wait_recv()
            if i == 1:
                ready(1)
            pass_half(r.e_in, 2 + i, i)
            for slot in slot_list:
                dg_part(slot)
                if i == 0:
                    link.start_whole(first_dg + slot, dg_source(slot))
                else:
                    link.start_near(first_dg + slot, dg_source(slot))
                if i == 1 and slot == WIDE[1]:
                    wait_ready(1)
                    for sent in WIDE[:2]:
                        link.start_far(first_dg + sent)
                if i == 1 and slot > WIDE[1]:
                    link.start_far(first_dg + slot)
        exchange_b.finish()
        transposed(r.e_in)
        exchange_d.start()
        link.finish(forward_order[:3])

    @pl.when(place.block == 1)
    def _():
        link.finish_whole(forward_order[:3])

    link.finish(forward_order[3:])

    def hidden_back(slot):
        @pl.when(place.block == 0)
        def _():
            (link.wait_whole if slot in NARROW else link.wait)(first_dg + slot)

        @pl.when(place.block == 1)
        def _():
            (link.wait_whole if slot in DG_STRAIGHT else link.wait)(first_dg + slot)

        grad = r.snd_dg[slot].astype(F32) + r.rcv_dg[slot].astype(F32)
        du_k = (grad * r.rcv_u[slot].astype(F32)).astype(BF16)
        r.du[slot] = du_k
        return mm_nt(du_k, slot_weight(slot, r.wu)), jnp.sum(du_k.astype(F32) * r.u[slot], axis=-1, keepdims=True)

    def flipped(value):
        return jnp.transpose(value.astype(F32)).astype(BF16)

    def up_grads(blocks):
        wide = flipped(r.xg[1])
        for block in blocks:
            part = mm(wide, r.du[2 + block])
            if block < 2:
                part = part + mm_tn(r.xg[0], r.du[block])
            r.wu[:, block * unit:(block + 1) * unit] = part.astype(BF16)
            if block < AHEAD:
                scatter.edges(block)

    def core_sum_start(i, slot_list):
        total = row = None
        for slot in slot_list:
            more, more_row = hidden_back(slot)
            total, row = (more, more_row) if total is None else (total + more, row + more_row)

            if i == 1 and slot - 2 < 8 - SHARED:
                @pl.when(place.block == 0)
                def _(slot=slot):
                    up_grads((slot - 2,))

        if i == 1:
            @pl.when(place.block == 0)
            def _():
                gather_u.step(1)

        r.snd_db[i] = total.astype(BF16)
        db_copy(i).start()
        r.snd_row[i] = to_row(row)
        row_copy(i, place.core_peer).start()

    def ffn_done(i):
        db_copy(i).wait_recv()
        row_copy(i, place.core_peer).wait_recv()
        mean = (from_row(r.snd_row[i]) + from_row(r.rcv_row[i])) * (1.0 / z.width)
        grad = r.snd_db[i].astype(F32) + r.rcv_db[i].astype(F32)
        factor = r.rf[i][:, :1]
        scaled = r.xf[i].astype(F32) * factor
        new = r.e_in[i].astype(F32) + factor * (grad * gain_f - scaled * mean)
        r.e[i] = new
        r.dc[i] = new.astype(BF16)
        core_copy(i).wait_send()
        r.snd_br[i, :, :mine] = mm(r.dc[i], r.wo[:, pl.ds(theirs, mine)]).astype(BF16)
        link.start(first_do + i, lambda rows: r.snd_br.at[i, rows, 0:mine])
        r.own_qkv[i, 0] = mm(r.dc[i], r.wo[:, pl.ds(ours, mine)])
        return jnp.sum(grad * scaled, axis=0, keepdims=True)

    core_sum_start(0, NARROW)
    gain_f_sum = ffn_done(0)
    core_sum_start(1, WIDE)
    gain_f_sum = gain_f_sum + ffn_done(1)
    r.gains[...] = jnp.zeros_like(r.gains)
    r.gains[1:2, :] = 0.5 * gain_f_sum
    emit_e1.prepare([r.dc[i, my_rows, :] for i in range(seqs)])

    @pl.when(place.block == 1)
    def _():
        exchange_d.finish()
        transposed(r.dc)
        exchange_c.start()

    rows = slice(0, share)
    inner = (me > 0) & (me < planes - 1)

    def grads_ready():
        exchange_flag.finish()
        for n in range(SLOTS):
            r.u[n, rows, :] = jnp.zeros_like(r.u[n, rows, :])
        flags_copy = pltpu.make_async_copy(r.every_flag, r.flags, r.block_sem.at[0])
        flags_copy.start()
        flags_copy.wait()

    def planes_of(part, first, last):
        def body(k, carry):
            part(jnp.where(me < planes // 2, lax.rem(me + k, planes), lax.rem(me + planes - k, planes)))
            return carry
        lax.fori_loop(lax.div(first * planes, 4), lax.div(last * planes, 4), body, 0)

    def fetched(*pairs):
        copies = [pltpu.make_async_copy(src, dst, r.block_sem.at[at]) for at, (src, dst) in enumerate(pairs)]
        for copy in copies:
            copy.start()
        for copy in copies:
            copy.wait()

    def down_part(n):
        block_g = r.snd_dg.at[0:SLOTS - 1]
        fetched(*((r.every_g.at[k, n], r.snd_dg.at[3 * k:3 * k + 3]) for k in range(3)), (r.every_d.at[n], r.block_d))
        on = r.flags[n][:1, :1]
        shared = block_g[1].astype(F32)
        upper, lower = (shared * on).astype(BF16), (shared * (1.0 - on)).astype(BF16)
        narrow, wide = r.block_d[:, :length], r.block_d[:, length:]
        for block in range(8):
            right = upper if block == 4 else block_g[2 + block if block < 4 else 1 + block]
            part = mm(wide, right)
            if block < 2:
                part = part + mm(narrow, block_g[0] if block == 0 else lower)
            r.u[block, rows, :] = r.u[block, rows, :] + part

    def out_part(n):
        fetched((r.every_o.at[n], r.xf), (r.every_c.at[n], r.block_c))
        for side in range(2):
            span = slice(side * unit, (side + 1) * unit)
            part = mm(r.block_c[:, :length], r.xf[0, :, span]) + mm(r.block_c[:, length:], r.xf[1, :, span])
            r.u[8 + side, rows, :] = r.u[8 + side, rows, :] + part

    def gather_done():
        for part in gathers:
            part.settle_all()

    def up_part(n):
        block_u, block_b = r.rcv_dg.at[0:SHARED], r.rcv_dg.at[SHARED, rows, 0:length]
        fetched((r.every_u.at[n], block_u), (r.every_b.at[n], block_b))
        for k in range(SHARED):
            r.own_qkv[k // 3, k % 3, rows, :] = r.own_qkv[k // 3, k % 3, rows, :] + mm(block_b[...], block_u[k])

    for i in range(seqs):
        link.wait(first_do + i)
        row = jnp.zeros((length, 1), F32)
        for j in range(z.heads):
            span = pl.ds(j * HEAD_DIM, HEAD_DIM)
            do_j = (r.own_qkv[i, 0, :, span] + r.rcv_do[i, :, span].astype(F32)).astype(BF16)
            q_j, k_j, v_j, probs = r.q[i, :, span], r.k[i, :, span], r.v[i, :, span], r.p[i, j]
            dp = mm_nt(do_j, v_j)
            dv = mm_tn(probs.astype(BF16), do_j)
            ds = (probs * (dp - jnp.sum(probs * dp, axis=-1, keepdims=True))).astype(BF16)
            dq = mm(ds, k_j) * scale
            dk = mm_tn(ds, q_j) * scale
            row = row + jnp.sum(dq * q_j.astype(F32) + dk * k_j.astype(F32) + dv * v_j.astype(F32), axis=-1, keepdims=True)
            at = pl.ds(pl.multiple_of(ours + j * HEAD_DIM, HEAD_DIM), HEAD_DIM)
            r.dqkv[i, 0, :, at] = (dq * cosine - turned(dq) * sine).astype(BF16)
            r.dqkv[i, 1, :, at] = (dk * cosine - turned(dk) * sine).astype(BF16)
            r.dqkv[i, 2, :, at] = dv.astype(BF16)
        r.snd_row[2 + i] = to_row(row)
        row_copy(2 + i, place.pair).start()
        for t in range(3):
            link.start(first_dqkv + 3 * i + t, lambda rows, i=i, t=t: r.dqkv.at[i, t, rows, pl.ds(ours, mine)])

    def first_grads():
        link.finish_whole(ffn_order[:len(NARROW)])
        link.finish(ffn_order[len(NARROW):])
        exchange_d.finish()
        transposed(r.dc)
        exchange_c.start()
        grads_ready()
        gather_done()

    @pl.when((place.block == 0) & inner)
    def _():
        first_grads()
        planes_of(down_part, 0, 1)

    for i in range(seqs):
        if i == 1:
            @pl.when(place.block == 0)
            def _():
                gather_u.step(2)

        part = jnp.zeros((length, feats), F32)
        for t in range(3):
            link.wait(first_dqkv + 3 * i + t)
            part = part + mm_nt(r.dqkv[i, t], r.wqkv[t])
        r.snd_db[2 + i] = part.astype(BF16)
        da_rows(i).start()
        row_copy(2 + i, place.pair).wait_recv()
        r.snd_row[4 + i] = r.snd_row[2 + i] + r.rcv_row[2 + i]
        row_copy(4 + i, place.core_peer).start()

    @pl.when(place.block == 0)
    def _():
        for i in range(seqs):
            x_copy(i).wait_send()

    gain_a_sum = jnp.zeros((1, feats), F32)
    for i in range(seqs):
        da_rows(i).wait_recv()
        row_copy(4 + i, place.core_peer).wait_recv()
        r.snd_row[6 + i] = (r.snd_row[4 + i] + r.rcv_row[4 + i]) * (1.0 / z.width)
        mean = from_row(r.snd_row[6 + i, :, my_rows])
        grad = r.snd_db[2 + i, my_rows, :].astype(F32) + r.rcv_half[i].astype(F32)
        factor = r.ra[i, my_rows, :][:, :1]
        scaled = r.xa[i, my_rows, :].astype(F32) * factor
        r.x2[i] = (r.e[i, my_rows, :] + factor * (grad * gain_a - scaled * mean)).astype(BF16)
        gain_a_sum = gain_a_sum + jnp.sum(grad * scaled, axis=0, keepdims=True)

        @pl.when(place.block == 1)
        def _():
            e_copy(i).start()

    r.gains[0:1, :] = gain_a_sum
    emit_e0.prepare([r.x2[i] for i in range(seqs)])

    def qkv_grad():
        for i in range(seqs):
            r.xg[i] = (r.xa[i].astype(F32) * r.ra[i][:, :1] * gain_a).astype(BF16)
        first, second = flipped(r.xg[0]), flipped(r.xg[1])
        for t in range(3):
            r.wd[:, t * z.cols:(t + 1) * z.cols] = (mm(first, r.dqkv[0, t]) + mm(second, r.dqkv[1, t])).astype(BF16)

    @pl.when(place.block == 1)
    def _():
        gather_o.rest(3)
        for part in gathers:
            part.step(2)
        normed_again()
        up_grads(range(8))
        qkv_grad()
        link.forward(ffn_order[len(NARROW):])
        scatter.turn(0)
        link.forward(do_order)
        link.forward(dqkv_order)
        scatter.turn(1)
        gathers[0].rest(3)
        scatter.turn(2)
        scatter.turn(3)
        gathers[1].rest(3)

    @pl.when(place.block == 0)
    def _():
        qkv_grad()
        for number in range(8 - SHARED, AHEAD):
            scatter.edges(number)

        @pl.when(jnp.logical_not(inner))
        def _():
            first_grads()
            planes_of(down_part, 0, 4)

        @pl.when(inner)
        def _():
            planes_of(down_part, 1, 4)

        gather_o.settle_all()
        gather_u.own().wait()
        gather_u.rest(3)
        for k in range(SHARED):
            r.own_qkv[k // 3, k % 3, rows, :] = jnp.zeros_like(r.own_qkv[k // 3, k % 3, rows, :])
        for turn in range(4):
            scatter.turn(turn)

            @pl.when(inner)
            def _(turn=turn):
                planes_of(up_part, turn, turn + 1)

    @pl.when(place.block == 1)
    def _():
        link.finish_whole(tuple(first_dg + slot for slot in DG_STRAIGHT))
        link.finish(tuple(first_dg + slot for slot in DG_MIDDLE + DG_LATE))
        grads_ready()

    emit_x1.start(0)
    emit_x2.start(1)
    emit_e1.start(1)
    emit_e0.start(0)
    gains_copy = remote(r.gains, r.core_gains, r.pair_send.at[0], r.pair_recv.at[0], place.core_peer)
    gains_copy.start()
    scatter.turn(4)
    gains_copy.wait()
    r.every_gain[me] = r.gains[...] + r.core_gains[...]
    exchange_gain = Exchange(place, lambda n: r.every_gain.at[me], r.every_gain, (r.gain_send, r.gain_recv, None))
    for n in range(1, planes):
        exchange_gain.copy(n).start()

    def grad_copy(n):
        dst = r.down_grad.at[:, n * unit:(n + 1) * unit] if n < 8 else r.out_grad.at[:, (n - 8) * unit:(n - 7) * unit]
        return pltpu.make_async_copy(r.u.at[n, rows, :], dst, r.grad_sem.at[n])

    def shared_copy(k):
        dst = r.up_grad.at[:, (8 - SHARED + k) * unit:(9 - SHARED + k) * unit]
        return pltpu.make_async_copy(r.own_qkv.at[k // 3, k % 3, rows, :], dst, r.shared_sem.at[k])

    def total_slot(number):
        at = lax.rem(number, 4)
        column = pl.multiple_of(lax.rem(at, 2) * unit, unit)
        return r.e.at[lax.div(at, 2), rows, pl.ds(column, unit)]

    def total_copy(number, action):
        chunk = which(number)
        src, sem = total_slot(number), r.total_sem.at[lax.rem(number, 4)]

        @pl.when(chunk < 8)
        def _():
            dst = r.up_grad.at[:, pl.ds(pl.multiple_of(chunk * unit, unit), unit)]
            action(pltpu.make_async_copy(src, dst, sem))

        @pl.when(chunk >= 8)
        def _():
            column = pl.multiple_of(lax.rem(chunk, 2) * unit, unit)
            dst = r.qkv_grad.at[lax.div(chunk - 8, 2), :, pl.ds(column, unit)]
            action(pltpu.make_async_copy(src, dst, sem))

    def final(number, carry):
        @pl.when(number >= 4)
        def _():
            total_copy(number - 4, lambda copy: copy.wait())

        scatter.last(number, total_slot(number))
        total_copy(number, lambda copy: copy.start())
        return carry

    finals = (
        {5: 3, **{turn: turn - 1 for turn in range(6, 16 - SHARED)}},
        {5: 1, 6: 2, 7: 3, 8: 4, 9: 5, 10: 6, 11: 7, 12: 9, 13: 11, 14: 13, 15: 14},
        {11: 8, 12: 10, 13: 11, 14: 13, 15: 14},
    )

    def finals_by(turn):
        first, inside, outside = (max([count for at, count in table.items() if at <= turn], default=0) for table in finals)
        return jnp.where(place.block == 0, first, jnp.where(inner, inside, outside))

    def once(block, where, body):
        pl.when((place.block == block) & (inner if where else jnp.logical_not(inner)))(body)

    def all_planes(*parts):
        for part in parts:
            planes_of(part, 0, 4)

    def edge_parts():
        gather_u.settle(1, gather_u.last - 1)
        planes_of(up_part, 0, 3)
        exchange_c.finish()
        planes_of(out_part, 0, 4)
        gather_u.settle(gather_u.last, gather_u.last)
        planes_of(up_part, 3, 4)

    def late_edge_parts():
        gather_done()
        gather_o.settle_all()
        exchange_c.finish()
        all_planes(down_part, out_part)

    def inner_start():
        gather_done()
        gather_o.settle_all()
        exchange_c.finish()

    def out_start():
        exchange_c.finish()
        planes_of(out_part, 0, 2)

    for turn in range(5, max(16, len(scatter.turns()))):
        scatter.turn(turn)
        if turn == 5:
            once(0, False, edge_parts)
        if turn == 12:
            once(1, False, late_edge_parts)
        lax.fori_loop(finals_by(turn - 1), finals_by(turn), final, 0)
        if turn == 5:
            pl.when(place.block == 1)(lambda: gathers[2].rest(3))
            once(0, True, out_start)
        if turn == 6:
            once(0, True, lambda: planes_of(out_part, 2, 4))
        if turn == 7:
            once(1, True, inner_start)
        if 7 <= turn < 11:
            once(1, True, lambda turn=turn: planes_of(down_part, turn - 7, turn - 6))
        if turn == 7:
            @pl.when(place.block == 0)
            def _():
                for n in range(SLOTS):
                    grad_copy(n).start()
                for k in range(SHARED):
                    shared_copy(k).start()
        if turn == 11:
            once(1, True, lambda: planes_of(out_part, 0, 4))
        if turn == 12:
            @pl.when(place.block == 1)
            def _():
                for n in range(SLOTS):
                    grad_copy(n).start()
    for n in range(1, planes):
        source = lax.rem(me + planes - n, planes)
        slot = r.every_gain.at[source]
        remote(slot, slot, r.gain_send.at[n], r.gain_recv.at[n], place.pair).wait_recv()
        exchange_gain.copy(n).wait_send()
    gain_total = r.every_gain[0]
    for n in range(1, planes):
        gain_total = gain_total + r.every_gain[n]
    own_first = (place.at[1] * 2 + core) * (feats // (2 * planes))
    r.gain_grads[...] = pltpu.roll(gain_total, lax.rem(feats - own_first, feats), 1)

    scatter.finish()
    for back in range(1, 5):
        total_copy(scatter.total - back, lambda copy: copy.wait())

    @pl.when(place.block == 0)
    def _():
        for k in range(SHARED):
            shared_copy(k).wait()

    for n in range(SLOTS):
        grad_copy(n).wait()
    for n in range(4):
        sq_copy(n).wait_send()
    for i in range(seqs):
        core_rows(i).wait_send()
        row_copy(i, place.core_peer).wait_send()
        row_copy(2 + i, place.pair).wait_send()
        row_copy(4 + i, place.core_peer).wait_send()
        db_copy(i).wait_send()
        da_rows(i).wait_send()
    link.finish(do_order + dqkv_order)

    @pl.when(place.block == 0)
    def _():
        link.finish_forward(forward_order[3:] + tuple(first_dg + slot for slot in DG_MIDDLE + DG_LATE) + do_order + dqkv_order)

    @pl.when(place.block == 1)
    def _():
        link.finish_forward(forward_order + ffn_order[len(NARROW):] + do_order + dqkv_order)
        for i in range(seqs):
            e_copy(i).wait_send()

    for part in (*gathers, gather_o):
        part.finish()
    pl.when(place.block == 0)(gather_u.finish)
    emit_x1.finish(0)
    emit_x2.finish(1)
    emit_e1.finish(1)
    emit_e0.finish(0)


def shape(dims, kind):
    return jax.ShapeDtypeStruct(dims, kind)


ANY = pl.BlockSpec(memory_space=pl.ANY)
IN_VMEM = pl.BlockSpec(memory_space=pltpu.VMEM)


def vmem(dims, kind):
    return pltpu.VMEM(tuple(dims), kind)


def run_main(width_index, x0, c0, gain_a, gain_f, wqkv, wo, wu, wd):
    seqs, tokens, width = x0.shape
    planes = lax.axis_size("dp")
    z = Sizes(wo.shape[0], wo.shape[1], wu.shape[1], tokens)
    share, chunks = z.feats // planes, 14
    cosine, sine = rotary(z.length, HEAD_DIM)
    args = {
        "width": width_index, "x0": x0, "c0": c0, "gain_a": gain_a, "gain_f": gain_f, "cosine": cosine, "sine": sine,
        "wqkv_hbm": wqkv, "wo_hbm": wo, "wu_hbm": wu, "wd_hbm": wd,
    }
    places = {"width": pl.BlockSpec(memory_space=pltpu.SMEM)}
    places.update({name: IN_VMEM for name in ("gain_a", "gain_f", "cosine", "sine", "gain_grads")})
    row = (8, z.feats)
    outs = {
        "layer_out": shape((seqs, tokens, width), BF16), "input_grad": shape((seqs, tokens, width), BF16),
        "qkv_grad": shape((3, share, z.cols), F32), "out_grad": shape((share, z.cols), F32),
        "up_grad": shape((share, 8 * z.unit), F32), "down_grad": shape((share, 8 * z.unit), F32), "gain_grads": shape(row, F32),
        "every_g": shape((3, planes, 3, z.length, z.unit), BF16), "every_o": shape((planes, seqs, z.length, z.cols), BF16),
        "every_d": shape((planes, share, seqs * z.length), BF16), "every_c": shape((planes, share, seqs * z.length), BF16),
        "every_u": shape((planes, SHARED, z.length, z.unit), BF16), "every_b": shape((planes, share, z.length), BF16),
        "every_flag": shape((planes, 8, 128), F32),
        "from_left": shape((planes, chunks, share, z.unit), BF16), "from_right": shape((planes, chunks, share, z.unit), BF16),
    }
    state, half_state, heads_state = (seqs, z.length, z.feats), (seqs, tokens, z.feats), (seqs, z.length, z.mine)
    slots, qkv, messages = (SLOTS, z.length, z.unit), (seqs, 3, z.length, z.mine), 12 + 2 * seqs + 2 * SLOTS
    small, factor, pair = (8, 8, z.length), (seqs, z.length, 128), (4, z.length, z.feats)
    scratch = {"wqkv": vmem(wqkv.shape, BF16), "wo": vmem(wo.shape, BF16), "wud": vmem((2, *wu.shape), BF16)}
    for dims, kind, group in (
        (state, BF16, "xa xf xg e_in dc"), (state, F32, "e"), (half_state, BF16, "x2 rcv_half"),
        (heads_state, BF16, "q k v rcv_do"),
        ((seqs, z.heads, z.length, z.length), F32, "p"), ((seqs, z.length, z.cols), BF16, "o"), (factor, F32, "ra rf"),
        (slots, F32, "u"), (slots, BF16, "g snd_u rcv_u du snd_dg rcv_dg"), (qkv, F32, "own_qkv"), (qkv, BF16, "snd_qkv rcv_qkv"),
        ((4, 8, z.length), F32, "snd_sq rcv_sq"), (small, F32, "snd_row rcv_row"), (pair, BF16, "snd_br snd_db"),
        ((2, z.length, z.feats), BF16, "rcv_br rcv_db"), ((z.feats, seqs * z.length), BF16, "dt"), ((4, *half_state), BF16, "stage"),
        ((seqs, 3, z.length, z.cols), BF16, "dqkv"), ((messages, z.length - DIRECT_ROWS, z.mine), BF16, "relay"),
        ((8, 128), F32, "wide"), ((planes, 8, 128), F32, "flags"), ((share, seqs * z.length), BF16, "block_d block_c"),
        (row, F32, "gains core_gains"), ((planes, *row), F32, "every_gain"),
    ):
        scratch.update({name: vmem(dims, kind) for name in group.split()})
    for count, group in (
        (4, "load_sem sq_send sq_recv core_send core_recv db_send db_recv in_send in_recv in_local block_sem"),
        (messages, "x_send x_recv far_send far_recv relay_send relay_recv"), (6, "row_send row_recv total_sem"),
        (2, "y_send y_recv"), (8, "out_send out_recv out_local"), (1, "o_local d_local c_local flag_local pair_send pair_recv"),
        (planes, "o_right o_left o_sem d_send d_recv c_send c_recv flag_send flag_recv gain_send gain_recv"),
        (2 * planes, "intake_sem"), (planes * chunks, "got_left got_right"), (4 * planes, "sum_right sum_left"), (SHARED, "shared_sem"),
        (planes, "u_right u_left u_sem b_send b_recv"), (1, "u_local b_local"), (SLOTS, "grad_sem"),
    ):
        scratch.update({name: pltpu.SemaphoreType.DMA((count,)) for name in group.split()})
    scratch["g_local"] = pltpu.SemaphoreType.DMA((3,))
    scratch.update({name: pltpu.SemaphoreType.DMA((3, planes)) for name in ("g_right", "g_left", "g_sem")})
    scratch["go_sem"] = pltpu.SemaphoreType.REGULAR((2,))
    results = pl.pallas_call(
        functools.partial(main_kernel, (*args, *outs, *scratch)),
        out_shape=tuple(outs.values()),
        in_specs=[places.get(name, ANY) for name in args],
        out_specs=tuple(places.get(name, ANY) for name in outs),
        scratch_shapes=list(scratch.values()),
        compiler_params=pltpu.CompilerParams(collective_id=1, has_side_effects=True, vmem_limit_bytes=VMEM_LIMIT),
        name="main",
    )(*args.values())
    return dict(zip(outs, results))


OUTPUTS = ("layer_out", "input_grad", "qkv_grad", "out_grad", "up_grad", "down_grad")
PARTS = 2


def deliver_kernel(*refs):
    count = len(OUTPUTS)
    gains, sources, (attn_out, ffn_out), targets = refs[0], refs[1:1 + count], refs[1 + count:3 + count], refs[3 + count:3 + 2 * count]
    held, load_sem, save_sem = refs[3 + 2 * count:-2], refs[-2], refs[-1]
    loads, saves = [], []
    for n, (src, mid, dst) in enumerate(zip(sources, held, targets)):
        rows = src.shape[-2] // PARTS
        lead = (slice(None),) * (len(src.shape) - 2)
        for part in range(PARTS):
            at = (*lead, slice(part * rows, (part + 1) * rows))
            loads.append(pltpu.make_async_copy(src.at[at], mid.at[at], load_sem.at[n * PARTS + part]))
            saves.append(pltpu.make_async_copy(mid.at[at], dst.at[at], save_sem.at[n * PARTS + part]))
    for copy in loads:
        copy.start()
    size = attn_out.shape[1]
    attn_out[...] = gains[0:1, :size]
    ffn_out[...] = gains[1:2, :size]
    for load, copy in zip(loads, saves):
        load.wait()
        copy.start()
    for copy in saves:
        copy.wait()


def local(inputs, cotangent, width_index, qkv_weight, out_weight, attn_gain, ffn_gain, up_weight, down_weight):
    found = run_main(width_index, inputs, cotangent, attn_gain, ffn_gain, qkv_weight, out_weight, up_weight, down_weight)
    sources = [found[name] for name in OUTPUTS]
    size = attn_gain.shape[0] // (2 * lax.axis_size("dp"))
    gain = jax.ShapeDtypeStruct((1, size), F32)
    attn_grad, ffn_grad, *results = pl.pallas_call(
        deliver_kernel,
        out_shape=(gain, gain, *(jax.ShapeDtypeStruct(source.shape, source.dtype) for source in sources)),
        in_specs=[IN_VMEM] + [ANY] * len(sources),
        out_specs=(IN_VMEM, IN_VMEM, *[ANY] * len(sources)),
        scratch_shapes=[vmem(source.shape, source.dtype) for source in sources] + [pltpu.SemaphoreType.DMA((len(sources) * PARTS,))] * 2,
        compiler_params=pltpu.CompilerParams(vmem_limit_bytes=VMEM_LIMIT),
        name="deliver",
    )(found["gain_grads"], *sources)
    layer_out, input_grad, qkv_grad, out_grad, up_grad, down_grad = results
    return (
        layer_out[None], input_grad[None], qkv_grad, out_grad, attn_grad.reshape(size), ffn_grad.reshape(size), up_grad, down_grad,
    )


def solution(mesh):
    in_specs = (
        P("dp", "mp", None),
        P("dp", "mp", None),
        P("dp"),
        P(None, "section", "mp"),
        P("section", "mp"),
        P("section"),
        P("section"),
        P("section", "mp"),
        P("section", "mp"),
    )
    out_specs = (
        P("section", "dp", "mp", None),
        P("section", "dp", "mp", None),
        P(None, ("section", "dp"), "mp"),
        P(("section", "dp"), "mp"),
        P(("section", "dp", "mp")),
        P(("section", "dp", "mp")),
        P(("section", "dp"), "mp"),
        P(("section", "dp"), "mp"),
    )
    return jax.shard_map(local, mesh=mesh, in_specs=in_specs, out_specs=out_specs, check_vma=False)
```

```python
import functools
import types

import jax
import jax.numpy as jnp
import numpy as np
from jax import lax
from jax.sharding import PartitionSpec as P
from jax.experimental import pallas as pl
from jax.experimental.pallas import tpu as pltpu

HEAD_DIM = 128
EPSILON = 1e-05
GELU_C = 0.7978845608028654
GELU_A = 0.044715
MESH = pl.DeviceIdType.MESH
SLOTS = 10
AHEAD = 3
SHARED = 3
DIRECT_ROWS = 144
URGENT_ROWS = 192
F32 = jnp.float32
BF16 = jnp.bfloat16
VMEM_LIMIT = 63 * 2**20


def mm(a, b):
    return lax.dot_general(a, b, (((1,), (0,)), ((), ())), preferred_element_type=F32)


def mm_nt(a, b):
    return lax.dot_general(a, b, (((1,), (1,)), ((), ())), preferred_element_type=F32)


def mm_tn(a, b):
    return lax.dot_general(a, b, (((0,), (0,)), ((), ())), preferred_element_type=F32)


def to_row(column):
    rows = column.shape[0]
    return jnp.transpose(jnp.broadcast_to(column, (rows, 128)))[:8]


def from_row(row):
    return jnp.transpose(row)[:, :1]


def rotary(length, head_size):
    half_dim = head_size // 2
    frequency = np.float32(10000.0) ** (np.float32(-2.0 / head_size) * np.arange(half_dim, dtype=np.float32))
    angles = np.arange(length, dtype=np.float32)[:, None] * frequency[None, :].astype(np.float32)
    cosine, sine = np.cos(angles).astype(np.float32), np.sin(angles).astype(np.float32)
    return jnp.asarray(np.concatenate([cosine, cosine], axis=1)), jnp.asarray(np.concatenate([-sine, sine], axis=1))


def turned(values):
    return pltpu.roll(values, HEAD_DIM // 2, 1)


def remote(src, dst, send_sem, recv_sem, device):
    return pltpu.make_async_remote_copy(
        src_ref=src, dst_ref=dst, send_sem=send_sem, recv_sem=recv_sem,
        device_id=device, device_id_type=MESH,
    )


class Place:
    def __init__(self):
        section, dp, mp = (lax.axis_index(name) for name in ("section", "dp", "mp"))
        self.block, self.half, self.core = section // 2, section % 2, mp
        other_half = 1 - self.half
        other_block = 1 - self.block
        self.at = (section, dp, mp)
        self.core_peer = (section, dp, 1 - mp)
        self.pair = (self.block * 2 + other_half, dp, mp)
        self.across = (other_block * 2 + self.half, dp, mp)
        self.corner = (other_block * 2 + other_half, dp, mp)

    def plane(self, n):
        section, dp, mp = self.at
        return (section, lax.rem(dp + n, lax.axis_size("dp")), mp)

    def barrier(self):
        sem = pltpu.get_barrier_semaphore()
        peers = [self.core_peer, self.pair, self.across, self.corner]
        peers += [self.plane(n) for n in range(1, lax.axis_size("dp"))]
        for peer in peers:
            pl.semaphore_signal(sem, inc=1, device_id=peer, device_id_type=MESH)
        pl.semaphore_wait(sem, len(peers))


class Exchange:
    def __init__(self, place, piece, slots, sems):
        self.place, self.piece, self.slots = place, piece, slots
        self.send, self.recv, self.local = sems
        self.me, self.count = lax.axis_index("dp"), lax.axis_size("dp")

    def copy(self, n):
        target = lax.rem(self.me + n, self.count)
        return remote(self.piece(target), self.slots.at[self.me], self.send.at[n], self.recv.at[n], self.place.plane(n))

    def own(self):
        return pltpu.make_async_copy(self.piece(self.me), self.slots.at[self.me], self.local.at[0])

    def start(self):
        self.own().start()
        for n in range(1, self.count):
            self.copy(n).start()

    def finish(self):
        self.own().wait()
        for n in range(1, self.count):
            source = lax.rem(self.me + self.count - n, self.count)
            held = self.slots.at[source]
            remote(held, held, self.send.at[n], self.recv.at[n], self.place.plane(n)).wait_recv()
            self.copy(n).wait_send()


class PairLink:
    def __init__(self, place, relay, sems, targets, urgent):
        self.place, self.relay, self.targets = place, relay, targets
        self.send, self.recv, self.far_send, self.far_recv, self.relay_send, self.relay_recv = sems
        self.rows = DIRECT_ROWS + relay.shape[1]
        self.urgent = urgent
        self.sources = {}

    def direct(self, index):
        return slice(0, URGENT_ROWS if index in self.urgent else DIRECT_ROWS)

    def detour(self, index):
        return slice(URGENT_ROWS if index in self.urgent else DIRECT_ROWS, self.rows)

    def held(self, index):
        rows = self.detour(index)
        return self.relay.at[index, 0:rows.stop - rows.start]

    def near(self, index):
        rows = self.direct(index)
        src, dst = self.sources[index](rows), self.targets(index, self.place.half, rows)
        return remote(src, dst, self.send.at[index], self.recv.at[index], self.place.pair)

    def far(self, index):
        src = self.sources[index](self.detour(index))
        return remote(src, self.held(index), self.far_send.at[index], self.relay_recv.at[index], self.place.across)

    def whole(self, index):
        rows, src = slice(0, self.rows), self.sources[index]
        dst = self.targets(index, self.place.half, rows)
        return remote(src(rows), dst, self.send.at[index], self.recv.at[index], self.place.pair)

    def start(self, index, src):
        self.sources[index] = src
        self.near(index).start()
        self.far(index).start()

    def start_near(self, index, src):
        self.sources[index] = src
        self.near(index).start()

    def start_far(self, index):
        self.far(index).start()

    def start_whole(self, index, src):
        self.sources[index] = src
        self.whole(index).start()

    def wait(self, index):
        other = 1 - self.place.half
        for rows, sem in ((self.direct(index), self.recv), (self.detour(index), self.far_recv)):
            dst = self.targets(index, other, rows)
            remote(dst, dst, self.send.at[index], sem.at[index], self.place.pair).wait_recv()

    def wait_whole(self, index):
        dst = self.targets(index, 1 - self.place.half, slice(0, self.rows))
        remote(dst, dst, self.send.at[index], self.recv.at[index], self.place.pair).wait_recv()

    def finish(self, indices):
        for index in indices:
            self.near(index).wait_send()
            self.far(index).wait_send()

    def finish_whole(self, indices):
        for index in indices:
            self.whole(index).wait_send()

    def passed(self, index):
        dst = self.targets(index, self.place.half, self.detour(index))
        return remote(self.held(index), dst, self.relay_send.at[index], self.far_recv.at[index], self.place.corner)

    def forward(self, indices):
        for index in indices:
            held = self.held(index)
            remote(held, held, self.relay_send.at[index], self.relay_recv.at[index], self.place.across).wait_recv()
            self.passed(index).start()

    def finish_forward(self, indices):
        for index in indices:
            self.passed(index).wait_send()


def spread(value, width):
    return jnp.broadcast_to(value, (value.shape[0], width))


def slot_block(slot):
    return (0, slot) if slot < 2 else (1, slot - 2)


def slot_weight(slot, weight):
    unit = weight.shape[1] // 8
    at = slot_block(slot)[1] * unit
    return weight[:, at:at + unit]


def mask_slot(slot, value, flag):
    if slot == 1:
        return value * (1.0 - flag)
    return value if slot < 6 else value * flag


NARROW, WIDE = (0, 1), tuple(range(2, SLOTS))
G_PLACE = (0, 1, 2, 3, 4, 5, 9, 6, 7, 8)
DG_STRAIGHT, DG_MIDDLE, DG_LATE = (0, 1, 2), (3, 4), (5, 6, 7, 8, 9)


class Sizes:
    def __init__(self, feats, cols, hidden, tokens):
        self.feats, self.cols, self.unit, self.tokens = feats, cols, hidden // 8, tokens
        self.mine, self.length, self.width = cols // 2, 2 * tokens, 2 * feats
        self.heads = self.mine // HEAD_DIM


class Emitter:
    def __init__(self, place, out, stage, swap, sems, first=0):
        self.place, self.out, self.stage, self.swap, self.sems, self.first = place, out, stage, swap, sems, first

    def span(self):
        feats = self.stage.shape[-1]
        return pl.ds(pl.multiple_of(self.place.half * feats, feats), feats)

    def far(self, i):
        at = self.first + i
        return remote(self.stage.at[i], self.out.at[i, :, self.span()], self.sems[0].at[at], self.sems[1].at[at], self.place.pair)

    def near(self, i):
        return pltpu.make_async_copy(self.stage.at[i], self.out.at[i, :, self.span()], self.sems[2].at[self.first + i])

    def prepare(self, values):
        narrow, wide = (value.astype(F32) for value in values)
        self.stage[0] = (narrow * (1.0 - self.swap) + wide * self.swap).astype(BF16)
        self.stage[1] = (wide * (1.0 - self.swap) + narrow * self.swap).astype(BF16)

    def start(self, owner):
        @pl.when(self.place.half == owner)
        def _():
            for i in range(2):
                self.near(i).start()

        @pl.when(self.place.half != owner)
        def _():
            for i in range(2):
                self.far(i).start()

    def finish(self, owner):
        @pl.when(self.place.half == owner)
        def _():
            for i in range(2):
                self.near(i).wait()
                self.far(i).wait_recv()

        @pl.when(self.place.half != owner)
        def _():
            for i in range(2):
                self.far(i).wait_send()


class Gather:
    def __init__(self, place, mine, every, sems):
        self.me, self.count = lax.axis_index("dp"), lax.axis_size("dp")
        self.place, self.mine, self.every = place, mine, every
        self.right, self.left, self.recv, self.local = sems
        self.last = self.count - 1

    def send(self, block, way, number):
        section, dp, mp = self.place.at
        sems = self.right if way > 0 else self.left
        src = self.mine if number == 1 else self.every.at[block]
        return remote(src, self.every.at[block], sems.at[block], self.recv.at[block], (section, dp + way, mp))

    def arrive(self, block):
        held = self.every.at[block]
        remote(held, held, self.right.at[block], self.recv.at[block], self.place.pair).wait_recv()

    def moves(self, number):
        me, last = self.me, self.count - 1
        right, left = me - number + 1, me + number - 1
        return ((1, right, (right >= 0) & (me < last)), (-1, left, (left <= last) & (me > 0)))

    def own(self):
        return pltpu.make_async_copy(self.mine, self.every.at[self.me], self.local.at[0])

    def step(self, number):
        if number == 1:
            self.own().start()
        if number > self.last:
            return
        for way, block, active in self.moves(number):
            @pl.when(active)
            def _(way=way, block=block):
                if number > 1:
                    self.arrive(block)
                self.send(block, way, number).start()

    def rest(self, number):
        for more in range(number, self.last + 1):
            self.step(more)

    def settle(self, first, last):
        for number in range(first, min(last, self.last) + 1):
            left, right = self.me - number, self.me + number
            done = number == self.last

            @pl.when((left >= 0) if done else (left >= 0) & (self.me == self.count - 1))
            def _(block=left):
                self.arrive(block)

            @pl.when((right < self.count) if done else (right < self.count) & (self.me == 0))
            def _(block=right):
                self.arrive(block)

    def settle_all(self):
        self.own().wait()
        self.settle(1, self.last)

    def finish(self):
        for number in range(1, self.last + 1):
            for way, block, active in self.moves(number):
                @pl.when(active)
                def _(way=way, block=block):
                    self.send(block, way, number).wait_send()


class Scatter:
    def __init__(self, place, piece, which, total, landing, sends, arrivals, slots, places, intake, in_sem, chunks):
        self.places = places
        self.place, self.piece, self.which, self.total = place, piece, which, total
        self.landing, self.sends, self.arrivals = landing, sends, arrivals
        self.slots, self.intake, self.in_sem, self.chunks = slots, intake, in_sem, chunks
        self.me, self.count = lax.axis_index("dp"), lax.axis_size("dp")

    def send(self, way, target, number, src):
        section, dp, mp = self.place.at
        dst = self.landing[way].at[target, number]
        send_sem = self.sends[way].at[target * 4 + lax.rem(number, 4)]
        return remote(src, dst, send_sem, self.arrivals[way].at[target * self.chunks + number], (section, dp + way, mp))

    def own(self, number, target):
        return self.piece(self.which(number), target)

    def arrived(self, way, target, number):
        held = self.landing[way].at[target, number]
        got = self.arrivals[way].at[target * self.chunks + number]
        remote(held, held, self.sends[way].at[0], got, self.place.pair).wait_recv()

    def taken(self, way, target, number, buffer):
        return pltpu.make_async_copy(self.landing[way].at[target, number], self.intake(buffer), self.in_sem.at[buffer])

    def each(self, way, body):
        def step_body(step, carry):
            body(step, self.count - 1 - step if way > 0 else step)
            return carry
        lax.fori_loop(0, self.count - 1, step_body, 0)

    def at_edge(self, way):
        return self.me == (0 if way > 0 else self.count - 1)

    def edges(self, number):
        for way in (1, -1):
            @pl.when(self.at_edge(way) & (number < self.total))
            def _(way=way):
                self.each(way, lambda step, target: self.send(way, target, number, self.own(number, target)).start())

    def between(self, way, target):
        if way > 0:
            return (self.me > 0) & (self.me < target)
        return (self.me < self.count - 1) & (self.me > target)

    def staging(self, way):
        live = jnp.maximum(self.count - 1 - self.me if way > 0 else self.me, 1)
        return jnp.minimum(lax.div(self.places, live), 4), live

    def turns(self):
        return range(self.chunks + max(self.count - 3, 0))

    def turn(self, turn):
        if turn + AHEAD < self.chunks:
            for way in (1, -1):
                @pl.when(self.at_edge(way) & (turn + AHEAD < self.total))
                def _(way=way):
                    self.each(way, lambda step, target: self.send(way, target, turn, self.own(turn, target)).wait_send())
            self.edges(turn + AHEAD)
        if self.count < 3 or turn not in self.turns():
            return

        ways = ((1, 0, lambda step: self.count - 1 - step), (-1, 1, lambda step: step))

        def number_of(way, target):
            depth = self.me if way > 0 else self.count - 1 - self.me
            number = turn + 1 - depth
            return number, self.between(way, target) & (number >= 0) & (number < self.total)

        def take(step, carry):
            for way, side, target_of in ways:
                target = target_of(step)
                number, active = number_of(way, target)

                @pl.when(active)
                def _(way=way, side=side, target=target, number=number):
                    self.arrived(way, target, number)
                    self.taken(way, target, number, 2 * step + side).start()
            return carry

        def pass_on(step, carry):
            for way, side, target_of in ways:
                target = target_of(step)
                number, active = number_of(way, target)

                @pl.when(active)
                def _(way=way, side=side, target=target, number=number):
                    depth, live = self.staging(way)
                    slot = self.slots(way, lax.rem(number, depth) * live + step)
                    buffer = 2 * step + side
                    self.taken(way, target, number, buffer).wait()
                    total = self.intake(buffer)[...].astype(F32) + self.own(number, target)[...].astype(F32)

                    @pl.when(number >= depth)
                    def _():
                        self.send(way, target, number - depth, slot).wait_send()

                    slot[...] = total.astype(BF16)
                    self.send(way, target, number, slot).start()
            return carry

        lax.fori_loop(0, self.count - 1, take, 0)
        lax.fori_loop(0, self.count - 1, pass_on, 0)

    def last(self, number, total_ref):
        ways = ((1, 0, self.me > 0), (-1, 1, self.me < self.count - 1))
        for way, side, there in ways:
            @pl.when(there)
            def _(way=way, side=side):
                self.arrived(way, self.me, number)
                self.taken(way, self.me, number, side).start()
        total_ref[...] = self.own(number, self.me)[...].astype(F32)
        for way, side, there in ways:
            @pl.when(there)
            def _(way=way, side=side):
                self.taken(way, self.me, number, side).wait()
                total_ref[...] = total_ref[...] + self.intake(side)[...].astype(F32)

    def finish(self):
        for way in (1, -1):
            depth, _ = self.staging(way)
            for back in range(1, 5):
                number = self.total - back

                def sent(step, target, way=way, back=back, number=number, depth=depth):
                    active = self.between(way, target) & (back <= depth)
                    if back <= AHEAD:
                        active = active | self.at_edge(way)

                    @pl.when(active)
                    def _():
                        self.send(way, target, number, self.own(number, target)).wait_send()

                self.each(way, sent)


def main_kernel(names, *refs):
    r = types.SimpleNamespace(**dict(zip(names, refs)))
    place = Place()
    half, core = place.half, place.core
    me, planes = lax.axis_index("dp"), lax.axis_size("dp")
    seqs, length, feats = r.xa.shape
    z = Sizes(feats, r.wo.shape[1], r.wud.shape[2], length // 2)
    mine, unit = z.mine, z.unit
    share = feats // planes

    r.wu, r.wd = r.wud.at[0], r.wud.at[1]
    weights = ((r.wqkv_hbm, r.wqkv), (r.wo_hbm, r.wo), (r.wu_hbm, r.wu), (r.wd_hbm, r.wd))

    @pl.when(place.block == 0)
    def _():
        for n in range(4):
            pltpu.make_async_copy(*weights[n], r.load_sem.at[n]).start()

    @pl.when(place.block == 1)
    def _():
        for n in range(3, -1, -1):
            pltpu.make_async_copy(*weights[n], r.load_sem.at[n]).start()

    def loaded(n):
        pltpu.make_async_copy(*weights[n], r.load_sem.at[n]).wait()

    first_width, second_width = r.width[0], r.width[1]
    r.wide[...] = jnp.zeros_like(r.wide)
    r.wide[0:1, :] = jnp.full((1, 128), 1.0 - 0.5 * (first_width * second_width).astype(F32), F32)
    r.wide[1:2, :] = jnp.full((1, 128), lax.shift_right_logical(first_width, 1).astype(F32), F32)
    flag, swap = r.wide[0:1, :1], r.wide[1:2, :1]
    gain_a = r.gain_a[...].reshape(1, feats).astype(F32)
    gain_f = r.gain_f[...].reshape(1, feats).astype(F32)

    place.barrier()

    first_u, first_dg = 6 + seqs, 6 + seqs + SLOTS
    first_do = first_dg + SLOTS
    first_dqkv = first_do + seqs

    def targets(index, sender_half, rows):
        span = pl.ds(pl.multiple_of(sender_half * mine, mine), mine)
        if index < 6:
            return r.rcv_qkv.at[index // 3, index % 3, rows, :]
        if index < first_u:
            return r.o.at[index - 6, rows, span]
        if index < first_dg:
            return r.rcv_u.at[index - first_u, rows, :]
        if index < first_do:
            return r.rcv_dg.at[index - first_dg, rows, :]
        if index < first_dqkv:
            return r.rcv_do.at[index - first_do, rows, :]
        n = index - first_dqkv
        return r.dqkv.at[n // 3, n % 3, rows, span]

    link = PairLink(place, r.relay, (r.x_send, r.x_recv, r.far_send, r.far_recv, r.relay_send, r.relay_recv), targets, (6, 7, first_do, first_do + 1))
    forward_order = tuple(range(first_dg))
    ffn_order = tuple(range(first_dg, first_do))
    do_order = tuple(range(first_do, first_dqkv))
    dqkv_order = tuple(range(first_dqkv, first_dqkv + 6))
    my_rows = pl.ds(pl.multiple_of(core * z.tokens, z.tokens), z.tokens)
    their_rows = pl.ds(pl.multiple_of((1 - core) * z.tokens, z.tokens), z.tokens)
    my_feats = pl.ds(pl.multiple_of(half * feats, feats), feats)

    def share_rows(n):
        return pl.ds(pl.multiple_of(n * share, share), share)

    gathers = [
        Gather(
            place, r.g.at[3 * n:3 * n + 3], r.every_g.at[n],
            (r.g_right.at[n], r.g_left.at[n], r.g_sem.at[n], r.g_local.at[n:n + 1]),
        )
        for n in range(3)
    ]
    gather_o = Gather(place, r.o, r.every_o, (r.o_right, r.o_left, r.o_sem, r.o_local))
    exchange_d = Exchange(place, lambda n: r.dt.at[share_rows(n), :], r.every_d, (r.d_send, r.d_recv, r.d_local))
    exchange_c = Exchange(place, lambda n: r.dt.at[share_rows(n), :], r.every_c, (r.c_send, r.c_recv, r.c_local))
    gather_u = Gather(place, r.du.at[SLOTS - SHARED:SLOTS], r.every_u, (r.u_right, r.u_left, r.u_sem, r.u_local))
    exchange_b = Exchange(place, lambda n: r.dt.at[share_rows(n), 0:length], r.every_b, (r.b_send, r.b_recv, r.b_local))
    exchange_flag = Exchange(place, lambda n: r.wide, r.every_flag, (r.flag_send, r.flag_recv, r.flag_local))
    exchange_flag.start()

    def local_copy(src, dst, n):
        return pltpu.make_async_copy(src, dst, r.in_local.at[n])

    def core_half(src, dst, n):
        return remote(src, dst, r.in_send.at[n], r.in_recv.at[n], place.core_peer)

    def x_copy(i):
        return remote(r.x2.at[i], r.xa.at[i, my_rows, :], r.y_send.at[i], r.y_recv.at[i], place.across)

    def e_copy(i):
        return remote(r.x2.at[i], r.e_in.at[i, my_rows, :], r.y_send.at[i], r.y_recv.at[i], place.across)

    def start_half(src_ref, dst_ref, first):
        for i in range(seqs):
            local_copy(src_ref.at[i, :, my_feats], dst_ref.at[i, my_rows, :], first + i).start()
            core_half(src_ref.at[i, :, my_feats], dst_ref.at[i, my_rows, :], first + i).start()

    def ordered_halves(raw_ref, dst_ref, first):
        for i in range(seqs):
            local_copy(raw_ref.at[i, my_rows, :], raw_ref.at[i, my_rows, :], first + i).wait()
            core_half(raw_ref.at[i, my_rows, :], raw_ref.at[i, my_rows, :], first + i).wait()
        for i in range(seqs):
            mixed = raw_ref[i].astype(F32) * (1.0 - swap) + raw_ref[1 - i].astype(F32) * swap
            dst_ref[i] = mixed.astype(BF16)

    def pass_half(dst_ref, n, i):
        core_half(dst_ref.at[i, my_rows, :], dst_ref.at[i, my_rows, :], n).start()
        core_half(dst_ref.at[i, my_rows, :], dst_ref.at[i, my_rows, :], n).wait()

    def sq_copy(n):
        return remote(r.snd_sq.at[n], r.rcv_sq.at[n], r.sq_send.at[n], r.sq_recv.at[n], place.pair)

    def core_copy(n):
        return remote(r.snd_br.at[n], r.rcv_br.at[n], r.core_send.at[n], r.core_recv.at[n], place.core_peer)

    def core_rows(i):
        return remote(r.snd_br.at[2 + i, their_rows, :], r.rcv_half.at[i], r.core_send.at[2 + i], r.core_recv.at[2 + i], place.core_peer)

    def row_copy(n, peer):
        return remote(r.snd_row.at[n], r.rcv_row.at[n], r.row_send.at[n], r.row_recv.at[n], peer)

    def db_copy(n):
        return remote(r.snd_db.at[n], r.rcv_db.at[n], r.db_send.at[n], r.db_recv.at[n], place.core_peer)

    def da_rows(i):
        return remote(r.snd_db.at[2 + i, their_rows, :], r.rcv_half.at[i], r.db_send.at[2 + i], r.db_recv.at[2 + i], place.core_peer)

    def ready(n):
        pl.semaphore_signal(r.go_sem.at[n], inc=1, device_id=place.pair, device_id_type=MESH)

    def wait_ready(n):
        pl.semaphore_wait(r.go_sem.at[n], 1)

    out_sems = (r.out_send, r.out_recv, r.out_local)
    emit_x1 = Emitter(place, r.layer_out, r.stage.at[0], swap, out_sems, 0)
    emit_x2 = Emitter(place, r.layer_out, r.stage.at[1], swap, out_sems, 2)
    emit_e1 = Emitter(place, r.input_grad, r.stage.at[2], swap, out_sems, 4)
    emit_e0 = Emitter(place, r.input_grad, r.stage.at[3], swap, out_sems, 6)
    theirs = pl.multiple_of((1 - half) * mine, mine)
    ours = pl.multiple_of(half * mine, mine)

    def dg_part(slot):
        r.snd_dg[slot] = mm(r.e_in[slot_block(slot)[0]], slot_weight(slot, r.wd)).astype(BF16)

    def dg_source(slot):
        return lambda rows: r.snd_dg.at[slot, rows, :]

    def transposed(src_ref):
        for i in range(seqs):
            r.dt[:, i * length:(i + 1) * length] = jnp.transpose(src_ref[i].astype(F32)).astype(BF16)

    @pl.when(place.block == 0)
    def _():
        start_half(r.x0, r.xf, 0)
        ordered_halves(r.xf, r.xa, 0)

    @pl.when(place.block == 1)
    def _():
        start_half(r.c0, r.dc, 2)
        loaded(3)
        ordered_halves(r.dc, r.e_in, 2)
        for slot in range(SLOTS):
            dg_part(slot)
        transposed(r.e_in)
        exchange_d.start()
        link.forward(forward_order[:6])
        link.start_whole(first_dg, dg_source(0))
        link.forward(forward_order[6:8])
        link.start_whole(first_dg + 1, dg_source(1))
        link.forward(forward_order[8:])
        link.start_whole(first_dg + 2, dg_source(2))

    for i in range(seqs):
        @pl.when(place.block == 1)
        def _():
            x_copy(i).wait_recv()
            if i == 1:
                ready(0)
            pass_half(r.xa, i, i)

        x = r.xa[i].astype(F32)
        r.snd_sq[i] = to_row(jnp.sum(x * x, axis=-1, keepdims=True))
        sq_copy(i).start()
        r.xg[i] = (x * gain_a).astype(BF16)
        if i == 0:
            loaded(0)
        for t in range(3):
            r.snd_qkv[i, t] = mm(r.xg[i], r.wqkv[t, :, pl.ds(theirs, mine)]).astype(BF16)
            source = lambda rows, i=i, t=t: r.snd_qkv.at[i, t, rows, :]

            @pl.when(place.block == 0)
            def _():
                link.start(3 * i + t, source)

            @pl.when(place.block == 1)
            def _():
                if i == 0:
                    link.start_whole(t, source)
                else:
                    link.start_near(3 + t, source)

    @pl.when(place.block == 1)
    def _():
        wait_ready(0)
        for t in range(3):
            link.start_far(3 + t)

    for i in range(seqs):
        for t in range(3):
            r.own_qkv[i, t] = mm(r.xg[i], r.wqkv[t, :, pl.ds(ours, mine)])

    cosine, sine = r.cosine[...], r.sine[...]
    scale = HEAD_DIM ** (-0.5)
    causal = lax.broadcasted_iota(jnp.int32, (length, length), 0) >= lax.broadcasted_iota(jnp.int32, (length, length), 1)
    for i in range(seqs):
        sq_copy(i).wait_recv()
        factor = lax.rsqrt((from_row(r.snd_sq[i]) + from_row(r.rcv_sq[i])) * (1.0 / z.width) + EPSILON)
        r.ra[i] = spread(factor, 128)
        if i == 0:
            @pl.when(place.block == 0)
            def _():
                for t in range(3):
                    link.wait(t)

            @pl.when(place.block == 1)
            def _():
                for t in range(3):
                    link.wait_whole(t)
        else:
            for t in range(3):
                link.wait(3 + t)
        for j in range(z.heads):
            span = pl.ds(j * HEAD_DIM, HEAD_DIM)
            raw = [(r.own_qkv[i, t, :, span] + r.rcv_qkv[i, t, :, span].astype(F32)) * factor for t in range(3)]
            q_j = (raw[0] * cosine + turned(raw[0]) * sine).astype(BF16)
            k_j = (raw[1] * cosine + turned(raw[1]) * sine).astype(BF16)
            v_j = raw[2].astype(BF16)
            r.q[i, :, span], r.k[i, :, span], r.v[i, :, span] = q_j, k_j, v_j
            scores = jnp.where(causal, mm_nt(q_j, k_j) * scale, -1e30)
            exponent = jnp.exp(scores - jnp.max(scores, axis=-1, keepdims=True))
            probs = exponent / jnp.sum(exponent, axis=-1, keepdims=True)
            r.p[i, j] = probs
            r.o[i, :, pl.ds(pl.multiple_of(ours + j * HEAD_DIM, HEAD_DIM), HEAD_DIM)] = mm(probs.astype(BF16), v_j).astype(BF16)
        link.start(6 + i, lambda rows, i=i: r.o.at[i, rows, pl.ds(ours, mine)])

    loaded(1)
    for i in range(seqs):
        link.wait(6 + i)
        r.snd_br[i] = mm_nt(r.o[i], r.wo[...]).astype(BF16)
        core_copy(i).start()

    @pl.when(place.block == 1)
    def _():
        for slot in DG_MIDDLE:
            link.start(first_dg + slot, dg_source(slot))

    gather_o.step(1)

    def slot_start(slot):
        part = mm(r.xg[slot_block(slot)[0]], slot_weight(slot, r.wu))
        r.u[slot] = part
        r.snd_u[slot] = part.astype(BF16)
        link.start(first_u + slot, lambda rows: r.snd_u.at[slot, rows, :])

    loaded(2)
    for i, slots in enumerate((NARROW, WIDE)):
        core_copy(i).wait_recv()
        r.xf[i] = (r.xa[i].astype(F32) + (r.snd_br[i].astype(F32) + r.rcv_br[i].astype(F32))).astype(BF16)
        x = r.xf[i].astype(F32)
        r.snd_sq[2 + i] = to_row(jnp.sum(x * x, axis=-1, keepdims=True))
        sq_copy(2 + i).start()
        r.xg[i] = (x * gain_f).astype(BF16)
        for slot in slots:
            slot_start(slot)

    @pl.when(place.block == 1)
    def _():
        for slot in DG_LATE:
            link.start(first_dg + slot, dg_source(slot))

    emit_x1.prepare([r.xf[i, my_rows, :] for i in range(seqs)])
    factors = {}

    def row_factor(i):
        sq_copy(2 + i).wait_recv()
        factors[i] = lax.rsqrt((from_row(r.snd_sq[2 + i]) + from_row(r.rcv_sq[2 + i])) * (1.0 / z.width) + EPSILON)
        r.rf[i] = spread(factors[i], 128)

    def activate(slot):
        link.wait(first_u + slot)
        value = (r.u[slot] + r.rcv_u[slot].astype(F32)) * factors[slot_block(slot)[0]]
        squared = value * value
        bent = jnp.tanh(GELU_C * (value + GELU_A * (squared * value)))
        slope = 0.5 * (1.0 + bent) + 0.5 * value * (1.0 - bent * bent) * (GELU_C * (1.0 + 3.0 * GELU_A * squared))
        r.u[slot] = value
        r.rcv_u[slot] = mask_slot(slot, slope, flag).astype(BF16)
        g_k = mask_slot(slot, 0.5 * value * (1.0 + bent), flag).astype(BF16)
        r.g[G_PLACE[slot]] = g_k
        return mm_nt(g_k, slot_weight(slot, r.wd))

    def finish_rows(i):
        core_rows(i).wait_recv()
        total = r.snd_br[2 + i, my_rows, :].astype(F32) + r.rcv_half[i].astype(F32)
        r.x2[i] = (r.xf[i, my_rows, :].astype(F32) + total).astype(BF16)

        @pl.when(place.block == 0)
        def _():
            x_copy(i).start()

    @pl.when(place.block == 0)
    def _():
        loaded(3)

    row_factor(0)
    r.snd_br[2] = (activate(0) + activate(1)).astype(BF16)
    core_rows(0).start()
    gather_o.step(2)
    row_factor(1)
    total = activate(2) + activate(3)
    finish_rows(0)
    for slot in WIDE[2:]:
        total = total + activate(slot)
    r.snd_br[3] = total.astype(BF16)
    core_rows(1).start()
    r.g[1] = r.g[1] + r.g[SLOTS - 1]
    finish_rows(1)
    emit_x2.prepare([r.x2[i] for i in range(seqs)])
    for part in gathers:
        part.step(1)

    def normed_again():
        for i in range(seqs):
            r.xg[i] = (r.xf[i].astype(F32) * r.rf[i][:, :1] * gain_f).astype(BF16)

    @pl.when(place.block == 0)
    def _():
        normed_again()
        r.dt[:, :length] = jnp.transpose(r.xg[1].astype(F32)).astype(BF16)
        exchange_b.start()

    def piece(chunk, target):
        column = pl.multiple_of(lax.rem(chunk, 8) * unit, unit)
        return r.wud.at[lax.div(chunk, 8), share_rows(target), pl.ds(column, unit)]

    per = max(length // share, 1)

    def slots(way, n):
        ref = r.snd_qkv if way > 0 else r.rcv_qkv
        at = lax.div(n, per)
        return ref.at[lax.div(at, 3), lax.rem(at, 3), share_rows(lax.rem(n, per)), :]

    def intake(n):
        return r.snd_u.at[lax.div(n, per), share_rows(lax.rem(n, per)), :]

    def which(number):
        first = 8 - SHARED
        after = min(number // first, 1) if isinstance(number, int) else jnp.minimum(lax.div(number, first), 1)
        return number + SHARED * after * (1 - place.block)

    scatter = Scatter(
        place, piece, which, 14 - SHARED * (1 - place.block), {1: r.from_left, -1: r.from_right}, {1: r.sum_right, -1: r.sum_left}, {1: r.got_left, -1: r.got_right},
        slots, 6 * per, intake, r.intake_sem, 14,
    )

    @pl.when(place.block == 0)
    def _():
        gather_o.rest(3)
        link.forward(forward_order[3:first_u])
        link.forward(tuple(first_dg + slot for slot in DG_MIDDLE))
        link.forward(forward_order[first_u:])
        for part in gathers:
            part.step(2)
        link.forward(tuple(first_dg + slot for slot in DG_LATE))
        link.forward(do_order + dqkv_order)
        for part in gathers:
            part.rest(3)
        for i, slot_list in enumerate((NARROW, WIDE)):
            e_copy(i).wait_recv()
            if i == 1:
                ready(1)
            pass_half(r.e_in, 2 + i, i)
            for slot in slot_list:
                dg_part(slot)
                if i == 0:
                    link.start_whole(first_dg + slot, dg_source(slot))
                else:
                    link.start_near(first_dg + slot, dg_source(slot))
                if i == 1 and slot == WIDE[1]:
                    wait_ready(1)
                    for sent in WIDE[:2]:
                        link.start_far(first_dg + sent)
                if i == 1 and slot > WIDE[1]:
                    link.start_far(first_dg + slot)
        exchange_b.finish()
        transposed(r.e_in)
        exchange_d.start()
        link.finish(forward_order[:3])

    @pl.when(place.block == 1)
    def _():
        link.finish_whole(forward_order[:3])

    link.finish(forward_order[3:])

    def hidden_back(slot):
        @pl.when(place.block == 0)
        def _():
            (link.wait_whole if slot in NARROW else link.wait)(first_dg + slot)

        @pl.when(place.block == 1)
        def _():
            (link.wait_whole if slot in DG_STRAIGHT else link.wait)(first_dg + slot)

        grad = r.snd_dg[slot].astype(F32) + r.rcv_dg[slot].astype(F32)
        du_k = (grad * r.rcv_u[slot].astype(F32)).astype(BF16)
        r.du[slot] = du_k
        return mm_nt(du_k, slot_weight(slot, r.wu)), jnp.sum(du_k.astype(F32) * r.u[slot], axis=-1, keepdims=True)

    def flipped(value):
        return jnp.transpose(value.astype(F32)).astype(BF16)

    def up_grads(blocks):
        wide = flipped(r.xg[1])
        for block in blocks:
            part = mm(wide, r.du[2 + block])
            if block < 2:
                part = part + mm_tn(r.xg[0], r.du[block])
            r.wu[:, block * unit:(block + 1) * unit] = part.astype(BF16)
            if block < AHEAD:
                scatter.edges(block)

    def core_sum_start(i, slot_list):
        total = row = None
        for slot in slot_list:
            more, more_row = hidden_back(slot)
            total, row = (more, more_row) if total is None else (total + more, row + more_row)

            if i == 1 and slot - 2 < 8 - SHARED:
                @pl.when(place.block == 0)
                def _(slot=slot):
                    up_grads((slot - 2,))

        if i == 1:
            @pl.when(place.block == 0)
            def _():
                gather_u.step(1)

        r.snd_db[i] = total.astype(BF16)
        db_copy(i).start()
        r.snd_row[i] = to_row(row)
        row_copy(i, place.core_peer).start()

    def ffn_done(i):
        db_copy(i).wait_recv()
        row_copy(i, place.core_peer).wait_recv()
        mean = (from_row(r.snd_row[i]) + from_row(r.rcv_row[i])) * (1.0 / z.width)
        grad = r.snd_db[i].astype(F32) + r.rcv_db[i].astype(F32)
        factor = r.rf[i][:, :1]
        scaled = r.xf[i].astype(F32) * factor
        new = r.e_in[i].astype(F32) + factor * (grad * gain_f - scaled * mean)
        r.e[i] = new
        r.dc[i] = new.astype(BF16)
        core_copy(i).wait_send()
        r.snd_br[i, :, :mine] = mm(r.dc[i], r.wo[:, pl.ds(theirs, mine)]).astype(BF16)
        link.start(first_do + i, lambda rows: r.snd_br.at[i, rows, 0:mine])
        r.own_qkv[i, 0] = mm(r.dc[i], r.wo[:, pl.ds(ours, mine)])
        return jnp.sum(grad * scaled, axis=0, keepdims=True)

    core_sum_start(0, NARROW)
    gain_f_sum = ffn_done(0)
    core_sum_start(1, WIDE)
    gain_f_sum = gain_f_sum + ffn_done(1)
    r.gains[...] = jnp.zeros_like(r.gains)
    r.gains[1:2, :] = 0.5 * gain_f_sum
    emit_e1.prepare([r.dc[i, my_rows, :] for i in range(seqs)])

    @pl.when(place.block == 1)
    def _():
        exchange_d.finish()
        transposed(r.dc)
        exchange_c.start()

    rows = slice(0, share)
    inner = (me > 0) & (me < planes - 1)

    def grads_ready():
        exchange_flag.finish()
        for n in range(SLOTS):
            r.u[n, rows, :] = jnp.zeros_like(r.u[n, rows, :])
        flags_copy = pltpu.make_async_copy(r.every_flag, r.flags, r.block_sem.at[0])
        flags_copy.start()
        flags_copy.wait()

    def planes_of(part, first, last):
        def body(k, carry):
            part(jnp.where(me < planes // 2, lax.rem(me + k, planes), lax.rem(me + planes - k, planes)))
            return carry
        lax.fori_loop(lax.div(first * planes, 4), lax.div(last * planes, 4), body, 0)

    def fetched(*pairs):
        copies = [pltpu.make_async_copy(src, dst, r.block_sem.at[at]) for at, (src, dst) in enumerate(pairs)]
        for copy in copies:
            copy.start()
        for copy in copies:
            copy.wait()

    def down_part(n):
        block_g = r.snd_dg.at[0:SLOTS - 1]
        fetched(*((r.every_g.at[k, n], r.snd_dg.at[3 * k:3 * k + 3]) for k in range(3)), (r.every_d.at[n], r.block_d))
        on = r.flags[n][:1, :1]
        shared = block_g[1].astype(F32)
        upper, lower = (shared * on).astype(BF16), (shared * (1.0 - on)).astype(BF16)
        narrow, wide = r.block_d[:, :length], r.block_d[:, length:]
        for block in range(8):
            right = upper if block == 4 else block_g[2 + block if block < 4 else 1 + block]
            part = mm(wide, right)
            if block < 2:
                part = part + mm(narrow, block_g[0] if block == 0 else lower)
            r.u[block, rows, :] = r.u[block, rows, :] + part

    def out_part(n):
        fetched((r.every_o.at[n], r.xf), (r.every_c.at[n], r.block_c))
        for side in range(2):
            span = slice(side * unit, (side + 1) * unit)
            part = mm(r.block_c[:, :length], r.xf[0, :, span]) + mm(r.block_c[:, length:], r.xf[1, :, span])
            r.u[8 + side, rows, :] = r.u[8 + side, rows, :] + part

    def gather_done():
        for part in gathers:
            part.settle_all()

    def up_part(n):
        block_u, block_b = r.rcv_dg.at[0:SHARED], r.rcv_dg.at[SHARED, rows, 0:length]
        fetched((r.every_u.at[n], block_u), (r.every_b.at[n], block_b))
        for k in range(SHARED):
            r.own_qkv[k // 3, k % 3, rows, :] = r.own_qkv[k // 3, k % 3, rows, :] + mm(block_b[...], block_u[k])

    for i in range(seqs):
        link.wait(first_do + i)
        row = jnp.zeros((length, 1), F32)
        for j in range(z.heads):
            span = pl.ds(j * HEAD_DIM, HEAD_DIM)
            do_j = (r.own_qkv[i, 0, :, span] + r.rcv_do[i, :, span].astype(F32)).astype(BF16)
            q_j, k_j, v_j, probs = r.q[i, :, span], r.k[i, :, span], r.v[i, :, span], r.p[i, j]
            dp = mm_nt(do_j, v_j)
            dv = mm_tn(probs.astype(BF16), do_j)
            ds = (probs * (dp - jnp.sum(probs * dp, axis=-1, keepdims=True))).astype(BF16)
            dq = mm(ds, k_j) * scale
            dk = mm_tn(ds, q_j) * scale
            row = row + jnp.sum(dq * q_j.astype(F32) + dk * k_j.astype(F32) + dv * v_j.astype(F32), axis=-1, keepdims=True)
            at = pl.ds(pl.multiple_of(ours + j * HEAD_DIM, HEAD_DIM), HEAD_DIM)
            r.dqkv[i, 0, :, at] = (dq * cosine - turned(dq) * sine).astype(BF16)
            r.dqkv[i, 1, :, at] = (dk * cosine - turned(dk) * sine).astype(BF16)
            r.dqkv[i, 2, :, at] = dv.astype(BF16)
        r.snd_row[2 + i] = to_row(row)
        row_copy(2 + i, place.pair).start()
        for t in range(3):
            link.start(first_dqkv + 3 * i + t, lambda rows, i=i, t=t: r.dqkv.at[i, t, rows, pl.ds(ours, mine)])

    def first_grads():
        link.finish_whole(ffn_order[:len(NARROW)])
        link.finish(ffn_order[len(NARROW):])
        exchange_d.finish()
        transposed(r.dc)
        exchange_c.start()
        grads_ready()
        gather_done()

    @pl.when((place.block == 0) & inner)
    def _():
        first_grads()
        planes_of(down_part, 0, 1)

    for i in range(seqs):
        if i == 1:
            @pl.when(place.block == 0)
            def _():
                gather_u.step(2)

        part = jnp.zeros((length, feats), F32)
        for t in range(3):
            link.wait(first_dqkv + 3 * i + t)
            part = part + mm_nt(r.dqkv[i, t], r.wqkv[t])
        r.snd_db[2 + i] = part.astype(BF16)
        da_rows(i).start()
        row_copy(2 + i, place.pair).wait_recv()
        r.snd_row[4 + i] = r.snd_row[2 + i] + r.rcv_row[2 + i]
        row_copy(4 + i, place.core_peer).start()

    @pl.when(place.block == 0)
    def _():
        for i in range(seqs):
            x_copy(i).wait_send()

    gain_a_sum = jnp.zeros((1, feats), F32)
    for i in range(seqs):
        da_rows(i).wait_recv()
        row_copy(4 + i, place.core_peer).wait_recv()
        r.snd_row[6 + i] = (r.snd_row[4 + i] + r.rcv_row[4 + i]) * (1.0 / z.width)
        mean = from_row(r.snd_row[6 + i, :, my_rows])
        grad = r.snd_db[2 + i, my_rows, :].astype(F32) + r.rcv_half[i].astype(F32)
        factor = r.ra[i, my_rows, :][:, :1]
        scaled = r.xa[i, my_rows, :].astype(F32) * factor
        r.x2[i] = (r.e[i, my_rows, :] + factor * (grad * gain_a - scaled * mean)).astype(BF16)
        gain_a_sum = gain_a_sum + jnp.sum(grad * scaled, axis=0, keepdims=True)

        @pl.when(place.block == 1)
        def _():
            e_copy(i).start()

    r.gains[0:1, :] = gain_a_sum
    emit_e0.prepare([r.x2[i] for i in range(seqs)])

    def qkv_grad():
        for i in range(seqs):
            r.xg[i] = (r.xa[i].astype(F32) * r.ra[i][:, :1] * gain_a).astype(BF16)
        first, second = flipped(r.xg[0]), flipped(r.xg[1])
        for t in range(3):
            r.wd[:, t * z.cols:(t + 1) * z.cols] = (mm(first, r.dqkv[0, t]) + mm(second, r.dqkv[1, t])).astype(BF16)

    @pl.when(place.block == 1)
    def _():
        gather_o.rest(3)
        for part in gathers:
            part.step(2)
        normed_again()
        up_grads(range(8))
        qkv_grad()
        link.forward(ffn_order[len(NARROW):])
        scatter.turn(0)
        link.forward(do_order)
        link.forward(dqkv_order)
        scatter.turn(1)
        gathers[0].rest(3)
        scatter.turn(2)
        scatter.turn(3)
        gathers[1].rest(3)

    @pl.when(place.block == 0)
    def _():
        qkv_grad()
        for number in range(8 - SHARED, AHEAD):
            scatter.edges(number)

        @pl.when(jnp.logical_not(inner))
        def _():
            first_grads()
            planes_of(down_part, 0, 4)

        @pl.when(inner)
        def _():
            planes_of(down_part, 1, 4)

        gather_o.settle_all()
        gather_u.own().wait()
        for k in range(SHARED):
            r.own_qkv[k // 3, k % 3, rows, :] = jnp.zeros_like(r.own_qkv[k // 3, k % 3, rows, :])
        for turn in range(4):
            scatter.turn(turn)
            if turn == 0:
                gather_u.rest(3)

            @pl.when(inner)
            def _(turn=turn):
                planes_of(up_part, turn, turn + 1)

    @pl.when(place.block == 1)
    def _():
        link.finish_whole(tuple(first_dg + slot for slot in DG_STRAIGHT))
        link.finish(tuple(first_dg + slot for slot in DG_MIDDLE + DG_LATE))
        grads_ready()

    emit_x1.start(0)
    emit_x2.start(1)
    emit_e1.start(1)
    emit_e0.start(0)
    gains_copy = remote(r.gains, r.core_gains, r.pair_send.at[0], r.pair_recv.at[0], place.core_peer)
    gains_copy.start()
    scatter.turn(4)
    gains_copy.wait()
    r.every_gain[me] = r.gains[...] + r.core_gains[...]
    exchange_gain = Exchange(place, lambda n: r.every_gain.at[me], r.every_gain, (r.gain_send, r.gain_recv, None))
    for n in range(1, planes):
        exchange_gain.copy(n).start()

    def grad_copy(n):
        dst = r.down_grad.at[:, n * unit:(n + 1) * unit] if n < 8 else r.out_grad.at[:, (n - 8) * unit:(n - 7) * unit]
        return pltpu.make_async_copy(r.u.at[n, rows, :], dst, r.grad_sem.at[n])

    def shared_copy(k):
        dst = r.up_grad.at[:, (8 - SHARED + k) * unit:(9 - SHARED + k) * unit]
        return pltpu.make_async_copy(r.own_qkv.at[k // 3, k % 3, rows, :], dst, r.shared_sem.at[k])

    def total_slot(number):
        at = lax.rem(number, 4)
        column = pl.multiple_of(lax.rem(at, 2) * unit, unit)
        return r.e.at[lax.div(at, 2), rows, pl.ds(column, unit)]

    def total_copy(number, action):
        chunk = which(number)
        src, sem = total_slot(number), r.total_sem.at[lax.rem(number, 4)]

        @pl.when(chunk < 8)
        def _():
            dst = r.up_grad.at[:, pl.ds(pl.multiple_of(chunk * unit, unit), unit)]
            action(pltpu.make_async_copy(src, dst, sem))

        @pl.when(chunk >= 8)
        def _():
            column = pl.multiple_of(lax.rem(chunk, 2) * unit, unit)
            dst = r.qkv_grad.at[lax.div(chunk - 8, 2), :, pl.ds(column, unit)]
            action(pltpu.make_async_copy(src, dst, sem))

    def final(number, carry):
        @pl.when(number >= 4)
        def _():
            total_copy(number - 4, lambda copy: copy.wait())

        scatter.last(number, total_slot(number))
        total_copy(number, lambda copy: copy.start())
        return carry

    finals = (
        {5: 3, **{turn: turn - 1 for turn in range(6, 16 - SHARED)}},
        {5: 1, 6: 2, 7: 3, 8: 4, 9: 5, 10: 6, 11: 7, 12: 9, 13: 11, 14: 13, 15: 14},
        {11: 8, 12: 10, 13: 11, 14: 13, 15: 14},
    )

    def finals_by(turn):
        first, inside, outside = (max([count for at, count in table.items() if at <= turn], default=0) for table in finals)
        return jnp.where(place.block == 0, first, jnp.where(inner, inside, outside))

    def once(block, where, body):
        pl.when((place.block == block) & (inner if where else jnp.logical_not(inner)))(body)

    def all_planes(*parts):
        for part in parts:
            planes_of(part, 0, 4)

    def edge_parts():
        gather_u.settle(1, gather_u.last - 1)
        planes_of(up_part, 0, 3)
        exchange_c.finish()
        planes_of(out_part, 0, 4)
        gather_u.settle(gather_u.last, gather_u.last)
        planes_of(up_part, 3, 4)

    def late_edge_parts():
        gather_done()
        gather_o.settle_all()
        exchange_c.finish()
        all_planes(down_part, out_part)

    def inner_start():
        gather_done()
        gather_o.settle_all()
        exchange_c.finish()

    def out_start():
        exchange_c.finish()
        planes_of(out_part, 0, 2)

    for turn in range(5, max(16, len(scatter.turns()))):
        scatter.turn(turn)
        if turn == 5:
            once(0, False, edge_parts)
        if turn == 12:
            once(1, False, late_edge_parts)
        lax.fori_loop(finals_by(turn - 1), finals_by(turn), final, 0)
        if turn == 5:
            pl.when(place.block == 1)(lambda: gathers[2].rest(3))
            once(0, True, out_start)
        if turn == 6:
            once(0, True, lambda: planes_of(out_part, 2, 4))
        if turn == 7:
            once(1, True, inner_start)
        if 7 <= turn < 11:
            once(1, True, lambda turn=turn: planes_of(down_part, turn - 7, turn - 6))
        if turn == 7:
            @pl.when(place.block == 0)
            def _():
                for n in range(SLOTS):
                    grad_copy(n).start()
                for k in range(SHARED):
                    shared_copy(k).start()
        if turn == 11:
            once(1, True, lambda: planes_of(out_part, 0, 4))
        if turn == 12:
            @pl.when(place.block == 1)
            def _():
                for n in range(SLOTS):
                    grad_copy(n).start()
    for n in range(1, planes):
        source = lax.rem(me + planes - n, planes)
        slot = r.every_gain.at[source]
        remote(slot, slot, r.gain_send.at[n], r.gain_recv.at[n], place.pair).wait_recv()
        exchange_gain.copy(n).wait_send()
    gain_total = r.every_gain[0]
    for n in range(1, planes):
        gain_total = gain_total + r.every_gain[n]
    own_first = (place.at[1] * 2 + core) * (feats // (2 * planes))
    r.gain_grads[...] = pltpu.roll(gain_total, lax.rem(feats - own_first, feats), 1)

    scatter.finish()
    for back in range(1, 5):
        total_copy(scatter.total - back, lambda copy: copy.wait())

    @pl.when(place.block == 0)
    def _():
        for k in range(SHARED):
            shared_copy(k).wait()

    for n in range(SLOTS):
        grad_copy(n).wait()
    for n in range(4):
        sq_copy(n).wait_send()
    for i in range(seqs):
        core_rows(i).wait_send()
        row_copy(i, place.core_peer).wait_send()
        row_copy(2 + i, place.pair).wait_send()
        row_copy(4 + i, place.core_peer).wait_send()
        db_copy(i).wait_send()
        da_rows(i).wait_send()
    link.finish(do_order + dqkv_order)

    @pl.when(place.block == 0)
    def _():
        link.finish_forward(forward_order[3:] + tuple(first_dg + slot for slot in DG_MIDDLE + DG_LATE) + do_order + dqkv_order)

    @pl.when(place.block == 1)
    def _():
        link.finish_forward(forward_order + ffn_order[len(NARROW):] + do_order + dqkv_order)
        for i in range(seqs):
            e_copy(i).wait_send()

    for part in (*gathers, gather_o):
        part.finish()
    pl.when(place.block == 0)(gather_u.finish)
    emit_x1.finish(0)
    emit_x2.finish(1)
    emit_e1.finish(1)
    emit_e0.finish(0)


def shape(dims, kind):
    return jax.ShapeDtypeStruct(dims, kind)


ANY = pl.BlockSpec(memory_space=pl.ANY)
IN_VMEM = pl.BlockSpec(memory_space=pltpu.VMEM)


def vmem(dims, kind):
    return pltpu.VMEM(tuple(dims), kind)


def run_main(width_index, x0, c0, gain_a, gain_f, wqkv, wo, wu, wd):
    seqs, tokens, width = x0.shape
    planes = lax.axis_size("dp")
    z = Sizes(wo.shape[0], wo.shape[1], wu.shape[1], tokens)
    share, chunks = z.feats // planes, 14
    cosine, sine = rotary(z.length, HEAD_DIM)
    args = {
        "width": width_index, "x0": x0, "c0": c0, "gain_a": gain_a, "gain_f": gain_f, "cosine": cosine, "sine": sine,
        "wqkv_hbm": wqkv, "wo_hbm": wo, "wu_hbm": wu, "wd_hbm": wd,
    }
    places = {"width": pl.BlockSpec(memory_space=pltpu.SMEM)}
    places.update({name: IN_VMEM for name in ("gain_a", "gain_f", "cosine", "sine", "gain_grads")})
    row = (8, z.feats)
    outs = {
        "layer_out": shape((seqs, tokens, width), BF16), "input_grad": shape((seqs, tokens, width), BF16),
        "qkv_grad": shape((3, share, z.cols), F32), "out_grad": shape((share, z.cols), F32),
        "up_grad": shape((share, 8 * z.unit), F32), "down_grad": shape((share, 8 * z.unit), F32), "gain_grads": shape(row, F32),
        "every_g": shape((3, planes, 3, z.length, z.unit), BF16), "every_o": shape((planes, seqs, z.length, z.cols), BF16),
        "every_d": shape((planes, share, seqs * z.length), BF16), "every_c": shape((planes, share, seqs * z.length), BF16),
        "every_u": shape((planes, SHARED, z.length, z.unit), BF16), "every_b": shape((planes, share, z.length), BF16),
        "every_flag": shape((planes, 8, 128), F32),
        "from_left": shape((planes, chunks, share, z.unit), BF16), "from_right": shape((planes, chunks, share, z.unit), BF16),
    }
    state, half_state, heads_state = (seqs, z.length, z.feats), (seqs, tokens, z.feats), (seqs, z.length, z.mine)
    slots, qkv, messages = (SLOTS, z.length, z.unit), (seqs, 3, z.length, z.mine), 12 + 2 * seqs + 2 * SLOTS
    small, factor, pair = (8, 8, z.length), (seqs, z.length, 128), (4, z.length, z.feats)
    scratch = {"wqkv": vmem(wqkv.shape, BF16), "wo": vmem(wo.shape, BF16), "wud": vmem((2, *wu.shape), BF16)}
    for dims, kind, group in (
        (state, BF16, "xa xf xg e_in dc"), (state, F32, "e"), (half_state, BF16, "x2 rcv_half"),
        (heads_state, BF16, "q k v rcv_do"),
        ((seqs, z.heads, z.length, z.length), F32, "p"), ((seqs, z.length, z.cols), BF16, "o"), (factor, F32, "ra rf"),
        (slots, F32, "u"), (slots, BF16, "g snd_u rcv_u du snd_dg rcv_dg"), (qkv, F32, "own_qkv"), (qkv, BF16, "snd_qkv rcv_qkv"),
        ((4, 8, z.length), F32, "snd_sq rcv_sq"), (small, F32, "snd_row rcv_row"), (pair, BF16, "snd_br snd_db"),
        ((2, z.length, z.feats), BF16, "rcv_br rcv_db"), ((z.feats, seqs * z.length), BF16, "dt"), ((4, *half_state), BF16, "stage"),
        ((seqs, 3, z.length, z.cols), BF16, "dqkv"), ((messages, z.length - DIRECT_ROWS, z.mine), BF16, "relay"),
        ((8, 128), F32, "wide"), ((planes, 8, 128), F32, "flags"), ((share, seqs * z.length), BF16, "block_d block_c"),
        (row, F32, "gains core_gains"), ((planes, *row), F32, "every_gain"),
    ):
        scratch.update({name: vmem(dims, kind) for name in group.split()})
    for count, group in (
        (4, "load_sem sq_send sq_recv core_send core_recv db_send db_recv in_send in_recv in_local block_sem"),
        (messages, "x_send x_recv far_send far_recv relay_send relay_recv"), (6, "row_send row_recv total_sem"),
        (2, "y_send y_recv"), (8, "out_send out_recv out_local"), (1, "o_local d_local c_local flag_local pair_send pair_recv"),
        (planes, "o_right o_left o_sem d_send d_recv c_send c_recv flag_send flag_recv gain_send gain_recv"),
        (2 * planes, "intake_sem"), (planes * chunks, "got_left got_right"), (4 * planes, "sum_right sum_left"), (SHARED, "shared_sem"),
        (planes, "u_right u_left u_sem b_send b_recv"), (1, "u_local b_local"), (SLOTS, "grad_sem"),
    ):
        scratch.update({name: pltpu.SemaphoreType.DMA((count,)) for name in group.split()})
    scratch["g_local"] = pltpu.SemaphoreType.DMA((3,))
    scratch.update({name: pltpu.SemaphoreType.DMA((3, planes)) for name in ("g_right", "g_left", "g_sem")})
    scratch["go_sem"] = pltpu.SemaphoreType.REGULAR((2,))
    results = pl.pallas_call(
        functools.partial(main_kernel, (*args, *outs, *scratch)),
        out_shape=tuple(outs.values()),
        in_specs=[places.get(name, ANY) for name in args],
        out_specs=tuple(places.get(name, ANY) for name in outs),
        scratch_shapes=list(scratch.values()),
        compiler_params=pltpu.CompilerParams(collective_id=1, has_side_effects=True, vmem_limit_bytes=VMEM_LIMIT),
        name="main",
    )(*args.values())
    return dict(zip(outs, results))


OUTPUTS = ("layer_out", "input_grad", "qkv_grad", "out_grad", "up_grad", "down_grad")
PARTS = 2


def deliver_kernel(*refs):
    count = len(OUTPUTS)
    gains, sources, (attn_out, ffn_out), targets = refs[0], refs[1:1 + count], refs[1 + count:3 + count], refs[3 + count:3 + 2 * count]
    held, load_sem, save_sem = refs[3 + 2 * count:-2], refs[-2], refs[-1]
    loads, saves = [], []
    for n, (src, mid, dst) in enumerate(zip(sources, held, targets)):
        rows = src.shape[-2] // PARTS
        lead = (slice(None),) * (len(src.shape) - 2)
        for part in range(PARTS):
            at = (*lead, slice(part * rows, (part + 1) * rows))
            loads.append(pltpu.make_async_copy(src.at[at], mid.at[at], load_sem.at[n * PARTS + part]))
            saves.append(pltpu.make_async_copy(mid.at[at], dst.at[at], save_sem.at[n * PARTS + part]))
    for copy in loads:
        copy.start()
    size = attn_out.shape[1]
    attn_out[...] = gains[0:1, :size]
    ffn_out[...] = gains[1:2, :size]
    for load, copy in zip(loads, saves):
        load.wait()
        copy.start()
    for copy in saves:
        copy.wait()


def local(inputs, cotangent, width_index, qkv_weight, out_weight, attn_gain, ffn_gain, up_weight, down_weight):
    found = run_main(width_index, inputs, cotangent, attn_gain, ffn_gain, qkv_weight, out_weight, up_weight, down_weight)
    sources = [found[name] for name in OUTPUTS]
    size = attn_gain.shape[0] // (2 * lax.axis_size("dp"))
    gain = jax.ShapeDtypeStruct((1, size), F32)
    attn_grad, ffn_grad, *results = pl.pallas_call(
        deliver_kernel,
        out_shape=(gain, gain, *(jax.ShapeDtypeStruct(source.shape, source.dtype) for source in sources)),
        in_specs=[IN_VMEM] + [ANY] * len(sources),
        out_specs=(IN_VMEM, IN_VMEM, *[ANY] * len(sources)),
        scratch_shapes=[vmem(source.shape, source.dtype) for source in sources] + [pltpu.SemaphoreType.DMA((len(sources) * PARTS,))] * 2,
        compiler_params=pltpu.CompilerParams(vmem_limit_bytes=VMEM_LIMIT),
        name="deliver",
    )(found["gain_grads"], *sources)
    layer_out, input_grad, qkv_grad, out_grad, up_grad, down_grad = results
    return (
        layer_out[None], input_grad[None], qkv_grad, out_grad, attn_grad.reshape(size), ffn_grad.reshape(size), up_grad, down_grad,
    )


def solution(mesh):
    in_specs = (
        P("dp", "mp", None),
        P("dp", "mp", None),
        P("dp"),
        P(None, "section", "mp"),
        P("section", "mp"),
        P("section"),
        P("section"),
        P("section", "mp"),
        P("section", "mp"),
    )
    out_specs = (
        P("section", "dp", "mp", None),
        P("section", "dp", "mp", None),
        P(None, ("section", "dp"), "mp"),
        P(("section", "dp"), "mp"),
        P(("section", "dp", "mp")),
        P(("section", "dp", "mp")),
        P(("section", "dp"), "mp"),
        P(("section", "dp"), "mp"),
    )
    return jax.shard_map(local, mesh=mesh, in_specs=in_specs, out_specs=out_specs, check_vma=False)
```
